32 devices in a mesh: dp: 16 (over z, y, core), seq: 2 (over x).
Axes of the slice: x: 2, y: 2, z: 4, core: 2. Of those that a mesh axis runs over, the one named last changes fastest.
Arguments:
- src_ids: int32 [32, 1024], P('dp', 'seq'), may hold values from 4 to 31999
- tgt_ids: int32 [32, 1024], P('dp', 'seq'), may hold values from 4 to 31999
- src_lengths: int32 [32, 32], P('dp'), may hold values from 1 to 512, as said below
- tgt_lengths: int32 [32, 32], P('dp'), may hold values from 1 to 512, as said below
- tgt_mask: int32 [32, 1024], P('dp', 'seq'), may hold values from 0 to 1
- attn_in: float32 [3, 512, 1536], P(None, 'dp'), may hold values from -0.25 to 0.25
- attn_in_m1: float32 [3, 512, 1536], P(None, 'dp'), may hold values from -7.1525574e-07 to 7.1525574e-07
- attn_in_m2: float32 [3, 512, 1536], P(None, 'dp'), may hold values from 3.3525727e-15 to 1.3829362e-14
- attn_out: float32 [3, 512, 512], P(None, 'dp'), may hold values from -1.5 to 1.5
- attn_out_m1: float32 [3, 512, 512], P(None, 'dp'), may hold values from -7.1525574e-07 to 7.1525574e-07
- attn_out_m2: float32 [3, 512, 512], P(None, 'dp'), may hold values from 3.3525727e-15 to 1.3829362e-14
- ffn_in: float32 [2, 512, 2048], P(None, 'dp'), may hold values from -0.25 to 0.25
- ffn_in_m1: float32 [2, 512, 2048], P(None, 'dp'), may hold values from -7.1525574e-07 to 7.1525574e-07
- ffn_in_m2: float32 [2, 512, 2048], P(None, 'dp'), may hold values from 3.3525727e-15 to 1.3829362e-14
- ffn_out: float32 [2, 2048, 512], P(None, 'dp'), may hold values from -0.125 to 0.125
- ffn_out_m1: float32 [2, 2048, 512], P(None, 'dp'), may hold values from -7.1525574e-07 to 7.1525574e-07
- ffn_out_m2: float32 [2, 2048, 512], P(None, 'dp'), may hold values from 3.3525727e-15 to 1.3829362e-14
- len_head: float32 [512, 256], P('dp'), may hold values from -0.25 to 0.25
- len_head_m1: float32 [512, 256], P('dp'), may hold values from -7.1525574e-07 to 7.1525574e-07
- len_head_m2: float32 [512, 256], P('dp'), may hold values from 3.3525727e-15 to 1.3829362e-14
- norms: float32 [2, 7, 512], P(None, None, 'dp')
- norms_m1: float32 [2, 7, 512], P(None, None, 'dp'), may hold values from -2.861023e-06 to 2.861023e-06
- norms_m2: float32 [2, 7, 512], P(None, None, 'dp'), may hold values from 5.4479306e-14 to 2.1791722e-13
- table: float32 [32000, 512], P(('seq', 'dp'))
- table_m1: float32 [32000, 512], P(('seq', 'dp')), may hold values from -7.1525574e-07 to 7.1525574e-07
- table_m2: float32 [32000, 512], P(('seq', 'dp'))
Outputs:
- token_loss_sum: float32 [], replicated
- mask_count: float32 [], replicated
- len_loss_sum: float32 [], replicated
- grad_norm: float32 [], replicated
- attn_in_new: float32 [3, 512, 1536], P(None, 'dp')
- attn_in_m1_new: float32 [3, 512, 1536], P(None, 'dp')
- attn_in_m2_new: float32 [3, 512, 1536], P(None, 'dp')
- attn_out_new: float32 [3, 512, 512], P(None, 'dp')
- attn_out_m1_new: float32 [3, 512, 512], P(None, 'dp')
- attn_out_m2_new: float32 [3, 512, 512], P(None, 'dp')
- ffn_in_new: float32 [2, 512, 2048], P(None, 'dp')
- ffn_in_m1_new: float32 [2, 512, 2048], P(None, 'dp')
- ffn_in_m2_new: float32 [2, 512, 2048], P(None, 'dp')
- ffn_out_new: float32 [2, 2048, 512], P(None, 'dp')
- ffn_out_m1_new: float32 [2, 2048, 512], P(None, 'dp')
- ffn_out_m2_new: float32 [2, 2048, 512], P(None, 'dp')
- len_head_new: float32 [512, 256], P('dp')
- len_head_m1_new: float32 [512, 256], P('dp')
- len_head_m2_new: float32 [512, 256], P('dp')
- norms_new: float32 [2, 7, 512], P(None, None, 'dp')
- norms_m1_new: float32 [2, 7, 512], P(None, None, 'dp')
- norms_m2_new: float32 [2, 7, 512], P(None, None, 'dp')
- table_new: float32 [32000, 512], P(('seq', 'dp'))
- table_m1_new: float32 [32000, 512], P(('seq', 'dp'))
- table_m2_new: float32 [32000, 512], P(('seq', 'dp'))
The draws below stay inside these ranges and needn't reach their ends.
Inputs may be any that keep to these rules, and one draw needn't show every extreme that they name: `src_lengths`: the 32 lengths of each row sum to 1024. `tgt_lengths`: the 32 lengths of each row sum to 1024.
All inputs are finite; a program needn't handle non-finite values.
Results may differ from the reference program's by a relative error of at most 0.0045.
The reference program's roundings to bfloat16 on the way (of `memory` and `final`) count: a program that leaves them out, or rounds other values in their place, can miss the bound.
Values may be sent and summed in bfloat16 or wider, within the bound.
No kernel may reach another device: no remote copies, remote signals or barrier semaphores. Data moves between devices by JAX's collectives and lax.ppermute only.
A program may use at most 448 MiB of HBM per device.

```python
import math
import jax
import jax.numpy as jnp
from jax import lax

D = 512
HEADS = 8
FF = 2048
V = 32000
LCLS = 256
ROW_LEN = 1024
SENTS = 32
ROWS_DEV = 2
NORMS = 7
STEP = 10
SEQ_ROWS = 512
ROWS = 32
NPARAM = 23862272


def cut_lengths(key):
    pick_key, score_key = jax.random.split(key)
    chosen = jax.random.randint(pick_key, (ROWS // ROWS_DEV,), 0, ROWS_DEV)
    special = jnp.arange(ROWS) % ROWS_DEV == jnp.repeat(chosen, ROWS_DEV)
    places = jnp.arange(1, ROW_LEN)
    rim = SEQ_ROWS // 2
    middle = (places > rim) & (places < ROW_LEN - rim)
    fixed_long = (places == rim) | (places == ROW_LEN - rim)
    fixed_half = places == ROW_LEN // 2
    scores = jax.random.randint(score_key, (ROWS, ROW_LEN - 1), 0, 1 << 19) * ROW_LEN + places[None, :]
    raise_mark = special[:, None] & middle[None, :]
    force_mark = jnp.where(special[:, None], fixed_long[None, :], fixed_half[None, :])
    scores = scores + jnp.where(raise_mark, 1 << 30, 0) - jnp.where(force_mark, 1 << 30, 0)
    picked = lax.top_k(-scores, SENTS - 1)[1]
    cuts = jnp.sort(places[picked], axis=-1).astype(jnp.int32)
    bounds = jnp.concatenate([jnp.zeros((ROWS, 1), jnp.int32), cuts, jnp.full((ROWS, 1), ROW_LEN, jnp.int32)], 1)
    return (bounds[:, 1:] - bounds[:, :-1]).astype(jnp.int32)


def draw_src_lengths(key, part):
    key = jax.random.fold_in(key, 11)
    return cut_lengths(key)


def draw_tgt_lengths(key, part):
    key = jax.random.fold_in(key, 12)
    return cut_lengths(key)


def draw_tgt_mask(key, part):
    key = jax.random.fold_in(key, 13)
    position = jnp.arange(ROW_LEN)
    threshold = ROW_LEN // 10 + 3 * position // 10
    values = jax.random.randint(key, (ROWS, ROW_LEN), 0, ROW_LEN)
    return (values < threshold[None, :]).astype(jnp.int32)


def draw_norms(key, part):
    key = jax.random.fold_in(key, 17)
    gain_key, bias_key = jax.random.split(key)
    ramp = jnp.arange(D).astype(jnp.float32) / D
    gains = (0.5 + ramp)[None, :] * (1.0 + 0.1 * jax.random.normal(gain_key, (NORMS, D), jnp.float32))
    biases = 0.2 * jax.random.normal(bias_key, (NORMS, D), jnp.float32)
    return jnp.stack([gains, biases]).astype(jnp.float32)


def draw_table(key, part):
    key = jax.random.fold_in(key, 19)
    ramp = jnp.arange(V).astype(jnp.float32)[:, None] / V
    values = jnp.clip(jax.random.normal(key, (V, D), jnp.float32), -6.0, 6.0) * (1.0 + 2.0 * ramp)
    return (values * D ** (-0.5)).astype(jnp.float32)


def draw_table_m2(key, part):
    key = jax.random.fold_in(key, 23)
    values = jnp.exp(jax.random.uniform(key, (V, D), jnp.float32, jnp.log(0.2), jnp.log(0.8)))
    return (values * (1e-06 / NPARAM)).astype(jnp.float32)


def plant(entries, rng, low, top_value):
    index_at = [jax.random.randint(jax.random.fold_in(rng, axis), (), 0, length) for axis, length in enumerate(entries.shape)]
    main_axis = entries.shape.index(max(entries.shape))
    next_to = index_at[:main_axis] + [(index_at[main_axis] + 1) % entries.shape[main_axis]] + index_at[main_axis + 1:]
    return entries.at[tuple(index_at)].set(low).at[tuple(next_to)].set(top_value)


def shard_levels(own_key, dims, cuts, low, high):
    level, own = 1.0, jax.random.fold_in(own_key, 6)
    for axis_at, parts in cuts:
        heights = jnp.exp(jax.random.uniform(jax.random.fold_in(own, axis_at), (parts,), jnp.float32, low / len(cuts), high / len(cuts)))
        level = level * jnp.repeat(heights, dims[axis_at] // parts).reshape([-1 if axis == axis_at else 1 for axis in range(len(dims))])
    return level


def noise(key, extent, scale, bound, pieces=(), held_as=jnp.bfloat16):
    array = jax.random.normal(key, extent, jnp.float32) * scale
    if len(pieces) > 0:
        array = shard_levels(key, extent, pieces, -0.22, 0.18) * array
    return jnp.clip(array, min=-bound, max=bound).astype(held_as)


def setup_inputs(seed: int = 0) -> dict:
    splits = jax.random.split(jax.random.key(seed), 27)
    return {
        "src_ids": plant(jax.random.randint(splits[0], (ROWS, ROW_LEN), 4, V), jax.random.fold_in(splits[0], 1), 4, V - 1).astype(jnp.int32),
        "tgt_ids": plant(jax.random.randint(splits[1], (ROWS, ROW_LEN), 4, V), jax.random.fold_in(splits[1], 1), 4, V - 1).astype(jnp.int32),
        "src_lengths": draw_src_lengths(jax.random.fold_in(splits[26], 71), 0),
        "tgt_lengths": draw_tgt_lengths(jax.random.fold_in(splits[26], 71), 0),
        "tgt_mask": draw_tgt_mask(jax.random.fold_in(splits[26], 71), 0),
        "attn_in": noise(splits[5], (3, D, 3 * D), D ** -0.5, 0.25, ((1, 16),), jnp.float32),
        "attn_in_m1": noise(splits[6], (3, D, 3 * D), (0.00022 * NPARAM ** -0.5), 7.152557373046875e-07, ((1, 16),), jnp.float32),
        "attn_in_m2": jnp.clip(jnp.exp(math.log(1.3829362087186981e-14) - 1.417066 * jax.random.uniform(splits[7], (3, D, 3 * D), jnp.float32) ** shard_levels(splits[7], (3, D, 3 * D), ((1, 16),), -0.2, 0.2)), 3.3525727106167554e-15, 1.3829362087186981e-14),
        "attn_out": noise(splits[8], (3, D, D), (D * SENTS // ROW_LEN) ** -0.5, 1.5, ((1, 16),), jnp.float32),
        "attn_out_m1": noise(splits[9], (3, D, D), (0.00022 * NPARAM ** -0.5), 7.152557373046875e-07, ((1, 16),), jnp.float32),
        "attn_out_m2": jnp.clip(jnp.exp(math.log(1.3829362087186981e-14) - 1.417066 * jax.random.uniform(splits[10], (3, D, D), jnp.float32) ** shard_levels(splits[10], (3, D, D), ((1, 16),), -0.2, 0.2)), 3.3525727106167554e-15, 1.3829362087186981e-14),
        "ffn_in": noise(splits[11], (2, D, FF), D ** -0.5, 0.25, ((1, 16),), jnp.float32),
        "ffn_in_m1": noise(splits[12], (2, D, FF), (0.00022 * NPARAM ** -0.5), 7.152557373046875e-07, ((1, 16),), jnp.float32),
        "ffn_in_m2": jnp.clip(jnp.exp(math.log(1.3829362087186981e-14) - 1.417066 * jax.random.uniform(splits[13], (2, D, FF), jnp.float32) ** shard_levels(splits[13], (2, D, FF), ((1, 16),), -0.2, 0.2)), 3.3525727106167554e-15, 1.3829362087186981e-14),
        "ffn_out": noise(splits[14], (2, FF, D), FF ** -0.5, 0.125, ((1, 16),), jnp.float32),
        "ffn_out_m1": noise(splits[15], (2, FF, D), (0.00022 * NPARAM ** -0.5), 7.152557373046875e-07, ((1, 16),), jnp.float32),
        "ffn_out_m2": jnp.clip(jnp.exp(math.log(1.3829362087186981e-14) - 1.417066 * jax.random.uniform(splits[16], (2, FF, D), jnp.float32) ** shard_levels(splits[16], (2, FF, D), ((1, 16),), -0.2, 0.2)), 3.3525727106167554e-15, 1.3829362087186981e-14),
        "len_head": noise(splits[17], (D, LCLS), D ** -0.5, 0.25, ((0, 16),), jnp.float32),
        "len_head_m1": noise(splits[18], (D, LCLS), (0.00022 * NPARAM ** -0.5), 7.152557373046875e-07, ((0, 16),), jnp.float32),
        "len_head_m2": jnp.clip(jnp.exp(math.log(1.3829362087186981e-14) - 1.417066 * jax.random.uniform(splits[19], (D, LCLS), jnp.float32) ** shard_levels(splits[19], (D, LCLS), ((0, 16),), -0.2, 0.2)), 3.3525727106167554e-15, 1.3829362087186981e-14),
        "norms": draw_norms(jax.random.fold_in(splits[26], 71), 0),
        "norms_m1": noise(splits[21], (2, NORMS, D), (0.0009 * NPARAM ** -0.5), 2.86102294921875e-06, ((2, 16),), jnp.float32),
        "norms_m2": jnp.clip(jnp.exp(math.log(2.1791722343723202e-13) - 1.3862944 * jax.random.uniform(splits[22], (2, NORMS, D), jnp.float32) ** shard_levels(splits[22], (2, NORMS, D), ((2, 16),), -0.2, 0.2)), 5.4479305859308005e-14, 2.1791722343723202e-13),
        "table": draw_table(jax.random.fold_in(splits[26], 71), 0),
        "table_m1": noise(splits[24], (V, D), (0.00022 * NPARAM ** -0.5), 7.152557373046875e-07, ((0, 32),), jnp.float32),
        "table_m2": draw_table_m2(jax.random.fold_in(splits[26], 71), 0),
    }


@jax.custom_vjp
def low(v):
    return lax.optimization_barrier(v.astype(jnp.bfloat16)).astype(jnp.float32)

@jax.custom_vjp
def low_back(v):
    return v

def low_keep(v):
    return (low(v), None)

def low_pass(kept, grad):
    return (grad,)

def back_keep(v):
    return (v, None)

def back_low(kept, grad):
    return (low(grad),)
low.defvjp(low_keep, low_pass)
low_back.defvjp(back_keep, back_low)
length_token = 1
mask_token = 2
clip_limit = 0.002
beta_one = 0.9
beta_two = 0.98
adam_eps = 1e-08
weight_decay = 0.01
step_rates = (0.05, 0.25, 0.05, 0.025, 0.05, 0.5, 0.1)
highest = lax.Precision.HIGHEST

def matmul(left, right):
    return jnp.dot(left, right, precision=highest, preferred_element_type=jnp.float32)

def layout(lengths, places):
    starts = (jnp.cumsum(lengths, -1) - lengths).astype(jnp.int32)
    covered = places[..., :, None] >= starts[..., None, :]
    segment = (lax.optimization_barrier(jnp.sum(covered.astype(jnp.int32), -1)) - 1).astype(jnp.int32)
    opening = lax.optimization_barrier(jnp.max(jnp.where(covered, starts[..., None, :], 0), -1)).astype(jnp.int32)
    return (segment, (places - opening).astype(jnp.int32), starts)

def sinusoid(positions, width):
    half_width = width // 2
    frequency = jnp.exp(jnp.arange(half_width).astype(jnp.float32) * (-math.log(10000.0) / half_width))
    angles = positions.astype(jnp.float32)[..., None] * frequency
    return jnp.concatenate([jnp.sin(angles), jnp.cos(angles)], -1)

def layer_norm(stream, norm_gain, norm_bias):
    average = lax.optimization_barrier(jnp.mean(stream, -1, keepdims=True))
    centred = stream - average
    variance = lax.optimization_barrier(jnp.mean(centred * centred, -1, keepdims=True))
    return centred * lax.rsqrt(variance + 1e-05) * norm_gain + norm_bias

def attention(query_in, memory_in, weight_in, weight_out, allowed):
    width = query_in.shape[-1]
    queries = low(low_back(matmul(query_in, weight_in[:, :width])))
    key_values = low(low_back(matmul(memory_in, weight_in[:, width:])))
    query_heads = queries.reshape(queries.shape[0], HEADS, -1)
    key_heads = key_values[:, :width].reshape(key_values.shape[0], HEADS, -1)
    value_heads = key_values[:, width:].reshape(key_values.shape[0], HEADS, -1)
    scaled = jnp.einsum('qhd,khd->hqk', query_heads, key_heads, precision=highest) * query_heads.shape[-1] ** (-0.5)
    masked = jnp.where(allowed[None], low_back(scaled), -1e+30)
    probs = low(jax.nn.softmax(masked, axis=-1))
    mixed = jnp.einsum('hqk,khd->qhd', probs, value_heads, precision=highest).reshape(queries.shape[0], width)
    return low_back(matmul(low(low_back(mixed)), weight_out))

def feed_forward(stream_in, weight_one, weight_two):
    hidden = low_back(matmul(stream_in, weight_one))
    return low_back(matmul(low(jax.nn.gelu(hidden)), weight_two))

def row_loss(weights, row):
    attn_in, attn_out, ffn_in, ffn_out, len_head, norms, table = weights
    src_row, tgt_row, src_len, tgt_len, masked = row
    places = jnp.arange(ROW_LEN).astype(jnp.int32)
    src_seg, src_pos, src_start = layout(src_len, places)
    tgt_seg, tgt_pos, tgt_start = layout(tgt_len, places)
    src_in = jnp.where(src_pos == 0, length_token, src_row).astype(jnp.int32)
    dec_in = jnp.where(masked == 1, mask_token, tgt_row).astype(jnp.int32)
    root = math.sqrt(D)

    def norm(stream, index):
        return layer_norm(stream, norms[0, index], norms[1, index])
    stream = table[src_in] * root + sinusoid(src_pos, D)
    inner = low(norm(stream, 0))
    stream = stream + attention(inner, inner, attn_in[0], attn_out[0], src_seg[:, None] == src_seg[None, :])
    inner = low(norm(stream, 1))
    stream = stream + feed_forward(inner, ffn_in[0], ffn_out[0])
    memory = low(norm(stream, 2))
    target = table[dec_in] * root + sinusoid(tgt_pos, D)
    inner = low(norm(target, 3))
    target = target + attention(inner, inner, attn_in[1], attn_out[1], tgt_seg[:, None] == tgt_seg[None, :])
    inner = low(norm(target, 4))
    target = target + attention(inner, memory, attn_in[2], attn_out[2], tgt_seg[:, None] == src_seg[None, :])
    inner = low(norm(target, 5))
    target = target + feed_forward(inner, ffn_in[1], ffn_out[1])
    final = low(norm(target, 6))
    logits = low_back(matmul(final, table.T))
    picked = jnp.take_along_axis(logits, tgt_row[:, None].astype(jnp.int32), -1)[:, 0]
    token_loss = jax.nn.logsumexp(logits, -1) - picked
    token_sum = jnp.sum(jnp.where(masked == 1, token_loss, 0.0))
    first = memory[src_start]
    len_logits = low_back(matmul(first, len_head))
    label = jnp.minimum(tgt_len, LCLS - 1).astype(jnp.int32)
    len_pick = jnp.take_along_axis(len_logits, label[:, None], -1)[:, 0]
    len_sum = jnp.sum(jax.nn.logsumexp(len_logits, -1) - len_pick)
    return (token_sum, len_sum)

def adam_update(weight, first, second, grad, rate):
    first = beta_one * first + (1 - beta_one) * grad
    second = beta_two * second + (1 - beta_two) * grad * grad
    first_hat = first / (1 - beta_one ** STEP)
    second_hat = second / (1 - beta_two ** STEP)
    weight = weight - rate * (first_hat / (jnp.sqrt(second_hat) + adam_eps) + weight_decay * weight)
    return (weight, first, second)

def reference(src_ids, tgt_ids, src_lengths, tgt_lengths, tgt_mask, attn_in, attn_in_m1, attn_in_m2, attn_out, attn_out_m1, attn_out_m2, ffn_in, ffn_in_m1, ffn_in_m2, ffn_out, ffn_out_m1, ffn_out_m2, len_head, len_head_m1, len_head_m2, norms, norms_m1, norms_m2, table, table_m1, table_m2):
    masters = (attn_in, attn_out, ffn_in, ffn_out, len_head, norms, table)
    firsts = (attn_in_m1, attn_out_m1, ffn_in_m1, ffn_out_m1, len_head_m1, norms_m1, table_m1)
    seconds = (attn_in_m2, attn_out_m2, ffn_in_m2, ffn_out_m2, len_head_m2, norms_m2, table_m2)
    count = jnp.sum(tgt_mask).astype(jnp.float32)
    sentences = float(src_lengths.shape[0] * src_lengths.shape[1])

    def total_loss(weights):
        lowered = tuple((low(weight) for weight in weights))

        def scan_step(carry, row):
            token_sum, len_sum = row_loss(lowered, row)
            return ((carry[0] + token_sum, carry[1] + len_sum), None)
        start = (jnp.zeros((), jnp.float32), jnp.zeros((), jnp.float32))
        sums, unused = lax.scan(jax.checkpoint(scan_step), start, (src_ids, tgt_ids, src_lengths, tgt_lengths, tgt_mask))
        return (sums[0] / count + 0.1 * sums[1] / sentences, sums)
    loss, pullback, sums = jax.vjp(total_loss, masters, has_aux=True)
    grads = pullback(jnp.ones((), jnp.float32))[0]
    square = sum((jnp.sum(grad * grad) for grad in grads))
    grad_norm = jnp.sqrt(square)
    factor = jnp.minimum(1.0, clip_limit / (grad_norm + 1e-06))
    updates = []
    for weight, first, second, grad, rate in zip(masters, firsts, seconds, grads, step_rates):
        updates.extend(adam_update(weight, first, second, grad * factor, rate))
    return (sums[0], count, sums[1], grad_norm, *updates)
```

```python
import functools
import math

import jax
import jax.numpy as jnp
from jax import lax
from jax.experimental import pallas as pl
from jax.experimental.pallas import tpu as pltpu
from jax.sharding import PartitionSpec as P

HEADS = 8
STEP = 10


length_token = 1
mask_token = 2
clip_limit = 0.002
beta_one = 0.9
beta_two = 0.98
adam_eps = 1e-08
weight_decay = 0.01
step_rates = (0.05, 0.25, 0.05, 0.025, 0.05, 0.5, 0.1)

low_type = jnp.bfloat16
f32 = jnp.float32
query_block = 128
key_block = 128
place_block = 128
exact_rows = 16
vmem_bytes = 56 * 1024 * 1024


def sinusoid(positions, width):
    half_width = width // 2
    frequency = jnp.exp(jnp.arange(half_width).astype(f32) * (-math.log(10000.0) / half_width))
    angles = positions.astype(f32)[..., None] * frequency
    return jnp.concatenate([jnp.sin(angles), jnp.cos(angles)], -1)


def layer_norm(stream, norm_gain, norm_bias):
    average = jnp.mean(stream, -1, keepdims=True)
    centred = stream - average
    variance = jnp.mean(centred * centred, -1, keepdims=True)
    return centred * lax.rsqrt(variance + 1e-05) * norm_gain + norm_bias


def norm_backward(stream, norm_gain, norm_bias, grad):
    return jax.vjp(layer_norm, stream, norm_gain, norm_bias)[1](grad)


def contract(left, right, left_dim, right_dim):
    return lax.dot_general(
        left, right, (((left_dim,), (right_dim,)), ((), ())), preferred_element_type=f32
    )


def attend_forward_kernel(bounds, q_ref, k_ref, v_ref, span_ref, out_ref, lse_ref, hold, *, head):
    step = pl.program_id(0)
    first, last = bounds[0, step], bounds[1, step]
    width, queries = q_ref.shape
    heads = width // head
    scale = head**-0.5
    low, high = span_ref[0:1, :], span_ref[1:2, :]
    inner = lax.broadcasted_iota(jnp.int32, (key_block, queries), 0)

    def fold(values, op):
        return op(values.reshape(key_block // 8, 8, queries), axis=0)

    def score(block, tops):
        start = pl.multiple_of(block * key_block, key_block)
        place = inner + start
        allowed = (place >= low) & (place < high)
        result = []
        for h in range(heads):
            rows = slice(h * head, (h + 1) * head)
            s = contract(k_ref[rows, pl.ds(start, key_block)], q_ref[rows, :], 0, 0) * scale
            s = jnp.where(allowed, s, -1e30)
            hold[h, pl.ds(start, key_block), :] = s
            result.append(jnp.maximum(tops[h], fold(s, jnp.max)))
        return tuple(result)

    tops = lax.fori_loop(
        first, last, score, tuple(jnp.full((8, queries), -1e30, f32) for _ in range(heads))
    )
    tops = [jnp.max(t, axis=0, keepdims=True) for t in tops]

    def power(block, sums):
        start = pl.multiple_of(block * key_block, key_block)
        result = []
        for h in range(heads):
            e = jnp.exp(hold[h, pl.ds(start, key_block), :] - tops[h])
            hold[h, pl.ds(start, key_block), :] = e
            result.append(sums[h] + fold(e, jnp.sum))
        return tuple(result)

    sums = lax.fori_loop(
        first, last, power, tuple(jnp.zeros((8, queries), f32) for _ in range(heads))
    )
    sums = [jnp.maximum(jnp.sum(t, axis=0, keepdims=True), 1e-30) for t in sums]
    inverse = [1.0 / t for t in sums]

    def mix(block, outs):
        start = pl.multiple_of(block * key_block, key_block)
        result = []
        for h in range(heads):
            rows = slice(h * head, (h + 1) * head)
            p = (hold[h, pl.ds(start, key_block), :] * inverse[h]).astype(low_type)
            result.append(outs[h] + contract(v_ref[rows, pl.ds(start, key_block)], p, 1, 0))
        return tuple(result)

    outs = lax.fori_loop(
        first, last, mix, tuple(jnp.zeros((head, queries), f32) for _ in range(heads))
    )
    for h in range(heads):
        out_ref[h * head : (h + 1) * head, :] = outs[h].astype(low_type)
        lse_ref[h : h + 1, :] = tops[h] + jnp.log(sums[h])


def attend_backward_kernel(
    bounds, q_ref, k_ref, v_ref, span_ref, lse_ref, do_ref, dq_ref, dkv_ref, p_hold, d_hold, acc,
    *, head
):
    step = pl.program_id(0)
    first, last = bounds[0, step], bounds[1, step]
    width, queries = q_ref.shape
    heads = width // head
    scale = head**-0.5
    low, high = span_ref[0:1, :], span_ref[1:2, :]
    inner = lax.broadcasted_iota(jnp.int32, (key_block, queries), 0)

    @pl.when(step == 0)
    def _():
        acc[...] = jnp.zeros_like(acc)

    def one(block, deltas):
        start = pl.multiple_of(block * key_block, key_block)
        keys = pl.ds(start, key_block)
        place = inner + start
        allowed = (place >= low) & (place < high)
        result = []
        for h in range(heads):
            rows = slice(h * head, (h + 1) * head)
            s = contract(k_ref[rows, keys], q_ref[rows, :], 0, 0) * scale
            p = jnp.exp(jnp.where(allowed, s, -1e30) - lse_ref[h : h + 1, :])
            dp = contract(v_ref[rows, keys], do_ref[rows, :], 0, 0)
            p_hold[h, keys, :] = p
            d_hold[h, keys, :] = dp
            result.append(
                deltas[h] + jnp.sum((p * dp).reshape(key_block // 8, 8, queries), axis=0)
            )
            below = slice(width + h * head, width + (h + 1) * head)
            acc[below, keys] += contract(do_ref[rows, :], p.astype(low_type), 1, 1)
        return tuple(result)

    deltas = lax.fori_loop(
        first, last, one, tuple(jnp.zeros((8, queries), f32) for _ in range(heads))
    )
    deltas = [jnp.sum(t, axis=0, keepdims=True) for t in deltas]

    def two(block, outs):
        start = pl.multiple_of(block * key_block, key_block)
        keys = pl.ds(start, key_block)
        result = []
        for h in range(heads):
            rows = slice(h * head, (h + 1) * head)
            ds = (p_hold[h, keys, :] * (d_hold[h, keys, :] - deltas[h])).astype(low_type)
            result.append(outs[h] + contract(k_ref[rows, keys], ds, 1, 0))
            acc[rows, keys] += contract(q_ref[rows, :], ds, 1, 1) * scale
        return tuple(result)

    outs = lax.fori_loop(
        first, last, two, tuple(jnp.zeros((head, queries), f32) for _ in range(heads))
    )
    for h in range(heads):
        dq_ref[h * head : (h + 1) * head, :] = (outs[h] * scale).astype(low_type)

    @pl.when(step == pl.num_programs(0) - 1)
    def _():
        dkv_ref[...] = acc[...].astype(low_type)


def attend_specs(width, length, block, shared):
    key_row = 1 if shared else 0
    return [
        pl.BlockSpec((width, block), lambda i, *_: (0, i)),
        pl.BlockSpec((width, length), lambda i, *_: (key_row, 0)),
        pl.BlockSpec((width, length), lambda i, *_: (key_row + 1, 0)),
        pl.BlockSpec((2, block), lambda i, *_: (0, i)),
    ]


def attend_forward(queries, keys, shared, spans, bounds):
    width = keys.shape[0] // (3 if shared else 2)
    places, length = queries.shape[1], keys.shape[1]
    block = min(query_block, places)
    return pl.pallas_call(
        functools.partial(attend_forward_kernel, head=width // HEADS),
        grid_spec=pltpu.PrefetchScalarGridSpec(
            num_scalar_prefetch=1,
            grid=(places // block,),
            in_specs=attend_specs(width, length, block, shared),
            out_specs=[
                pl.BlockSpec((width, block), lambda i, *_: (0, i)),
                pl.BlockSpec((HEADS, block), lambda i, *_: (0, i)),
            ],
            scratch_shapes=[pltpu.VMEM((HEADS, length, block), f32)],
        ),
        out_shape=[
            jax.ShapeDtypeStruct((width, places), low_type),
            jax.ShapeDtypeStruct((HEADS, places), f32),
        ],
        compiler_params=pltpu.CompilerParams(vmem_limit_bytes=vmem_bytes),
        name="attend_forward",
    )(bounds, queries, keys, keys, spans)


def attend_backward(queries, keys, shared, spans, bounds, lse, d_mixed):
    width = keys.shape[0] // (3 if shared else 2)
    places, length = queries.shape[1], keys.shape[1]
    block = min(query_block, places)
    return pl.pallas_call(
        functools.partial(attend_backward_kernel, head=width // HEADS),
        grid_spec=pltpu.PrefetchScalarGridSpec(
            num_scalar_prefetch=1,
            grid=(places // block,),
            in_specs=attend_specs(width, length, block, shared)
            + [
                pl.BlockSpec((HEADS, block), lambda i, *_: (0, i)),
                pl.BlockSpec((width, block), lambda i, *_: (0, i)),
            ],
            out_specs=[
                pl.BlockSpec((width, block), lambda i, *_: (0, i)),
                pl.BlockSpec((2 * width, length), lambda i, *_: (0, 0)),
            ],
            scratch_shapes=[
                pltpu.VMEM((HEADS, length, block), f32),
                pltpu.VMEM((HEADS, length, block), f32),
                pltpu.VMEM((2 * width, length), f32),
            ],
        ),
        out_shape=[
            jax.ShapeDtypeStruct((width, places), low_type),
            jax.ShapeDtypeStruct((2 * width, length), low_type),
        ],
        compiler_params=pltpu.CompilerParams(vmem_limit_bytes=vmem_bytes),
        name="attend_backward",
    )(bounds, queries, keys, keys, spans, lse, d_mixed)


def head_stats_kernel(chunks, table_ref, rows_ref, target_ref, stats_ref, tops, sums, picks, *, group):
    step = pl.program_id(0)
    words = table_ref.shape[0]

    @pl.when(step == 0)
    def _():
        tops[...] = jnp.full_like(tops, -1e30)
        sums[...] = jnp.zeros_like(sums)
        picks[...] = jnp.zeros_like(picks)

    inner = lax.broadcasted_iota(jnp.int32, (words, place_block), 0) + step * words

    def fold(values, op):
        return op(values.reshape(words // 8, 8, place_block), axis=0)

    for source in range(rows_ref.shape[0] // group):

        def visit(chunk, carry):
            start = pl.multiple_of(source * group + chunk * place_block, place_block)
            here = pl.ds(start, place_block)
            logits = contract(table_ref[...], rows_ref[here, :], 1, 1)
            old = tops[:, here]
            top = jnp.maximum(old, fold(logits, jnp.max))
            spread = jnp.exp(logits.reshape(words // 8, 8, place_block) - top[None])
            sums[:, here] = sums[:, here] * jnp.exp(old - top) + jnp.sum(spread, axis=0)
            tops[:, here] = top
            hit = inner == target_ref[:, here]
            picks[:, here] += fold(jnp.where(hit, logits, 0.0), jnp.sum)
            return carry

        lax.fori_loop(0, chunks[source], visit, 0)

    @pl.when(step == pl.num_programs(0) - 1)
    def _():
        top = jnp.max(tops[...], axis=0, keepdims=True)
        stats_ref[0:1, :] = top
        stats_ref[1:2, :] = jnp.sum(sums[...] * jnp.exp(tops[...] - top), axis=0, keepdims=True)
        stats_ref[2:3, :] = jnp.sum(picks[...], axis=0, keepdims=True)


def head_back_kernel(chunks, table_ref, rows_ref, target_ref, log_ref, weight_ref, dt_ref, dr_ref, turned, *, group):
    step = pl.program_id(0)
    words = table_ref.shape[0]

    @pl.when(step == 0)
    def _():
        dr_ref[...] = jnp.zeros_like(dr_ref)

    dt_ref[...] = jnp.zeros_like(dt_ref)
    turned[...] = table_ref[...].T
    inner = lax.broadcasted_iota(jnp.int32, (words, place_block), 0) + step * words

    for source in range(rows_ref.shape[0] // group):

        def visit(chunk, carry):
            start = pl.multiple_of(source * group + chunk * place_block, place_block)
            here = pl.ds(start, place_block)
            rows = rows_ref[here, :]
            logits = contract(table_ref[...], rows, 1, 1)
            probs = jnp.exp(logits - log_ref[:, here])
            hot = jnp.where(inner == target_ref[:, here], 1.0, 0.0)
            d_logits = ((probs - hot) * weight_ref[:, here]).astype(low_type)
            dt_ref[...] += contract(d_logits, rows, 1, 0)
            dr_ref[:, here] += contract(turned[...], d_logits, 1, 0)
            return carry

        lax.fori_loop(0, chunks[source], visit, 0)


def word_block(words):
    return max(n for n in range(16, 641, 16) if words % n == 0)


def head_specs(words, width, places):
    return [
        pl.BlockSpec((words, width), lambda i, *_: (i, 0)),
        pl.BlockSpec((places, width), lambda i, *_: (0, 0)),
        pl.BlockSpec((1, places), lambda i, *_: (0, 0)),
    ]


def head_stats(chunks, table_part, rows, targets, group):
    words = word_block(table_part.shape[0])
    places, width = rows.shape
    return pl.pallas_call(
        functools.partial(head_stats_kernel, group=group),
        grid_spec=pltpu.PrefetchScalarGridSpec(
            num_scalar_prefetch=1,
            grid=(table_part.shape[0] // words,),
            in_specs=head_specs(words, width, places),
            out_specs=pl.BlockSpec((3, places), lambda i, *_: (0, 0)),
            scratch_shapes=[pltpu.VMEM((8, places), f32) for _ in range(3)],
        ),
        out_shape=jax.ShapeDtypeStruct((3, places), f32),
        compiler_params=pltpu.CompilerParams(vmem_limit_bytes=vmem_bytes),
        name="head_stats",
    )(chunks, table_part, rows, targets)


def head_back(chunks, table_part, rows, targets, logs, weights, group):
    words = word_block(table_part.shape[0])
    places, width = rows.shape
    return pl.pallas_call(
        functools.partial(head_back_kernel, group=group),
        grid_spec=pltpu.PrefetchScalarGridSpec(
            num_scalar_prefetch=1,
            grid=(table_part.shape[0] // words,),
            in_specs=head_specs(words, width, places)
            + [pl.BlockSpec((1, places), lambda i, *_: (0, 0)) for _ in range(2)],
            out_specs=[
                pl.BlockSpec((words, width), lambda i, *_: (i, 0)),
                pl.BlockSpec((width, places), lambda i, *_: (0, 0)),
            ],
            scratch_shapes=[pltpu.VMEM((width, words), low_type)],
        ),
        out_shape=[
            jax.ShapeDtypeStruct(table_part.shape, f32),
            jax.ShapeDtypeStruct((width, places), f32),
        ],
        compiler_params=pltpu.CompilerParams(vmem_limit_bytes=vmem_bytes),
        name="head_back",
    )(chunks, table_part, rows, targets, logs, weights)


def swap(values, axis, bit):
    size = lax.axis_size(axis)
    return lax.ppermute(values, axis, [(i, i ^ bit) for i in range(size)])


def power_of_two(size):
    return size & (size - 1) == 0


def sum_everywhere(values):
    for axis in ("dp", "seq"):
        size = lax.axis_size(axis)
        if power_of_two(size):
            bit = 1
            while bit < size:
                values = values + swap(values, axis, bit)
                bit *= 2
        else:
            values = lax.psum(values, axis)
    return values


def pick(values, dim, index):
    return lax.dynamic_index_in_dim(values, index, dim, False)


def gather_seq(values, dim):
    if lax.axis_size("seq") == 2:
        other = swap(values, "seq", 1)
        first = lax.axis_index("seq") == 0
        return jnp.stack([jnp.where(first, values, other), jnp.where(first, other, values)], dim)
    return lax.all_gather(values, "seq", axis=dim)


def scatter_seq(values):
    if lax.axis_size("seq") == 2:
        index = lax.axis_index("seq")
        return pick(values, 0, index), swap(pick(values, 0, 1 - index), "seq", 1)
    return lax.psum_scatter(values, "seq", scatter_dimension=0, tiled=False), None


def dp_bits():
    bits, bit = [], 1
    while bit < lax.axis_size("dp"):
        bits.append(bit)
        bit *= 2
    return bits


def layer_to_owner(grad):
    owners, seqs = lax.axis_size("dp"), lax.axis_size("seq")
    rows, columns = grad.shape[0] // owners, grad.shape[1]
    if not power_of_two(owners) or seqs != 2 or rows % 16:
        part = lax.psum_scatter(grad, "dp", scatter_dimension=0, tiled=True)
        part = lax.psum(part, "seq")
        return part, jnp.where(lax.axis_index("seq") == 0, jnp.sum(part * part), 0.0)
    bits = dp_bits()
    index, side = lax.axis_index("dp"), lax.axis_index("seq")
    part = grad.reshape((owners // 2, 2, rows, columns))
    mine = index & 1
    part = pick(part, 1, mine) + swap(pick(part, 1, 1 - mine), "dp", 1)
    part = part.reshape((owners // 2, 2, rows // 2, columns))
    part = pick(part, 1, side) + swap(pick(part, 1, 1 - side).astype(low_type), "seq", 1).astype(
        f32
    )
    for bit in bits[1:]:
        part = part.reshape((-1, 2, rows // 2, columns))
        mine = (index // bit) & 1
        part = pick(part, 1, mine) + swap(pick(part, 1, 1 - mine), "dp", bit)
    part = part.reshape((rows // 2, columns))
    other = swap(part, "seq", 1)
    first = side == 0
    whole = jnp.concatenate([jnp.where(first, part, other), jnp.where(first, other, part)], 0)
    return whole, jnp.sum(part * part)


def table_to_owner(grad, pieces):
    owners = lax.axis_size("dp")
    rows, width = grad.shape[0] // owners, grad.shape[1]
    if not power_of_two(owners) or rows < exact_rows or rows % 8 or width % (128 * pieces):
        return lax.psum_scatter(grad, "dp", scatter_dimension=0, tiled=True)
    bits = dp_bits()
    index = lax.axis_index("dp")
    out = []
    for piece in range(pieces):
        columns = width // pieces
        part = grad[:, piece * columns : (piece + 1) * columns]
        part = part.reshape((owners // 2, 2, rows, columns))
        mine = index & 1
        part = pick(part, 1, mine) + swap(pick(part, 1, 1 - mine), "dp", 1)
        for bit in bits[1:]:
            part = part.reshape((-1, 2, rows, columns))
            mine = (index // bit) & 1
            away = pick(part, 1, 1 - mine)
            high = lax.reduce_precision(away, 8, 7)
            rest = (away - high)[:, :exact_rows]
            got = swap(jnp.concatenate([high, rest], 1).astype(low_type), "dp", bit).astype(f32)
            added = got[:, :rows]
            added = added.at[:, :exact_rows].add(got[:, rows:])
            part = pick(part, 1, mine) + added
        out.append(part.reshape((rows, columns)))
    return jnp.concatenate(out, 1)


def adam_update(weight, first, second, grad, rate):
    first = beta_one * first + (1 - beta_one) * grad
    second = beta_two * second + (1 - beta_two) * grad * grad
    first_hat = first / (1 - beta_one**STEP)
    second_hat = second / (1 - beta_two**STEP)
    weight = weight - rate * (first_hat / (jnp.sqrt(second_hat) + adam_eps) + weight_decay * weight)
    return (weight, first, second)


def place_spans(starts, lengths, places):
    covered = places[:, None] >= starts[None, :]
    number = jnp.sum(covered.astype(jnp.int32), -1) - 1
    return number, jnp.max(jnp.where(covered, starts[None, :], 0), -1)


def key_spans(number, starts, lengths, block):
    hot = number[:, None] == jnp.arange(starts.shape[0])[None, :]
    first = jnp.sum(jnp.where(hot, starts[None, :], 0), -1)
    last = jnp.sum(jnp.where(hot, (starts + lengths)[None, :], 0), -1)
    first_block = jnp.min(first.reshape(-1, block), -1) // key_block
    last_block = (jnp.max(last.reshape(-1, block), -1) + key_block - 1) // key_block
    return (
        jnp.stack([first, last]).astype(jnp.int32),
        jnp.stack([first_block, last_block]).astype(jnp.int32),
    )


def on_device(
    src_ids,
    tgt_ids,
    src_lengths,
    tgt_lengths,
    tgt_mask,
    attn_in,
    attn_in_m1,
    attn_in_m2,
    attn_out,
    attn_out_m1,
    attn_out_m2,
    ffn_in,
    ffn_in_m1,
    ffn_in_m2,
    ffn_out,
    ffn_out_m1,
    ffn_out_m2,
    len_head,
    len_head_m1,
    len_head_m2,
    norms,
    norms_m1,
    norms_m2,
    table,
    table_m1,
    table_m2,
):
    rows_here, seq_rows = src_ids.shape
    seqs, owners = lax.axis_size("seq"), lax.axis_size("dp")
    row_len = seq_rows * seqs
    side = lax.axis_index("seq")
    group = seqs // rows_here
    span = row_len // group
    row, offset = side // group, (side % group) * span
    sharers = [[r * group + i for i in range(group)] for r in range(rows_here)]
    width = table.shape[1]
    classes = len_head.shape[1]
    vocab_width = table.shape[0] * owners
    vocab_base = side * vocab_width
    norm_count = norms.shape[1]

    table_part = lax.all_gather(table.astype(low_type), "dp", axis=0, tiled=True)

    def gather_columns(parts):
        joined = jnp.concatenate([part.astype(low_type) for part in parts], 1)
        whole = lax.all_gather(joined, "dp", axis=0, tiled=True)
        result, at = [], 0
        for part in parts:
            result.append(whole[:, at : at + part.shape[1]])
            at += part.shape[1]
        return result

    norm_columns = jnp.pad(norms.reshape(-1, norms.shape[2]).T, ((0, 0), (0, 128 - 2 * norm_count)))
    w_in0, w_out0, f_in0, w_len, norm_low = gather_columns(
        [attn_in[0], attn_out[0], ffn_in[0], len_head, norm_columns]
    )
    f_out0 = lax.all_gather(ffn_out[0].astype(low_type), "dp", axis=0, tiled=True)
    w_in1, w_out1, w_in2, w_out2, f_in1 = gather_columns(
        [attn_in[1], attn_out[1], attn_in[2], attn_out[2], ffn_in[1]]
    )
    f_out1 = lax.all_gather(ffn_out[1].astype(low_type), "dp", axis=0, tiled=True)
    norm_low = norm_low[:, : 2 * norm_count].T.astype(f32)
    gains, biases = norm_low[:norm_count], norm_low[norm_count:]

    count = sum_everywhere(jnp.sum(tgt_mask).astype(f32).reshape(1, 1))[0, 0]
    ids = gather_seq(jnp.stack([src_ids, tgt_ids, tgt_mask]), 2).reshape(3, rows_here, row_len)
    src_starts = jnp.cumsum(src_lengths, -1) - src_lengths
    tgt_starts = jnp.cumsum(tgt_lengths, -1) - tgt_lengths
    places = jnp.arange(row_len)
    opens = jnp.any(places[None, :, None] == src_starts[:, None, :], -1)
    src_in = jnp.where(opens, length_token, ids[0]).reshape(seqs, span)
    masked = (ids[2] == 1).reshape(seqs, span)
    labels = ids[1].reshape(seqs, span)
    dec_in = jnp.where(masked, mask_token, labels)
    own_places = offset + jnp.arange(span)
    src_start, src_length = pick(src_starts, 0, row), pick(src_lengths, 0, row)
    tgt_start, tgt_length = pick(tgt_starts, 0, row), pick(tgt_lengths, 0, row)
    src_number, src_open = place_spans(src_start, src_length, own_places)
    tgt_number, tgt_open = place_spans(tgt_start, tgt_length, own_places)
    block = min(query_block, span)
    enc_spans = key_spans(src_number, src_start, src_length, block)
    self_spans = key_spans(tgt_number, tgt_start, tgt_length, block)
    cross_spans = key_spans(tgt_number, src_start, src_length, block)
    src_wave, tgt_wave = lax.optimization_barrier(
        (sinusoid(own_places - src_open, width), sinusoid(own_places - tgt_open, width))
    )

    rank = jnp.cumsum(masked.astype(jnp.int32), -1) - 1
    counts = rank[:, -1] + 1
    chosen = (rank[:, None, :] == jnp.arange(span)[None, :, None]) & masked[:, None, :]
    packed_labels = jnp.sum(jnp.where(chosen, labels[:, None, :], 0), -1)
    valid = jnp.arange(span)[None, :] < counts[:, None]
    targets = jnp.where(valid, packed_labels - vocab_base, -1).reshape(1, -1)
    chunks = (counts + place_block - 1) // place_block
    own_chosen = pick(chosen, 0, side).astype(low_type)

    def lookup(token_ids):
        local = token_ids - vocab_base
        inside = (local >= 0) & (local < vocab_width)
        found = jnp.take(table_part, jnp.clip(local, 0, vocab_width - 1), axis=0)
        return jnp.where(inside[..., None], found, 0.0).astype(low_type)

    def embed(token_ids):
        if seqs == 2:
            away = swap(lookup(pick(token_ids, 0, 1 - side)), "seq", 1)
            return lookup(pick(token_ids, 0, side)).astype(f32) + away.astype(f32)
        return lax.psum_scatter(lookup(token_ids), "seq", scatter_dimension=0).astype(f32)

    root = math.sqrt(width)
    stream0 = embed(src_in) * root + src_wave
    target0 = embed(dec_in) * root + tgt_wave

    def norm(stream, index):
        return layer_norm(stream, gains[index], biases[index])

    def keys_of_row(part):
        if group == 1:
            return part
        return lax.all_gather(part, "seq", axis=1, tiled=True, axis_index_groups=sharers)

    def keys_to_place(part):
        if group == 1:
            return part
        return lax.psum_scatter(
            part, "seq", scatter_dimension=1, tiled=True, axis_index_groups=sharers
        )

    def self_attention(inner, weight_in, weight_out, spans):
        triple = contract(weight_in, inner, 0, 1).astype(low_type)
        keys = triple if group == 1 else keys_of_row(triple[width:])
        mixed, lse = attend_forward(triple, keys, group == 1, *spans)
        return contract(mixed, weight_out, 0, 0), (triple, keys, mixed, lse)

    def self_attention_back(inner, weight_in, weight_out, spans, kept, grad):
        triple, keys, mixed, lse = kept
        grad_low = grad.astype(low_type)
        d_out = contract(mixed, grad_low, 1, 0)
        d_mixed = contract(weight_out, grad_low, 1, 1).astype(low_type)
        d_query, d_keys = attend_backward(triple, keys, group == 1, *spans, lse, d_mixed)
        d_triple = jnp.concatenate([d_query, keys_to_place(d_keys)], 0)
        return contract(d_triple, weight_in, 0, 1), contract(inner, d_triple, 0, 1), d_out

    def cross_attention(inner, memory, weight_in, weight_out, spans):
        queries = contract(weight_in[:, :width], inner, 0, 1).astype(low_type)
        keys = keys_of_row(contract(weight_in[:, width:], memory, 0, 1).astype(low_type))
        mixed, lse = attend_forward(queries, keys, False, *spans)
        return contract(mixed, weight_out, 0, 0), (queries, keys, mixed, lse)

    def cross_attention_back(inner, memory, weight_in, weight_out, spans, kept, grad):
        queries, keys, mixed, lse = kept
        grad_low = grad.astype(low_type)
        d_out = contract(mixed, grad_low, 1, 0)
        d_mixed = contract(weight_out, grad_low, 1, 1).astype(low_type)
        d_query, d_keys = attend_backward(queries, keys, False, *spans, lse, d_mixed)
        d_keys = keys_to_place(d_keys)
        d_in = jnp.concatenate([contract(inner, d_query, 0, 1), contract(memory, d_keys, 0, 1)], 1)
        return (
            contract(d_query, weight_in[:, :width], 0, 1),
            contract(d_keys, weight_in[:, width:], 0, 1),
            d_in,
            d_out,
        )

    def ffn(inner, weight_one, weight_two):
        hidden = contract(inner, weight_one, 1, 0)
        active = jax.nn.gelu(hidden).astype(low_type)
        return contract(active, weight_two, 1, 0), (hidden, active)

    def ffn_back(inner, weight_one, weight_two, kept, grad):
        hidden, active = kept
        grad_low = grad.astype(low_type)
        d_two = contract(active, grad_low, 0, 0)
        d_active = contract(grad_low, weight_two, 1, 1)
        d_hidden = jax.vjp(jax.nn.gelu, hidden)[1](d_active)[0].astype(low_type)
        return contract(d_hidden, weight_one, 1, 1), contract(inner, d_hidden, 0, 0), d_two

    inner0 = norm(stream0, 0).astype(low_type)
    branch0, keep0 = self_attention(inner0, w_in0, w_out0, enc_spans)
    stream1 = stream0 + branch0
    inner1 = norm(stream1, 1).astype(low_type)
    branch1, keep1 = ffn(inner1, f_in0, f_out0)
    stream2 = stream1 + branch1
    memory = norm(stream2, 2).astype(low_type)
    inner3 = norm(target0, 3).astype(low_type)
    branch3, keep3 = self_attention(inner3, w_in1, w_out1, self_spans)
    target1 = target0 + branch3
    inner4 = norm(target1, 4).astype(low_type)
    branch4, keep4 = cross_attention(inner4, memory, w_in2, w_out2, cross_spans)
    target2 = target1 + branch4
    inner5 = norm(target2, 5).astype(low_type)
    branch5, keep5 = ffn(inner5, f_in1, f_out1)
    target3 = target2 + branch5
    final = norm(target3, 6).astype(low_type)

    packed = contract(own_chosen, final, 1, 0).astype(low_type)
    pieces = gather_seq(packed, 0).reshape(seqs * span, width)
    stats = head_stats(chunks, table_part, pieces, targets, span)
    every = gather_seq(stats, 0)
    top_logit = jnp.max(every[:, 0], 0)
    totals = jnp.sum(every[:, 1] * jnp.exp(every[:, 0] - top_logit[None]), 0)
    log_total = jnp.where(valid.reshape(-1), top_logit + jnp.log(totals), 0.0)
    target_logit = jnp.sum(every[:, 2], 0)
    loss_rows = jnp.where(valid.reshape(-1), log_total - target_logit, 0.0).reshape(seqs, span)
    token_local = jnp.sum(pick(loss_rows, 0, side))
    weights = valid.astype(f32).reshape(1, -1) / count
    d_table, d_pieces = head_back(
        chunks, table_part, pieces, targets, log_total[None], weights, span
    )
    if seqs == 2:
        d_packed = lax.dynamic_slice_in_dim(d_pieces, side * span, span, 1) + swap(
            lax.dynamic_slice_in_dim(d_pieces, (1 - side) * span, span, 1), "seq", 1
        )
    else:
        d_packed = lax.psum_scatter(d_pieces, "seq", scatter_dimension=1, tiled=True)
    d_high = lax.reduce_precision(d_packed, 8, 7)
    d_rest = (d_packed - d_high).astype(low_type)
    d_final = contract(own_chosen, d_high.astype(low_type), 0, 1) + contract(
        own_chosen, d_rest, 0, 1
    )

    first_place = own_places[None, :] == src_start[:, None]
    mine = jnp.any(first_place, -1)
    first_rows = contract(first_place.astype(low_type), memory, 1, 0).astype(low_type)
    len_logits = contract(first_rows, w_len, 1, 0)
    len_label = jnp.minimum(tgt_length, classes - 1)
    len_hot = jnp.arange(classes)[None, :] == len_label[:, None]
    len_loss = jax.nn.logsumexp(len_logits, -1) - jnp.sum(jnp.where(len_hot, len_logits, 0.0), -1)
    len_local = jnp.sum(jnp.where(mine, len_loss, 0.0))
    sentences = rows_here * src_lengths.shape[1] * owners
    len_prob = jax.nn.softmax(len_logits, -1)
    d_len_logits = (
        jnp.where(mine[:, None], len_prob - len_hot.astype(f32), 0.0) * (0.1 / sentences)
    ).astype(low_type)
    d_w_len = contract(first_rows, d_len_logits, 0, 0)
    d_first = contract(d_len_logits, w_len, 1, 1)
    d_memory = lax.dot_general(
        first_place.astype(f32),
        d_first,
        (((0,), (0,)), ((), ())),
        precision=lax.Precision.HIGHEST,
        preferred_element_type=f32,
    )

    d_target3, gain6, bias6 = norm_backward(target3, gains[6], biases[6], d_final)
    d_inner5, d_fin1, d_fout1 = ffn_back(inner5, f_in1, f_out1, keep5, d_target3)
    d_target2, gain5, bias5 = norm_backward(target2, gains[5], biases[5], d_inner5)
    d_target2 = d_target2 + d_target3
    d_inner4, d_cross, d_win2, d_wout2 = cross_attention_back(
        inner4, memory, w_in2, w_out2, cross_spans, keep4, d_target2
    )
    d_target1, gain4, bias4 = norm_backward(target1, gains[4], biases[4], d_inner4)
    d_target1 = d_target1 + d_target2
    d_inner3, d_win1, d_wout1 = self_attention_back(
        inner3, w_in1, w_out1, self_spans, keep3, d_target1
    )
    d_target0, gain3, bias3 = norm_backward(target0, gains[3], biases[3], d_inner3)
    d_target0 = d_target0 + d_target1
    d_stream2, gain2, bias2 = norm_backward(stream2, gains[2], biases[2], d_memory + d_cross)
    d_inner1, d_fin0, d_fout0 = ffn_back(inner1, f_in0, f_out0, keep1, d_stream2)
    d_stream1, gain1, bias1 = norm_backward(stream1, gains[1], biases[1], d_inner1)
    d_stream1 = d_stream1 + d_stream2
    d_inner0, d_win0, d_wout0 = self_attention_back(
        inner0, w_in0, w_out0, enc_spans, keep0, d_stream1
    )
    d_stream0, gain0, bias0 = norm_backward(stream0, gains[0], biases[0], d_inner0)
    d_stream0 = d_stream0 + d_stream1

    def spread(base, token_ids, grads):
        local = (token_ids - vocab_base).reshape(-1)
        inside = (local >= 0) & (local < vocab_width)
        terms = jnp.where(inside[:, None], grads.reshape(-1, width).astype(f32), 0.0)
        return base.at[jnp.clip(local, 0, vocab_width - 1)].add(terms)

    d_dec_all = gather_seq((d_target0 * root).astype(low_type), 0)
    d_src_all = gather_seq((d_stream0 * root).astype(low_type), 0)
    d_table = spread(spread(d_table, dec_in, d_dec_all), src_in, d_src_all)
    table_grad = table_to_owner(d_table, 4)
    norm_grads = [gain0, gain1, gain2, gain3, gain4, gain5, gain6]
    norm_grads += [bias0, bias1, bias2, bias3, bias4, bias5, bias6]
    small = jnp.concatenate(
        [d_w_len, jnp.pad(jnp.stack(norm_grads, 1), ((0, 0), (0, 128 - 2 * norm_count)))], 1
    )
    g_fout1, sq0 = layer_to_owner(d_fout1)
    g_fin1, sq1 = layer_to_owner(d_fin1)
    g_wout2, sq2 = layer_to_owner(d_wout2)
    g_win2, sq3 = layer_to_owner(d_win2)
    g_wout1, sq4 = layer_to_owner(d_wout1)
    g_win1, sq5 = layer_to_owner(d_win1)
    g_fout0, sq6 = layer_to_owner(d_fout0)
    g_fin0, sq7 = layer_to_owner(d_fin0)
    g_wout0, sq8 = layer_to_owner(d_wout0)
    g_win0, sq9 = layer_to_owner(d_win0)
    g_small, sq10 = layer_to_owner(small)
    square = sq0 + sq1 + sq2 + sq3 + sq4 + sq5 + sq6 + sq7 + sq8 + sq9 + sq10
    square = square + jnp.sum(table_grad * table_grad)
    sums = sum_everywhere(jnp.stack([token_local, len_local, square]).reshape(1, 3))[0]
    token_sum, len_sum, grad_norm = sums[0], sums[1], jnp.sqrt(sums[2])
    factor = jnp.minimum(1.0, clip_limit / (grad_norm + 1e-06))
    grads = (
        jnp.stack([g_win0, g_win1, g_win2]),
        jnp.stack([g_wout0, g_wout1, g_wout2]),
        jnp.stack([g_fin0, g_fin1]),
        jnp.stack([g_fout0, g_fout1]),
        g_small[:, :classes],
        g_small[:, classes : classes + 2 * norm_count].T.reshape(norms.shape),
        table_grad,
    )
    masters = (attn_in, attn_out, ffn_in, ffn_out, len_head, norms, table)
    firsts = (attn_in_m1, attn_out_m1, ffn_in_m1, ffn_out_m1, len_head_m1, norms_m1, table_m1)
    seconds = (attn_in_m2, attn_out_m2, ffn_in_m2, ffn_out_m2, len_head_m2, norms_m2, table_m2)
    updates = []
    for weight, first, second, grad, rate in zip(masters, firsts, seconds, grads, step_rates):
        updates.extend(adam_update(weight, first, second, grad * factor, rate))
    return (token_sum, count, len_sum, grad_norm, *updates)


def solution(mesh):
    layer, head, scales, words = P(None, "dp", None), P("dp", None), P(None, None, "dp"), P(("seq", "dp"), None)
    owned = (layer,) * 12 + (head,) * 3 + (scales,) * 3 + (words,) * 3
    ids, lengths = P("dp", "seq"), P("dp", None)
    in_specs = (ids, ids, lengths, lengths, ids) + owned
    out_specs = (P(), P(), P(), P()) + owned
    return jax.shard_map(
        on_device, mesh=mesh, in_specs=in_specs, out_specs=out_specs, check_vma=False
    )
```

```python
import functools
import math

import jax
import jax.numpy as jnp
from jax import lax
from jax.experimental import pallas as pl
from jax.experimental.pallas import tpu as pltpu
from jax.sharding import PartitionSpec as P

HEADS = 8
STEP = 10


length_token = 1
mask_token = 2
clip_limit = 0.002
beta_one = 0.9
beta_two = 0.98
adam_eps = 1e-08
weight_decay = 0.01
step_rates = (0.05, 0.25, 0.05, 0.025, 0.05, 0.5, 0.1)

low_type = jnp.bfloat16
f32 = jnp.float32
query_block = 128
key_block = 128
place_block = 256
vmem_bytes = 56 * 1024 * 1024


def sinusoid(positions, width):
    half_width = width // 2
    frequency = jnp.exp(jnp.arange(half_width).astype(f32) * (-math.log(10000.0) / half_width))
    angles = positions.astype(f32)[..., None] * frequency
    return jnp.concatenate([jnp.sin(angles), jnp.cos(angles)], -1)


def layer_norm(stream, norm_gain, norm_bias):
    average = jnp.mean(stream, -1, keepdims=True)
    centred = stream - average
    variance = jnp.mean(centred * centred, -1, keepdims=True)
    return centred * lax.rsqrt(variance + 1e-05) * norm_gain + norm_bias


def norm_backward(stream, norm_gain, norm_bias, grad):
    return jax.vjp(layer_norm, stream, norm_gain, norm_bias)[1](grad)


def contract(left, right, left_dim, right_dim):
    return lax.dot_general(
        left, right, (((left_dim,), (right_dim,)), ((), ())), preferred_element_type=f32
    )


def attend_forward_kernel(bounds, q_ref, k_ref, v_ref, span_ref, out_ref, lse_ref, hold, *, head):
    step = pl.program_id(0)
    first, last = bounds[0, step], bounds[1, step]
    width, queries = q_ref.shape
    heads = width // head
    scale = head**-0.5
    low, high = span_ref[0:1, :], span_ref[1:2, :]
    inner = lax.broadcasted_iota(jnp.int32, (key_block, queries), 0)

    def fold(values, op):
        return op(values.reshape(key_block // 8, 8, queries), axis=0)

    def score(block, tops):
        start = pl.multiple_of(block * key_block, key_block)
        place = inner + start
        allowed = (place >= low) & (place < high)
        result = []
        for h in range(heads):
            rows = slice(h * head, (h + 1) * head)
            s = contract(k_ref[rows, pl.ds(start, key_block)], q_ref[rows, :], 0, 0) * scale
            s = jnp.where(allowed, s, -1e30)
            hold[h, pl.ds(start, key_block), :] = s
            result.append(jnp.maximum(tops[h], fold(s, jnp.max)))
        return tuple(result)

    tops = lax.fori_loop(
        first, last, score, tuple(jnp.full((8, queries), -1e30, f32) for _ in range(heads))
    )
    tops = [jnp.max(t, axis=0, keepdims=True) for t in tops]

    def power(block, sums):
        start = pl.multiple_of(block * key_block, key_block)
        result = []
        for h in range(heads):
            e = jnp.exp(hold[h, pl.ds(start, key_block), :] - tops[h])
            hold[h, pl.ds(start, key_block), :] = e
            result.append(sums[h] + fold(e, jnp.sum))
        return tuple(result)

    sums = lax.fori_loop(
        first, last, power, tuple(jnp.zeros((8, queries), f32) for _ in range(heads))
    )
    sums = [jnp.maximum(jnp.sum(t, axis=0, keepdims=True), 1e-30) for t in sums]
    inverse = [1.0 / t for t in sums]

    def mix(block, outs):
        start = pl.multiple_of(block * key_block, key_block)
        result = []
        for h in range(heads):
            rows = slice(h * head, (h + 1) * head)
            p = (hold[h, pl.ds(start, key_block), :] * inverse[h]).astype(low_type)
            result.append(outs[h] + contract(v_ref[rows, pl.ds(start, key_block)], p, 1, 0))
        return tuple(result)

    outs = lax.fori_loop(
        first, last, mix, tuple(jnp.zeros((head, queries), f32) for _ in range(heads))
    )
    for h in range(heads):
        out_ref[h * head : (h + 1) * head, :] = outs[h].astype(low_type)
        lse_ref[h : h + 1, :] = tops[h] + jnp.log(sums[h])


def attend_backward_kernel(
    bounds, q_ref, k_ref, v_ref, span_ref, lse_ref, do_ref, dq_ref, dkv_ref, p_hold, d_hold, acc,
    *, head
):
    step = pl.program_id(0)
    first, last = bounds[0, step], bounds[1, step]
    width, queries = q_ref.shape
    heads = width // head
    scale = head**-0.5
    low, high = span_ref[0:1, :], span_ref[1:2, :]
    inner = lax.broadcasted_iota(jnp.int32, (key_block, queries), 0)

    @pl.when(step == 0)
    def _():
        acc[...] = jnp.zeros_like(acc)

    def one(block, deltas):
        start = pl.multiple_of(block * key_block, key_block)
        keys = pl.ds(start, key_block)
        place = inner + start
        allowed = (place >= low) & (place < high)
        result = []
        for h in range(heads):
            rows = slice(h * head, (h + 1) * head)
            s = contract(k_ref[rows, keys], q_ref[rows, :], 0, 0) * scale
            p = jnp.exp(jnp.where(allowed, s, -1e30) - lse_ref[h : h + 1, :])
            dp = contract(v_ref[rows, keys], do_ref[rows, :], 0, 0)
            p_hold[h, keys, :] = p
            d_hold[h, keys, :] = dp
            result.append(
                deltas[h] + jnp.sum((p * dp).reshape(key_block // 8, 8, queries), axis=0)
            )
            below = slice(width + h * head, width + (h + 1) * head)
            acc[below, keys] += contract(do_ref[rows, :], p.astype(low_type), 1, 1)
        return tuple(result)

    deltas = lax.fori_loop(
        first, last, one, tuple(jnp.zeros((8, queries), f32) for _ in range(heads))
    )
    deltas = [jnp.sum(t, axis=0, keepdims=True) for t in deltas]

    def two(block, outs):
        start = pl.multiple_of(block * key_block, key_block)
        keys = pl.ds(start, key_block)
        result = []
        for h in range(heads):
            rows = slice(h * head, (h + 1) * head)
            ds = (p_hold[h, keys, :] * (d_hold[h, keys, :] - deltas[h])).astype(low_type)
            result.append(outs[h] + contract(k_ref[rows, keys], ds, 1, 0))
            acc[rows, keys] += contract(q_ref[rows, :], ds, 1, 1) * scale
        return tuple(result)

    outs = lax.fori_loop(
        first, last, two, tuple(jnp.zeros((head, queries), f32) for _ in range(heads))
    )
    for h in range(heads):
        dq_ref[h * head : (h + 1) * head, :] = (outs[h] * scale).astype(low_type)

    @pl.when(step == pl.num_programs(0) - 1)
    def _():
        dkv_ref[...] = acc[...].astype(low_type)


def attend_specs(width, length, block, shared):
    key_row = 1 if shared else 0
    return [
        pl.BlockSpec((width, block), lambda i, *_: (0, i)),
        pl.BlockSpec((width, length), lambda i, *_: (key_row, 0)),
        pl.BlockSpec((width, length), lambda i, *_: (key_row + 1, 0)),
        pl.BlockSpec((2, block), lambda i, *_: (0, i)),
    ]


def attend_forward(queries, keys, shared, spans, bounds):
    width = keys.shape[0] // (3 if shared else 2)
    places, length = queries.shape[1], keys.shape[1]
    block = min(query_block, places)
    return pl.pallas_call(
        functools.partial(attend_forward_kernel, head=width // HEADS),
        grid_spec=pltpu.PrefetchScalarGridSpec(
            num_scalar_prefetch=1,
            grid=(places // block,),
            in_specs=attend_specs(width, length, block, shared),
            out_specs=[
                pl.BlockSpec((width, block), lambda i, *_: (0, i)),
                pl.BlockSpec((HEADS, block), lambda i, *_: (0, i)),
            ],
            scratch_shapes=[pltpu.VMEM((HEADS, length, block), f32)],
        ),
        out_shape=[
            jax.ShapeDtypeStruct((width, places), low_type),
            jax.ShapeDtypeStruct((HEADS, places), f32),
        ],
        compiler_params=pltpu.CompilerParams(vmem_limit_bytes=vmem_bytes),
        name="attend_forward",
    )(bounds, queries, keys, keys, spans)


def attend_backward(queries, keys, shared, spans, bounds, lse, d_mixed):
    width = keys.shape[0] // (3 if shared else 2)
    places, length = queries.shape[1], keys.shape[1]
    block = min(query_block, places)
    return pl.pallas_call(
        functools.partial(attend_backward_kernel, head=width // HEADS),
        grid_spec=pltpu.PrefetchScalarGridSpec(
            num_scalar_prefetch=1,
            grid=(places // block,),
            in_specs=attend_specs(width, length, block, shared)
            + [
                pl.BlockSpec((HEADS, block), lambda i, *_: (0, i)),
                pl.BlockSpec((width, block), lambda i, *_: (0, i)),
            ],
            out_specs=[
                pl.BlockSpec((width, block), lambda i, *_: (0, i)),
                pl.BlockSpec((2 * width, length), lambda i, *_: (0, 0)),
            ],
            scratch_shapes=[
                pltpu.VMEM((HEADS, length, block), f32),
                pltpu.VMEM((HEADS, length, block), f32),
                pltpu.VMEM((2 * width, length), f32),
            ],
        ),
        out_shape=[
            jax.ShapeDtypeStruct((width, places), low_type),
            jax.ShapeDtypeStruct((2 * width, length), low_type),
        ],
        compiler_params=pltpu.CompilerParams(vmem_limit_bytes=vmem_bytes),
        name="attend_backward",
    )(bounds, queries, keys, keys, spans, lse, d_mixed)


def each_chunk(chunks, visit):
    def wide(chunk, carry):
        visit(pl.multiple_of(chunk * place_block, place_block), place_block)
        return carry

    lax.fori_loop(0, chunks[0], wide, 0)

    @pl.when(chunks[1] > 0)
    def _():
        visit(pl.multiple_of(chunks[0] * place_block, place_block), place_block // 2)


def head_stats_kernel(chunks, table_ref, rows_ref, stats_ref, tops, sums):
    step = pl.program_id(0)
    words = table_ref.shape[0]

    @pl.when(step == 0)
    def _():
        tops[...] = jnp.full_like(tops, -1e30)
        sums[...] = jnp.zeros_like(sums)

    def visit(start, size):
        here = pl.ds(start, size)
        logits = contract(table_ref[...], rows_ref[here, :], 1, 1).reshape(words // 8, 8, size)
        old = tops[:, here]
        top = jnp.maximum(old, jnp.max(logits, axis=0))
        powers = jnp.sum(jnp.exp(logits - top[None]), axis=0)
        sums[:, here] = sums[:, here] * jnp.exp(old - top) + powers
        tops[:, here] = top

    each_chunk(chunks, visit)

    @pl.when(step == pl.num_programs(0) - 1)
    def _():
        top = jnp.max(tops[...], axis=0, keepdims=True)
        stats_ref[0:1, :] = top
        stats_ref[1:2, :] = jnp.sum(sums[...] * jnp.exp(tops[...] - top), axis=0, keepdims=True)


def head_back_kernel(
    chunks, table_ref, rows_ref, target_ref, log_ref, weight_ref, dt_ref, dr_ref, pick_ref, turned
):
    step = pl.program_id(0)
    words = table_ref.shape[0]

    @pl.when(step == 0)
    def _():
        dr_ref[...] = jnp.zeros_like(dr_ref)
        pick_ref[...] = jnp.zeros_like(pick_ref)

    dt_ref[...] = jnp.zeros_like(dt_ref)
    turned[...] = table_ref[...].T

    def visit(start, size):
        here = pl.ds(start, size)
        rows = rows_ref[here, :]
        inner = lax.broadcasted_iota(jnp.int32, (words, size), 0)
        logits = contract(table_ref[...], rows, 1, 1)
        scaled = jnp.exp(logits - log_ref[:, here])
        hit = inner == target_ref[:, here] - step * words
        picked = jnp.where(hit, logits, 0.0).reshape(words // 8, 8, size)
        pick_ref[:, here] += jnp.sum(picked, axis=0)
        d_logits = jnp.where(hit, scaled - weight_ref[:, here], scaled).astype(low_type)
        dt_ref[...] += contract(d_logits, rows, 1, 0)
        dr_ref[:, here] += contract(turned[...], d_logits, 1, 0)

    each_chunk(chunks, visit)


def word_block(words):
    return max(n for n in range(16, 1601, 16) if words % n == 0)


def head_specs(words, width, places):
    return [
        pl.BlockSpec((words, width), lambda i, *_: (i, 0)),
        pl.BlockSpec((places, width), lambda i, *_: (0, 0)),
    ]


def head_stats(chunks, table_part, rows):
    words = word_block(table_part.shape[0])
    places, width = rows.shape
    return pl.pallas_call(
        head_stats_kernel,
        grid_spec=pltpu.PrefetchScalarGridSpec(
            num_scalar_prefetch=1,
            grid=(table_part.shape[0] // words,),
            in_specs=head_specs(words, width, places),
            out_specs=pl.BlockSpec((2, places), lambda i, *_: (0, 0)),
            scratch_shapes=[pltpu.VMEM((8, places), f32) for _ in range(2)],
        ),
        out_shape=jax.ShapeDtypeStruct((2, places), f32),
        compiler_params=pltpu.CompilerParams(vmem_limit_bytes=vmem_bytes),
        name="head_stats",
    )(chunks, table_part, rows)


def head_back(chunks, table_part, rows, targets, logs, weights):
    words = word_block(table_part.shape[0])
    places, width = rows.shape
    return pl.pallas_call(
        head_back_kernel,
        grid_spec=pltpu.PrefetchScalarGridSpec(
            num_scalar_prefetch=1,
            grid=(table_part.shape[0] // words,),
            in_specs=head_specs(words, width, places)
            + [pl.BlockSpec((1, places), lambda i, *_: (0, 0)) for _ in range(3)],
            out_specs=[
                pl.BlockSpec((words, width), lambda i, *_: (i, 0)),
                pl.BlockSpec((width, places), lambda i, *_: (0, 0)),
                pl.BlockSpec((8, places), lambda i, *_: (0, 0)),
            ],
            scratch_shapes=[pltpu.VMEM((width, words), low_type)],
        ),
        out_shape=[
            jax.ShapeDtypeStruct(table_part.shape, f32),
            jax.ShapeDtypeStruct((width, places), f32),
            jax.ShapeDtypeStruct((8, places), f32),
        ],
        compiler_params=pltpu.CompilerParams(vmem_limit_bytes=vmem_bytes),
        name="head_back",
    )(chunks, table_part, rows, targets, logs, weights)


def swap(values, axis, bit):
    size = lax.axis_size(axis)
    return lax.ppermute(values, axis, [(i, i ^ bit) for i in range(size)])


def power_of_two(size):
    return size & (size - 1) == 0


def everywhere(values, combine, reduce):
    for axis in ("dp", "seq"):
        size = lax.axis_size(axis)
        if power_of_two(size):
            bit = 1
            while bit < size:
                values = combine(values, swap(values, axis, bit))
                bit *= 2
        else:
            values = reduce(values, axis)
    return values


def pick(values, dim, index):
    return lax.dynamic_index_in_dim(values, index, dim, False)


def gather_seq(values, dim):
    if lax.axis_size("seq") == 2:
        other = swap(values, "seq", 1)
        first = lax.axis_index("seq") == 0
        return jnp.stack([jnp.where(first, values, other), jnp.where(first, other, values)], dim)
    return lax.all_gather(values, "seq", axis=dim)


def swap_rows(values, cut, more):
    rest = lax.cond(
        more, lambda part: swap(part, "seq", 1), lambda part: jnp.zeros_like(part), values[cut:]
    )
    return jnp.concatenate([swap(values[:cut], "seq", 1), rest], 0)


def to_each(values):
    return lax.all_to_all(values, ("seq", "dp"), 0, 0)


class Halving:
    def __init__(self, parts, joint):
        self.parts, self.joint = parts, joint
        self.rows = parts[0].shape[1]
        bits = []
        bit = 1
        while bit < lax.axis_size("dp"):
            bits.append(("dp", bit))
            bit *= 2
        self.steps = bits[:1] + ([("seq", 1)] if joint else []) + bits[1:]
        self.fast = power_of_two(lax.axis_size("dp")) and (
            not joint or (lax.axis_size("seq") == 2 and self.rows % 16 == 0)
        )
        self.fast = self.fast and all(part.shape[2] % 128 == 0 for part in parts)
        self.fast = self.fast and self.rows % 8 == 0
        self.pending, self.value, self.square = None, None, None
        if self.fast:
            self.launch()

    def launch(self):
        if self.value is not None:
            return
        if not self.steps:
            self.pending = swap(self.parts[0], "seq", 1)
            return
        axis, bit = self.steps[0]
        rows = self.rows // 2 if axis == "seq" else self.rows
        index = lax.axis_index(axis)
        mine = (index // bit) & 1
        halves = [part.reshape((-1, 2, rows, part.shape[2])) for part in self.parts]
        away = [pick(half, 1, 1 - mine).astype(low_type) for half in halves]
        self.parts = [pick(half, 1, mine) for half in halves]
        self.rows = rows
        self.pending = swap(jnp.concatenate(away, 2), axis, bit)

    def absorb(self, got):
        self.pending = None
        if not self.steps:
            first = lax.axis_index("seq") == 0
            part = self.parts[0]
            self.value = jnp.concatenate(
                [jnp.where(first, part, got), jnp.where(first, got, part)], 0
            )
            return
        self.steps.pop(0)
        self.parts = [jnp.concatenate(self.parts, 2) + got.astype(f32)]
        if not self.steps:
            self.parts = [self.parts[0].reshape(self.rows, -1)]
            self.square = jnp.sum(self.parts[0] * self.parts[0])
            if not self.joint:
                self.value = self.parts[0]

    def finish(self):
        if self.fast:
            return
        whole = jnp.concatenate(self.parts, 2)
        part = lax.psum_scatter(whole, "dp", scatter_dimension=0)
        if self.joint:
            part = lax.psum(part, "seq")
        self.value, self.square = part, jnp.sum(part * part)
        if self.joint:
            self.square = jnp.where(lax.axis_index("seq") == 0, self.square, 0.0)


def advance(main, chains):
    live = [chain for chain in chains if chain.pending is not None]
    main, got = lax.optimization_barrier((main, [chain.pending for chain in live]))
    for chain, arrived in zip(live, got):
        chain.absorb(arrived)
        chain.launch()
    return main


def adam_update(weight, first, second, grad, rate):
    first = beta_one * first + (1 - beta_one) * grad
    second = beta_two * second + (1 - beta_two) * grad * grad
    first_hat = first / (1 - beta_one**STEP)
    second_hat = second / (1 - beta_two**STEP)
    weight = weight - rate * (first_hat / (jnp.sqrt(second_hat) + adam_eps) + weight_decay * weight)
    return (weight, first, second)


def place_spans(starts, places):
    covered = places[:, None] >= starts[None, :]
    number = jnp.sum(covered.astype(jnp.int32), -1) - 1
    return number, jnp.max(jnp.where(covered, starts[None, :], 0), -1)


def key_spans(number, starts, lengths, block):
    hot = number[:, None] == jnp.arange(starts.shape[0])[None, :]
    first = jnp.sum(jnp.where(hot, starts[None, :], 0), -1)
    last = jnp.sum(jnp.where(hot, (starts + lengths)[None, :], 0), -1)
    first_block = jnp.min(first.reshape(-1, block), -1) // key_block
    last_block = (jnp.max(last.reshape(-1, block), -1) + key_block - 1) // key_block
    return (
        jnp.stack([first, last]).astype(jnp.int32),
        jnp.stack([first_block, last_block]).astype(jnp.int32),
    )


def on_device(
    src_ids,
    tgt_ids,
    src_lengths,
    tgt_lengths,
    tgt_mask,
    attn_in,
    attn_in_m1,
    attn_in_m2,
    attn_out,
    attn_out_m1,
    attn_out_m2,
    ffn_in,
    ffn_in_m1,
    ffn_in_m2,
    ffn_out,
    ffn_out_m1,
    ffn_out_m2,
    len_head,
    len_head_m1,
    len_head_m2,
    norms,
    norms_m1,
    norms_m2,
    table,
    table_m1,
    table_m2,
):
    rows_here, seq_rows = src_ids.shape
    seqs, owners = lax.axis_size("seq"), lax.axis_size("dp")
    devices = seqs * owners
    row_len = seq_rows * seqs
    side = lax.axis_index("seq")
    group = seqs // rows_here
    span = row_len // group
    row, offset = side // group, (side % group) * span
    sharers = [[r * group + i for i in range(group)] for r in range(rows_here)]
    own_words, width = table.shape
    classes = len_head.shape[1]
    vocab_width = own_words * owners
    vocab_base = side * vocab_width
    norm_count = norms.shape[1]
    norm_columns = 128

    def columns_of(weight, rows):
        return [weight[at : at + rows] for at in range(0, weight.shape[0], rows)]

    def gather_columns(parts):
        joined = jnp.concatenate([part.astype(low_type) for part in parts], 1)
        whole = lax.all_gather(joined, "dp", axis=0, tiled=True)
        result, at = [], 0
        for part in parts:
            result.append(whole[:, at : at + part.shape[1]])
            at += part.shape[1]
        return result

    def join_rows(pieces):
        blocks = [piece.reshape(owners, -1, piece.shape[1]) for piece in pieces]
        return jnp.concatenate(blocks, 1).reshape(-1, pieces[0].shape[1])

    share = attn_in.shape[1]
    norm_part = jnp.pad(
        norms.reshape(-1, norms.shape[2]).T, ((0, 0), (0, norm_columns - 2 * norm_count))
    )
    first_parts = [attn_in[0], attn_out[0], len_head, norm_part, ffn_in[0]]
    first_parts += columns_of(ffn_out[0], share)
    w_in0, w_out0, w_len, norm_low, f_in0, *f_out0 = gather_columns(first_parts)
    next_parts = [attn_in[1], attn_out[1], attn_in[2], attn_out[2], ffn_in[1]]
    next_parts += columns_of(ffn_out[1], share)
    w_in1, w_out1, w_in2, w_out2, f_in1, *f_out1 = gather_columns(next_parts)
    f_out0, f_out1 = join_rows(f_out0), join_rows(f_out1)
    table_low = table.astype(low_type)
    table_part = lax.all_gather(table_low, "dp", axis=0, tiled=True)
    norm_low = norm_low[:, : 2 * norm_count].T.astype(f32)
    gains, biases = norm_low[:norm_count], norm_low[norm_count:]

    ids = gather_seq(jnp.stack([src_ids, tgt_ids, tgt_mask]), 2).reshape(3, rows_here, row_len)
    src_starts = jnp.cumsum(src_lengths, -1) - src_lengths
    tgt_starts = jnp.cumsum(tgt_lengths, -1) - tgt_lengths
    places = jnp.arange(row_len)
    opens = jnp.any(places[None, :, None] == src_starts[:, None, :], -1)
    src_in = pick(jnp.where(opens, length_token, ids[0]).reshape(seqs, span), 0, side)
    masked = (ids[2] == 1).reshape(seqs, span)
    labels = ids[1].reshape(seqs, span)
    dec_in = pick(jnp.where(masked, mask_token, labels), 0, side)
    counts = jnp.sum(masked.astype(jnp.int32), -1)

    slots = -(-(2 * span // devices) // 16) * 16
    slots = max(slots, 16)

    def ask(token_ids):
        same = token_ids[:, None] == token_ids[None, :]
        index = jnp.arange(span)
        earlier = index[None, :] < index[:, None]
        leader = jnp.logical_not(jnp.any(same & earlier, 1))
        holder = token_ids // own_words
        rank = jnp.sum(
            (earlier & leader[None, :] & (holder[:, None] == holder[None, :])).astype(jnp.int32), 1
        )
        rank = jnp.sum(jnp.where(same & leader[None, :], rank[None, :], 0), 1)
        return token_ids % own_words, holder, rank, jnp.max(rank) // slots + 1

    def round_of(asked, turn):
        local, holder, rank, _ = asked
        code = jnp.where(rank // slots == turn, holder * slots + rank % slots, -1)
        chosen = code[:, None] == jnp.arange(devices * slots)[None, :]
        wanted = jnp.max(jnp.where(chosen, local[:, None], -1), 0)
        wanted = to_each(wanted.reshape(devices, slots)).reshape(-1)
        held = wanted[:, None] == jnp.arange(own_words)[None, :]
        return chosen.astype(low_type), held.astype(low_type)

    def fetch(maps):
        chosen, held = maps
        found = contract(held, table_low, 1, 0).astype(low_type)
        found = to_each(found.reshape(devices, slots, width)).reshape(-1, width)
        return contract(chosen, found, 1, 0)

    def give(maps, grads):
        chosen, held = maps
        sums = contract(chosen, grads.astype(low_type), 0, 0).astype(low_type)
        sums = to_each(sums.reshape(devices, slots, width)).reshape(-1, width)
        return contract(held, sums, 0, 0)

    def later_rounds(asked, rounds, value, visit):
        def body(turn, carry):
            return carry + visit(round_of(asked, turn))

        return lax.fori_loop(1, rounds, body, value)

    src_ask, dec_ask = ask(src_in), ask(dec_in)
    local_facts = [
        jnp.sum(tgt_mask),
        jnp.max(counts),
        src_ask[3],
        dec_ask[3],
    ]

    def combine(first, second):
        added = jnp.arange(len(local_facts))[None, :] == 0
        return jnp.where(added, first + second, jnp.maximum(first, second))

    def reduce(values, axis):
        return jnp.concatenate([lax.psum(values[:, :1], axis), lax.pmax(values[:, 1:], axis)], 1)

    facts = everywhere(jnp.stack(local_facts).astype(jnp.int32).reshape(1, -1), combine, reduce)[0]
    count = facts[0].astype(f32)
    cut = -(-(span * 3 // 8) // 128) * 128
    more = facts[1] > cut
    src_maps = round_of(src_ask, 0)
    src_found = fetch(src_maps)
    dec_maps = round_of(dec_ask, 0)
    dec_found = fetch(dec_maps)

    starts_at = jnp.cumsum(counts) - counts
    total = jnp.sum(counts)
    rank = jnp.cumsum(masked.astype(jnp.int32), -1) - 1
    slot_of = jnp.where(masked, rank + starts_at[:, None], -1)
    slot_index = jnp.arange(seqs * span)
    slot_label = jnp.sum(
        jnp.where(slot_of.reshape(1, -1) == slot_index[:, None], labels.reshape(1, -1), 0), -1
    )
    valid = slot_index < total
    targets = jnp.where(valid, slot_label - vocab_base, -1).reshape(1, -1)
    left = total % place_block
    chunks = jnp.stack(
        [
            total // place_block + (left > place_block // 2).astype(jnp.int32),
            ((left > 0) & (left <= place_block // 2)).astype(jnp.int32),
        ]
    )
    own_rank = pick(jnp.where(masked, rank, -1), 0, side)
    own_chosen = (own_rank[None, :] == jnp.arange(span)[:, None]).astype(low_type)
    own_slots = (pick(slot_of, 0, side)[:, None] == slot_index[None, :]).astype(low_type)

    own_places = offset + jnp.arange(span)
    src_start, src_length = pick(src_starts, 0, row), pick(src_lengths, 0, row)
    tgt_start, tgt_length = pick(tgt_starts, 0, row), pick(tgt_lengths, 0, row)
    src_number, src_open = place_spans(src_start, own_places)
    tgt_number, tgt_open = place_spans(tgt_start, own_places)
    block = min(query_block, span)
    enc_spans = key_spans(src_number, src_start, src_length, block)
    self_spans = key_spans(tgt_number, tgt_start, tgt_length, block)
    cross_spans = key_spans(tgt_number, src_start, src_length, block)
    src_wave, tgt_wave = lax.optimization_barrier(
        (sinusoid(own_places - src_open, width), sinusoid(own_places - tgt_open, width))
    )

    root = math.sqrt(width)
    src_found = later_rounds(src_ask, facts[2], src_found, fetch)
    dec_found = later_rounds(dec_ask, facts[3], dec_found, fetch)
    stream0 = src_found * root + src_wave
    target0 = dec_found * root + tgt_wave

    def norm(stream, index):
        return layer_norm(stream, gains[index], biases[index])

    def keys_of_row(part):
        if group == 1:
            return part
        return lax.all_gather(part, "seq", axis=1, tiled=True, axis_index_groups=sharers)

    def keys_to_place(part):
        if group == 1:
            return part
        return lax.psum_scatter(
            part, "seq", scatter_dimension=1, tiled=True, axis_index_groups=sharers
        )

    def self_attention(inner, weight_in, weight_out, spans):
        triple = contract(weight_in, inner, 0, 1).astype(low_type)
        keys = triple if group == 1 else keys_of_row(triple[width:])
        mixed, lse = attend_forward(triple, keys, group == 1, *spans)
        return contract(mixed, weight_out, 0, 0), (triple, keys, mixed, lse)

    def self_attention_back(inner, weight_in, weight_out, spans, kept, grad):
        triple, keys, mixed, lse = kept
        grad_low = grad.astype(low_type)
        d_out = contract(mixed, grad_low, 1, 0)
        d_mixed = contract(weight_out, grad_low, 1, 1).astype(low_type)
        d_query, d_keys = attend_backward(triple, keys, group == 1, *spans, lse, d_mixed)
        d_triple = jnp.concatenate([d_query, keys_to_place(d_keys)], 0)
        return contract(d_triple, weight_in, 0, 1), contract(inner, d_triple, 0, 1), d_out

    def cross_attention(inner, memory, weight_in, weight_out, spans):
        queries = contract(weight_in[:, :width], inner, 0, 1).astype(low_type)
        keys = keys_of_row(contract(weight_in[:, width:], memory, 0, 1).astype(low_type))
        mixed, lse = attend_forward(queries, keys, False, *spans)
        return contract(mixed, weight_out, 0, 0), (queries, keys, mixed, lse)

    def cross_attention_back(inner, memory, weight_in, weight_out, spans, kept, grad):
        queries, keys, mixed, lse = kept
        grad_low = grad.astype(low_type)
        d_out = contract(mixed, grad_low, 1, 0)
        d_mixed = contract(weight_out, grad_low, 1, 1).astype(low_type)
        d_query, d_keys = attend_backward(queries, keys, False, *spans, lse, d_mixed)
        d_keys = keys_to_place(d_keys)
        d_in = jnp.concatenate([contract(inner, d_query, 0, 1), contract(memory, d_keys, 0, 1)], 1)
        return (
            contract(d_query, weight_in[:, :width], 0, 1),
            contract(d_keys, weight_in[:, width:], 0, 1),
            d_in,
            d_out,
        )

    def ffn(inner, weight_one, weight_two):
        hidden = contract(inner, weight_one, 1, 0)
        active = jax.nn.gelu(hidden).astype(low_type)
        return contract(active, weight_two, 1, 0), (hidden, active)

    def ffn_back(inner, weight_one, weight_two, kept, grad):
        hidden, active = kept
        grad_low = grad.astype(low_type)
        d_two = contract(active, grad_low, 0, 0)
        d_active = contract(grad_low, weight_two, 1, 1)
        d_hidden = jax.vjp(jax.nn.gelu, hidden)[1](d_active)[0].astype(low_type)
        return contract(d_hidden, weight_one, 1, 1), contract(inner, d_hidden, 0, 0), d_two

    inner0 = norm(stream0, 0).astype(low_type)
    branch0, keep0 = self_attention(inner0, w_in0, w_out0, enc_spans)
    stream1 = stream0 + branch0
    inner1 = norm(stream1, 1).astype(low_type)
    branch1, keep1 = ffn(inner1, f_in0, f_out0)
    stream2 = stream1 + branch1
    memory = norm(stream2, 2).astype(low_type)
    inner3 = norm(target0, 3).astype(low_type)
    branch3, keep3 = self_attention(inner3, w_in1, w_out1, self_spans)
    target1 = target0 + branch3
    inner4 = norm(target1, 4).astype(low_type)
    branch4, keep4 = cross_attention(inner4, memory, w_in2, w_out2, cross_spans)
    target2 = target1 + branch4
    inner5 = norm(target2, 5).astype(low_type)
    branch5, keep5 = ffn(inner5, f_in1, f_out1)
    target3 = target2 + branch5
    final = norm(target3, 6).astype(low_type)

    packed = contract(own_chosen, final, 1, 0).astype(low_type)
    if seqs == 2:
        other = swap_rows(packed, cut, more)
        packs = [jnp.where(side == 0, packed, other), jnp.where(side == 0, other, packed)]
    else:
        packs = lax.all_gather(packed, "seq", axis=0)
        packs = [packs[s] for s in range(seqs)]
    rows = jnp.zeros((seqs * span, width), low_type)
    pieces = sum(
        lax.dynamic_update_slice_in_dim(rows, packs[s], starts_at[s], 0) for s in range(seqs)
    )
    every = gather_seq(head_stats(chunks, table_part, pieces), 0)
    top_logit = jnp.max(every[:, 0], 0)
    totals = jnp.sum(every[:, 1] * jnp.exp(every[:, 0] - top_logit[None]), 0)
    log_total = top_logit + jnp.log(jnp.where(valid, totals, 1.0))
    own_start = pick(starts_at, 0, side)
    mine = (slot_index >= own_start) & (slot_index < own_start + pick(counts, 0, side))
    token_local = jnp.sum(jnp.where(mine, log_total, 0.0))
    logs = jnp.where(valid, log_total + jnp.log(count), 1e30)
    weights = jnp.where(valid, 1.0 / count, 0.0)
    d_table, d_pieces, picks = head_back(
        chunks, table_part, pieces, targets, logs[None], weights[None]
    )
    token_local = token_local - jnp.sum(picks)
    owned_table = d_table.reshape(owners, own_words, width)
    half = width // 2
    table_one = Halving([owned_table[:, :, :half]], False)
    if seqs != 2:
        d_pieces = lax.psum(d_pieces, "seq")
    d_high = lax.reduce_precision(d_pieces, 8, 7)
    d_rest = (d_pieces - d_high).astype(low_type)
    d_high = d_high.astype(low_type)
    d_final = contract(own_slots, d_high, 1, 1) + contract(own_slots, d_rest, 1, 1)
    if seqs == 2:
        away_start, away_count = pick(starts_at, 0, 1 - side), pick(counts, 0, 1 - side)
        index = jnp.arange(span)[:, None]
        away = (slot_index[None, :] == index + away_start) & (index < away_count)
        away = contract(away.astype(low_type), d_high, 1, 1).astype(low_type)
        d_final = d_final + contract(own_chosen, swap_rows(away, cut, more), 0, 0)

    first_place = own_places[None, :] == src_start[:, None]
    mine = jnp.any(first_place, -1)
    first_rows = contract(first_place.astype(low_type), memory, 1, 0).astype(low_type)
    len_logits = contract(first_rows, w_len, 1, 0)
    len_label = jnp.minimum(tgt_length, classes - 1)
    len_hot = jnp.arange(classes)[None, :] == len_label[:, None]
    len_loss = jax.nn.logsumexp(len_logits, -1) - jnp.sum(jnp.where(len_hot, len_logits, 0.0), -1)
    len_local = jnp.sum(jnp.where(mine, len_loss, 0.0))
    sentences = rows_here * src_lengths.shape[1] * owners
    len_prob = jax.nn.softmax(len_logits, -1)
    d_len_logits = (
        jnp.where(mine[:, None], len_prob - len_hot.astype(f32), 0.0) * (0.1 / sentences)
    ).astype(low_type)
    d_w_len = contract(first_rows, d_len_logits, 0, 0)
    d_first = contract(d_len_logits, w_len, 1, 1)
    d_memory = lax.dot_general(
        first_place.astype(f32),
        d_first,
        (((0,), (0,)), ((), ())),
        precision=lax.Precision.HIGHEST,
        preferred_element_type=f32,
    )

    def owned(grad):
        return grad.reshape(owners, -1, grad.shape[1])

    def owned_columns(grad):
        whole = owned(grad)
        return [whole[:, at : at + share] for at in range(0, whole.shape[1], share)]

    d_target3, gain6, bias6 = norm_backward(target3, gains[6], biases[6], d_final)
    d_inner5, d_fin1, d_fout1 = ffn_back(inner5, f_in1, f_out1, keep5, d_target3)
    chains = [table_one]
    (d_inner5, d_target3, owned_table) = advance((d_inner5, d_target3, owned_table), chains)
    table_two = Halving([owned_table[:, :, half:]], False)
    chain_a = Halving([owned(d_fin1)] + owned_columns(d_fout1), True)
    d_target2, gain5, bias5 = norm_backward(target2, gains[5], biases[5], d_inner5)
    d_target2 = d_target2 + d_target3
    d_inner4, d_cross, d_win2, d_wout2 = cross_attention_back(
        inner4, memory, w_in2, w_out2, cross_spans, keep4, d_target2
    )
    chains += [table_two, chain_a]
    d_inner4, d_target2, d_cross = advance((d_inner4, d_target2, d_cross), chains)
    chain_b = Halving([owned(d_win2), owned(d_wout2)], True)
    d_target1, gain4, bias4 = norm_backward(target1, gains[4], biases[4], d_inner4)
    d_target1 = d_target1 + d_target2
    d_inner3, d_win1, d_wout1 = self_attention_back(
        inner3, w_in1, w_out1, self_spans, keep3, d_target1
    )
    chains += [chain_b]
    d_inner3, d_target1 = advance((d_inner3, d_target1), chains)
    chain_c = Halving([owned(d_win1), owned(d_wout1)], True)
    d_target0, gain3, bias3 = norm_backward(target0, gains[3], biases[3], d_inner3)
    d_target0 = d_target0 + d_target1
    dec_grad = d_target0 * root
    dec_given = give(dec_maps, dec_grad)
    d_stream2, gain2, bias2 = norm_backward(stream2, gains[2], biases[2], d_memory + d_cross)
    d_inner1, d_fin0, d_fout0 = ffn_back(inner1, f_in0, f_out0, keep1, d_stream2)
    chains += [chain_c]
    d_inner1, d_stream2 = advance((d_inner1, d_stream2), chains)
    chain_d = Halving([owned(d_fin0)] + owned_columns(d_fout0), True)
    d_stream1, gain1, bias1 = norm_backward(stream1, gains[1], biases[1], d_inner1)
    d_stream1 = d_stream1 + d_stream2
    d_inner0, d_win0, d_wout0 = self_attention_back(
        inner0, w_in0, w_out0, enc_spans, keep0, d_stream1
    )
    chains += [chain_d]
    d_inner0, d_stream1 = advance((d_inner0, d_stream1), chains)
    d_stream0, gain0, bias0 = norm_backward(stream0, gains[0], biases[0], d_inner0)
    d_stream0 = d_stream0 + d_stream1
    src_grad = d_stream0 * root
    src_given = give(src_maps, src_grad)
    norm_grads = [gain0, gain1, gain2, gain3, gain4, gain5, gain6]
    norm_grads += [bias0, bias1, bias2, bias3, bias4, bias5, bias6]
    g_norms = everywhere(jnp.stack(norm_grads), jnp.add, lax.psum)
    norm_square = jnp.where((side == 0) & (lax.axis_index("dp") == 0), jnp.sum(g_norms * g_norms), 0.0)
    norm_share = norms.shape[2]
    g_norms = lax.dynamic_slice_in_dim(g_norms, lax.axis_index("dp") * norm_share, norm_share, 1)
    chain_e = Halving([owned(d_win0), owned(d_wout0), owned(d_w_len)], True)
    chains += [chain_e]
    while any(chain.pending is not None for chain in chains):
        advance((), chains)
    for chain in chains:
        chain.finish()

    given = dec_given + src_given
    given = later_rounds(dec_ask, facts[3], given, lambda maps: give(maps, dec_grad))
    given = later_rounds(src_ask, facts[2], given, lambda maps: give(maps, src_grad))
    table_grad = jnp.concatenate(
        [table_one.value.reshape(own_words, -1), table_two.value.reshape(own_words, -1)], 1
    )
    table_grad = table_grad + given
    square = sum(chain.square for chain in (chain_a, chain_b, chain_c, chain_d, chain_e))
    square = square + jnp.sum(table_grad * table_grad) + norm_square
    sums = everywhere(
        jnp.stack([token_local, len_local, square]).reshape(1, 3), jnp.add, lax.psum
    )[0]
    token_sum, len_sum, grad_norm = sums[0], sums[1], jnp.sqrt(sums[2])
    factor = jnp.minimum(1.0, clip_limit / (grad_norm + 1e-06))

    def cut_columns(chain, sizes):
        result, at = [], 0
        value = chain.value.reshape(share, -1)
        for size in sizes:
            result.append(value[:, at : at + size])
            at += size
        return result

    hidden_width = ffn_in.shape[2]
    pieces_out = ffn_out.shape[1] // share
    ffn_sizes = [hidden_width] + [width] * pieces_out
    attn_sizes = [3 * width, width]
    g_fin1, *g_fout1 = cut_columns(chain_a, ffn_sizes)
    g_win2, g_wout2 = cut_columns(chain_b, attn_sizes)
    g_win1, g_wout1 = cut_columns(chain_c, attn_sizes)
    g_fin0, *g_fout0 = cut_columns(chain_d, ffn_sizes)
    g_win0, g_wout0, g_len = cut_columns(chain_e, attn_sizes + [classes])
    grads = (
        jnp.stack([g_win0, g_win1, g_win2]),
        jnp.stack([g_wout0, g_wout1, g_wout2]),
        jnp.stack([g_fin0, g_fin1]),
        jnp.stack([jnp.concatenate(g_fout0, 0), jnp.concatenate(g_fout1, 0)]),
        g_len,
        g_norms.reshape(norms.shape),
        table_grad,
    )
    masters = (attn_in, attn_out, ffn_in, ffn_out, len_head, norms, table)
    firsts = (attn_in_m1, attn_out_m1, ffn_in_m1, ffn_out_m1, len_head_m1, norms_m1, table_m1)
    seconds = (attn_in_m2, attn_out_m2, ffn_in_m2, ffn_out_m2, len_head_m2, norms_m2, table_m2)
    updates = []
    for weight, first, second, grad, rate in zip(masters, firsts, seconds, grads, step_rates):
        updates.extend(adam_update(weight, first, second, grad * factor, rate))
    return (token_sum, count, len_sum, grad_norm, *updates)


def solution(mesh):
    layer, head, scales, words = P(None, "dp", None), P("dp", None), P(None, None, "dp"), P(("seq", "dp"), None)
    owned = (layer,) * 12 + (head,) * 3 + (scales,) * 3 + (words,) * 3
    ids, lengths = P("dp", "seq"), P("dp", None)
    in_specs = (ids, ids, lengths, lengths, ids) + owned
    out_specs = (P(), P(), P(), P()) + owned
    return jax.shard_map(
        on_device, mesh=mesh, in_specs=in_specs, out_specs=out_specs, check_vma=False
    )
```

```python
import functools
import math

import jax
import jax.numpy as jnp
from jax import lax
from jax.experimental import pallas as pl
from jax.experimental.pallas import tpu as pltpu
from jax.sharding import PartitionSpec as P

HEADS = 8
STEP = 10


length_token = 1
mask_token = 2
clip_limit = 0.002
beta_one = 0.9
beta_two = 0.98
adam_eps = 1e-08
weight_decay = 0.01
step_rates = (0.05, 0.25, 0.05, 0.025, 0.05, 0.5, 0.1)

low_type = jnp.bfloat16
f32 = jnp.float32
query_block = 256
key_block = 128
place_block = 256
vmem_bytes = 56 * 1024 * 1024


def sinusoid(positions, width):
    half_width = width // 2
    frequency = jnp.exp(jnp.arange(half_width).astype(f32) * (-math.log(10000.0) / half_width))
    angles = positions.astype(f32)[..., None] * frequency
    return jnp.concatenate([jnp.sin(angles), jnp.cos(angles)], -1)


def layer_norm(stream, norm_gain, norm_bias):
    average = jnp.mean(stream, -1, keepdims=True)
    centred = stream - average
    variance = jnp.mean(centred * centred, -1, keepdims=True)
    return centred * lax.rsqrt(variance + 1e-05) * norm_gain + norm_bias


def contract(left, right, left_dim, right_dim):
    return lax.dot_general(
        left, right, (((left_dim,), (right_dim,)), ((), ())), preferred_element_type=f32
    )


def attend_forward_kernel(bounds, q_ref, k_ref, v_ref, span_ref, out_ref, lse_ref, hold, *, head):
    step = pl.program_id(0)
    first, last = bounds[0, step], bounds[1, step]
    width, queries = q_ref.shape
    heads = width // head
    scale = head**-0.5
    low, high = span_ref[0:1, :], span_ref[1:2, :]
    inner = lax.broadcasted_iota(jnp.int32, (key_block, queries), 0)

    def fold(values, op):
        return op(values.reshape(key_block // 8, 8, queries), axis=0)

    def score(block, tops):
        start = pl.multiple_of(block * key_block, key_block)
        place = inner + start
        allowed = (place >= low) & (place < high)
        result = []
        for h in range(heads):
            rows = slice(h * head, (h + 1) * head)
            s = contract(k_ref[rows, pl.ds(start, key_block)], q_ref[rows, :], 0, 0) * scale
            s = jnp.where(allowed, s, -1e30)
            hold[h, pl.ds(start, key_block), :] = s
            result.append(jnp.maximum(tops[h], fold(s, jnp.max)))
        return tuple(result)

    tops = lax.fori_loop(
        first, last, score, tuple(jnp.full((8, queries), -1e30, f32) for _ in range(heads))
    )
    tops = [jnp.max(t, axis=0, keepdims=True) for t in tops]

    def power(block, sums):
        start = pl.multiple_of(block * key_block, key_block)
        result = []
        for h in range(heads):
            e = jnp.exp(hold[h, pl.ds(start, key_block), :] - tops[h])
            hold[h, pl.ds(start, key_block), :] = e
            result.append(sums[h] + fold(e, jnp.sum))
        return tuple(result)

    sums = lax.fori_loop(
        first, last, power, tuple(jnp.zeros((8, queries), f32) for _ in range(heads))
    )
    sums = [jnp.maximum(jnp.sum(t, axis=0, keepdims=True), 1e-30) for t in sums]
    inverse = [1.0 / t for t in sums]

    def mix(block, outs):
        start = pl.multiple_of(block * key_block, key_block)
        result = []
        for h in range(heads):
            rows = slice(h * head, (h + 1) * head)
            p = (hold[h, pl.ds(start, key_block), :] * inverse[h]).astype(low_type)
            result.append(outs[h] + contract(v_ref[rows, pl.ds(start, key_block)], p, 1, 0))
        return tuple(result)

    outs = lax.fori_loop(
        first, last, mix, tuple(jnp.zeros((head, queries), f32) for _ in range(heads))
    )
    for h in range(heads):
        out_ref[h * head : (h + 1) * head, :] = outs[h].astype(low_type)
        lse_ref[h : h + 1, :] = tops[h] + jnp.log(sums[h])


def attend_backward_kernel(
    bounds, q_ref, k_ref, v_ref, span_ref, lse_ref, do_ref, dq_ref, dkv_ref, p_hold, d_hold, acc,
    *, head
):
    step = pl.program_id(0)
    first, last = bounds[0, step], bounds[1, step]
    width, queries = q_ref.shape
    heads = width // head
    scale = head**-0.5
    low, high = span_ref[0:1, :], span_ref[1:2, :]
    inner = lax.broadcasted_iota(jnp.int32, (key_block, queries), 0)

    @pl.when(step == 0)
    def _():
        acc[...] = jnp.zeros_like(acc)

    def one(block, deltas):
        start = pl.multiple_of(block * key_block, key_block)
        keys = pl.ds(start, key_block)
        place = inner + start
        allowed = (place >= low) & (place < high)
        result = []
        for h in range(heads):
            rows = slice(h * head, (h + 1) * head)
            s = contract(k_ref[rows, keys], q_ref[rows, :], 0, 0) * scale
            p = jnp.exp(jnp.where(allowed, s, -1e30) - lse_ref[h : h + 1, :])
            dp = contract(v_ref[rows, keys], do_ref[rows, :], 0, 0)
            p_hold[h, keys, :] = p
            d_hold[h, keys, :] = dp
            result.append(
                deltas[h] + jnp.sum((p * dp).reshape(key_block // 8, 8, queries), axis=0)
            )
            below = slice(width + h * head, width + (h + 1) * head)
            acc[below, keys] += contract(do_ref[rows, :], p.astype(low_type), 1, 1)
        return tuple(result)

    deltas = lax.fori_loop(
        first, last, one, tuple(jnp.zeros((8, queries), f32) for _ in range(heads))
    )
    deltas = [jnp.sum(t, axis=0, keepdims=True) for t in deltas]

    def two(block, outs):
        start = pl.multiple_of(block * key_block, key_block)
        keys = pl.ds(start, key_block)
        result = []
        for h in range(heads):
            rows = slice(h * head, (h + 1) * head)
            ds = (p_hold[h, keys, :] * (d_hold[h, keys, :] - deltas[h])).astype(low_type)
            result.append(outs[h] + contract(k_ref[rows, keys], ds, 1, 0))
            acc[rows, keys] += contract(q_ref[rows, :], ds, 1, 1) * scale
        return tuple(result)

    outs = lax.fori_loop(
        first, last, two, tuple(jnp.zeros((head, queries), f32) for _ in range(heads))
    )
    for h in range(heads):
        dq_ref[h * head : (h + 1) * head, :] = (outs[h] * scale).astype(low_type)

    @pl.when(step == pl.num_programs(0) - 1)
    def _():
        dkv_ref[...] = acc[...].astype(low_type)


def attend_specs(width, length, block, shared):
    key_row = 1 if shared else 0
    return [
        pl.BlockSpec((width, block), lambda i, *_: (0, i)),
        pl.BlockSpec((width, length), lambda i, *_: (key_row, 0)),
        pl.BlockSpec((width, length), lambda i, *_: (key_row + 1, 0)),
        pl.BlockSpec((2, block), lambda i, *_: (0, i)),
    ]


def attend_forward(queries, keys, shared, spans, bounds):
    width = keys.shape[0] // (3 if shared else 2)
    places, length = queries.shape[1], keys.shape[1]
    block = min(query_block, places)
    return pl.pallas_call(
        functools.partial(attend_forward_kernel, head=width // HEADS),
        grid_spec=pltpu.PrefetchScalarGridSpec(
            num_scalar_prefetch=1,
            grid=(places // block,),
            in_specs=attend_specs(width, length, block, shared),
            out_specs=[
                pl.BlockSpec((width, block), lambda i, *_: (0, i)),
                pl.BlockSpec((HEADS, block), lambda i, *_: (0, i)),
            ],
            scratch_shapes=[pltpu.VMEM((HEADS, length, block), f32)],
        ),
        out_shape=[
            jax.ShapeDtypeStruct((width, places), low_type),
            jax.ShapeDtypeStruct((HEADS, places), f32),
        ],
        compiler_params=pltpu.CompilerParams(vmem_limit_bytes=vmem_bytes),
        name="attend_forward",
    )(bounds, queries, keys, keys, spans)


def attend_backward(queries, keys, shared, spans, bounds, lse, d_mixed):
    width = keys.shape[0] // (3 if shared else 2)
    places, length = queries.shape[1], keys.shape[1]
    block = min(query_block, places)
    return pl.pallas_call(
        functools.partial(attend_backward_kernel, head=width // HEADS),
        grid_spec=pltpu.PrefetchScalarGridSpec(
            num_scalar_prefetch=1,
            grid=(places // block,),
            in_specs=attend_specs(width, length, block, shared)
            + [
                pl.BlockSpec((HEADS, block), lambda i, *_: (0, i)),
                pl.BlockSpec((width, block), lambda i, *_: (0, i)),
            ],
            out_specs=[
                pl.BlockSpec((width, block), lambda i, *_: (0, i)),
                pl.BlockSpec((2 * width, length), lambda i, *_: (0, 0)),
            ],
            scratch_shapes=[
                pltpu.VMEM((HEADS, length, block), f32),
                pltpu.VMEM((HEADS, length, block), f32),
                pltpu.VMEM((2 * width, length), f32),
            ],
        ),
        out_shape=[
            jax.ShapeDtypeStruct((width, places), low_type),
            jax.ShapeDtypeStruct((2 * width, length), low_type),
        ],
        compiler_params=pltpu.CompilerParams(vmem_limit_bytes=vmem_bytes),
        name="attend_backward",
    )(bounds, queries, keys, keys, spans, lse, d_mixed)


def norm_back_kernel(stream_ref, gain_ref, grad_ref, rest_ref, out_ref, sums_ref):
    @pl.when(pl.program_id(0) == 0)
    def _():
        sums_ref[...] = jnp.zeros_like(sums_ref)

    stream, grad = stream_ref[...], grad_ref[...]
    rows, width = stream.shape
    average = jnp.mean(stream, -1, keepdims=True)
    centred = stream - average
    variance = jnp.mean(centred * centred, -1, keepdims=True)
    inverse = lax.rsqrt(variance + 1e-05)
    unit = centred * inverse
    scaled = grad * gain_ref[...]
    along = jnp.mean(scaled * unit, -1, keepdims=True)
    level = jnp.mean(scaled, -1, keepdims=True)
    out_ref[...] = rest_ref[...] + (scaled - level - unit * along) * inverse
    sums_ref[0:8, :] += jnp.sum((grad * unit).reshape(rows // 8, 8, width), 0)
    sums_ref[8:16, :] += jnp.sum(grad.reshape(rows // 8, 8, width), 0)


def norm_backward(stream, gain, grad, rest):
    places, width = stream.shape
    rows = min(256, places)
    block = pl.BlockSpec((rows, width), lambda i: (i, 0))
    out, sums = pl.pallas_call(
        norm_back_kernel,
        grid=(places // rows,),
        in_specs=[block, pl.BlockSpec((1, width), lambda i: (0, 0)), block, block],
        out_specs=[block, pl.BlockSpec((16, width), lambda i: (0, 0))],
        out_shape=[
            jax.ShapeDtypeStruct((places, width), f32),
            jax.ShapeDtypeStruct((16, width), f32),
        ],
        compiler_params=pltpu.CompilerParams(vmem_limit_bytes=vmem_bytes),
        name="norm_backward",
    )(stream, gain[None], grad, rest)
    return out, jnp.sum(sums[:8], 0), jnp.sum(sums[8:], 0)


def each_chunk(plan, visit):
    wides = plan.shape[0] - 2

    def wide(index, carry):
        visit(pl.multiple_of(plan[2 + index], place_block // 2), place_block)
        return carry

    def narrow(index, carry):
        visit(pl.multiple_of(plan[wides + 1 - index], place_block // 2), place_block // 2)
        return carry

    lax.fori_loop(0, plan[0], wide, 0)
    lax.fori_loop(0, plan[1], narrow, 0)


def chunk_plan(counts, span):
    half = place_block // 2
    left = counts % place_block
    wides = counts // place_block + (left > half).astype(jnp.int32)
    narrows = ((left > 0) & (left <= half)).astype(jnp.int32)
    segments = counts.shape[0]
    base = jnp.arange(segments) * span
    index = jnp.arange(span // place_block)
    used = (index[None, :] < wides[:, None]).reshape(-1)
    begins = (base[:, None] + index[None, :] * place_block).reshape(-1)
    total = used.shape[0] + segments
    at = jnp.where(used, jnp.cumsum(used.astype(jnp.int32)) - 1, -1)
    narrow_at = jnp.where(narrows > 0, total - jnp.cumsum(narrows), -1)
    at = jnp.concatenate([at, narrow_at])
    begins = jnp.concatenate([begins, base + wides * place_block])
    listed = jnp.sum(jnp.where(at[None, :] == jnp.arange(total)[:, None], begins[None, :], 0), 1)
    return jnp.concatenate([jnp.stack([jnp.sum(wides), jnp.sum(narrows)]), listed]).astype(jnp.int32)


def parts_of(words):
    for count in (5, 4, 2):
        if words % (16 * count) == 0:
            return [slice(i * (words // count), (i + 1) * (words // count)) for i in range(count)]
    return [slice(0, words)]


def head_stats_kernel(plan, table_ref, rows_ref, stats_ref, tops, sums):
    step = pl.program_id(0)

    @pl.when(step == 0)
    def _():
        tops[...] = jnp.full_like(tops, -1e30)
        sums[...] = jnp.zeros_like(sums)

    def visit(start, size):
        here = pl.ds(start, size)
        rows = rows_ref[here, :]
        old, total = tops[:, here], sums[:, here]
        for part in parts_of(table_ref.shape[0]):
            logits = contract(table_ref[part, :], rows, 1, 1)
            logits = logits.reshape(logits.shape[0] // 8, 8, size)
            top = jnp.maximum(old, jnp.max(logits, axis=0))
            powers = jnp.sum(jnp.exp(logits - top[None]), axis=0)
            total = total * jnp.exp(old - top) + powers
            old = top
        sums[:, here] = total
        tops[:, here] = old

    each_chunk(plan, visit)

    @pl.when(step == pl.num_programs(0) - 1)
    def _():
        top = jnp.max(tops[...], axis=0, keepdims=True)
        stats_ref[0:1, :] = top
        stats_ref[1:2, :] = jnp.sum(sums[...] * jnp.exp(tops[...] - top), axis=0, keepdims=True)


def head_back_kernel(
    plan, table_ref, rows_ref, target_ref, log_ref, weight_ref, one_ref, two_ref, dr_ref, pick_ref
):
    step = pl.program_id(0)
    words, width = table_ref.shape
    half = one_ref.shape[1]

    @pl.when(step == 0)
    def _():
        dr_ref[...] = jnp.zeros_like(dr_ref)
        pick_ref[...] = jnp.zeros_like(pick_ref)

    one_ref[...] = jnp.zeros_like(one_ref)
    two_ref[...] = jnp.zeros_like(two_ref)

    def visit(start, size):
        here = pl.ds(start, size)
        rows = rows_ref[here, :]
        target = target_ref[:, here] - step * words
        log, weight = log_ref[:, here], weight_ref[:, here]
        back = jnp.zeros((size, width), f32)
        found = jnp.zeros((8, size), f32)
        for part in parts_of(words):
            block = table_ref[part, :]
            count = block.shape[0]
            inner = lax.broadcasted_iota(jnp.int32, (count, size), 0) + part.start
            logits = contract(block, rows, 1, 1)
            scaled = jnp.exp(logits - log)
            hit = inner == target
            found += jnp.sum(jnp.where(hit, logits, 0.0).reshape(count // 8, 8, size), axis=0)
            d_logits = jnp.where(hit, scaled - weight, scaled).astype(low_type)
            one_ref[part, :] += contract(d_logits, rows[:, :half], 1, 0)
            two_ref[part, :] += contract(d_logits, rows[:, half:], 1, 0)
            back += contract(d_logits, block, 0, 0)
        pick_ref[:, here] += found
        dr_ref[here, :] += back

    each_chunk(plan, visit)


def word_block(words):
    return max(n for n in range(16, 1601, 16) if words % n == 0)


def head_specs(words, width, places):
    return [
        pl.BlockSpec((words, width), lambda i, *_: (i, 0)),
        pl.BlockSpec((places, width), lambda i, *_: (0, 0)),
    ]


def head_stats(plan, table_part, rows):
    words = word_block(table_part.shape[0])
    places, width = rows.shape
    return pl.pallas_call(
        head_stats_kernel,
        grid_spec=pltpu.PrefetchScalarGridSpec(
            num_scalar_prefetch=1,
            grid=(table_part.shape[0] // words,),
            in_specs=head_specs(words, width, places),
            out_specs=pl.BlockSpec((2, places), lambda i, *_: (0, 0)),
            scratch_shapes=[pltpu.VMEM((8, places), f32) for _ in range(2)],
        ),
        out_shape=jax.ShapeDtypeStruct((2, places), f32),
        compiler_params=pltpu.CompilerParams(vmem_limit_bytes=vmem_bytes),
        name="head_stats",
    )(plan, table_part, rows)


def head_back(plan, table_part, rows, targets, logs, weights):
    words = word_block(table_part.shape[0])
    places, width = rows.shape
    half = width // 2
    return pl.pallas_call(
        head_back_kernel,
        grid_spec=pltpu.PrefetchScalarGridSpec(
            num_scalar_prefetch=1,
            grid=(table_part.shape[0] // words,),
            in_specs=head_specs(words, width, places)
            + [pl.BlockSpec((1, places), lambda i, *_: (0, 0)) for _ in range(3)],
            out_specs=[
                pl.BlockSpec((words, half), lambda i, *_: (i, 0)),
                pl.BlockSpec((words, half), lambda i, *_: (i, 0)),
                pl.BlockSpec((places, width), lambda i, *_: (0, 0)),
                pl.BlockSpec((8, places), lambda i, *_: (0, 0)),
            ],
        ),
        out_shape=[
            jax.ShapeDtypeStruct((table_part.shape[0], half), f32),
            jax.ShapeDtypeStruct((table_part.shape[0], half), f32),
            jax.ShapeDtypeStruct((places, width), f32),
            jax.ShapeDtypeStruct((8, places), f32),
        ],
        compiler_params=pltpu.CompilerParams(vmem_limit_bytes=vmem_bytes),
        name="head_back",
    )(plan, table_part, rows, targets, logs, weights)


def swap(values, axis, bit):
    size = lax.axis_size(axis)
    return lax.ppermute(values, axis, [(i, i ^ bit) for i in range(size)])


def power_of_two(size):
    return size & (size - 1) == 0


def everywhere(values, combine, reduce):
    for axis in ("dp", "seq"):
        size = lax.axis_size(axis)
        if power_of_two(size):
            bit = 1
            while bit < size:
                values = combine(values, swap(values, axis, bit))
                bit *= 2
        else:
            values = reduce(values, axis)
    return values


def pick(values, dim, index):
    return lax.dynamic_index_in_dim(values, index, dim, False)


def gather_seq(values, dim):
    if lax.axis_size("seq") == 2:
        other = swap(values, "seq", 1)
        first = lax.axis_index("seq") == 0
        return jnp.stack([jnp.where(first, values, other), jnp.where(first, other, values)], dim)
    return lax.all_gather(values, "seq", axis=dim)


def swap_rows(values, cut, more):
    rest = lax.cond(
        more, lambda part: swap(part, "seq", 1), lambda part: jnp.zeros_like(part), values[cut:]
    )
    return jnp.concatenate([swap(values[:cut], "seq", 1), rest], 0)


def to_each(values):
    return lax.all_to_all(values, ("seq", "dp"), 0, 0)


class Halving:
    def __init__(self, parts, joint):
        self.parts, self.joint = parts, joint
        self.rows = parts[0].shape[1]
        bits = []
        bit = 1
        while bit < lax.axis_size("dp"):
            bits.append(("dp", bit))
            bit *= 2
        self.steps = bits[:1] + ([("seq", 1)] if joint else []) + bits[1:]
        self.fast = power_of_two(lax.axis_size("dp")) and (
            not joint or (lax.axis_size("seq") == 2 and self.rows % 16 == 0)
        )
        self.fast = self.fast and all(part.shape[2] % 128 == 0 for part in parts)
        self.fast = self.fast and self.rows % 8 == 0
        self.pending, self.value, self.square, self.got = None, None, None, None
        if self.fast:
            self.launch()

    def launch(self):
        if self.value is not None:
            return
        if not self.steps:
            self.pending = swap(self.parts[0], "seq", 1)
            return
        axis, bit = self.steps[0]
        rows = self.rows // 2 if axis == "seq" else self.rows
        index = lax.axis_index(axis)
        mine = (index // bit) & 1

        def half(side):
            halves = [
                pick(part.reshape((-1, 2, rows, part.shape[2])), 1, side) for part in self.parts
            ]
            if self.got is not None:
                halves[0] = halves[0] + pick(
                    self.got.reshape((-1, 2, rows, self.got.shape[2])), 1, side
                ).astype(f32)
            return halves

        away = [part.astype(low_type) for part in half(1 - mine)]
        self.parts = [jnp.concatenate(half(mine), 2)]
        self.rows, self.got = rows, None
        self.pending = swap(jnp.concatenate(away, 2), axis, bit)

    def absorb(self, got):
        self.pending = None
        if not self.steps:
            first = lax.axis_index("seq") == 0
            part = self.parts[0]
            self.value = jnp.concatenate(
                [jnp.where(first, part, got), jnp.where(first, got, part)], 0
            )
            return
        self.steps.pop(0)
        self.got = got
        if not self.steps:
            part = (self.parts[0] + got.astype(f32)).reshape(self.rows, -1)
            self.parts = [part]
            self.square = jnp.sum(part * part)
            if not self.joint:
                self.value = part

    def finish(self):
        if self.fast:
            return
        whole = jnp.concatenate(self.parts, 2)
        part = lax.psum_scatter(whole, "dp", scatter_dimension=0)
        if self.joint:
            part = lax.psum(part, "seq")
        self.value, self.square = part, jnp.sum(part * part)
        if self.joint:
            self.square = jnp.where(lax.axis_index("seq") == 0, self.square, 0.0)


def advance(main, chains):
    live = [chain for chain in chains if chain.pending is not None]
    main, got = lax.optimization_barrier((main, [chain.pending for chain in live]))
    for chain, arrived in zip(live, got):
        chain.absorb(arrived)
        chain.launch()
    return main


def adam_update(weight, first, second, grad, rate):
    first = beta_one * first + (1 - beta_one) * grad
    second = beta_two * second + (1 - beta_two) * grad * grad
    first_hat = first / (1 - beta_one**STEP)
    second_hat = second / (1 - beta_two**STEP)
    weight = weight - rate * (first_hat / (jnp.sqrt(second_hat) + adam_eps) + weight_decay * weight)
    return (weight, first, second)


def place_spans(starts, places):
    covered = places[:, None] >= starts[None, :]
    number = jnp.sum(covered.astype(jnp.int32), -1) - 1
    return number, jnp.max(jnp.where(covered, starts[None, :], 0), -1)


def key_spans(number, starts, lengths, block):
    hot = number[:, None] == jnp.arange(starts.shape[0])[None, :]
    first = jnp.sum(jnp.where(hot, starts[None, :], 0), -1)
    last = jnp.sum(jnp.where(hot, (starts + lengths)[None, :], 0), -1)
    first_block = jnp.min(first.reshape(-1, block), -1) // key_block
    last_block = (jnp.max(last.reshape(-1, block), -1) + key_block - 1) // key_block
    return (
        jnp.stack([first, last]).astype(jnp.int32),
        jnp.stack([first_block, last_block]).astype(jnp.int32),
    )


def on_device(
    src_ids,
    tgt_ids,
    src_lengths,
    tgt_lengths,
    tgt_mask,
    attn_in,
    attn_in_m1,
    attn_in_m2,
    attn_out,
    attn_out_m1,
    attn_out_m2,
    ffn_in,
    ffn_in_m1,
    ffn_in_m2,
    ffn_out,
    ffn_out_m1,
    ffn_out_m2,
    len_head,
    len_head_m1,
    len_head_m2,
    norms,
    norms_m1,
    norms_m2,
    table,
    table_m1,
    table_m2,
):
    rows_here, seq_rows = src_ids.shape
    seqs, owners = lax.axis_size("seq"), lax.axis_size("dp")
    devices = seqs * owners
    row_len = seq_rows * seqs
    side = lax.axis_index("seq")
    group = seqs // rows_here
    span = row_len // group
    row, offset = side // group, (side % group) * span
    sharers = [[r * group + i for i in range(group)] for r in range(rows_here)]
    own_words, width = table.shape
    classes = len_head.shape[1]
    vocab_width = own_words * owners
    vocab_base = side * vocab_width
    norm_count = norms.shape[1]
    norm_columns = 128

    def columns_of(weight, rows):
        return [weight[at : at + rows] for at in range(0, weight.shape[0], rows)]

    def gather_columns(parts):
        joined = jnp.concatenate([part.astype(low_type) for part in parts], 1)
        if joined.shape[0] % (16 * seqs) == 0:
            rows = joined.shape[0] // seqs
            joined = lax.dynamic_slice_in_dim(joined, side * rows, rows, 0)
            whole = lax.all_gather(joined, ("dp", "seq"), axis=0, tiled=True)
        else:
            whole = lax.all_gather(joined, "dp", axis=0, tiled=True)
        result, at = [], 0
        for part in parts:
            result.append(whole[:, at : at + part.shape[1]])
            at += part.shape[1]
        return result

    def join_rows(pieces):
        blocks = [piece.reshape(owners, -1, piece.shape[1]) for piece in pieces]
        return jnp.concatenate(blocks, 1).reshape(-1, pieces[0].shape[1])

    share = attn_in.shape[1]
    norm_part = jnp.pad(
        norms.reshape(-1, norms.shape[2]).T, ((0, 0), (0, norm_columns - 2 * norm_count))
    )
    first_parts = [attn_in[0], attn_out[0], len_head, norm_part, ffn_in[0]]
    first_parts += columns_of(ffn_out[0], share)
    w_in0, w_out0, w_len, norm_low, f_in0, *f_out0 = gather_columns(first_parts)
    next_parts = [attn_in[1], attn_out[1], attn_in[2], attn_out[2], ffn_in[1]]
    next_parts += columns_of(ffn_out[1], share)
    w_in1, w_out1, w_in2, w_out2, f_in1, *f_out1 = gather_columns(next_parts)
    f_out0, f_out1 = join_rows(f_out0), join_rows(f_out1)
    table_low = table.astype(low_type)
    table_part = lax.all_gather(table_low, "dp", axis=0, tiled=True)
    norm_low = norm_low[:, : 2 * norm_count].T.astype(f32)
    gains, biases = norm_low[:norm_count], norm_low[norm_count:]

    ids = gather_seq(jnp.stack([src_ids, tgt_ids, tgt_mask]), 2).reshape(3, rows_here, row_len)
    src_starts = jnp.cumsum(src_lengths, -1) - src_lengths
    tgt_starts = jnp.cumsum(tgt_lengths, -1) - tgt_lengths
    places = jnp.arange(row_len)
    opens = jnp.any(places[None, :, None] == src_starts[:, None, :], -1)
    src_in = pick(jnp.where(opens, length_token, ids[0]).reshape(seqs, span), 0, side)
    masked = (ids[2] == 1).reshape(seqs, span)
    labels = ids[1].reshape(seqs, span)
    dec_in = pick(jnp.where(masked, mask_token, labels), 0, side)
    counts = jnp.sum(masked.astype(jnp.int32), -1)

    def slots_for(expected):
        return max(-(-expected // 16) * 16, 16)

    src_slots, dec_slots = slots_for(2 * span // devices), slots_for(3 * span // (2 * devices))

    def ask(token_ids, slots):
        same = token_ids[:, None] == token_ids[None, :]
        index = jnp.arange(span)
        earlier = index[None, :] < index[:, None]
        leader = jnp.logical_not(jnp.any(same & earlier, 1))
        holder = token_ids // own_words
        rank = jnp.sum(
            (earlier & leader[None, :] & (holder[:, None] == holder[None, :])).astype(jnp.int32), 1
        )
        rank = jnp.sum(jnp.where(same & leader[None, :], rank[None, :], 0), 1)
        return token_ids % own_words, holder, rank, slots

    def chosen_of(asked, turn):
        local, holder, rank, slots = asked
        code = jnp.where(rank // slots == turn, holder * slots + rank % slots, -1)
        return code[:, None] == jnp.arange(devices * slots)[None, :]

    def wanted_of(asked, chosen):
        return jnp.max(jnp.where(chosen, asked[0][:, None], -1), 0).reshape(devices, -1)

    def maps_of(chosen, wanted):
        held = wanted.reshape(-1)[:, None] == jnp.arange(own_words)[None, :]
        return chosen.astype(low_type), held.astype(low_type)

    def round_of(asked, turn):
        chosen = chosen_of(asked, turn)
        return maps_of(chosen, to_each(wanted_of(asked, chosen)))

    def fetch(maps):
        chosen, held = maps
        found = contract(held, table_low, 1, 0).astype(low_type)
        found = to_each(found.reshape(devices, -1, width)).reshape(-1, width)
        return contract(chosen, found, 1, 0)

    def give(maps, grads):
        chosen, held = maps
        sums = contract(chosen, grads.astype(low_type), 0, 0).astype(low_type)
        sums = to_each(sums.reshape(devices, -1, width)).reshape(-1, width)
        return contract(held, sums, 0, 0)

    def later_rounds(rounds, value, visit):
        return lax.fori_loop(1, rounds, lambda turn, carry: carry + visit(turn), value)

    src_ask, dec_ask = ask(src_in, src_slots), ask(dec_in, dec_slots)
    src_chosen, dec_chosen = chosen_of(src_ask, 0), chosen_of(dec_ask, 0)
    facts = jnp.stack(
        [
            jnp.sum(tgt_mask),
            jnp.max(counts),
            jnp.max(src_ask[2]) // src_slots + 1,
            jnp.max(dec_ask[2]) // dec_slots + 1,
        ]
    )
    facts = jnp.broadcast_to(jnp.pad(facts, (0, 12))[None, :], (devices, 16))
    asked = [wanted_of(src_ask, src_chosen), wanted_of(dec_ask, dec_chosen), facts]
    asked = to_each(jnp.concatenate(asked, 1).astype(jnp.int32))
    facts = asked[:, src_slots + dec_slots :]
    count = jnp.sum(facts[:, 0]).astype(f32)
    cut = -(-(span * 3 // 8) // 128) * 128
    more = jnp.max(facts[:, 1]) > cut
    src_rounds, dec_rounds = jnp.max(facts[:, 2]), jnp.max(facts[:, 3])
    src_maps = maps_of(src_chosen, asked[:, :src_slots])
    src_found = fetch(src_maps)
    dec_maps = maps_of(dec_chosen, asked[:, src_slots : src_slots + dec_slots])
    dec_found = fetch(dec_maps)

    order = jnp.stack([side, 1 - side]) if seqs == 2 else jnp.arange(seqs)
    masked, labels, counts = masked[order], labels[order], counts[order]
    rank = jnp.where(masked, jnp.cumsum(masked.astype(jnp.int32), -1) - 1, -1)
    chosen = rank[:, None, :] == jnp.arange(span)[None, :, None]
    slot_label = jnp.sum(jnp.where(chosen, labels[:, None, :], 0), -1).reshape(-1)
    valid = (jnp.arange(span)[None, :] < counts[:, None]).reshape(-1)
    targets = jnp.where(valid, slot_label - vocab_base, -1).reshape(1, -1)
    plan = chunk_plan(counts, span)
    own_segment = 0 if seqs == 2 else side
    own_chosen = pick(chosen, 0, own_segment).astype(low_type)

    own_places = offset + jnp.arange(span)
    src_start, src_length = pick(src_starts, 0, row), pick(src_lengths, 0, row)
    tgt_start, tgt_length = pick(tgt_starts, 0, row), pick(tgt_lengths, 0, row)
    src_number, src_open = place_spans(src_start, own_places)
    tgt_number, tgt_open = place_spans(tgt_start, own_places)
    block = min(query_block, span)
    enc_spans = key_spans(src_number, src_start, src_length, block)
    self_spans = key_spans(tgt_number, tgt_start, tgt_length, block)
    cross_spans = key_spans(tgt_number, src_start, src_length, block)
    src_wave, tgt_wave = lax.optimization_barrier(
        (sinusoid(own_places - src_open, width), sinusoid(own_places - tgt_open, width))
    )

    root = math.sqrt(width)
    src_found = later_rounds(src_rounds, src_found, lambda turn: fetch(round_of(src_ask, turn)))
    dec_found = later_rounds(dec_rounds, dec_found, lambda turn: fetch(round_of(dec_ask, turn)))
    stream0 = src_found * root + src_wave
    target0 = dec_found * root + tgt_wave

    def norm(stream, index):
        return layer_norm(stream, gains[index], biases[index])

    def keys_of_row(part):
        if group == 1:
            return part
        return lax.all_gather(part, "seq", axis=1, tiled=True, axis_index_groups=sharers)

    def keys_to_place(part):
        if group == 1:
            return part
        return lax.psum_scatter(
            part, "seq", scatter_dimension=1, tiled=True, axis_index_groups=sharers
        )

    def self_attention(inner, weight_in, weight_out, spans):
        triple = contract(weight_in, inner, 0, 1).astype(low_type)
        keys = triple if group == 1 else keys_of_row(triple[width:])
        mixed, lse = attend_forward(triple, keys, group == 1, *spans)
        return contract(mixed, weight_out, 0, 0), (triple, keys, mixed, lse)

    def self_attention_back(inner, weight_in, weight_out, spans, kept, grad):
        triple, keys, mixed, lse = kept
        grad_low = grad.astype(low_type)
        d_out = contract(mixed, grad_low, 1, 0)
        d_mixed = contract(weight_out, grad_low, 1, 1).astype(low_type)
        d_query, d_keys = attend_backward(triple, keys, group == 1, *spans, lse, d_mixed)
        d_triple = jnp.concatenate([d_query, keys_to_place(d_keys)], 0)
        return contract(d_triple, weight_in, 0, 1), contract(inner, d_triple, 0, 1), d_out

    def cross_attention(inner, memory, weight_in, weight_out, spans):
        queries = contract(weight_in[:, :width], inner, 0, 1).astype(low_type)
        keys = keys_of_row(contract(weight_in[:, width:], memory, 0, 1).astype(low_type))
        mixed, lse = attend_forward(queries, keys, False, *spans)
        return contract(mixed, weight_out, 0, 0), (queries, keys, mixed, lse)

    def cross_attention_back(inner, memory, weight_in, weight_out, spans, kept, grad):
        queries, keys, mixed, lse = kept
        grad_low = grad.astype(low_type)
        d_out = contract(mixed, grad_low, 1, 0)
        d_mixed = contract(weight_out, grad_low, 1, 1).astype(low_type)
        d_query, d_keys = attend_backward(queries, keys, False, *spans, lse, d_mixed)
        d_keys = keys_to_place(d_keys)
        d_in = jnp.concatenate([contract(inner, d_query, 0, 1), contract(memory, d_keys, 0, 1)], 1)
        return (
            contract(d_query, weight_in[:, :width], 0, 1),
            contract(d_keys, weight_in[:, width:], 0, 1),
            d_in,
            d_out,
        )

    def ffn(inner, weight_one, weight_two):
        hidden = contract(inner, weight_one, 1, 0)
        active = jax.nn.gelu(hidden).astype(low_type)
        return contract(active, weight_two, 1, 0), (hidden, active)

    def ffn_back(inner, weight_one, weight_two, kept, grad):
        hidden, active = kept
        grad_low = grad.astype(low_type)
        d_two = contract(active, grad_low, 0, 0)
        d_active = contract(grad_low, weight_two, 1, 1)
        d_hidden = jax.vjp(jax.nn.gelu, hidden)[1](d_active)[0].astype(low_type)
        return contract(d_hidden, weight_one, 1, 1), contract(inner, d_hidden, 0, 0), d_two

    inner0 = norm(stream0, 0).astype(low_type)
    branch0, keep0 = self_attention(inner0, w_in0, w_out0, enc_spans)
    stream1 = stream0 + branch0
    inner1 = norm(stream1, 1).astype(low_type)
    branch1, keep1 = ffn(inner1, f_in0, f_out0)
    stream2 = stream1 + branch1
    memory = norm(stream2, 2).astype(low_type)
    inner3 = norm(target0, 3).astype(low_type)
    branch3, keep3 = self_attention(inner3, w_in1, w_out1, self_spans)
    target1 = target0 + branch3
    inner4 = norm(target1, 4).astype(low_type)
    branch4, keep4 = cross_attention(inner4, memory, w_in2, w_out2, cross_spans)
    target2 = target1 + branch4
    inner5 = norm(target2, 5).astype(low_type)
    branch5, keep5 = ffn(inner5, f_in1, f_out1)
    target3 = target2 + branch5
    final = norm(target3, 6).astype(low_type)

    packed = contract(own_chosen, final, 1, 0).astype(low_type)
    if seqs == 2:
        pieces = jnp.concatenate([packed, swap_rows(packed, cut, more)], 0)
    else:
        pieces = lax.all_gather(packed, "seq", axis=0, tiled=True)
    stats = head_stats(plan, table_part, pieces)
    if seqs == 2:
        every = jnp.stack([stats, jnp.roll(swap(stats, "seq", 1), span, 1)])
    else:
        every = lax.all_gather(stats, "seq", axis=0)
    top_logit = jnp.max(every[:, 0], 0)
    totals = jnp.sum(every[:, 1] * jnp.exp(every[:, 0] - top_logit[None]), 0)
    log_total = top_logit + jnp.log(jnp.where(valid, totals, 1.0))
    own_logs = pick(jnp.where(valid, log_total, 0.0).reshape(seqs, span), 0, own_segment)
    logs = jnp.where(valid, log_total + jnp.log(count), 1e30)
    weights = jnp.where(valid, 1.0 / count, 0.0)
    d_one, d_two, d_pieces, picks = head_back(
        plan, table_part, pieces, targets, logs[None], weights[None]
    )
    token_local = jnp.sum(own_logs) - jnp.sum(picks)
    table_one = Halving([d_one.reshape(owners, own_words, -1)], False)

    def to_places(first, last):
        own = lax.dynamic_slice_in_dim(d_pieces, own_segment * span + first, last - first, 0)
        if seqs == 2:
            away = d_pieces[span + first : span + last].astype(low_type)
            own = own + swap(away, "seq", 1).astype(f32)
        high = lax.reduce_precision(own, 8, 7)
        rest = (own - high).astype(low_type)
        chosen_here = own_chosen[first:last]
        return contract(chosen_here, high.astype(low_type), 0, 0) + contract(chosen_here, rest, 0, 0)

    if seqs == 2:
        d_final = to_places(0, cut)
        if cut < span:
            d_final = lax.cond(
                more, lambda part: part + to_places(cut, span), lambda part: part, d_final
            )
    else:
        d_pieces = lax.psum(d_pieces, "seq")
        d_final = to_places(0, span)

    first_place = own_places[None, :] == src_start[:, None]
    mine = jnp.any(first_place, -1)
    first_rows = contract(first_place.astype(low_type), memory, 1, 0).astype(low_type)
    len_logits = contract(first_rows, w_len, 1, 0)
    len_label = jnp.minimum(tgt_length, classes - 1)
    len_hot = jnp.arange(classes)[None, :] == len_label[:, None]
    len_loss = jax.nn.logsumexp(len_logits, -1) - jnp.sum(jnp.where(len_hot, len_logits, 0.0), -1)
    len_local = jnp.sum(jnp.where(mine, len_loss, 0.0))
    sentences = rows_here * src_lengths.shape[1] * owners
    len_prob = jax.nn.softmax(len_logits, -1)
    d_len_logits = (
        jnp.where(mine[:, None], len_prob - len_hot.astype(f32), 0.0) * (0.1 / sentences)
    ).astype(low_type)
    d_w_len = contract(first_rows, d_len_logits, 0, 0)
    d_first = contract(d_len_logits, w_len, 1, 1)
    d_memory = lax.dot_general(
        first_place.astype(f32),
        d_first,
        (((0,), (0,)), ((), ())),
        precision=lax.Precision.HIGHEST,
        preferred_element_type=f32,
    )

    def owned(grad):
        return grad.reshape(owners, -1, grad.shape[1])

    def owned_columns(grad):
        whole = owned(grad)
        return [whole[:, at : at + share] for at in range(0, whole.shape[1], share)]

    none = jnp.zeros_like(stream0)
    d_target3, gain6, bias6 = norm_backward(target3, gains[6], d_final, none)
    d_inner5, d_fin1, d_fout1 = ffn_back(inner5, f_in1, f_out1, keep5, d_target3)
    chains = [table_one]
    (d_inner5, d_target3, d_two) = advance((d_inner5, d_target3, d_two), chains)
    table_two = Halving([d_two.reshape(owners, own_words, -1)], False)
    chain_a = Halving([owned(d_fin1)] + owned_columns(d_fout1), True)
    d_target2, gain5, bias5 = norm_backward(target2, gains[5], d_inner5, d_target3)
    d_inner4, d_cross, d_win2, d_wout2 = cross_attention_back(
        inner4, memory, w_in2, w_out2, cross_spans, keep4, d_target2
    )
    chains += [table_two, chain_a]
    d_inner4, d_target2, d_cross = advance((d_inner4, d_target2, d_cross), chains)
    chain_b = Halving([owned(d_win2), owned(d_wout2)], True)
    d_target1, gain4, bias4 = norm_backward(target1, gains[4], d_inner4, d_target2)
    d_inner3, d_win1, d_wout1 = self_attention_back(
        inner3, w_in1, w_out1, self_spans, keep3, d_target1
    )
    chains += [chain_b]
    d_inner3, d_target1 = advance((d_inner3, d_target1), chains)
    chain_c = Halving([owned(d_win1), owned(d_wout1)], True)
    d_target0, gain3, bias3 = norm_backward(target0, gains[3], d_inner3, d_target1)
    dec_grad = d_target0 * root
    dec_given = give(dec_maps, dec_grad)
    d_stream2, gain2, bias2 = norm_backward(stream2, gains[2], d_memory + d_cross, none)
    d_inner1, d_fin0, d_fout0 = ffn_back(inner1, f_in0, f_out0, keep1, d_stream2)
    chains += [chain_c]
    d_inner1, d_stream2 = advance((d_inner1, d_stream2), chains)
    chain_d = Halving([owned(d_fin0)] + owned_columns(d_fout0), True)
    d_stream1, gain1, bias1 = norm_backward(stream1, gains[1], d_inner1, d_stream2)
    d_inner0, d_win0, d_wout0 = self_attention_back(
        inner0, w_in0, w_out0, enc_spans, keep0, d_stream1
    )
    chains += [chain_d]
    d_inner0, d_stream1, dec_given = advance((d_inner0, d_stream1, dec_given), chains)
    d_stream0, gain0, bias0 = norm_backward(stream0, gains[0], d_inner0, d_stream1)
    src_grad = d_stream0 * root
    src_given = give(src_maps, src_grad)
    norm_grads = [gain0, gain1, gain2, gain3, gain4, gain5, gain6]
    norm_grads += [bias0, bias1, bias2, bias3, bias4, bias5, bias6]
    g_norms = jnp.sum(lax.all_gather(jnp.stack(norm_grads), ("dp", "seq"), axis=0), 0)
    norm_square = jnp.where(
        (side == 0) & (lax.axis_index("dp") == 0), jnp.sum(g_norms * g_norms), 0.0
    )
    norm_share = norms.shape[2]
    g_norms = lax.dynamic_slice_in_dim(g_norms, lax.axis_index("dp") * norm_share, norm_share, 1)
    chain_e = Halving([owned(d_win0), owned(d_wout0), owned(d_w_len)], True)
    chains += [chain_e]
    while any(chain.pending is not None for chain in chains):
        advance((), chains)
    for chain in chains:
        chain.finish()

    given = dec_given + src_given
    given = later_rounds(
        jnp.maximum(src_rounds, dec_rounds),
        given,
        lambda turn: give(round_of(dec_ask, turn), dec_grad)
        + give(round_of(src_ask, turn), src_grad),
    )
    table_grad = jnp.concatenate(
        [table_one.value.reshape(own_words, -1), table_two.value.reshape(own_words, -1)], 1
    )
    table_grad = table_grad + given
    square = sum(chain.square for chain in (chain_a, chain_b, chain_c, chain_d, chain_e))
    square = square + jnp.sum(table_grad * table_grad) + norm_square
    sums = everywhere(
        jnp.stack([token_local, len_local, square]).reshape(1, 3), jnp.add, lax.psum
    )[0]
    token_sum, len_sum, grad_norm = sums[0], sums[1], jnp.sqrt(sums[2])
    factor = jnp.minimum(1.0, clip_limit / (grad_norm + 1e-06))

    def cut_columns(chain, sizes):
        result, at = [], 0
        value = chain.value.reshape(share, -1)
        for size in sizes:
            result.append(value[:, at : at + size])
            at += size
        return result

    hidden_width = ffn_in.shape[2]
    pieces_out = ffn_out.shape[1] // share
    ffn_sizes = [hidden_width] + [width] * pieces_out
    attn_sizes = [3 * width, width]
    g_fin1, *g_fout1 = cut_columns(chain_a, ffn_sizes)
    g_win2, g_wout2 = cut_columns(chain_b, attn_sizes)
    g_win1, g_wout1 = cut_columns(chain_c, attn_sizes)
    g_fin0, *g_fout0 = cut_columns(chain_d, ffn_sizes)
    g_win0, g_wout0, g_len = cut_columns(chain_e, attn_sizes + [classes])
    grads = (
        jnp.stack([g_win0, g_win1, g_win2]),
        jnp.stack([g_wout0, g_wout1, g_wout2]),
        jnp.stack([g_fin0, g_fin1]),
        jnp.stack([jnp.concatenate(g_fout0, 0), jnp.concatenate(g_fout1, 0)]),
        g_len,
        g_norms.reshape(norms.shape),
        table_grad,
    )
    masters = (attn_in, attn_out, ffn_in, ffn_out, len_head, norms, table)
    firsts = (attn_in_m1, attn_out_m1, ffn_in_m1, ffn_out_m1, len_head_m1, norms_m1, table_m1)
    seconds = (attn_in_m2, attn_out_m2, ffn_in_m2, ffn_out_m2, len_head_m2, norms_m2, table_m2)
    updates = []
    for weight, first, second, grad, rate in zip(masters, firsts, seconds, grads, step_rates):
        updates.extend(adam_update(weight, first, second, grad * factor, rate))
    return (token_sum, count, len_sum, grad_norm, *updates)


def solution(mesh):
    layer, head, scales, words = P(None, "dp", None), P("dp", None), P(None, None, "dp"), P(("seq", "dp"), None)
    owned = (layer,) * 12 + (head,) * 3 + (scales,) * 3 + (words,) * 3
    ids, lengths = P("dp", "seq"), P("dp", None)
    in_specs = (ids, ids, lengths, lengths, ids) + owned
    out_specs = (P(), P(), P(), P()) + owned
    return jax.shard_map(
        on_device, mesh=mesh, in_specs=in_specs, out_specs=out_specs, check_vma=False
    )
```

```python
import functools
import math

import jax
import jax.numpy as jnp
from jax import lax
from jax.experimental import pallas as pl
from jax.experimental.pallas import tpu as pltpu
from jax.sharding import PartitionSpec as P

HEADS = 8
STEP = 10


length_token = 1
mask_token = 2
clip_limit = 0.002
beta_one = 0.9
beta_two = 0.98
adam_eps = 1e-08
weight_decay = 0.01
step_rates = (0.05, 0.25, 0.05, 0.025, 0.05, 0.5, 0.1)

low_type = jnp.bfloat16
f32 = jnp.float32
query_block = 256
key_block = 128
place_block = 512
vmem_bytes = 56 * 1024 * 1024


def sinusoid(positions, width):
    half_width = width // 2
    frequency = jnp.exp(jnp.arange(half_width).astype(f32) * (-math.log(10000.0) / half_width))
    angles = frequency[:, None] * positions.astype(f32)[None, :]
    return jnp.concatenate([jnp.sin(angles), jnp.cos(angles)], 0)


def layer_norm(stream, norm_gain, norm_bias):
    average = jnp.mean(stream, 0, keepdims=True)
    centred = stream - average
    variance = jnp.mean(centred * centred, 0, keepdims=True)
    return centred * lax.rsqrt(variance + 1e-05) * norm_gain[:, None] + norm_bias[:, None]


def contract(left, right, left_dim, right_dim):
    return lax.dot_general(
        left, right, (((left_dim,), (right_dim,)), ((), ())), preferred_element_type=f32
    )


def attend_forward_kernel(bounds, q_ref, k_ref, v_ref, span_ref, out_ref, lse_ref, hold, *, head):
    step = pl.program_id(0)
    first, last = bounds[0, step], bounds[1, step]
    width, queries = q_ref.shape
    heads = width // head
    scale = head**-0.5
    low, high = span_ref[0:1, :], span_ref[1:2, :]
    inner = lax.broadcasted_iota(jnp.int32, (key_block, queries), 0)

    def fold(values, op):
        return op(values.reshape(key_block // 8, 8, queries), axis=0)

    def score(block, tops):
        start = pl.multiple_of(block * key_block, key_block)
        place = inner + start
        allowed = (place >= low) & (place < high)
        result = []
        for h in range(heads):
            rows = slice(h * head, (h + 1) * head)
            s = contract(k_ref[rows, pl.ds(start, key_block)], q_ref[rows, :], 0, 0) * scale
            s = jnp.where(allowed, s, -1e30)
            hold[h, pl.ds(start, key_block), :] = s
            result.append(jnp.maximum(tops[h], fold(s, jnp.max)))
        return tuple(result)

    tops = lax.fori_loop(
        first, last, score, tuple(jnp.full((8, queries), -1e30, f32) for _ in range(heads))
    )
    tops = [jnp.max(t, axis=0, keepdims=True) for t in tops]

    def power(block, sums):
        start = pl.multiple_of(block * key_block, key_block)
        result = []
        for h in range(heads):
            e = jnp.exp(hold[h, pl.ds(start, key_block), :] - tops[h])
            hold[h, pl.ds(start, key_block), :] = e
            result.append(sums[h] + fold(e, jnp.sum))
        return tuple(result)

    sums = lax.fori_loop(
        first, last, power, tuple(jnp.zeros((8, queries), f32) for _ in range(heads))
    )
    sums = [jnp.maximum(jnp.sum(t, axis=0, keepdims=True), 1e-30) for t in sums]
    inverse = [1.0 / t for t in sums]

    def mix(block, outs):
        start = pl.multiple_of(block * key_block, key_block)
        result = []
        for h in range(heads):
            rows = slice(h * head, (h + 1) * head)
            p = (hold[h, pl.ds(start, key_block), :] * inverse[h]).astype(low_type)
            result.append(outs[h] + contract(v_ref[rows, pl.ds(start, key_block)], p, 1, 0))
        return tuple(result)

    outs = lax.fori_loop(
        first, last, mix, tuple(jnp.zeros((head, queries), f32) for _ in range(heads))
    )
    for h in range(heads):
        out_ref[h * head : (h + 1) * head, :] = outs[h].astype(low_type)
        lse_ref[h : h + 1, :] = tops[h] + jnp.log(sums[h])


def attend_backward_kernel(
    bounds, q_ref, k_ref, v_ref, span_ref, lse_ref, do_ref, dq_ref, dkv_ref, p_hold, d_hold, acc,
    *, head
):
    step = pl.program_id(0)
    first, last = bounds[0, step], bounds[1, step]
    width, queries = q_ref.shape
    heads = width // head
    scale = head**-0.5
    low, high = span_ref[0:1, :], span_ref[1:2, :]
    inner = lax.broadcasted_iota(jnp.int32, (key_block, queries), 0)

    @pl.when(step == 0)
    def _():
        acc[...] = jnp.zeros_like(acc)

    def one(block, deltas):
        start = pl.multiple_of(block * key_block, key_block)
        keys = pl.ds(start, key_block)
        place = inner + start
        allowed = (place >= low) & (place < high)
        result = []
        for h in range(heads):
            rows = slice(h * head, (h + 1) * head)
            s = contract(k_ref[rows, keys], q_ref[rows, :], 0, 0) * scale
            p = jnp.exp(jnp.where(allowed, s, -1e30) - lse_ref[h : h + 1, :])
            dp = contract(v_ref[rows, keys], do_ref[rows, :], 0, 0)
            p_hold[h, keys, :] = p
            d_hold[h, keys, :] = dp
            result.append(
                deltas[h] + jnp.sum((p * dp).reshape(key_block // 8, 8, queries), axis=0)
            )
            below = slice(width + h * head, width + (h + 1) * head)
            acc[below, keys] += contract(do_ref[rows, :], p.astype(low_type), 1, 1)
        return tuple(result)

    deltas = lax.fori_loop(
        first, last, one, tuple(jnp.zeros((8, queries), f32) for _ in range(heads))
    )
    deltas = [jnp.sum(t, axis=0, keepdims=True) for t in deltas]

    def two(block, outs):
        start = pl.multiple_of(block * key_block, key_block)
        keys = pl.ds(start, key_block)
        result = []
        for h in range(heads):
            rows = slice(h * head, (h + 1) * head)
            ds = (p_hold[h, keys, :] * (d_hold[h, keys, :] - deltas[h])).astype(low_type)
            result.append(outs[h] + contract(k_ref[rows, keys], ds, 1, 0))
            acc[rows, keys] += contract(q_ref[rows, :], ds, 1, 1) * scale
        return tuple(result)

    outs = lax.fori_loop(
        first, last, two, tuple(jnp.zeros((head, queries), f32) for _ in range(heads))
    )
    for h in range(heads):
        dq_ref[h * head : (h + 1) * head, :] = (outs[h] * scale).astype(low_type)

    @pl.when(step == pl.num_programs(0) - 1)
    def _():
        dkv_ref[...] = acc[...].astype(low_type)


def attend_specs(width, length, block, shared):
    key_row = 1 if shared else 0
    return [
        pl.BlockSpec((width, block), lambda i, *_: (0, i)),
        pl.BlockSpec((width, length), lambda i, *_: (key_row, 0)),
        pl.BlockSpec((width, length), lambda i, *_: (key_row + 1, 0)),
        pl.BlockSpec((2, block), lambda i, *_: (0, i)),
    ]


def attend_forward(queries, keys, shared, spans, bounds):
    width = keys.shape[0] // (3 if shared else 2)
    places, length = queries.shape[1], keys.shape[1]
    block = min(query_block, places)
    return pl.pallas_call(
        functools.partial(attend_forward_kernel, head=width // HEADS),
        grid_spec=pltpu.PrefetchScalarGridSpec(
            num_scalar_prefetch=1,
            grid=(places // block,),
            in_specs=attend_specs(width, length, block, shared),
            out_specs=[
                pl.BlockSpec((width, block), lambda i, *_: (0, i)),
                pl.BlockSpec((HEADS, block), lambda i, *_: (0, i)),
            ],
            scratch_shapes=[pltpu.VMEM((HEADS, length, block), f32)],
        ),
        out_shape=[
            jax.ShapeDtypeStruct((width, places), low_type),
            jax.ShapeDtypeStruct((HEADS, places), f32),
        ],
        compiler_params=pltpu.CompilerParams(vmem_limit_bytes=vmem_bytes),
        name="attend_forward",
    )(bounds, queries, keys, keys, spans)


def attend_backward(queries, keys, shared, spans, bounds, lse, d_mixed):
    width = keys.shape[0] // (3 if shared else 2)
    places, length = queries.shape[1], keys.shape[1]
    block = min(query_block, places)
    return pl.pallas_call(
        functools.partial(attend_backward_kernel, head=width // HEADS),
        grid_spec=pltpu.PrefetchScalarGridSpec(
            num_scalar_prefetch=1,
            grid=(places // block,),
            in_specs=attend_specs(width, length, block, shared)
            + [
                pl.BlockSpec((HEADS, block), lambda i, *_: (0, i)),
                pl.BlockSpec((width, block), lambda i, *_: (0, i)),
            ],
            out_specs=[
                pl.BlockSpec((width, block), lambda i, *_: (0, i)),
                pl.BlockSpec((2 * width, length), lambda i, *_: (0, 0)),
            ],
            scratch_shapes=[
                pltpu.VMEM((HEADS, length, block), f32),
                pltpu.VMEM((HEADS, length, block), f32),
                pltpu.VMEM((2 * width, length), f32),
            ],
        ),
        out_shape=[
            jax.ShapeDtypeStruct((width, places), low_type),
            jax.ShapeDtypeStruct((2 * width, length), low_type),
        ],
        compiler_params=pltpu.CompilerParams(vmem_limit_bytes=vmem_bytes),
        name="attend_backward",
    )(bounds, queries, keys, keys, spans, lse, d_mixed)


def norm_back_kernel(stream_ref, gain_ref, grad_ref, rest_ref, out_ref, sums_ref):
    @pl.when(pl.program_id(0) == 0)
    def _():
        sums_ref[...] = jnp.zeros_like(sums_ref)

    stream, grad = stream_ref[...], grad_ref[...]
    width, places = stream.shape
    average = jnp.mean(stream, 0, keepdims=True)
    centred = stream - average
    variance = jnp.mean(centred * centred, 0, keepdims=True)
    inverse = lax.rsqrt(variance + 1e-05)
    unit = centred * inverse
    scaled = grad * gain_ref[...]
    along = jnp.mean(scaled * unit, 0, keepdims=True)
    level = jnp.mean(scaled, 0, keepdims=True)
    out_ref[...] = rest_ref[...] + (scaled - level - unit * along) * inverse
    weighted = grad * unit
    for at in range(0, places, 128):
        sums_ref[0] += weighted[:, at : at + 128]
        sums_ref[1] += grad[:, at : at + 128]


def norm_backward(stream, gain, grad, rest):
    width, places = stream.shape
    columns = min(256, places)
    block = pl.BlockSpec((width, columns), lambda i: (0, i))
    return pl.pallas_call(
        norm_back_kernel,
        grid=(places // columns,),
        in_specs=[block, pl.BlockSpec((width, 1), lambda i: (0, 0)), block, block],
        out_specs=[block, pl.BlockSpec((2, width, 128), lambda i: (0, 0, 0))],
        out_shape=[
            jax.ShapeDtypeStruct((width, places), f32),
            jax.ShapeDtypeStruct((2, width, 128), f32),
        ],
        compiler_params=pltpu.CompilerParams(vmem_limit_bytes=vmem_bytes),
        name="norm_backward",
    )(stream, gain[:, None], grad, rest)


def chunk_plan(total):
    quarter = place_block // 4
    units = (jnp.maximum(total - place_block, 0) + quarter - 1) // quarter
    left = units % 4
    wides = units // 4 + (left == 3).astype(jnp.int32)
    return jnp.stack([wides, left == 2, left == 1]).astype(jnp.int32)


def each_chunk(plan, visit):
    visit(0, place_block, True)

    def wide(index, carry):
        visit(pl.multiple_of((index + 1) * place_block, place_block), place_block, False)
        return carry

    lax.fori_loop(0, plan[0], wide, 0)
    after = pl.multiple_of((plan[0] + 1) * place_block, place_block)
    for index, share in ((1, 2), (2, 4)):

        @pl.when(plan[index] > 0)
        def _(share=share):
            visit(after, place_block // share, False)


def parts_of(words):
    for count in (5, 4, 2):
        if words % (16 * count) == 0:
            return [slice(i * (words // count), (i + 1) * (words // count)) for i in range(count)]
    return [slice(0, words)]


def head_stats_kernel(plan, table_ref, turned_ref, stats_ref, tops, sums):
    step = pl.program_id(0)

    @pl.when(step == 0)
    def _():
        tops[...] = jnp.full_like(tops, -1e30)
        sums[...] = jnp.zeros_like(sums)

    def visit(start, size, first):
        here = pl.ds(start, size)
        turned = turned_ref[:, here]
        old, total = tops[:, here], sums[:, here]
        for part in parts_of(table_ref.shape[0]):
            logits = contract(table_ref[part, :], turned, 1, 0)
            logits = logits.reshape(logits.shape[0] // 8, 8, size)
            top = jnp.maximum(old, jnp.max(logits, axis=0))
            powers = jnp.sum(jnp.exp(logits - top[None]), axis=0)
            total = total * jnp.exp(old - top) + powers
            old = top
        sums[:, here] = total
        tops[:, here] = old

    each_chunk(plan, visit)

    @pl.when(step == pl.num_programs(0) - 1)
    def _():
        top = jnp.max(tops[...], axis=0, keepdims=True)
        stats_ref[0:1, :] = top
        stats_ref[1:2, :] = jnp.sum(sums[...] * jnp.exp(tops[...] - top), axis=0, keepdims=True)


def head_back_kernel(
    plan, table_ref, rows_ref, turned_ref, target_ref, log_ref, weight_ref, *refs, owned
):
    (*out_refs, dr_ref, pick_ref, acc) = refs
    step = pl.program_id(0)
    words, width = table_ref.shape

    @pl.when(step == 0)
    def _():
        dr_ref[...] = jnp.zeros_like(dr_ref)
        pick_ref[...] = jnp.zeros_like(pick_ref)

    def visit(start, size, first):
        here = pl.ds(start, size)
        rows, turned = rows_ref[here, :], turned_ref[:, here]
        target = target_ref[:, here] - step * words
        log, weight = log_ref[:, here], weight_ref[:, here]
        found = jnp.zeros((8, size), f32)
        for part in parts_of(words):
            block = table_ref[part, :]
            count = block.shape[0]
            inner = lax.broadcasted_iota(jnp.int32, (count, size), 0) + part.start
            logits = contract(block, turned, 1, 0)
            scaled = jnp.exp(logits - log)
            hit = inner == target
            found += jnp.sum(jnp.where(hit, logits, 0.0).reshape(count // 8, 8, size), axis=0)
            d_logits = jnp.where(hit, scaled - weight, scaled).astype(low_type)
            if first:
                acc[part, :] = contract(d_logits, rows, 1, 0)
            else:
                acc[part, :] += contract(d_logits, rows, 1, 0)
            dr_ref[here, :] += contract(d_logits, block, 0, 0)
        pick_ref[:, here] += found

    each_chunk(plan, visit)
    if not owned:
        out_refs[0][...] = acc[...]
        return
    mine = plan[3]
    half = width // 2
    keep = pl.ds(pl.multiple_of(mine * owned, 8), owned)
    away = pl.ds(pl.multiple_of((1 - mine) * owned, 8), owned)
    out_refs[0][0] = acc[keep, :half]
    out_refs[1][0] = acc[keep, half:]
    out_refs[2][0] = acc[away, :half].astype(low_type)
    out_refs[3][0] = acc[away, half:].astype(low_type)


def word_block(words):
    return max(n for n in range(16, 1601, 16) if words % n == 0)


def head_stats(plan, table_part, turned):
    words = word_block(table_part.shape[0])
    width, places = turned.shape
    return pl.pallas_call(
        head_stats_kernel,
        grid_spec=pltpu.PrefetchScalarGridSpec(
            num_scalar_prefetch=1,
            grid=(table_part.shape[0] // words,),
            in_specs=[
                pl.BlockSpec((words, width), lambda i, *_: (i, 0)),
                pl.BlockSpec((width, places), lambda i, *_: (0, 0)),
            ],
            out_specs=pl.BlockSpec((2, places), lambda i, *_: (0, 0)),
            scratch_shapes=[pltpu.VMEM((8, places), f32) for _ in range(2)],
        ),
        out_shape=jax.ShapeDtypeStruct((2, places), f32),
        compiler_params=pltpu.CompilerParams(vmem_limit_bytes=vmem_bytes),
        name="head_stats",
    )(plan, table_part, turned)


def head_back(plan, table_part, rows, turned, targets, logs, weights, owned):
    total = table_part.shape[0]
    words = 2 * owned if owned else word_block(total)
    places, width = rows.shape
    half = width // 2
    row = pl.BlockSpec((1, places), lambda i, *_: (0, 0))
    if owned:
        share = pl.BlockSpec((1, owned, half), lambda i, *_: (i, 0, 0))
        out_specs = [share] * 4
        shape = (total // words, owned, half)
        out_shape = [jax.ShapeDtypeStruct(shape, t) for t in (f32, f32, low_type, low_type)]
    else:
        out_specs = [pl.BlockSpec((words, width), lambda i, *_: (i, 0))]
        out_shape = [jax.ShapeDtypeStruct((total, width), f32)]
    return pl.pallas_call(
        functools.partial(head_back_kernel, owned=owned),
        grid_spec=pltpu.PrefetchScalarGridSpec(
            num_scalar_prefetch=1,
            grid=(total // words,),
            in_specs=[
                pl.BlockSpec((words, width), lambda i, *_: (i, 0)),
                pl.BlockSpec((places, width), lambda i, *_: (0, 0)),
                pl.BlockSpec((width, places), lambda i, *_: (0, 0)),
                row,
                row,
                row,
            ],
            out_specs=out_specs
            + [
                pl.BlockSpec((places, width), lambda i, *_: (0, 0)),
                pl.BlockSpec((8, places), lambda i, *_: (0, 0)),
            ],
            scratch_shapes=[pltpu.VMEM((words, width), f32)],
        ),
        out_shape=out_shape
        + [
            jax.ShapeDtypeStruct((places, width), f32),
            jax.ShapeDtypeStruct((8, places), f32),
        ],
        compiler_params=pltpu.CompilerParams(vmem_limit_bytes=vmem_bytes),
        name="head_back",
    )(plan, table_part, rows, turned, targets, logs, weights)


def swap(values, axis, bit):
    size = lax.axis_size(axis)
    return lax.ppermute(values, axis, [(i, i ^ bit) for i in range(size)])


def power_of_two(size):
    return size & (size - 1) == 0


def everywhere(values, combine, reduce):
    for axis in ("dp", "seq"):
        size = lax.axis_size(axis)
        if power_of_two(size):
            bit = 1
            while bit < size:
                values = combine(values, swap(values, axis, bit))
                bit *= 2
        else:
            values = reduce(values, axis)
    return values


def pick(values, dim, index):
    return lax.dynamic_index_in_dim(values, index, dim, False)


def gather_seq(values, dim):
    if lax.axis_size("seq") == 2:
        other = swap(values, "seq", 1)
        first = lax.axis_index("seq") == 0
        return jnp.stack([jnp.where(first, values, other), jnp.where(first, other, values)], dim)
    return lax.all_gather(values, "seq", axis=dim)


def to_each(values):
    return lax.all_to_all(values, ("seq", "dp"), 0, 0)


def halving_fits(rows, columns, joint):
    owners, seqs = lax.axis_size("dp"), lax.axis_size("seq")
    fits = power_of_two(owners) and owners > 2 and columns % 128 == 0
    return fits and (rows % 16 == 0 and seqs == 2 if joint else rows % 8 == 0)


class Chain:
    pending = value = square = None

class LayerChain(Chain):
    def __init__(self, parts):
        self.parts, self.step = parts, 0
        self.rows = parts[0].shape[1]
        self.fast = halving_fits(self.rows, parts[0].shape[2], True)
        if self.fast:
            self.launch()

    def launch(self):
        owners = lax.axis_size("dp")
        if self.step == 4:
            return
        if self.step == 3:
            self.pending = swap(self.part, "seq", 1)
        elif self.step == 2:
            groups = [list(range(core, owners, 2)) for core in range(2)]
            whole = (self.part + self.got.astype(f32)).astype(low_type)
            self.pending = lax.all_to_all(whole, "dp", 0, 0, axis_index_groups=groups)
        else:
            axis = ("dp", "seq")[self.step]
            mine = lax.axis_index(axis) & 1
            if self.step == 1:
                self.rows //= 2

            def half(side):
                if self.step == 0:
                    shape = (owners // 2, 2, self.rows)
                    parts = [part.reshape(shape + part.shape[2:]) for part in self.parts]
                    return jnp.concatenate([pick(part, 1, side) for part in parts], 2)
                shape = (owners // 2, 2, self.rows, -1)
                first, second = self.part.reshape(shape), self.got.reshape(shape)
                return pick(first, 1, side) + pick(second, 1, side).astype(f32)

            away = half(1 - mine).astype(low_type)
            self.part = half(mine)
            self.pending = swap(away, axis, 1)

    def absorb(self, got):
        self.pending = None
        self.step += 1
        if self.step < 3:
            self.got = got
        elif self.step == 3:
            self.part = jnp.sum(got.astype(f32), 0)
            self.square = jnp.sum(self.part * self.part)
        else:
            first = lax.axis_index("seq") == 0
            part = self.part
            self.value = jnp.concatenate(
                [jnp.where(first, part, got), jnp.where(first, got, part)], 0
            )

    def finish(self):
        if not self.fast:
            whole = jnp.concatenate(self.parts, 2)
            part = lax.psum(lax.psum_scatter(whole, "dp", scatter_dimension=0), "seq")
            self.value = part
            self.square = jnp.where(lax.axis_index("seq") == 0, jnp.sum(part * part), 0.0)


class TableChain(Chain):
    def __init__(self, keep, away):
        self.part, self.got = keep, None
        self.rows, self.bit = keep.shape[1], 2
        self.pending = swap(away, "dp", 1)

    def launch(self):
        if self.bit == lax.axis_size("dp"):
            return
        mine = (lax.axis_index("dp") // self.bit) & 1
        shape = (-1, 2, self.rows, self.part.shape[2])
        first, second = self.part.reshape(shape), self.got.reshape(shape)

        def half(side):
            return pick(first, 1, side) + pick(second, 1, side).astype(f32)

        away = half(1 - mine).astype(low_type)
        self.part = half(mine)
        self.pending = swap(away, "dp", self.bit)
        self.bit *= 2

    def absorb(self, got):
        self.pending, self.got = None, got
        if self.bit == lax.axis_size("dp"):
            self.value = (self.part + got.astype(f32)).reshape(self.rows, -1)


def advance(main, chains):
    live = [chain for chain in chains if chain.pending is not None]
    main, got = lax.optimization_barrier((main, [chain.pending for chain in live]))
    for chain, arrived in zip(live, got):
        chain.absorb(arrived)
        chain.launch()
    return main


def adam_update(weight, first, second, grad, rate):
    first = beta_one * first + (1 - beta_one) * grad
    second = beta_two * second + (1 - beta_two) * grad * grad
    first_hat = first / (1 - beta_one**STEP)
    second_hat = second / (1 - beta_two**STEP)
    weight = weight - rate * (first_hat / (jnp.sqrt(second_hat) + adam_eps) + weight_decay * weight)
    return (weight, first, second)


def place_spans(starts, places):
    covered = places[:, None] >= starts[None, :]
    number = jnp.sum(covered.astype(jnp.int32), -1) - 1
    return number, jnp.max(jnp.where(covered, starts[None, :], 0), -1)


def key_spans(number, starts, lengths, block):
    hot = number[:, None] == jnp.arange(starts.shape[0])[None, :]
    first = jnp.sum(jnp.where(hot, starts[None, :], 0), -1)
    last = jnp.sum(jnp.where(hot, (starts + lengths)[None, :], 0), -1)
    first_block = jnp.min(first.reshape(-1, block), -1) // key_block
    last_block = (jnp.max(last.reshape(-1, block), -1) + key_block - 1) // key_block
    return (
        jnp.stack([first, last]).astype(jnp.int32),
        jnp.stack([first_block, last_block]).astype(jnp.int32),
    )


def on_device(
    src_ids,
    tgt_ids,
    src_lengths,
    tgt_lengths,
    tgt_mask,
    attn_in,
    attn_in_m1,
    attn_in_m2,
    attn_out,
    attn_out_m1,
    attn_out_m2,
    ffn_in,
    ffn_in_m1,
    ffn_in_m2,
    ffn_out,
    ffn_out_m1,
    ffn_out_m2,
    len_head,
    len_head_m1,
    len_head_m2,
    norms,
    norms_m1,
    norms_m2,
    table,
    table_m1,
    table_m2,
):
    rows_here, seq_rows = src_ids.shape
    seqs, owners = lax.axis_size("seq"), lax.axis_size("dp")
    devices = seqs * owners
    row_len = seq_rows * seqs
    side = lax.axis_index("seq")
    group = seqs // rows_here
    span = row_len // group
    row, offset = side // group, (side % group) * span
    sharers = [[r * group + i for i in range(group)] for r in range(rows_here)]
    own_words, width = table.shape
    classes = len_head.shape[1]
    vocab_width = own_words * owners
    vocab_base = side * vocab_width
    norm_count = norms.shape[1]
    norm_columns = 128

    def columns_of(weight, rows):
        return [weight[at : at + rows] for at in range(0, weight.shape[0], rows)]

    def gather_columns(parts):
        joined = jnp.concatenate([part.astype(low_type) for part in parts], 1)
        if joined.shape[0] % (16 * seqs) == 0:
            rows = joined.shape[0] // seqs
            joined = lax.dynamic_slice_in_dim(joined, side * rows, rows, 0)
            whole = lax.all_gather(joined, ("dp", "seq"), axis=0, tiled=True)
        else:
            whole = lax.all_gather(joined, "dp", axis=0, tiled=True)
        result, at = [], 0
        for part in parts:
            result.append(whole[:, at : at + part.shape[1]])
            at += part.shape[1]
        return result

    def join_rows(pieces):
        blocks = [piece.reshape(owners, -1, piece.shape[1]) for piece in pieces]
        return jnp.concatenate(blocks, 1).reshape(-1, pieces[0].shape[1])

    share = attn_in.shape[1]
    norm_part = jnp.pad(
        norms.reshape(-1, norms.shape[2]).T, ((0, 0), (0, norm_columns - 2 * norm_count))
    )
    first_parts = [attn_in[0], attn_out[0], len_head, norm_part, ffn_in[0]]
    first_parts += columns_of(ffn_out[0], share)
    w_in0, w_out0, w_len, norm_low, f_in0, *f_out0 = gather_columns(first_parts)
    next_parts = [attn_in[1], attn_out[1], attn_in[2], attn_out[2], ffn_in[1]]
    next_parts += columns_of(ffn_out[1], share)
    w_in1, w_out1, w_in2, w_out2, f_in1, *f_out1 = gather_columns(next_parts)
    f_out0, f_out1 = join_rows(f_out0), join_rows(f_out1)
    table_low = table.astype(low_type)
    table_part = lax.all_gather(table_low, "dp", axis=0, tiled=True)
    norm_low = norm_low[:, : 2 * norm_count].T.astype(f32)
    gains, biases = norm_low[:norm_count], norm_low[norm_count:]

    ids = gather_seq(jnp.stack([src_ids, tgt_ids, tgt_mask]), 2).reshape(3, rows_here, row_len)
    src_starts = jnp.cumsum(src_lengths, -1) - src_lengths
    tgt_starts = jnp.cumsum(tgt_lengths, -1) - tgt_lengths
    places = jnp.arange(row_len)
    opens = jnp.any(places[None, :, None] == src_starts[:, None, :], -1)
    src_in = pick(jnp.where(opens, length_token, ids[0]).reshape(seqs, span), 0, side)
    masked = (ids[2] == 1).reshape(seqs, span)
    labels = ids[1].reshape(seqs, span)
    dec_in = pick(jnp.where(masked, mask_token, labels), 0, side)
    counts = jnp.sum(masked.astype(jnp.int32), -1)

    def slots_for(expected):
        return max(-(-expected // 16) * 16, 16)

    src_slots, dec_slots = slots_for(2 * span // devices), slots_for(3 * span // (2 * devices))

    def ask(token_ids, slots):
        same = token_ids[:, None] == token_ids[None, :]
        index = jnp.arange(span)
        earlier = index[None, :] < index[:, None]
        leader = jnp.logical_not(jnp.any(same & earlier, 1))
        holder = token_ids // own_words
        rank = jnp.sum(
            (earlier & leader[None, :] & (holder[:, None] == holder[None, :])).astype(jnp.int32), 1
        )
        rank = jnp.sum(jnp.where(same & leader[None, :], rank[None, :], 0), 1)
        return token_ids % own_words, holder, rank, slots

    def chosen_of(asked, turn):
        local, holder, rank, slots = asked
        code = jnp.where(rank // slots == turn, holder * slots + rank % slots, -1)
        return code[:, None] == jnp.arange(devices * slots)[None, :]

    def wanted_of(asked, chosen):
        return jnp.max(jnp.where(chosen, asked[0][:, None], -1), 0).reshape(devices, -1)

    def maps_of(chosen, wanted):
        held = wanted.reshape(-1)[:, None] == jnp.arange(own_words)[None, :]
        return chosen.astype(low_type), held.astype(low_type)

    def round_of(asked, turn):
        chosen = chosen_of(asked, turn)
        return maps_of(chosen, to_each(wanted_of(asked, chosen)))

    def send_rows(held):
        found = contract(held, table_low, 1, 0).astype(low_type)
        return to_each(found.reshape(devices, -1, width)).reshape(-1, width)

    def fetch(maps):
        chosen, held = maps
        return contract(send_rows(held), chosen, 0, 1)

    def give(maps, grads):
        chosen, held = maps
        sums = contract(chosen, grads.astype(low_type), 0, 1).astype(low_type)
        sums = to_each(sums.reshape(devices, -1, width)).reshape(-1, width)
        return contract(held, sums, 0, 0)

    def later_rounds(rounds, value, visit):
        return lax.fori_loop(1, rounds, lambda turn, carry: carry + visit(turn), value)

    src_ask, dec_ask = ask(src_in, src_slots), ask(dec_in, dec_slots)
    src_chosen, dec_chosen = chosen_of(src_ask, 0), chosen_of(dec_ask, 0)
    facts = jnp.stack(
        [
            jnp.sum(tgt_mask),
            jnp.max(counts),
            jnp.max(src_ask[2]) // src_slots + 1,
            jnp.max(dec_ask[2]) // dec_slots + 1,
        ]
    )
    facts = jnp.broadcast_to(jnp.pad(facts, (0, 12))[None, :], (devices, 16))
    asked = [wanted_of(src_ask, src_chosen), wanted_of(dec_ask, dec_chosen), facts]
    asked = to_each(jnp.concatenate(asked, 1).astype(jnp.int32))
    facts = asked[:, src_slots + dec_slots :]
    count = jnp.sum(facts[:, 0]).astype(f32)
    cut = -(-(span * 3 // 8) // 128) * 128
    more = jnp.max(facts[:, 1]) > cut
    src_rounds, dec_rounds = jnp.max(facts[:, 2]), jnp.max(facts[:, 3])
    src_maps = maps_of(src_chosen, asked[:, :src_slots])
    src_found = fetch(src_maps)
    dec_maps = maps_of(dec_chosen, asked[:, src_slots : src_slots + dec_slots])
    dec_rows = send_rows(dec_maps[1])

    starts_at = jnp.cumsum(counts) - counts
    total = jnp.sum(counts)
    rank = jnp.where(masked, jnp.cumsum(masked.astype(jnp.int32), -1) - 1, -1)
    slot_of = jnp.where(masked, rank + starts_at[:, None], -1)
    slot_index = jnp.arange(seqs * span)
    slot_label = jnp.sum(
        jnp.where(slot_of.reshape(1, -1) == slot_index[:, None], labels.reshape(1, -1), 0), -1
    )
    valid = slot_index < total
    targets = jnp.where(valid, slot_label - vocab_base, -1).reshape(1, -1)
    plan = jnp.concatenate([chunk_plan(total), lax.axis_index("dp")[None] & 1]).astype(jnp.int32)
    own_rank, own_slot = pick(rank, 0, side), pick(slot_of, 0, side)

    def packing(slots, rows):
        slot, index = jnp.arange(slots), jnp.arange(rows)
        far_start, far_count = pick(starts_at, 0, 1 - side), pick(counts, 0, 1 - side)
        far = jnp.where(index < far_count, index + far_start, -1)
        return (
            (own_rank[None, :] == index[:, None]).astype(low_type),
            (own_slot[None, :] == slot[:, None]).astype(low_type),
            (far[None, :] == slot[:, None]).astype(low_type),
        )

    own_places = offset + jnp.arange(span)
    src_start, src_length = pick(src_starts, 0, row), pick(src_lengths, 0, row)
    tgt_start, tgt_length = pick(tgt_starts, 0, row), pick(tgt_lengths, 0, row)
    src_number, src_open = place_spans(src_start, own_places)
    tgt_number, tgt_open = place_spans(tgt_start, own_places)
    block = min(query_block, span)
    enc_spans = key_spans(src_number, src_start, src_length, block)
    self_spans = key_spans(tgt_number, tgt_start, tgt_length, block)
    cross_spans = key_spans(tgt_number, src_start, src_length, block)
    src_wave, tgt_wave = lax.optimization_barrier(
        (sinusoid(own_places - src_open, width), sinusoid(own_places - tgt_open, width))
    )

    root = math.sqrt(width)
    src_found = later_rounds(src_rounds, src_found, lambda turn: fetch(round_of(src_ask, turn)))
    stream0 = src_found * root + src_wave

    def norm(stream, index):
        return layer_norm(stream, gains[index], biases[index])

    def keys_of_row(part):
        if group == 1:
            return part
        return lax.all_gather(part, "seq", axis=1, tiled=True, axis_index_groups=sharers)

    def keys_to_place(part):
        if group == 1:
            return part
        return lax.psum_scatter(
            part, "seq", scatter_dimension=1, tiled=True, axis_index_groups=sharers
        )

    def self_attention(inner, weight_in, weight_out, spans):
        triple = contract(weight_in, inner, 0, 0).astype(low_type)
        keys = triple if group == 1 else keys_of_row(triple[width:])
        mixed, lse = attend_forward(triple, keys, group == 1, *spans)
        return contract(weight_out, mixed, 0, 0), (triple, keys, mixed, lse)

    def self_attention_back(inner, weight_in, weight_out, spans, kept, grad):
        triple, keys, mixed, lse = kept
        grad_low = grad.astype(low_type)
        d_out = contract(mixed, grad_low, 1, 1)
        d_mixed = contract(weight_out, grad_low, 1, 0).astype(low_type)
        d_query, d_keys = attend_backward(triple, keys, group == 1, *spans, lse, d_mixed)
        d_triple = jnp.concatenate([d_query, keys_to_place(d_keys)], 0)
        return contract(weight_in, d_triple, 1, 0), contract(inner, d_triple, 1, 1), d_out

    def cross_attention(inner, memory, weight_in, weight_out, spans):
        queries = contract(weight_in[:, :width], inner, 0, 0).astype(low_type)
        keys = keys_of_row(contract(weight_in[:, width:], memory, 0, 0).astype(low_type))
        mixed, lse = attend_forward(queries, keys, False, *spans)
        return contract(weight_out, mixed, 0, 0), (queries, keys, mixed, lse)

    def cross_attention_back(inner, memory, weight_in, weight_out, spans, kept, grad):
        queries, keys, mixed, lse = kept
        grad_low = grad.astype(low_type)
        d_out = contract(mixed, grad_low, 1, 1)
        d_mixed = contract(weight_out, grad_low, 1, 0).astype(low_type)
        d_query, d_keys = attend_backward(queries, keys, False, *spans, lse, d_mixed)
        d_keys = keys_to_place(d_keys)
        d_in = jnp.concatenate([contract(inner, d_query, 1, 1), contract(memory, d_keys, 1, 1)], 1)
        return (
            contract(weight_in[:, :width], d_query, 1, 0),
            contract(weight_in[:, width:], d_keys, 1, 0),
            d_in,
            d_out,
        )

    def ffn(inner, weight_one, weight_two):
        hidden = contract(weight_one, inner, 0, 0)
        active = jax.nn.gelu(hidden).astype(low_type)
        return contract(weight_two, active, 0, 0), (hidden, active)

    def ffn_back(inner, weight_one, weight_two, kept, grad):
        hidden, active = kept
        grad_low = grad.astype(low_type)
        d_two = contract(active, grad_low, 1, 1)
        d_active = contract(weight_two, grad_low, 1, 0)
        d_hidden = jax.vjp(jax.nn.gelu, hidden)[1](d_active)[0].astype(low_type)
        return contract(weight_one, d_hidden, 1, 0), contract(inner, d_hidden, 1, 1), d_two

    inner0 = norm(stream0, 0).astype(low_type)
    branch0, keep0 = self_attention(inner0, w_in0, w_out0, enc_spans)
    stream1 = stream0 + branch0
    inner1 = norm(stream1, 1).astype(low_type)
    branch1, keep1 = ffn(inner1, f_in0, f_out0)
    stream2 = stream1 + branch1
    memory = norm(stream2, 2).astype(low_type)
    memory, dec_chosen = lax.optimization_barrier((memory, dec_maps[0]))
    dec_found = contract(dec_rows, dec_chosen, 0, 1)
    dec_found = later_rounds(dec_rounds, dec_found, lambda turn: fetch(round_of(dec_ask, turn)))
    target0 = dec_found * root + tgt_wave
    inner3 = norm(target0, 3).astype(low_type)
    branch3, keep3 = self_attention(inner3, w_in1, w_out1, self_spans)
    target1 = target0 + branch3
    inner4 = norm(target1, 4).astype(low_type)
    branch4, keep4 = cross_attention(inner4, memory, w_in2, w_out2, cross_spans)
    target2 = target1 + branch4
    inner5 = norm(target2, 5).astype(low_type)
    branch5, keep5 = ffn(inner5, f_in1, f_out1)
    target3 = target2 + branch5
    final = norm(target3, 6).astype(low_type)

    def pack(slots, rows):
        own_chosen, own_slots, far_slots = packing(slots, rows)
        far = swap(contract(own_chosen, final, 1, 1).astype(low_type), "seq", 1)
        packed = contract(own_slots, final, 1, 1) + contract(far_slots, far, 1, 0)
        return jnp.pad(packed.astype(low_type), ((0, seqs * span - slots), (0, 0)))

    def unpack(slots, rows):
        own_chosen, own_slots, far_slots = packing(slots, rows)
        high = lax.reduce_precision(d_pieces[:slots], 8, 7)
        rest = (d_pieces[:slots] - high).astype(low_type)
        high = high.astype(low_type)
        far = swap(contract(far_slots, high, 0, 0).astype(low_type), "seq", 1)
        return (
            contract(high, own_slots, 0, 0)
            + contract(rest, own_slots, 0, 0)
            + contract(far, own_chosen, 0, 0)
        )

    if seqs == 2:
        pieces = lax.cond(
            more, lambda: pack(2 * span, span), lambda: pack(min(2 * cut, 2 * span), cut)
        )
    else:
        own_slots = packing(seqs * span, span)[1]
        pieces = lax.psum(contract(own_slots, final, 1, 1), "seq").astype(low_type)
    turned = pieces.T
    every = gather_seq(head_stats(plan, table_part, turned), 0)
    top_logit = jnp.max(every[:, 0], 0)
    totals = jnp.sum(every[:, 1] * jnp.exp(every[:, 0] - top_logit[None]), 0)
    log_total = top_logit + jnp.log(jnp.where(valid, totals, 1.0))
    own_start = pick(starts_at, 0, side)
    mine = (slot_index >= own_start) & (slot_index < own_start + pick(counts, 0, side))
    token_local = jnp.sum(jnp.where(mine, log_total, 0.0))
    logs = jnp.where(valid, log_total + jnp.log(count), 1e30)
    weights = jnp.where(valid, 1.0 / count, 0.0)
    split = halving_fits(own_words, width // 2, False) and own_words % 8 == 0
    *d_table, d_pieces, picks = head_back(
        plan, table_part, pieces, turned, targets, logs[None], weights[None], split and own_words
    )
    token_local = token_local - jnp.sum(picks)
    if split:
        table_chains = [TableChain(d_table[0], d_table[2])]
    if seqs == 2:
        d_final = lax.cond(
            more, lambda: unpack(2 * span, span), lambda: unpack(min(2 * cut, 2 * span), cut)
        )
    else:
        d_pieces = lax.psum(d_pieces, "seq")
        high = lax.reduce_precision(d_pieces, 8, 7)
        rest = (d_pieces - high).astype(low_type)
        d_final = contract(high.astype(low_type), own_slots, 0, 0) + contract(rest, own_slots, 0, 0)

    first_place = own_places[None, :] == src_start[:, None]
    mine = jnp.any(first_place, -1)
    first_rows = contract(first_place.astype(low_type), memory, 1, 1).astype(low_type)
    len_logits = contract(first_rows, w_len, 1, 0)
    len_label = jnp.minimum(tgt_length, classes - 1)
    len_hot = jnp.arange(classes)[None, :] == len_label[:, None]
    len_loss = jax.nn.logsumexp(len_logits, -1) - jnp.sum(jnp.where(len_hot, len_logits, 0.0), -1)
    len_local = jnp.sum(jnp.where(mine, len_loss, 0.0))
    sentences = rows_here * src_lengths.shape[1] * owners
    len_prob = jax.nn.softmax(len_logits, -1)
    d_len_logits = (
        jnp.where(mine[:, None], len_prob - len_hot.astype(f32), 0.0) * (0.1 / sentences)
    ).astype(low_type)
    d_w_len = contract(first_rows, d_len_logits, 0, 0)
    d_first = contract(d_len_logits, w_len, 1, 1)
    d_memory = lax.dot_general(
        d_first,
        first_place.astype(f32),
        (((0,), (0,)), ((), ())),
        precision=lax.Precision.HIGHEST,
        preferred_element_type=f32,
    )

    def owned(grad):
        return grad.reshape(owners, -1, grad.shape[1])

    def owned_columns(grad):
        whole = owned(grad)
        return [whole[:, at : at + share] for at in range(0, whole.shape[1], share)]

    none = jnp.zeros_like(stream0)
    d_target3, scale6 = norm_backward(target3, gains[6], d_final, none)
    d_inner5, d_fin1, d_fout1 = ffn_back(inner5, f_in1, f_out1, keep5, d_target3)
    chains = list(table_chains) if split else []
    d_inner5, d_target3, d_table = advance((d_inner5, d_target3, d_table), chains)
    if split:
        table_chains.append(TableChain(d_table[1], d_table[3]))
    chain_a = LayerChain([owned(d_fin1)] + owned_columns(d_fout1))
    d_target2, scale5 = norm_backward(target2, gains[5], d_inner5, d_target3)
    d_inner4, d_cross, d_win2, d_wout2 = cross_attention_back(
        inner4, memory, w_in2, w_out2, cross_spans, keep4, d_target2
    )
    chains = (table_chains if split else []) + [chain_a]
    d_inner4, d_target2, d_cross = advance((d_inner4, d_target2, d_cross), chains)
    chain_b = LayerChain([owned(d_win2), owned(d_wout2)])
    d_target1, scale4 = norm_backward(target1, gains[4], d_inner4, d_target2)
    d_inner3, d_win1, d_wout1 = self_attention_back(
        inner3, w_in1, w_out1, self_spans, keep3, d_target1
    )
    chains += [chain_b]
    d_inner3, d_target1 = advance((d_inner3, d_target1), chains)
    chain_c = LayerChain([owned(d_win1), owned(d_wout1)])
    d_target0, scale3 = norm_backward(target0, gains[3], d_inner3, d_target1)
    dec_grad = d_target0 * root
    dec_given = give(dec_maps, dec_grad)
    d_stream2, scale2 = norm_backward(stream2, gains[2], d_memory + d_cross, none)
    d_inner1, d_fin0, d_fout0 = ffn_back(inner1, f_in0, f_out0, keep1, d_stream2)
    chains += [chain_c]
    d_inner1, d_stream2 = advance((d_inner1, d_stream2), chains)
    chain_d = LayerChain([owned(d_fin0)] + owned_columns(d_fout0))
    d_stream1, scale1 = norm_backward(stream1, gains[1], d_inner1, d_stream2)
    d_inner0, d_win0, d_wout0 = self_attention_back(
        inner0, w_in0, w_out0, enc_spans, keep0, d_stream1
    )
    chains += [chain_d]
    d_inner0, d_stream1, dec_given = advance((d_inner0, d_stream1, dec_given), chains)
    d_stream0, scale0 = norm_backward(stream0, gains[0], d_inner0, d_stream1)
    src_grad = d_stream0 * root
    src_given = give(src_maps, src_grad)
    chain_e = LayerChain([owned(d_win0), owned(d_wout0), owned(d_w_len)])
    norm_share = norms.shape[2]
    scales = jnp.sum(jnp.stack([scale0, scale1, scale2, scale3, scale4, scale5, scale6], 1), 3)
    scales = scales.reshape(2 * norm_count, owners, norm_share).transpose(1, 0, 2)
    scales = jnp.broadcast_to(scales[None], (seqs,) + scales.shape)
    g_norms = jnp.sum(to_each(scales.reshape((devices,) + scales.shape[2:])), 0)
    norm_square = jnp.where(side == 0, jnp.sum(g_norms * g_norms), 0.0)
    chains += [chain_e]
    while any(chain.pending is not None for chain in chains):
        advance((), chains)
    layer_chains = [chain_a, chain_b, chain_c, chain_d, chain_e]
    for chain in layer_chains:
        chain.finish()

    given = dec_given + src_given
    given = later_rounds(
        jnp.maximum(src_rounds, dec_rounds),
        given,
        lambda turn: give(round_of(dec_ask, turn), dec_grad)
        + give(round_of(src_ask, turn), src_grad),
    )
    if split:
        table_grad = jnp.concatenate([chain.value for chain in table_chains], 1)
    else:
        table_grad = lax.psum_scatter(d_table[0], "dp", scatter_dimension=0, tiled=True)
    table_grad = table_grad + given
    square = sum(chain.square for chain in layer_chains)
    square = square + jnp.sum(table_grad * table_grad) + norm_square
    sums = everywhere(
        jnp.stack([token_local, len_local, square]).reshape(1, 3), jnp.add, lax.psum
    )[0]
    token_sum, len_sum, grad_norm = sums[0], sums[1], jnp.sqrt(sums[2])
    factor = jnp.minimum(1.0, clip_limit / (grad_norm + 1e-06))

    def cut_columns(chain, sizes):
        result, at = [], 0
        value = chain.value.reshape(share, -1)
        for size in sizes:
            result.append(value[:, at : at + size])
            at += size
        return result

    hidden_width = ffn_in.shape[2]
    pieces_out = ffn_out.shape[1] // share
    ffn_sizes = [hidden_width] + [width] * pieces_out
    attn_sizes = [3 * width, width]
    g_fin1, *g_fout1 = cut_columns(chain_a, ffn_sizes)
    g_win2, g_wout2 = cut_columns(chain_b, attn_sizes)
    g_win1, g_wout1 = cut_columns(chain_c, attn_sizes)
    g_fin0, *g_fout0 = cut_columns(chain_d, ffn_sizes)
    g_win0, g_wout0, g_len = cut_columns(chain_e, attn_sizes + [classes])
    grads = (
        jnp.stack([g_win0, g_win1, g_win2]),
        jnp.stack([g_wout0, g_wout1, g_wout2]),
        jnp.stack([g_fin0, g_fin1]),
        jnp.stack([jnp.concatenate(g_fout0, 0), jnp.concatenate(g_fout1, 0)]),
        g_len,
        g_norms.reshape(norms.shape),
        table_grad,
    )
    masters = (attn_in, attn_out, ffn_in, ffn_out, len_head, norms, table)
    firsts = (attn_in_m1, attn_out_m1, ffn_in_m1, ffn_out_m1, len_head_m1, norms_m1, table_m1)
    seconds = (attn_in_m2, attn_out_m2, ffn_in_m2, ffn_out_m2, len_head_m2, norms_m2, table_m2)
    updates = []
    for weight, first, second, grad, rate in zip(masters, firsts, seconds, grads, step_rates):
        updates.extend(adam_update(weight, first, second, grad * factor, rate))
    return (token_sum, count, len_sum, grad_norm, *updates)


def solution(mesh):
    layer, head, scales, words = P(None, "dp", None), P("dp", None), P(None, None, "dp"), P(("seq", "dp"), None)
    owned = (layer,) * 12 + (head,) * 3 + (scales,) * 3 + (words,) * 3
    ids, lengths = P("dp", "seq"), P("dp", None)
    in_specs = (ids, ids, lengths, lengths, ids) + owned
    out_specs = (P(), P(), P(), P()) + owned
    return jax.shard_map(
        on_device, mesh=mesh, in_specs=in_specs, out_specs=out_specs, check_vma=False
    )
```

```python
import functools
import math

import jax
import jax.numpy as jnp
from jax import lax
from jax.experimental import pallas as pl
from jax.experimental.pallas import tpu as pltpu
from jax.sharding import PartitionSpec as P

HEADS = 8
STEP = 10


length_token = 1
mask_token = 2
clip_limit = 0.002
beta_one = 0.9
beta_two = 0.98
adam_eps = 1e-08
weight_decay = 0.01
step_rates = (0.05, 0.25, 0.05, 0.025, 0.05, 0.5, 0.1)

low_type = jnp.bfloat16
f32 = jnp.float32
query_block = 256
key_block = 128
place_block = 512
vmem_bytes = 56 * 1024 * 1024


def sinusoid(positions, width):
    half_width = width // 2
    frequency = jnp.exp(jnp.arange(half_width).astype(f32) * (-math.log(10000.0) / half_width))
    angles = frequency[:, None] * positions.astype(f32)[None, :]
    return jnp.concatenate([jnp.sin(angles), jnp.cos(angles)], 0)


def layer_norm(stream, norm_gain, norm_bias):
    average = jnp.mean(stream, 0, keepdims=True)
    centred = stream - average
    variance = jnp.mean(centred * centred, 0, keepdims=True)
    return centred * lax.rsqrt(variance + 1e-05) * norm_gain[:, None] + norm_bias[:, None]


def contract(left, right, left_dim, right_dim):
    return lax.dot_general(
        left, right, (((left_dim,), (right_dim,)), ((), ())), preferred_element_type=f32
    )


def attend_forward_kernel(bounds, q_ref, k_ref, v_ref, span_ref, out_ref, lse_ref, hold, *, head):
    step = pl.program_id(0)
    first, last = bounds[0, step], bounds[1, step]
    width, queries = q_ref.shape
    heads = width // head
    scale = head**-0.5
    low, high = span_ref[0:1, :], span_ref[1:2, :]
    inner = lax.broadcasted_iota(jnp.int32, (key_block, queries), 0)

    def fold(values, op):
        return op(values.reshape(key_block // 8, 8, queries), axis=0)

    def score(block, tops):
        start = pl.multiple_of(block * key_block, key_block)
        place = inner + start
        allowed = (place >= low) & (place < high)
        result = []
        for h in range(heads):
            rows = slice(h * head, (h + 1) * head)
            s = contract(k_ref[rows, pl.ds(start, key_block)], q_ref[rows, :], 0, 0) * scale
            s = jnp.where(allowed, s, -1e30)
            hold[h, pl.ds(start, key_block), :] = s
            result.append(jnp.maximum(tops[h], fold(s, jnp.max)))
        return tuple(result)

    tops = lax.fori_loop(
        first, last, score, tuple(jnp.full((8, queries), -1e30, f32) for _ in range(heads))
    )
    tops = [jnp.max(t, axis=0, keepdims=True) for t in tops]

    def power(block, sums):
        start = pl.multiple_of(block * key_block, key_block)
        result = []
        for h in range(heads):
            e = jnp.exp(hold[h, pl.ds(start, key_block), :] - tops[h])
            hold[h, pl.ds(start, key_block), :] = e
            result.append(sums[h] + fold(e, jnp.sum))
        return tuple(result)

    sums = lax.fori_loop(
        first, last, power, tuple(jnp.zeros((8, queries), f32) for _ in range(heads))
    )
    sums = [jnp.maximum(jnp.sum(t, axis=0, keepdims=True), 1e-30) for t in sums]
    inverse = [1.0 / t for t in sums]

    def mix(block, outs):
        start = pl.multiple_of(block * key_block, key_block)
        result = []
        for h in range(heads):
            rows = slice(h * head, (h + 1) * head)
            p = (hold[h, pl.ds(start, key_block), :] * inverse[h]).astype(low_type)
            result.append(outs[h] + contract(v_ref[rows, pl.ds(start, key_block)], p, 1, 0))
        return tuple(result)

    outs = lax.fori_loop(
        first, last, mix, tuple(jnp.zeros((head, queries), f32) for _ in range(heads))
    )
    for h in range(heads):
        out_ref[h * head : (h + 1) * head, :] = outs[h].astype(low_type)
        lse_ref[h : h + 1, :] = tops[h] + jnp.log(sums[h])


def attend_backward_kernel(
    bounds, q_ref, k_ref, v_ref, span_ref, lse_ref, do_ref, dq_ref, dkv_ref, p_hold, d_hold, acc,
    *, head
):
    step = pl.program_id(0)
    first, last = bounds[0, step], bounds[1, step]
    width, queries = q_ref.shape
    heads = width // head
    scale = head**-0.5
    low, high = span_ref[0:1, :], span_ref[1:2, :]
    inner = lax.broadcasted_iota(jnp.int32, (key_block, queries), 0)

    @pl.when(step == 0)
    def _():
        acc[...] = jnp.zeros_like(acc)

    def one(block, deltas):
        start = pl.multiple_of(block * key_block, key_block)
        keys = pl.ds(start, key_block)
        place = inner + start
        allowed = (place >= low) & (place < high)
        result = []
        for h in range(heads):
            rows = slice(h * head, (h + 1) * head)
            s = contract(k_ref[rows, keys], q_ref[rows, :], 0, 0) * scale
            p = jnp.exp(jnp.where(allowed, s, -1e30) - lse_ref[h : h + 1, :])
            dp = contract(v_ref[rows, keys], do_ref[rows, :], 0, 0)
            p_hold[h, keys, :] = p
            d_hold[h, keys, :] = dp
            result.append(
                deltas[h] + jnp.sum((p * dp).reshape(key_block // 8, 8, queries), axis=0)
            )
            below = slice(width + h * head, width + (h + 1) * head)
            acc[below, keys] += contract(do_ref[rows, :], p.astype(low_type), 1, 1)
        return tuple(result)

    deltas = lax.fori_loop(
        first, last, one, tuple(jnp.zeros((8, queries), f32) for _ in range(heads))
    )
    deltas = [jnp.sum(t, axis=0, keepdims=True) for t in deltas]

    def two(block, outs):
        start = pl.multiple_of(block * key_block, key_block)
        keys = pl.ds(start, key_block)
        result = []
        for h in range(heads):
            rows = slice(h * head, (h + 1) * head)
            ds = (p_hold[h, keys, :] * (d_hold[h, keys, :] - deltas[h])).astype(low_type)
            result.append(outs[h] + contract(k_ref[rows, keys], ds, 1, 0))
            acc[rows, keys] += contract(q_ref[rows, :], ds, 1, 1) * scale
        return tuple(result)

    outs = lax.fori_loop(
        first, last, two, tuple(jnp.zeros((head, queries), f32) for _ in range(heads))
    )
    for h in range(heads):
        dq_ref[h * head : (h + 1) * head, :] = (outs[h] * scale).astype(low_type)

    @pl.when(step == pl.num_programs(0) - 1)
    def _():
        dkv_ref[...] = acc[...].astype(low_type)


def attend_specs(width, length, block, shared):
    key_row = 1 if shared else 0
    return [
        pl.BlockSpec((width, block), lambda i, *_: (0, i)),
        pl.BlockSpec((width, length), lambda i, *_: (key_row, 0)),
        pl.BlockSpec((width, length), lambda i, *_: (key_row + 1, 0)),
        pl.BlockSpec((2, block), lambda i, *_: (0, i)),
    ]


def attend_forward(queries, keys, shared, spans, bounds):
    width = keys.shape[0] // (3 if shared else 2)
    places, length = queries.shape[1], keys.shape[1]
    block = min(query_block, places)
    return pl.pallas_call(
        functools.partial(attend_forward_kernel, head=width // HEADS),
        grid_spec=pltpu.PrefetchScalarGridSpec(
            num_scalar_prefetch=1,
            grid=(places // block,),
            in_specs=attend_specs(width, length, block, shared),
            out_specs=[
                pl.BlockSpec((width, block), lambda i, *_: (0, i)),
                pl.BlockSpec((HEADS, block), lambda i, *_: (0, i)),
            ],
            scratch_shapes=[pltpu.VMEM((HEADS, length, block), f32)],
        ),
        out_shape=[
            jax.ShapeDtypeStruct((width, places), low_type),
            jax.ShapeDtypeStruct((HEADS, places), f32),
        ],
        compiler_params=pltpu.CompilerParams(vmem_limit_bytes=vmem_bytes),
        name="attend_forward",
    )(bounds, queries, keys, keys, spans)


def attend_backward(queries, keys, shared, spans, bounds, lse, d_mixed):
    width = keys.shape[0] // (3 if shared else 2)
    places, length = queries.shape[1], keys.shape[1]
    block = min(query_block, places)
    return pl.pallas_call(
        functools.partial(attend_backward_kernel, head=width // HEADS),
        grid_spec=pltpu.PrefetchScalarGridSpec(
            num_scalar_prefetch=1,
            grid=(places // block,),
            in_specs=attend_specs(width, length, block, shared)
            + [
                pl.BlockSpec((HEADS, block), lambda i, *_: (0, i)),
                pl.BlockSpec((width, block), lambda i, *_: (0, i)),
            ],
            out_specs=[
                pl.BlockSpec((width, block), lambda i, *_: (0, i)),
                pl.BlockSpec((2 * width, length), lambda i, *_: (0, 0)),
            ],
            scratch_shapes=[
                pltpu.VMEM((HEADS, length, block), f32),
                pltpu.VMEM((HEADS, length, block), f32),
                pltpu.VMEM((2 * width, length), f32),
            ],
        ),
        out_shape=[
            jax.ShapeDtypeStruct((width, places), low_type),
            jax.ShapeDtypeStruct((2 * width, length), low_type),
        ],
        compiler_params=pltpu.CompilerParams(vmem_limit_bytes=vmem_bytes),
        name="attend_backward",
    )(bounds, queries, keys, keys, spans, lse, d_mixed)


def norm_back_kernel(stream_ref, gain_ref, grad_ref, rest_ref, out_ref, sums_ref):
    @pl.when(pl.program_id(0) == 0)
    def _():
        sums_ref[...] = jnp.zeros_like(sums_ref)

    stream, grad = stream_ref[...], grad_ref[...]
    width, places = stream.shape
    average = jnp.mean(stream, 0, keepdims=True)
    centred = stream - average
    variance = jnp.mean(centred * centred, 0, keepdims=True)
    inverse = lax.rsqrt(variance + 1e-05)
    unit = centred * inverse
    scaled = grad * gain_ref[...]
    along = jnp.mean(scaled * unit, 0, keepdims=True)
    level = jnp.mean(scaled, 0, keepdims=True)
    out_ref[...] = rest_ref[...] + (scaled - level - unit * along) * inverse
    weighted = grad * unit
    for at in range(0, places, 128):
        sums_ref[0] += weighted[:, at : at + 128]
        sums_ref[1] += grad[:, at : at + 128]


def norm_backward(stream, gain, grad, rest):
    width, places = stream.shape
    columns = min(256, places)
    block = pl.BlockSpec((width, columns), lambda i: (0, i))
    return pl.pallas_call(
        norm_back_kernel,
        grid=(places // columns,),
        in_specs=[block, pl.BlockSpec((width, 1), lambda i: (0, 0)), block, block],
        out_specs=[block, pl.BlockSpec((2, width, 128), lambda i: (0, 0, 0))],
        out_shape=[
            jax.ShapeDtypeStruct((width, places), f32),
            jax.ShapeDtypeStruct((2, width, 128), f32),
        ],
        compiler_params=pltpu.CompilerParams(vmem_limit_bytes=vmem_bytes),
        name="norm_backward",
    )(stream, gain[:, None], grad, rest)


def chunk_plan(total):
    quarter = place_block // 4
    units = (jnp.maximum(total - place_block, 0) + quarter - 1) // quarter
    left = units % 4
    wides = units // 4 + (left == 3).astype(jnp.int32)
    return jnp.stack([wides, left == 2, left == 1]).astype(jnp.int32)


def each_chunk(plan, visit):
    visit(0, place_block, True)

    def wide(index, carry):
        visit(pl.multiple_of((index + 1) * place_block, place_block), place_block, False)
        return carry

    lax.fori_loop(0, plan[0], wide, 0)
    after = pl.multiple_of((plan[0] + 1) * place_block, place_block)
    for index, share in ((1, 2), (2, 4)):

        @pl.when(plan[index] > 0)
        def _(share=share):
            visit(after, place_block // share, False)


def parts_of(words):
    for count in (5, 4, 2):
        if words % (16 * count) == 0:
            return [slice(i * (words // count), (i + 1) * (words // count)) for i in range(count)]
    return [slice(0, words)]


def head_stats_kernel(plan, table_ref, turned_ref, stats_ref, tops, sums):
    step = pl.program_id(0)

    @pl.when(step == 0)
    def _():
        tops[...] = jnp.full_like(tops, -1e30)
        sums[...] = jnp.zeros_like(sums)

    def visit(start, size, first):
        here = pl.ds(start, size)
        turned = turned_ref[:, here]
        old, total = tops[:, here], sums[:, here]
        for part in parts_of(table_ref.shape[0]):
            logits = contract(table_ref[part, :], turned, 1, 0)
            logits = logits.reshape(logits.shape[0] // 8, 8, size)
            top = jnp.maximum(old, jnp.max(logits, axis=0))
            powers = jnp.sum(jnp.exp(logits - top[None]), axis=0)
            total = total * jnp.exp(old - top) + powers
            old = top
        sums[:, here] = total
        tops[:, here] = old

    each_chunk(plan, visit)

    @pl.when(step == pl.num_programs(0) - 1)
    def _():
        top = jnp.max(tops[...], axis=0, keepdims=True)
        stats_ref[0:1, :] = top
        stats_ref[1:2, :] = jnp.sum(sums[...] * jnp.exp(tops[...] - top), axis=0, keepdims=True)


def head_back_kernel(
    plan, table_ref, rows_ref, turned_ref, target_ref, log_ref, weight_ref, *refs, owned
):
    (*out_refs, dr_ref, pick_ref, acc) = refs
    step = pl.program_id(0)
    words, width = table_ref.shape

    @pl.when(step == 0)
    def _():
        dr_ref[...] = jnp.zeros_like(dr_ref)
        pick_ref[...] = jnp.zeros_like(pick_ref)

    def visit(start, size, first):
        here = pl.ds(start, size)
        rows, turned = rows_ref[here, :], turned_ref[:, here]
        target = target_ref[:, here] - step * words
        log, weight = log_ref[:, here], weight_ref[:, here]
        found = jnp.zeros((8, size), f32)
        for part in parts_of(words):
            block = table_ref[part, :]
            count = block.shape[0]
            inner = lax.broadcasted_iota(jnp.int32, (count, size), 0) + part.start
            logits = contract(block, turned, 1, 0)
            scaled = jnp.exp(logits - log)
            hit = inner == target
            found += jnp.sum(jnp.where(hit, logits, 0.0).reshape(count // 8, 8, size), axis=0)
            d_logits = jnp.where(hit, scaled - weight, scaled).astype(low_type)
            if first:
                acc[part, :] = contract(d_logits, rows, 1, 0)
            else:
                acc[part, :] += contract(d_logits, rows, 1, 0)
            dr_ref[here, :] += contract(d_logits, block, 0, 0)
        pick_ref[:, here] += found

    each_chunk(plan, visit)
    if not owned:
        out_refs[0][...] = acc[...]
        return
    mine = plan[3]
    keep = pl.ds(pl.multiple_of(mine * owned, 8), owned)
    away = pl.ds(pl.multiple_of((1 - mine) * owned, 8), owned)
    out_refs[0][0] = acc[keep, :]
    out_refs[1][0] = acc[away, :].astype(low_type)


def word_block(words):
    return max(n for n in range(16, 1601, 16) if words % n == 0)


def head_stats(plan, table_part, turned):
    words = word_block(table_part.shape[0])
    width, places = turned.shape
    return pl.pallas_call(
        head_stats_kernel,
        grid_spec=pltpu.PrefetchScalarGridSpec(
            num_scalar_prefetch=1,
            grid=(table_part.shape[0] // words,),
            in_specs=[
                pl.BlockSpec((words, width), lambda i, *_: (i, 0)),
                pl.BlockSpec((width, places), lambda i, *_: (0, 0)),
            ],
            out_specs=pl.BlockSpec((2, places), lambda i, *_: (0, 0)),
            scratch_shapes=[pltpu.VMEM((8, places), f32) for _ in range(2)],
        ),
        out_shape=jax.ShapeDtypeStruct((2, places), f32),
        compiler_params=pltpu.CompilerParams(vmem_limit_bytes=vmem_bytes),
        name="head_stats",
    )(plan, table_part, turned)


def head_back(plan, table_part, rows, turned, targets, logs, weights, owned):
    total = table_part.shape[0]
    words = 2 * owned if owned else word_block(total)
    places, width = rows.shape
    row = pl.BlockSpec((1, places), lambda i, *_: (0, 0))
    if owned:
        out_specs = [pl.BlockSpec((1, owned, width), lambda i, *_: (i, 0, 0))] * 2
        shape = (total // words, owned, width)
        out_shape = [jax.ShapeDtypeStruct(shape, f32), jax.ShapeDtypeStruct(shape, low_type)]
    else:
        out_specs = [pl.BlockSpec((words, width), lambda i, *_: (i, 0))]
        out_shape = [jax.ShapeDtypeStruct((total, width), f32)]
    return pl.pallas_call(
        functools.partial(head_back_kernel, owned=owned),
        grid_spec=pltpu.PrefetchScalarGridSpec(
            num_scalar_prefetch=1,
            grid=(total // words,),
            in_specs=[
                pl.BlockSpec((words, width), lambda i, *_: (i, 0)),
                pl.BlockSpec((places, width), lambda i, *_: (0, 0)),
                pl.BlockSpec((width, places), lambda i, *_: (0, 0)),
                row,
                row,
                row,
            ],
            out_specs=out_specs
            + [
                pl.BlockSpec((places, width), lambda i, *_: (0, 0)),
                pl.BlockSpec((8, places), lambda i, *_: (0, 0)),
            ],
            scratch_shapes=[pltpu.VMEM((words, width), f32)],
        ),
        out_shape=out_shape
        + [
            jax.ShapeDtypeStruct((places, width), f32),
            jax.ShapeDtypeStruct((8, places), f32),
        ],
        compiler_params=pltpu.CompilerParams(vmem_limit_bytes=vmem_bytes),
        name="head_back",
    )(plan, table_part, rows, turned, targets, logs, weights)


def swap(values, axis, bit):
    size = lax.axis_size(axis)
    return lax.ppermute(values, axis, [(i, i ^ bit) for i in range(size)])


def power_of_two(size):
    return size & (size - 1) == 0


def pick(values, dim, index):
    return lax.dynamic_index_in_dim(values, index, dim, False)


def gather_seq(values, dim):
    if lax.axis_size("seq") == 2:
        other = swap(values, "seq", 1)
        first = lax.axis_index("seq") == 0
        return jnp.stack([jnp.where(first, values, other), jnp.where(first, other, values)], dim)
    return lax.all_gather(values, "seq", axis=dim)


def to_each(values):
    return lax.all_to_all(values, ("seq", "dp"), 0, 0)


def halving_fits(rows, columns, joint):
    owners, seqs = lax.axis_size("dp"), lax.axis_size("seq")
    fits = power_of_two(owners) and owners > 2 and columns % 128 == 0
    return fits and (rows % 16 == 0 and seqs == 2 if joint else rows % 8 == 0)


class Chain:
    pending = value = square = None

class LayerChain(Chain):
    def __init__(self, parts):
        self.parts, self.step = parts, 0
        self.rows = parts[0].shape[1]
        self.fast = halving_fits(self.rows, parts[0].shape[2], True)
        if self.fast:
            self.launch()

    def launch(self):
        owners = lax.axis_size("dp")
        if self.step == 4:
            return
        if self.step == 3:
            self.pending = swap(self.part, "seq", 1)
        elif self.step == 2:
            groups = [list(range(core, owners, 2)) for core in range(2)]
            whole = (self.part + self.got.astype(f32)).astype(low_type)
            self.pending = lax.all_to_all(whole, "dp", 0, 0, axis_index_groups=groups)
        else:
            axis = ("dp", "seq")[self.step]
            mine = lax.axis_index(axis) & 1
            if self.step == 1:
                self.rows //= 2

            def half(side):
                if self.step == 0:
                    shape = (owners // 2, 2, self.rows)
                    parts = [part.reshape(shape + part.shape[2:]) for part in self.parts]
                    return jnp.concatenate([pick(part, 1, side) for part in parts], 2)
                shape = (owners // 2, 2, self.rows, -1)
                first, second = self.part.reshape(shape), self.got.reshape(shape)
                return pick(first, 1, side) + pick(second, 1, side).astype(f32)

            away = half(1 - mine).astype(low_type)
            self.part = half(mine)
            self.pending = swap(away, axis, 1)

    def absorb(self, got):
        self.pending = None
        self.step += 1
        if self.step < 3:
            self.got = got
        elif self.step == 3:
            self.part = jnp.sum(got.astype(f32), 0)
            self.square = jnp.sum(self.part * self.part)
        else:
            first = lax.axis_index("seq") == 0
            part = self.part
            self.value = jnp.concatenate(
                [jnp.where(first, part, got), jnp.where(first, got, part)], 0
            )

    def finish(self):
        if not self.fast:
            whole = jnp.concatenate(self.parts, 2)
            part = lax.psum(lax.psum_scatter(whole, "dp", scatter_dimension=0), "seq")
            self.value = part
            self.square = jnp.where(lax.axis_index("seq") == 0, jnp.sum(part * part), 0.0)


class TableChain(Chain):
    def __init__(self, keep, away):
        self.part, self.got = keep, None
        self.rows, self.bit = keep.shape[1], 2
        self.pending = swap(away, "dp", 1)

    def launch(self):
        if self.bit == lax.axis_size("dp"):
            return
        mine = (lax.axis_index("dp") // self.bit) & 1
        shape = (-1, 2, self.rows, self.part.shape[2])
        first, second = self.part.reshape(shape), self.got.reshape(shape)

        def half(side):
            return pick(first, 1, side) + pick(second, 1, side).astype(f32)

        away = half(1 - mine).astype(low_type)
        self.part = half(mine)
        self.pending = swap(away, "dp", self.bit)
        self.bit *= 2

    def absorb(self, got):
        self.pending, self.got = None, got
        if self.bit == lax.axis_size("dp"):
            self.value = (self.part + got.astype(f32)).reshape(self.rows, -1)


def advance(main, chains):
    live = [chain for chain in chains if chain.pending is not None]
    main, got = lax.optimization_barrier((main, [chain.pending for chain in live]))
    for chain, arrived in zip(live, got):
        chain.absorb(arrived)
        chain.launch()
    return main


def adam_update(weight, first, second, grad, rate):
    first = beta_one * first + (1 - beta_one) * grad
    second = beta_two * second + (1 - beta_two) * grad * grad
    first_hat = first / (1 - beta_one**STEP)
    second_hat = second / (1 - beta_two**STEP)
    weight = weight - rate * (first_hat / (jnp.sqrt(second_hat) + adam_eps) + weight_decay * weight)
    return (weight, first, second)


def place_spans(starts, places):
    covered = places[:, None] >= starts[None, :]
    number = jnp.sum(covered.astype(jnp.int32), -1) - 1
    return number, jnp.max(jnp.where(covered, starts[None, :], 0), -1)


def key_spans(number, starts, lengths, block):
    hot = number[:, None] == jnp.arange(starts.shape[0])[None, :]
    first = jnp.sum(jnp.where(hot, starts[None, :], 0), -1)
    last = jnp.sum(jnp.where(hot, (starts + lengths)[None, :], 0), -1)
    first_block = jnp.min(first.reshape(-1, block), -1) // key_block
    last_block = (jnp.max(last.reshape(-1, block), -1) + key_block - 1) // key_block
    return (
        jnp.stack([first, last]).astype(jnp.int32),
        jnp.stack([first_block, last_block]).astype(jnp.int32),
    )


def on_device(
    src_ids,
    tgt_ids,
    src_lengths,
    tgt_lengths,
    tgt_mask,
    attn_in,
    attn_in_m1,
    attn_in_m2,
    attn_out,
    attn_out_m1,
    attn_out_m2,
    ffn_in,
    ffn_in_m1,
    ffn_in_m2,
    ffn_out,
    ffn_out_m1,
    ffn_out_m2,
    len_head,
    len_head_m1,
    len_head_m2,
    norms,
    norms_m1,
    norms_m2,
    table,
    table_m1,
    table_m2,
):
    rows_here, seq_rows = src_ids.shape
    seqs, owners = lax.axis_size("seq"), lax.axis_size("dp")
    devices = seqs * owners
    row_len = seq_rows * seqs
    side = lax.axis_index("seq")
    group = seqs // rows_here
    span = row_len // group
    row, offset = side // group, (side % group) * span
    sharers = [[r * group + i for i in range(group)] for r in range(rows_here)]
    own_words, width = table.shape
    classes = len_head.shape[1]
    vocab_width = own_words * owners
    vocab_base = side * vocab_width
    norm_count = norms.shape[1]
    norm_columns = 128

    def columns_of(weight, rows):
        return [weight[at : at + rows] for at in range(0, weight.shape[0], rows)]

    def cut_parts(whole, parts):
        result, at = [], 0
        for part in parts:
            result.append(whole[:, at : at + part.shape[1]])
            at += part.shape[1]
        return result

    def gather_columns(parts):
        joined = jnp.concatenate([part.astype(low_type) for part in parts], 1)
        if joined.shape[0] % (16 * seqs) == 0:
            rows = joined.shape[0] // seqs
            joined = lax.dynamic_slice_in_dim(joined, side * rows, rows, 0)
            whole = lax.all_gather(joined, ("dp", "seq"), axis=0, tiled=True)
        else:
            whole = lax.all_gather(joined, "dp", axis=0, tiled=True)
        return cut_parts(whole, parts)

    def gather_by_swaps(parts, after):
        if seqs != 2 or share % 32 or not power_of_two(owners):
            return gather_columns(parts)
        joined = jnp.concatenate([part.astype(low_type) for part in parts], 1)
        rows = share // 2
        part = lax.dynamic_slice_in_dim(joined, side * rows, rows, 0)
        part = lax.optimization_barrier((part, after))[0]
        bits = []
        bit = owners // 2
        while bit > 1:
            bits.append(bit)
            bit //= 2
        index = lax.axis_index("dp")
        steps = [("dp", bit, at) for at, bit in enumerate(bits)]
        steps += [("seq", 1, len(bits)), ("dp", 1, len(bits))]
        for axis, bit, at in steps:
            other = swap(part, axis, bit)
            first = (lax.axis_index(axis) // bit) & 1 == 0
            part = jnp.stack([jnp.where(first, part, other), jnp.where(first, other, part)], at)
        return cut_parts(part.reshape(-1, part.shape[-1]), parts)

    def join_rows(pieces):
        blocks = [piece.reshape(owners, -1, piece.shape[1]) for piece in pieces]
        return jnp.concatenate(blocks, 1).reshape(-1, pieces[0].shape[1])

    share = attn_in.shape[1]
    norm_part = jnp.pad(
        norms.reshape(-1, norms.shape[2]).T, ((0, 0), (0, norm_columns - 2 * norm_count))
    )
    first_parts = [attn_in[0], attn_out[0], len_head, norm_part, ffn_in[0]]
    first_parts += columns_of(ffn_out[0], share)
    w_in0, w_out0, w_len, norm_low, f_in0, *f_out0 = gather_columns(first_parts)
    next_parts = [attn_in[1], attn_out[1], attn_in[2], attn_out[2], ffn_in[1]]
    next_parts += columns_of(ffn_out[1], share)
    f_out0 = join_rows(f_out0)
    table_low = table.astype(low_type)
    table_part = lax.all_gather(table_low, "dp", axis=0, tiled=True)
    norm_low = norm_low[:, : 2 * norm_count].T.astype(f32)
    gains, biases = norm_low[:norm_count], norm_low[norm_count:]

    ids = gather_seq(jnp.stack([src_ids, tgt_ids, tgt_mask]), 2).reshape(3, rows_here, row_len)
    src_starts = jnp.cumsum(src_lengths, -1) - src_lengths
    tgt_starts = jnp.cumsum(tgt_lengths, -1) - tgt_lengths
    places = jnp.arange(row_len)
    opens = jnp.any(places[None, :, None] == src_starts[:, None, :], -1)
    src_in = pick(jnp.where(opens, length_token, ids[0]).reshape(seqs, span), 0, side)
    masked = (ids[2] == 1).reshape(seqs, span)
    labels = ids[1].reshape(seqs, span)
    dec_in = pick(jnp.where(masked, mask_token, labels), 0, side)
    counts = jnp.sum(masked.astype(jnp.int32), -1)

    def slots_for(expected):
        return max(-(-expected // 16) * 16, 16)

    src_slots, dec_slots = slots_for(2 * span // devices), slots_for(3 * span // (2 * devices))

    def ask(token_ids, slots):
        same = token_ids[:, None] == token_ids[None, :]
        index = jnp.arange(span)
        earlier = index[None, :] < index[:, None]
        leader = jnp.logical_not(jnp.any(same & earlier, 1))
        holder = token_ids // own_words
        rank = jnp.sum(
            (earlier & leader[None, :] & (holder[:, None] == holder[None, :])).astype(jnp.int32), 1
        )
        rank = jnp.sum(jnp.where(same & leader[None, :], rank[None, :], 0), 1)
        return token_ids % own_words, holder, rank, slots

    def chosen_of(asked, turn):
        local, holder, rank, slots = asked
        code = jnp.where(rank // slots == turn, holder * slots + rank % slots, -1)
        return code[:, None] == jnp.arange(devices * slots)[None, :]

    def wanted_of(asked, chosen):
        return jnp.max(jnp.where(chosen, asked[0][:, None], -1), 0).reshape(devices, -1)

    def maps_of(chosen, wanted):
        held = wanted.reshape(-1)[:, None] == jnp.arange(own_words)[None, :]
        return chosen.astype(low_type), held.astype(low_type)

    def round_of(asked, turn):
        chosen = chosen_of(asked, turn)
        return maps_of(chosen, to_each(wanted_of(asked, chosen)))

    def send_rows(held):
        found = contract(held, table_low, 1, 0).astype(low_type)
        return to_each(found.reshape(devices, -1, width)).reshape(-1, width)

    def fetch(maps):
        chosen, held = maps
        return contract(send_rows(held), chosen, 0, 1)

    def give_rows(chosen, grads):
        sums = contract(chosen, grads.astype(low_type), 0, 1).astype(low_type)
        return to_each(sums.reshape(devices, -1, width)).reshape(-1, width)

    def give(maps, grads):
        return contract(maps[1], give_rows(maps[0], grads), 0, 0)

    def later_rounds(rounds, value, visit):
        return lax.fori_loop(1, rounds, lambda turn, carry: carry + visit(turn), value)

    src_ask, dec_ask = ask(src_in, src_slots), ask(dec_in, dec_slots)
    src_chosen, dec_chosen = chosen_of(src_ask, 0), chosen_of(dec_ask, 0)
    facts = jnp.stack(
        [
            jnp.sum(tgt_mask),
            jnp.max(counts),
            jnp.max(src_ask[2]) // src_slots + 1,
            jnp.max(dec_ask[2]) // dec_slots + 1,
        ]
    )
    facts = jnp.broadcast_to(jnp.pad(facts, (0, 12))[None, :], (devices, 16))
    asked = [wanted_of(src_ask, src_chosen), wanted_of(dec_ask, dec_chosen), facts]
    asked = to_each(jnp.concatenate(asked, 1).astype(jnp.int32))
    facts = asked[:, src_slots + dec_slots :]
    w_in1, w_out1, w_in2, w_out2, f_in1, *f_out1 = gather_by_swaps(next_parts, asked)
    f_out1 = join_rows(f_out1)
    count = jnp.sum(facts[:, 0]).astype(f32)
    cut = -(-(span * 3 // 8) // 128) * 128
    more = jnp.max(facts[:, 1]) > cut
    src_rounds, dec_rounds = jnp.max(facts[:, 2]), jnp.max(facts[:, 3])
    src_maps = maps_of(src_chosen, asked[:, :src_slots])
    src_found = fetch(src_maps)
    dec_maps = maps_of(dec_chosen, asked[:, src_slots : src_slots + dec_slots])
    dec_rows = send_rows(dec_maps[1])

    starts_at = jnp.cumsum(counts) - counts
    total = jnp.sum(counts)
    rank = jnp.where(masked, jnp.cumsum(masked.astype(jnp.int32), -1) - 1, -1)
    slot_of = jnp.where(masked, rank + starts_at[:, None], -1)
    slot_index = jnp.arange(seqs * span)
    slot_label = jnp.sum(
        jnp.where(slot_of.reshape(1, -1) == slot_index[:, None], labels.reshape(1, -1), 0), -1
    )
    valid = slot_index < total
    targets = jnp.where(valid, slot_label - vocab_base, -1).reshape(1, -1)
    plan = jnp.concatenate([chunk_plan(total), lax.axis_index("dp")[None] & 1]).astype(jnp.int32)
    own_rank, own_slot = pick(rank, 0, side), pick(slot_of, 0, side)

    def packing(slots, rows):
        slot, index = jnp.arange(slots), jnp.arange(rows)
        far_start, far_count = pick(starts_at, 0, 1 - side), pick(counts, 0, 1 - side)
        far = jnp.where(index < far_count, index + far_start, -1)
        return (
            (own_rank[None, :] == index[:, None]).astype(low_type),
            (own_slot[None, :] == slot[:, None]).astype(low_type),
            (far[None, :] == slot[:, None]).astype(low_type),
        )

    own_places = offset + jnp.arange(span)
    src_start, src_length = pick(src_starts, 0, row), pick(src_lengths, 0, row)
    tgt_start, tgt_length = pick(tgt_starts, 0, row), pick(tgt_lengths, 0, row)
    src_number, src_open = place_spans(src_start, own_places)
    tgt_number, tgt_open = place_spans(tgt_start, own_places)
    block = min(query_block, span)
    enc_spans = key_spans(src_number, src_start, src_length, block)
    self_spans = key_spans(tgt_number, tgt_start, tgt_length, block)
    cross_spans = key_spans(tgt_number, src_start, src_length, block)
    src_wave, tgt_wave = lax.optimization_barrier(
        (sinusoid(own_places - src_open, width), sinusoid(own_places - tgt_open, width))
    )

    root = math.sqrt(width)
    src_found = later_rounds(src_rounds, src_found, lambda turn: fetch(round_of(src_ask, turn)))
    stream0 = src_found * root + src_wave

    def norm(stream, index):
        return layer_norm(stream, gains[index], biases[index])

    def keys_of_row(part):
        if group == 1:
            return part
        return lax.all_gather(part, "seq", axis=1, tiled=True, axis_index_groups=sharers)

    def keys_to_place(part):
        if group == 1:
            return part
        return lax.psum_scatter(
            part, "seq", scatter_dimension=1, tiled=True, axis_index_groups=sharers
        )

    def self_attention(inner, weight_in, weight_out, spans):
        triple = contract(weight_in, inner, 0, 0).astype(low_type)
        keys = triple if group == 1 else keys_of_row(triple[width:])
        mixed, lse = attend_forward(triple, keys, group == 1, *spans)
        return contract(weight_out, mixed, 0, 0), (triple, keys, mixed, lse)

    def self_attention_back(inner, weight_in, weight_out, spans, kept, grad):
        triple, keys, mixed, lse = kept
        grad_low = grad.astype(low_type)
        d_out = contract(mixed, grad_low, 1, 1)
        d_mixed = contract(weight_out, grad_low, 1, 0).astype(low_type)
        d_query, d_keys = attend_backward(triple, keys, group == 1, *spans, lse, d_mixed)
        d_triple = jnp.concatenate([d_query, keys_to_place(d_keys)], 0)
        return contract(weight_in, d_triple, 1, 0), contract(inner, d_triple, 1, 1), d_out

    def cross_attention(inner, memory, weight_in, weight_out, spans):
        queries = contract(weight_in[:, :width], inner, 0, 0).astype(low_type)
        keys = keys_of_row(contract(weight_in[:, width:], memory, 0, 0).astype(low_type))
        mixed, lse = attend_forward(queries, keys, False, *spans)
        return contract(weight_out, mixed, 0, 0), (queries, keys, mixed, lse)

    def cross_attention_back(inner, memory, weight_in, weight_out, spans, kept, grad):
        queries, keys, mixed, lse = kept
        grad_low = grad.astype(low_type)
        d_out = contract(mixed, grad_low, 1, 1)
        d_mixed = contract(weight_out, grad_low, 1, 0).astype(low_type)
        d_query, d_keys = attend_backward(queries, keys, False, *spans, lse, d_mixed)
        d_keys = keys_to_place(d_keys)
        d_in = jnp.concatenate([contract(inner, d_query, 1, 1), contract(memory, d_keys, 1, 1)], 1)
        return (
            contract(weight_in[:, :width], d_query, 1, 0),
            contract(weight_in[:, width:], d_keys, 1, 0),
            d_in,
            d_out,
        )

    def ffn(inner, weight_one, weight_two):
        hidden = contract(weight_one, inner, 0, 0)
        active = jax.nn.gelu(hidden).astype(low_type)
        return contract(weight_two, active, 0, 0), (hidden, active)

    def ffn_back(inner, weight_one, weight_two, kept, grad):
        hidden, active = kept
        grad_low = grad.astype(low_type)
        d_two = contract(active, grad_low, 1, 1)
        d_active = contract(weight_two, grad_low, 1, 0)
        d_hidden = jax.vjp(jax.nn.gelu, hidden)[1](d_active)[0].astype(low_type)
        return contract(weight_one, d_hidden, 1, 0), contract(inner, d_hidden, 1, 1), d_two

    inner0 = norm(stream0, 0).astype(low_type)
    branch0, keep0 = self_attention(inner0, w_in0, w_out0, enc_spans)
    stream1 = stream0 + branch0
    inner1 = norm(stream1, 1).astype(low_type)
    branch1, keep1 = ffn(inner1, f_in0, f_out0)
    stream2 = stream1 + branch1
    memory = norm(stream2, 2).astype(low_type)
    memory, dec_chosen = lax.optimization_barrier((memory, dec_maps[0]))
    dec_found = contract(dec_rows, dec_chosen, 0, 1)
    dec_found = later_rounds(dec_rounds, dec_found, lambda turn: fetch(round_of(dec_ask, turn)))
    target0 = dec_found * root + tgt_wave
    inner3 = norm(target0, 3).astype(low_type)
    branch3, keep3 = self_attention(inner3, w_in1, w_out1, self_spans)
    target1 = target0 + branch3
    inner4 = norm(target1, 4).astype(low_type)
    branch4, keep4 = cross_attention(inner4, memory, w_in2, w_out2, cross_spans)
    target2 = target1 + branch4
    inner5 = norm(target2, 5).astype(low_type)
    branch5, keep5 = ffn(inner5, f_in1, f_out1)
    target3 = target2 + branch5
    final = norm(target3, 6).astype(low_type)

    def pack(slots, rows):
        own_chosen, own_slots, far_slots = packing(slots, rows)
        far = swap(contract(own_chosen, final, 1, 1).astype(low_type), "seq", 1)
        packed = contract(own_slots, final, 1, 1) + contract(far_slots, far, 1, 0)
        return jnp.pad(packed.astype(low_type), ((0, seqs * span - slots), (0, 0)))

    def unpack(slots, rows):
        own_chosen, own_slots, far_slots = packing(slots, rows)
        high = lax.reduce_precision(d_pieces[:slots], 8, 7)
        rest = (d_pieces[:slots] - high).astype(low_type)
        high = high.astype(low_type)
        far = swap(contract(far_slots, high, 0, 0).astype(low_type), "seq", 1)
        return (
            contract(high, own_slots, 0, 0)
            + contract(rest, own_slots, 0, 0)
            + contract(far, own_chosen, 0, 0)
        )

    if seqs == 2:
        pieces = lax.cond(
            more, lambda: pack(2 * span, span), lambda: pack(min(2 * cut, 2 * span), cut)
        )
    else:
        own_slots = packing(seqs * span, span)[1]
        pieces = lax.psum(contract(own_slots, final, 1, 1), "seq").astype(low_type)
    turned = pieces.T
    every = gather_seq(head_stats(plan, table_part, turned), 0)
    top_logit = jnp.max(every[:, 0], 0)
    totals = jnp.sum(every[:, 1] * jnp.exp(every[:, 0] - top_logit[None]), 0)
    log_total = top_logit + jnp.log(jnp.where(valid, totals, 1.0))
    own_start = pick(starts_at, 0, side)
    mine = (slot_index >= own_start) & (slot_index < own_start + pick(counts, 0, side))
    token_local = jnp.sum(jnp.where(mine, log_total, 0.0))
    logs = jnp.where(valid, log_total + jnp.log(count), 1e30)
    weights = jnp.where(valid, 1.0 / count, 0.0)
    split = halving_fits(own_words, width, False)
    *d_table, d_pieces, picks = head_back(
        plan, table_part, pieces, turned, targets, logs[None], weights[None], split and own_words
    )
    token_local = token_local - jnp.sum(picks)
    table_chain = [TableChain(*d_table)] if split else []
    if seqs == 2:
        d_final = lax.cond(
            more, lambda: unpack(2 * span, span), lambda: unpack(min(2 * cut, 2 * span), cut)
        )
    else:
        d_pieces = lax.psum(d_pieces, "seq")
        high = lax.reduce_precision(d_pieces, 8, 7)
        rest = (d_pieces - high).astype(low_type)
        d_final = contract(high.astype(low_type), own_slots, 0, 0) + contract(rest, own_slots, 0, 0)

    first_place = own_places[None, :] == src_start[:, None]
    mine = jnp.any(first_place, -1)
    first_rows = contract(first_place.astype(low_type), memory, 1, 1).astype(low_type)
    len_logits = contract(first_rows, w_len, 1, 0)
    len_label = jnp.minimum(tgt_length, classes - 1)
    len_hot = jnp.arange(classes)[None, :] == len_label[:, None]
    len_loss = jax.nn.logsumexp(len_logits, -1) - jnp.sum(jnp.where(len_hot, len_logits, 0.0), -1)
    len_local = jnp.sum(jnp.where(mine, len_loss, 0.0))
    sentences = rows_here * src_lengths.shape[1] * owners
    len_prob = jax.nn.softmax(len_logits, -1)
    d_len_logits = (
        jnp.where(mine[:, None], len_prob - len_hot.astype(f32), 0.0) * (0.1 / sentences)
    ).astype(low_type)
    d_w_len = contract(first_rows, d_len_logits, 0, 0)
    d_first = contract(d_len_logits, w_len, 1, 1)
    d_memory = lax.dot_general(
        d_first,
        first_place.astype(f32),
        (((0,), (0,)), ((), ())),
        precision=lax.Precision.HIGHEST,
        preferred_element_type=f32,
    )

    def owned(grad):
        return grad.reshape(owners, -1, grad.shape[1])

    def owned_columns(grad):
        whole = owned(grad)
        return [whole[:, at : at + share] for at in range(0, whole.shape[1], share)]

    none = jnp.zeros_like(stream0)
    d_target3, scale6 = norm_backward(target3, gains[6], d_final, none)
    d_inner5, d_fin1, d_fout1 = ffn_back(inner5, f_in1, f_out1, keep5, d_target3)
    d_inner5, d_target3 = advance((d_inner5, d_target3), table_chain)
    d_target2, scale5 = norm_backward(target2, gains[5], d_inner5, d_target3)
    d_inner4, d_cross, d_win2, d_wout2 = cross_attention_back(
        inner4, memory, w_in2, w_out2, cross_spans, keep4, d_target2
    )
    chain_one = LayerChain([owned(d_fin1)] + owned_columns(d_fout1) + [owned(d_win2), owned(d_wout2)])
    d_target1, scale4 = norm_backward(target1, gains[4], d_inner4, d_target2)
    d_inner3, d_win1, d_wout1 = self_attention_back(
        inner3, w_in1, w_out1, self_spans, keep3, d_target1
    )
    chains = table_chain + [chain_one]
    d_inner3, d_target1, d_cross = advance((d_inner3, d_target1, d_cross), chains)
    d_target0, scale3 = norm_backward(target0, gains[3], d_inner3, d_target1)
    dec_grad = d_target0 * root
    dec_sums = give_rows(dec_maps[0], dec_grad)
    d_stream2, scale2 = norm_backward(stream2, gains[2], d_memory + d_cross, none)
    d_inner1, d_fin0, d_fout0 = ffn_back(inner1, f_in0, f_out0, keep1, d_stream2)
    d_inner1, d_stream2 = advance((d_inner1, d_stream2), chains)
    chain_two = LayerChain([owned(d_win1), owned(d_wout1), owned(d_fin0)] + owned_columns(d_fout0))
    d_stream1, scale1 = norm_backward(stream1, gains[1], d_inner1, d_stream2)
    d_inner0, d_win0, d_wout0 = self_attention_back(
        inner0, w_in0, w_out0, enc_spans, keep0, d_stream1
    )
    chains += [chain_two]
    d_inner0, d_stream1, dec_sums = advance((d_inner0, d_stream1, dec_sums), chains)
    d_stream0, scale0 = norm_backward(stream0, gains[0], d_inner0, d_stream1)
    src_grad = d_stream0 * root
    src_sums = give_rows(src_maps[0], src_grad)
    chain_three = LayerChain([owned(d_win0), owned(d_wout0), owned(d_w_len)])
    norm_share = norms.shape[2]
    scales = jnp.sum(jnp.stack([scale0, scale1, scale2, scale3, scale4, scale5, scale6], 1), 3)
    scales = scales.reshape(2 * norm_count, owners, norm_share).transpose(1, 0, 2)
    scales = jnp.broadcast_to(scales[None], (seqs,) + scales.shape)
    scales = to_each(scales.reshape((devices,) + scales.shape[2:]))
    chains += [chain_three]
    advance((), chains)
    src_sums, scales = advance((src_sums, scales), chains)
    while any(chain.pending is not None for chain in chains):
        advance((), chains)
    layer_chains = [chain_one, chain_two, chain_three]
    for chain in layer_chains:
        chain.finish()

    g_norms = jnp.sum(scales, 0)
    norm_square = jnp.where(side == 0, jnp.sum(g_norms * g_norms), 0.0)
    given = contract(dec_maps[1], dec_sums, 0, 0) + contract(src_maps[1], src_sums, 0, 0)
    given = later_rounds(
        jnp.maximum(src_rounds, dec_rounds),
        given,
        lambda turn: give(round_of(dec_ask, turn), dec_grad)
        + give(round_of(src_ask, turn), src_grad),
    )
    if split:
        table_grad = table_chain[0].value
    else:
        table_grad = lax.psum_scatter(d_table[0], "dp", scatter_dimension=0, tiled=True)
    table_grad = table_grad + given
    square = sum(chain.square for chain in layer_chains)
    square = square + jnp.sum(table_grad * table_grad) + norm_square
    sums = jnp.pad(jnp.stack([token_local, len_local, square]), (0, 5))
    sums = jnp.sum(to_each(jnp.broadcast_to(sums[None], (devices, 8))), 0)
    token_sum, len_sum, grad_norm = sums[0], sums[1], jnp.sqrt(sums[2])
    factor = jnp.minimum(1.0, clip_limit / (grad_norm + 1e-06))

    def cut_columns(chain, sizes):
        result, at = [], 0
        value = chain.value.reshape(share, -1)
        for size in sizes:
            result.append(value[:, at : at + size])
            at += size
        return result

    hidden_width = ffn_in.shape[2]
    pieces_out = ffn_out.shape[1] // share
    ffn_sizes = [hidden_width] + [width] * pieces_out
    attn_sizes = [3 * width, width]
    g_fin1, *g_fout1, g_win2, g_wout2 = cut_columns(chain_one, ffn_sizes + attn_sizes)
    g_win1, g_wout1, g_fin0, *g_fout0 = cut_columns(chain_two, attn_sizes + ffn_sizes)
    g_win0, g_wout0, g_len = cut_columns(chain_three, attn_sizes + [classes])
    grads = (
        jnp.stack([g_win0, g_win1, g_win2]),
        jnp.stack([g_wout0, g_wout1, g_wout2]),
        jnp.stack([g_fin0, g_fin1]),
        jnp.stack([jnp.concatenate(g_fout0, 0), jnp.concatenate(g_fout1, 0)]),
        g_len,
        g_norms.reshape(norms.shape),
        table_grad,
    )
    masters = (attn_in, attn_out, ffn_in, ffn_out, len_head, norms, table)
    firsts = (attn_in_m1, attn_out_m1, ffn_in_m1, ffn_out_m1, len_head_m1, norms_m1, table_m1)
    seconds = (attn_in_m2, attn_out_m2, ffn_in_m2, ffn_out_m2, len_head_m2, norms_m2, table_m2)
    updates = []
    for weight, first, second, grad, rate in zip(masters, firsts, seconds, grads, step_rates):
        updates.extend(adam_update(weight, first, second, grad * factor, rate))
    return (token_sum, count, len_sum, grad_norm, *updates)


def solution(mesh):
    layer, head, scales, words = P(None, "dp", None), P("dp", None), P(None, None, "dp"), P(("seq", "dp"), None)
    owned = (layer,) * 12 + (head,) * 3 + (scales,) * 3 + (words,) * 3
    ids, lengths = P("dp", "seq"), P("dp", None)
    in_specs = (ids, ids, lengths, lengths, ids) + owned
    out_specs = (P(), P(), P(), P()) + owned
    return jax.shard_map(
        on_device, mesh=mesh, in_specs=in_specs, out_specs=out_specs, check_vma=False
    )
```

```python
import functools
import math

import jax
import jax.numpy as jnp
from jax import lax
from jax.experimental import pallas as pl
from jax.experimental.pallas import tpu as pltpu
from jax.sharding import PartitionSpec as P

HEADS = 8
STEP = 10


length_token = 1
mask_token = 2
clip_limit = 0.002
beta_one = 0.9
beta_two = 0.98
adam_eps = 1e-08
weight_decay = 0.01
step_rates = (0.05, 0.25, 0.05, 0.025, 0.05, 0.5, 0.1)

low_type = jnp.bfloat16
f32 = jnp.float32
query_block = 256
key_block = 128
place_block = 512
vmem_bytes = 56 * 1024 * 1024


def sinusoid(positions, width):
    half_width = width // 2
    frequency = jnp.exp(jnp.arange(half_width).astype(f32) * (-math.log(10000.0) / half_width))
    angles = frequency[:, None] * positions.astype(f32)[None, :]
    return jnp.concatenate([jnp.sin(angles), jnp.cos(angles)], 0)


def layer_norm(stream, norm_gain, norm_bias):
    average = jnp.mean(stream, 0, keepdims=True)
    centred = stream - average
    variance = jnp.mean(centred * centred, 0, keepdims=True)
    return centred * lax.rsqrt(variance + 1e-05) * norm_gain[:, None] + norm_bias[:, None]


def contract(left, right, left_dim, right_dim):
    return lax.dot_general(
        left, right, (((left_dim,), (right_dim,)), ((), ())), preferred_element_type=f32
    )


def attend_forward_kernel(bounds, q_ref, k_ref, v_ref, span_ref, out_ref, lse_ref, hold, *, head):
    step = pl.program_id(0)
    first, last = bounds[0, step], bounds[1, step]
    width, queries = q_ref.shape
    heads = width // head
    scale = head**-0.5
    low, high = span_ref[0:1, :], span_ref[1:2, :]
    inner = lax.broadcasted_iota(jnp.int32, (key_block, queries), 0)

    def fold(values, op):
        return op(values.reshape(key_block // 8, 8, queries), axis=0)

    def score(block, tops):
        start = pl.multiple_of(block * key_block, key_block)
        place = inner + start
        allowed = (place >= low) & (place < high)
        result = []
        for h in range(heads):
            rows = slice(h * head, (h + 1) * head)
            s = contract(k_ref[rows, pl.ds(start, key_block)], q_ref[rows, :], 0, 0) * scale
            s = jnp.where(allowed, s, -1e30)
            hold[h, pl.ds(start, key_block), :] = s
            result.append(jnp.maximum(tops[h], fold(s, jnp.max)))
        return tuple(result)

    tops = lax.fori_loop(
        first, last, score, tuple(jnp.full((8, queries), -1e30, f32) for _ in range(heads))
    )
    tops = [jnp.max(t, axis=0, keepdims=True) for t in tops]

    def power(block, sums):
        start = pl.multiple_of(block * key_block, key_block)
        result = []
        for h in range(heads):
            e = jnp.exp(hold[h, pl.ds(start, key_block), :] - tops[h])
            hold[h, pl.ds(start, key_block), :] = e
            result.append(sums[h] + fold(e, jnp.sum))
        return tuple(result)

    sums = lax.fori_loop(
        first, last, power, tuple(jnp.zeros((8, queries), f32) for _ in range(heads))
    )
    sums = [jnp.maximum(jnp.sum(t, axis=0, keepdims=True), 1e-30) for t in sums]
    inverse = [1.0 / t for t in sums]

    def mix(block, outs):
        start = pl.multiple_of(block * key_block, key_block)
        result = []
        for h in range(heads):
            rows = slice(h * head, (h + 1) * head)
            p = (hold[h, pl.ds(start, key_block), :] * inverse[h]).astype(low_type)
            result.append(outs[h] + contract(v_ref[rows, pl.ds(start, key_block)], p, 1, 0))
        return tuple(result)

    outs = lax.fori_loop(
        first, last, mix, tuple(jnp.zeros((head, queries), f32) for _ in range(heads))
    )
    for h in range(heads):
        out_ref[h * head : (h + 1) * head, :] = outs[h].astype(low_type)
        lse_ref[h : h + 1, :] = tops[h] + jnp.log(sums[h])


def attend_backward_kernel(
    bounds, q_ref, k_ref, v_ref, span_ref, lse_ref, do_ref, dq_ref, dkv_ref, p_hold, d_hold, acc,
    *, head
):
    step = pl.program_id(0)
    first, last = bounds[0, step], bounds[1, step]
    width, queries = q_ref.shape
    heads = width // head
    scale = head**-0.5
    low, high = span_ref[0:1, :], span_ref[1:2, :]
    inner = lax.broadcasted_iota(jnp.int32, (key_block, queries), 0)

    @pl.when(step == 0)
    def _():
        acc[...] = jnp.zeros_like(acc)

    def one(block, deltas):
        start = pl.multiple_of(block * key_block, key_block)
        keys = pl.ds(start, key_block)
        place = inner + start
        allowed = (place >= low) & (place < high)
        result = []
        for h in range(heads):
            rows = slice(h * head, (h + 1) * head)
            s = contract(k_ref[rows, keys], q_ref[rows, :], 0, 0) * scale
            p = jnp.exp(jnp.where(allowed, s, -1e30) - lse_ref[h : h + 1, :])
            dp = contract(v_ref[rows, keys], do_ref[rows, :], 0, 0)
            p_hold[h, keys, :] = p
            d_hold[h, keys, :] = dp
            result.append(
                deltas[h] + jnp.sum((p * dp).reshape(key_block // 8, 8, queries), axis=0)
            )
            below = slice(width + h * head, width + (h + 1) * head)
            acc[below, keys] += contract(do_ref[rows, :], p.astype(low_type), 1, 1)
        return tuple(result)

    deltas = lax.fori_loop(
        first, last, one, tuple(jnp.zeros((8, queries), f32) for _ in range(heads))
    )
    deltas = [jnp.sum(t, axis=0, keepdims=True) for t in deltas]

    def two(block, outs):
        start = pl.multiple_of(block * key_block, key_block)
        keys = pl.ds(start, key_block)
        result = []
        for h in range(heads):
            rows = slice(h * head, (h + 1) * head)
            ds = (p_hold[h, keys, :] * (d_hold[h, keys, :] - deltas[h])).astype(low_type)
            result.append(outs[h] + contract(k_ref[rows, keys], ds, 1, 0))
            acc[rows, keys] += contract(q_ref[rows, :], ds, 1, 1) * scale
        return tuple(result)

    outs = lax.fori_loop(
        first, last, two, tuple(jnp.zeros((head, queries), f32) for _ in range(heads))
    )
    for h in range(heads):
        dq_ref[h * head : (h + 1) * head, :] = (outs[h] * scale).astype(low_type)

    @pl.when(step == pl.num_programs(0) - 1)
    def _():
        dkv_ref[...] = acc[...].astype(low_type)


def attend_specs(width, length, block, shared):
    key_row = 1 if shared else 0
    return [
        pl.BlockSpec((width, block), lambda i, *_: (0, i)),
        pl.BlockSpec((width, length), lambda i, *_: (key_row, 0)),
        pl.BlockSpec((width, length), lambda i, *_: (key_row + 1, 0)),
        pl.BlockSpec((2, block), lambda i, *_: (0, i)),
    ]


def attend_forward(queries, keys, shared, spans, bounds):
    width = keys.shape[0] // (3 if shared else 2)
    places, length = queries.shape[1], keys.shape[1]
    block = min(query_block, places)
    return pl.pallas_call(
        functools.partial(attend_forward_kernel, head=width // HEADS),
        grid_spec=pltpu.PrefetchScalarGridSpec(
            num_scalar_prefetch=1,
            grid=(places // block,),
            in_specs=attend_specs(width, length, block, shared),
            out_specs=[
                pl.BlockSpec((width, block), lambda i, *_: (0, i)),
                pl.BlockSpec((HEADS, block), lambda i, *_: (0, i)),
            ],
            scratch_shapes=[pltpu.VMEM((HEADS, length, block), f32)],
        ),
        out_shape=[
            jax.ShapeDtypeStruct((width, places), low_type),
            jax.ShapeDtypeStruct((HEADS, places), f32),
        ],
        compiler_params=pltpu.CompilerParams(vmem_limit_bytes=vmem_bytes),
        name="attend_forward",
    )(bounds, queries, keys, keys, spans)


def attend_backward(queries, keys, shared, spans, bounds, lse, d_mixed):
    width = keys.shape[0] // (3 if shared else 2)
    places, length = queries.shape[1], keys.shape[1]
    block = min(query_block, places)
    return pl.pallas_call(
        functools.partial(attend_backward_kernel, head=width // HEADS),
        grid_spec=pltpu.PrefetchScalarGridSpec(
            num_scalar_prefetch=1,
            grid=(places // block,),
            in_specs=attend_specs(width, length, block, shared)
            + [
                pl.BlockSpec((HEADS, block), lambda i, *_: (0, i)),
                pl.BlockSpec((width, block), lambda i, *_: (0, i)),
            ],
            out_specs=[
                pl.BlockSpec((width, block), lambda i, *_: (0, i)),
                pl.BlockSpec((2 * width, length), lambda i, *_: (0, 0)),
            ],
            scratch_shapes=[
                pltpu.VMEM((HEADS, length, block), f32),
                pltpu.VMEM((HEADS, length, block), f32),
                pltpu.VMEM((2 * width, length), f32),
            ],
        ),
        out_shape=[
            jax.ShapeDtypeStruct((width, places), low_type),
            jax.ShapeDtypeStruct((2 * width, length), low_type),
        ],
        compiler_params=pltpu.CompilerParams(vmem_limit_bytes=vmem_bytes),
        name="attend_backward",
    )(bounds, queries, keys, keys, spans, lse, d_mixed)


def norm_back_kernel(stream_ref, gain_ref, grad_ref, rest_ref, out_ref, sums_ref):
    @pl.when(pl.program_id(0) == 0)
    def _():
        sums_ref[...] = jnp.zeros_like(sums_ref)

    stream, grad = stream_ref[...], grad_ref[...]
    width, places = stream.shape
    average = jnp.mean(stream, 0, keepdims=True)
    centred = stream - average
    variance = jnp.mean(centred * centred, 0, keepdims=True)
    inverse = lax.rsqrt(variance + 1e-05)
    unit = centred * inverse
    scaled = grad * gain_ref[...]
    along = jnp.mean(scaled * unit, 0, keepdims=True)
    level = jnp.mean(scaled, 0, keepdims=True)
    out_ref[...] = rest_ref[...] + (scaled - level - unit * along) * inverse
    weighted = grad * unit
    for at in range(0, places, 128):
        sums_ref[0] += weighted[:, at : at + 128]
        sums_ref[1] += grad[:, at : at + 128]


def norm_backward(stream, gain, grad, rest):
    width, places = stream.shape
    columns = min(256, places)
    block = pl.BlockSpec((width, columns), lambda i: (0, i))
    return pl.pallas_call(
        norm_back_kernel,
        grid=(places // columns,),
        in_specs=[block, pl.BlockSpec((width, 1), lambda i: (0, 0)), block, block],
        out_specs=[block, pl.BlockSpec((2, width, 128), lambda i: (0, 0, 0))],
        out_shape=[
            jax.ShapeDtypeStruct((width, places), f32),
            jax.ShapeDtypeStruct((2, width, 128), f32),
        ],
        compiler_params=pltpu.CompilerParams(vmem_limit_bytes=vmem_bytes),
        name="norm_backward",
    )(stream, gain[:, None], grad, rest)


def chunk_plan(total):
    quarter = place_block // 4
    units = (jnp.maximum(total - place_block, 0) + quarter - 1) // quarter
    left = units % 4
    wides = units // 4 + (left == 3).astype(jnp.int32)
    return jnp.stack([wides, left == 2, left == 1]).astype(jnp.int32)


def each_chunk(plan, visit):
    visit(0, place_block, True)

    def wide(index, carry):
        visit(pl.multiple_of((index + 1) * place_block, place_block), place_block, False)
        return carry

    lax.fori_loop(0, plan[0], wide, 0)
    after = pl.multiple_of((plan[0] + 1) * place_block, place_block)
    for index, share in ((1, 2), (2, 4)):

        @pl.when(plan[index] > 0)
        def _(share=share):
            visit(after, place_block // share, False)


def parts_of(words):
    for count in (5, 4, 2):
        if words % (16 * count) == 0:
            return [slice(i * (words // count), (i + 1) * (words // count)) for i in range(count)]
    return [slice(0, words)]


def head_stats_kernel(plan, table_ref, turned_ref, stats_ref, tops, sums):
    step = pl.program_id(0)

    @pl.when(step == 0)
    def _():
        tops[...] = jnp.full_like(tops, -1e30)
        sums[...] = jnp.zeros_like(sums)

    def visit(start, size, first):
        here = pl.ds(start, size)
        turned = turned_ref[:, here]
        old, total = tops[:, here], sums[:, here]
        for part in parts_of(table_ref.shape[0]):
            logits = contract(table_ref[part, :], turned, 1, 0)
            logits = logits.reshape(logits.shape[0] // 8, 8, size)
            top = jnp.maximum(old, jnp.max(logits, axis=0))
            powers = jnp.sum(jnp.exp(logits - top[None]), axis=0)
            total = total * jnp.exp(old - top) + powers
            old = top
        sums[:, here] = total
        tops[:, here] = old

    each_chunk(plan, visit)

    @pl.when(step == pl.num_programs(0) - 1)
    def _():
        top = jnp.max(tops[...], axis=0, keepdims=True)
        stats_ref[0:1, :] = top
        stats_ref[1:2, :] = jnp.sum(sums[...] * jnp.exp(tops[...] - top), axis=0, keepdims=True)


def head_back_kernel(
    plan, table_ref, rows_ref, turned_ref, target_ref, log_ref, weight_ref, *refs, owned
):
    (*out_refs, dr_ref, pick_ref, acc) = refs
    step = pl.program_id(0)
    words, width = table_ref.shape

    @pl.when(step == 0)
    def _():
        dr_ref[...] = jnp.zeros_like(dr_ref)
        pick_ref[...] = jnp.zeros_like(pick_ref)

    def visit(start, size, first):
        here = pl.ds(start, size)
        rows, turned = rows_ref[here, :], turned_ref[:, here]
        target = target_ref[:, here] - step * words
        log, weight = log_ref[:, here], weight_ref[:, here]
        found = jnp.zeros((8, size), f32)
        for part in parts_of(words):
            block = table_ref[part, :]
            count = block.shape[0]
            inner = lax.broadcasted_iota(jnp.int32, (count, size), 0) + part.start
            logits = contract(block, turned, 1, 0)
            scaled = jnp.exp(logits - log)
            hit = inner == target
            found += jnp.sum(jnp.where(hit, logits, 0.0).reshape(count // 8, 8, size), axis=0)
            d_logits = jnp.where(hit, scaled - weight, scaled).astype(low_type)
            if first:
                acc[part, :] = contract(d_logits, rows, 1, 0)
            else:
                acc[part, :] += contract(d_logits, rows, 1, 0)
            dr_ref[here, :] += contract(d_logits, block, 0, 0)
        pick_ref[:, here] += found

    each_chunk(plan, visit)
    if not owned:
        out_refs[0][...] = acc[...]
        return
    mine = plan[3]
    keep = pl.ds(pl.multiple_of(mine * owned, 8), owned)
    away = pl.ds(pl.multiple_of((1 - mine) * owned, 8), owned)
    out_refs[0][0] = acc[keep, :]
    out_refs[1][0] = acc[away, :].astype(low_type)


def word_block(words):
    return max(n for n in range(16, 1601, 16) if words % n == 0)


def head_stats(plan, table_part, turned):
    words = word_block(table_part.shape[0])
    width, places = turned.shape
    return pl.pallas_call(
        head_stats_kernel,
        grid_spec=pltpu.PrefetchScalarGridSpec(
            num_scalar_prefetch=1,
            grid=(table_part.shape[0] // words,),
            in_specs=[
                pl.BlockSpec((words, width), lambda i, *_: (i, 0)),
                pl.BlockSpec((width, places), lambda i, *_: (0, 0)),
            ],
            out_specs=pl.BlockSpec((2, places), lambda i, *_: (0, 0)),
            scratch_shapes=[pltpu.VMEM((8, places), f32) for _ in range(2)],
        ),
        out_shape=jax.ShapeDtypeStruct((2, places), f32),
        compiler_params=pltpu.CompilerParams(vmem_limit_bytes=vmem_bytes),
        name="head_stats",
    )(plan, table_part, turned)


def head_back(plan, table_part, rows, turned, targets, logs, weights, owned):
    total = table_part.shape[0]
    words = 2 * owned if owned else word_block(total)
    places, width = rows.shape
    row = pl.BlockSpec((1, places), lambda i, *_: (0, 0))
    if owned:
        out_specs = [pl.BlockSpec((1, owned, width), lambda i, *_: (i, 0, 0))] * 2
        shape = (total // words, owned, width)
        out_shape = [jax.ShapeDtypeStruct(shape, f32), jax.ShapeDtypeStruct(shape, low_type)]
    else:
        out_specs = [pl.BlockSpec((words, width), lambda i, *_: (i, 0))]
        out_shape = [jax.ShapeDtypeStruct((total, width), f32)]
    return pl.pallas_call(
        functools.partial(head_back_kernel, owned=owned),
        grid_spec=pltpu.PrefetchScalarGridSpec(
            num_scalar_prefetch=1,
            grid=(total // words,),
            in_specs=[
                pl.BlockSpec((words, width), lambda i, *_: (i, 0)),
                pl.BlockSpec((places, width), lambda i, *_: (0, 0)),
                pl.BlockSpec((width, places), lambda i, *_: (0, 0)),
                row,
                row,
                row,
            ],
            out_specs=out_specs
            + [
                pl.BlockSpec((places, width), lambda i, *_: (0, 0)),
                pl.BlockSpec((8, places), lambda i, *_: (0, 0)),
            ],
            scratch_shapes=[pltpu.VMEM((words, width), f32)],
        ),
        out_shape=out_shape
        + [
            jax.ShapeDtypeStruct((places, width), f32),
            jax.ShapeDtypeStruct((8, places), f32),
        ],
        compiler_params=pltpu.CompilerParams(vmem_limit_bytes=vmem_bytes),
        name="head_back",
    )(plan, table_part, rows, turned, targets, logs, weights)


def swap(values, axis, bit):
    size = lax.axis_size(axis)
    return lax.ppermute(values, axis, [(i, i ^ bit) for i in range(size)])


def power_of_two(size):
    return size & (size - 1) == 0


def pick(values, dim, index):
    return lax.dynamic_index_in_dim(values, index, dim, False)


def gather_seq(values, dim):
    if lax.axis_size("seq") == 2:
        other = swap(values, "seq", 1)
        first = lax.axis_index("seq") == 0
        return jnp.stack([jnp.where(first, values, other), jnp.where(first, other, values)], dim)
    return lax.all_gather(values, "seq", axis=dim)


def to_each(values):
    return lax.all_to_all(values, ("seq", "dp"), 0, 0)


def halving_fits(rows, columns, joint):
    owners, seqs = lax.axis_size("dp"), lax.axis_size("seq")
    fits = power_of_two(owners) and owners > 2 and columns % 128 == 0
    return fits and (rows % 16 == 0 and seqs == 2 if joint else rows % 8 == 0)


class Chain:
    pending = value = square = None

class LayerChain(Chain):
    def __init__(self, parts):
        self.parts, self.step = parts, 0
        self.rows = parts[0].shape[1]
        self.fast = halving_fits(self.rows, parts[0].shape[2], True)
        if self.fast:
            self.launch()

    def launch(self):
        owners = lax.axis_size("dp")
        if self.step == 4:
            return
        if self.step == 3:
            self.pending = swap(self.part, "seq", 1)
        elif self.step == 2:
            groups = [list(range(core, owners, 2)) for core in range(2)]
            whole = (self.part + self.got.astype(f32)).astype(low_type)
            self.pending = lax.all_to_all(whole, "dp", 0, 0, axis_index_groups=groups)
        else:
            axis = ("dp", "seq")[self.step]
            mine = lax.axis_index(axis) & 1
            if self.step == 1:
                self.rows //= 2

            def half(side):
                if self.step == 0:
                    shape = (owners // 2, 2, self.rows)
                    parts = [part.reshape(shape + part.shape[2:]) for part in self.parts]
                    return jnp.concatenate([pick(part, 1, side) for part in parts], 2)
                shape = (owners // 2, 2, self.rows, -1)
                first, second = self.part.reshape(shape), self.got.reshape(shape)
                return pick(first, 1, side) + pick(second, 1, side).astype(f32)

            away = half(1 - mine).astype(low_type)
            self.part = half(mine)
            self.pending = swap(away, axis, 1)

    def absorb(self, got):
        self.pending = None
        self.step += 1
        if self.step < 3:
            self.got = got
        elif self.step == 3:
            self.part = jnp.sum(got.astype(f32), 0)
            self.square = jnp.sum(self.part * self.part)
        else:
            first = lax.axis_index("seq") == 0
            part = self.part
            self.value = jnp.concatenate(
                [jnp.where(first, part, got), jnp.where(first, got, part)], 0
            )

    def finish(self):
        if not self.fast:
            whole = jnp.concatenate(self.parts, 2)
            part = lax.psum(lax.psum_scatter(whole, "dp", scatter_dimension=0), "seq")
            self.value = part
            self.square = jnp.where(lax.axis_index("seq") == 0, jnp.sum(part * part), 0.0)


def table_to_owner(keep, arrived):
    owners = lax.axis_size("dp")
    groups = [list(range(core, owners, 2)) for core in range(2)]
    return lax.psum_scatter(
        keep + arrived.astype(f32), "dp", scatter_dimension=0, axis_index_groups=groups
    )


def advance(main, chains):
    live = [chain for chain in chains if chain.pending is not None]
    main, got = lax.optimization_barrier((main, [chain.pending for chain in live]))
    for chain, arrived in zip(live, got):
        chain.absorb(arrived)
        chain.launch()
    return main


def adam_update(weight, first, second, grad, rate):
    first = beta_one * first + (1 - beta_one) * grad
    second = beta_two * second + (1 - beta_two) * grad * grad
    first_hat = first / (1 - beta_one**STEP)
    second_hat = second / (1 - beta_two**STEP)
    weight = weight - rate * (first_hat / (jnp.sqrt(second_hat) + adam_eps) + weight_decay * weight)
    return (weight, first, second)


def place_spans(starts, places):
    covered = places[:, None] >= starts[None, :]
    number = jnp.sum(covered.astype(jnp.int32), -1) - 1
    return number, jnp.max(jnp.where(covered, starts[None, :], 0), -1)


def key_spans(number, starts, lengths, block):
    hot = number[:, None] == jnp.arange(starts.shape[0])[None, :]
    first = jnp.sum(jnp.where(hot, starts[None, :], 0), -1)
    last = jnp.sum(jnp.where(hot, (starts + lengths)[None, :], 0), -1)
    first_block = jnp.min(first.reshape(-1, block), -1) // key_block
    last_block = (jnp.max(last.reshape(-1, block), -1) + key_block - 1) // key_block
    return (
        jnp.stack([first, last]).astype(jnp.int32),
        jnp.stack([first_block, last_block]).astype(jnp.int32),
    )


def on_device(
    src_ids,
    tgt_ids,
    src_lengths,
    tgt_lengths,
    tgt_mask,
    attn_in,
    attn_in_m1,
    attn_in_m2,
    attn_out,
    attn_out_m1,
    attn_out_m2,
    ffn_in,
    ffn_in_m1,
    ffn_in_m2,
    ffn_out,
    ffn_out_m1,
    ffn_out_m2,
    len_head,
    len_head_m1,
    len_head_m2,
    norms,
    norms_m1,
    norms_m2,
    table,
    table_m1,
    table_m2,
):
    rows_here, seq_rows = src_ids.shape
    seqs, owners = lax.axis_size("seq"), lax.axis_size("dp")
    devices = seqs * owners
    row_len = seq_rows * seqs
    side = lax.axis_index("seq")
    group = seqs // rows_here
    span = row_len // group
    row, offset = side // group, (side % group) * span
    sharers = [[r * group + i for i in range(group)] for r in range(rows_here)]
    own_words, width = table.shape
    classes = len_head.shape[1]
    vocab_width = own_words * owners
    vocab_base = side * vocab_width
    norm_count = norms.shape[1]
    norm_columns = 128

    def columns_of(weight, rows):
        return [weight[at : at + rows] for at in range(0, weight.shape[0], rows)]

    def cut_parts(whole, parts):
        result, at = [], 0
        for part in parts:
            result.append(whole[:, at : at + part.shape[1]])
            at += part.shape[1]
        return result

    def gather_columns(parts):
        joined = jnp.concatenate([part.astype(low_type) for part in parts], 1)
        if joined.shape[0] % (16 * seqs) == 0:
            rows = joined.shape[0] // seqs
            joined = lax.dynamic_slice_in_dim(joined, side * rows, rows, 0)
            whole = lax.all_gather(joined, ("dp", "seq"), axis=0, tiled=True)
        else:
            whole = lax.all_gather(joined, "dp", axis=0, tiled=True)
        return cut_parts(whole, parts)

    def join_rows(pieces):
        blocks = [piece.reshape(owners, -1, piece.shape[1]) for piece in pieces]
        return jnp.concatenate(blocks, 1).reshape(-1, pieces[0].shape[1])

    share = attn_in.shape[1]
    norm_part = jnp.pad(
        norms.reshape(-1, norms.shape[2]).T, ((0, 0), (0, norm_columns - 2 * norm_count))
    )
    out_pieces = ffn_out.shape[1] // share
    parts = [attn_in[0], attn_out[0], len_head, norm_part, ffn_in[0]]
    parts += columns_of(ffn_out[0], share)
    parts += [attn_in[1], attn_out[1], attn_in[2], attn_out[2], ffn_in[1]]
    parts += columns_of(ffn_out[1], share)
    w_in0, w_out0, w_len, norm_low, f_in0, *others = gather_columns(parts)
    f_out0 = join_rows(others[:out_pieces])
    w_in1, w_out1, w_in2, w_out2, f_in1, *f_out1 = others[out_pieces:]
    f_out1 = join_rows(f_out1)
    table_low = table.astype(low_type)
    table_part = lax.all_gather(table_low, "dp", axis=0, tiled=True)
    norm_low = norm_low[:, : 2 * norm_count].T.astype(f32)
    gains, biases = norm_low[:norm_count], norm_low[norm_count:]

    ids = gather_seq(jnp.stack([src_ids, tgt_ids, tgt_mask]), 2).reshape(3, rows_here, row_len)
    src_starts = jnp.cumsum(src_lengths, -1) - src_lengths
    tgt_starts = jnp.cumsum(tgt_lengths, -1) - tgt_lengths
    places = jnp.arange(row_len)
    opens = jnp.any(places[None, :, None] == src_starts[:, None, :], -1)
    src_in = pick(jnp.where(opens, length_token, ids[0]).reshape(seqs, span), 0, side)
    masked = (ids[2] == 1).reshape(seqs, span)
    labels = ids[1].reshape(seqs, span)
    dec_in = pick(jnp.where(masked, mask_token, labels), 0, side)
    counts = jnp.sum(masked.astype(jnp.int32), -1)

    def slots_for(expected):
        return max(-(-expected // 16) * 16, 16)

    src_slots, dec_slots = slots_for(2 * span // devices), slots_for(3 * span // (2 * devices))

    def ask(token_ids, slots):
        same = token_ids[:, None] == token_ids[None, :]
        index = jnp.arange(span)
        earlier = index[None, :] < index[:, None]
        leader = jnp.logical_not(jnp.any(same & earlier, 1))
        holder = token_ids // own_words
        rank = jnp.sum(
            (earlier & leader[None, :] & (holder[:, None] == holder[None, :])).astype(jnp.int32), 1
        )
        rank = jnp.sum(jnp.where(same & leader[None, :], rank[None, :], 0), 1)
        return token_ids % own_words, holder, rank, slots

    def chosen_of(asked, turn):
        local, holder, rank, slots = asked
        code = jnp.where(rank // slots == turn, holder * slots + rank % slots, -1)
        return code[:, None] == jnp.arange(devices * slots)[None, :]

    def wanted_of(asked, chosen):
        return jnp.max(jnp.where(chosen, asked[0][:, None], -1), 0).reshape(devices, -1)

    def maps_of(chosen, wanted):
        held = wanted.reshape(-1)[:, None] == jnp.arange(own_words)[None, :]
        return chosen.astype(low_type), held.astype(low_type)

    def round_of(asked, turn):
        chosen = chosen_of(asked, turn)
        return maps_of(chosen, to_each(wanted_of(asked, chosen)))

    def send_rows(held):
        found = contract(held, table_low, 1, 0).astype(low_type)
        return to_each(found.reshape(devices, -1, width)).reshape(-1, width)

    def fetch(maps):
        chosen, held = maps
        return contract(send_rows(held), chosen, 0, 1)

    def give_rows(chosen, grads):
        sums = contract(chosen, grads.astype(low_type), 0, 1).astype(low_type)
        return to_each(sums.reshape(devices, -1, width)).reshape(-1, width)

    def give(maps, grads):
        return contract(maps[1], give_rows(maps[0], grads), 0, 0)

    def later_rounds(rounds, value, visit):
        return lax.fori_loop(1, rounds, lambda turn, carry: carry + visit(turn), value)

    src_ask, dec_ask = ask(src_in, src_slots), ask(dec_in, dec_slots)
    src_chosen, dec_chosen = chosen_of(src_ask, 0), chosen_of(dec_ask, 0)
    facts = jnp.stack(
        [
            jnp.sum(tgt_mask),
            jnp.max(counts),
            jnp.max(src_ask[2]) // src_slots + 1,
            jnp.max(dec_ask[2]) // dec_slots + 1,
        ]
    )
    facts = jnp.broadcast_to(jnp.pad(facts, (0, 12))[None, :], (devices, 16))
    asked = [wanted_of(src_ask, src_chosen), wanted_of(dec_ask, dec_chosen), facts]
    asked = to_each(jnp.concatenate(asked, 1).astype(jnp.int32))
    facts = asked[:, src_slots + dec_slots :]
    count = jnp.sum(facts[:, 0]).astype(f32)
    cut = -(-(span * 3 // 8) // 128) * 128
    more = jnp.max(facts[:, 1]) > cut
    src_rounds, dec_rounds = jnp.max(facts[:, 2]), jnp.max(facts[:, 3])
    src_maps = maps_of(src_chosen, asked[:, :src_slots])
    src_found = fetch(src_maps)
    dec_maps = maps_of(dec_chosen, asked[:, src_slots : src_slots + dec_slots])
    dec_rows = send_rows(dec_maps[1])

    starts_at = jnp.cumsum(counts) - counts
    total = jnp.sum(counts)
    rank = jnp.where(masked, jnp.cumsum(masked.astype(jnp.int32), -1) - 1, -1)
    slot_of = jnp.where(masked, rank + starts_at[:, None], -1)
    slot_index = jnp.arange(seqs * span)
    slot_label = jnp.sum(
        jnp.where(slot_of.reshape(1, -1) == slot_index[:, None], labels.reshape(1, -1), 0), -1
    )
    valid = slot_index < total
    targets = jnp.where(valid, slot_label - vocab_base, -1).reshape(1, -1)
    plan = jnp.concatenate([chunk_plan(total), lax.axis_index("dp")[None] & 1]).astype(jnp.int32)
    own_rank, own_slot = pick(rank, 0, side), pick(slot_of, 0, side)

    def packing(slots, rows):
        slot, index = jnp.arange(slots), jnp.arange(rows)
        far_start, far_count = pick(starts_at, 0, 1 - side), pick(counts, 0, 1 - side)
        far = jnp.where(index < far_count, index + far_start, -1)
        return (
            (own_rank[None, :] == index[:, None]).astype(low_type),
            (own_slot[None, :] == slot[:, None]).astype(low_type),
            (far[None, :] == slot[:, None]).astype(low_type),
        )

    own_places = offset + jnp.arange(span)
    src_start, src_length = pick(src_starts, 0, row), pick(src_lengths, 0, row)
    tgt_start, tgt_length = pick(tgt_starts, 0, row), pick(tgt_lengths, 0, row)
    src_number, src_open = place_spans(src_start, own_places)
    tgt_number, tgt_open = place_spans(tgt_start, own_places)
    block = min(query_block, span)
    enc_spans = key_spans(src_number, src_start, src_length, block)
    self_spans = key_spans(tgt_number, tgt_start, tgt_length, block)
    cross_spans = key_spans(tgt_number, src_start, src_length, block)
    src_wave, tgt_wave = lax.optimization_barrier(
        (sinusoid(own_places - src_open, width), sinusoid(own_places - tgt_open, width))
    )

    root = math.sqrt(width)
    src_found = later_rounds(src_rounds, src_found, lambda turn: fetch(round_of(src_ask, turn)))
    stream0 = src_found * root + src_wave

    def norm(stream, index):
        return layer_norm(stream, gains[index], biases[index])

    def keys_of_row(part):
        if group == 1:
            return part
        return lax.all_gather(part, "seq", axis=1, tiled=True, axis_index_groups=sharers)

    def keys_to_place(part):
        if group == 1:
            return part
        return lax.psum_scatter(
            part, "seq", scatter_dimension=1, tiled=True, axis_index_groups=sharers
        )

    def self_attention(inner, weight_in, weight_out, spans):
        triple = contract(weight_in, inner, 0, 0).astype(low_type)
        keys = triple if group == 1 else keys_of_row(triple[width:])
        mixed, lse = attend_forward(triple, keys, group == 1, *spans)
        return contract(weight_out, mixed, 0, 0), (triple, keys, mixed, lse)

    def self_attention_back(inner, weight_in, weight_out, spans, kept, grad):
        triple, keys, mixed, lse = kept
        grad_low = grad.astype(low_type)
        d_out = contract(mixed, grad_low, 1, 1)
        d_mixed = contract(weight_out, grad_low, 1, 0).astype(low_type)
        d_query, d_keys = attend_backward(triple, keys, group == 1, *spans, lse, d_mixed)
        d_triple = jnp.concatenate([d_query, keys_to_place(d_keys)], 0)
        return contract(weight_in, d_triple, 1, 0), contract(inner, d_triple, 1, 1), d_out

    def cross_attention(inner, memory, weight_in, weight_out, spans):
        queries = contract(weight_in[:, :width], inner, 0, 0).astype(low_type)
        keys = keys_of_row(contract(weight_in[:, width:], memory, 0, 0).astype(low_type))
        mixed, lse = attend_forward(queries, keys, False, *spans)
        return contract(weight_out, mixed, 0, 0), (queries, keys, mixed, lse)

    def cross_attention_back(inner, memory, weight_in, weight_out, spans, kept, grad):
        queries, keys, mixed, lse = kept
        grad_low = grad.astype(low_type)
        d_out = contract(mixed, grad_low, 1, 1)
        d_mixed = contract(weight_out, grad_low, 1, 0).astype(low_type)
        d_query, d_keys = attend_backward(queries, keys, False, *spans, lse, d_mixed)
        d_keys = keys_to_place(d_keys)
        d_in = jnp.concatenate([contract(inner, d_query, 1, 1), contract(memory, d_keys, 1, 1)], 1)
        return (
            contract(weight_in[:, :width], d_query, 1, 0),
            contract(weight_in[:, width:], d_keys, 1, 0),
            d_in,
            d_out,
        )

    def ffn(inner, weight_one, weight_two):
        hidden = contract(weight_one, inner, 0, 0)
        active = jax.nn.gelu(hidden).astype(low_type)
        return contract(weight_two, active, 0, 0), (hidden, active)

    def ffn_back(inner, weight_one, weight_two, kept, grad):
        hidden, active = kept
        grad_low = grad.astype(low_type)
        d_two = contract(active, grad_low, 1, 1)
        d_active = contract(weight_two, grad_low, 1, 0)
        d_hidden = jax.vjp(jax.nn.gelu, hidden)[1](d_active)[0].astype(low_type)
        return contract(weight_one, d_hidden, 1, 0), contract(inner, d_hidden, 1, 1), d_two

    inner0 = norm(stream0, 0).astype(low_type)
    branch0, keep0 = self_attention(inner0, w_in0, w_out0, enc_spans)
    stream1 = stream0 + branch0
    stream1, dec_rows = lax.optimization_barrier((stream1, dec_rows))
    inner1 = norm(stream1, 1).astype(low_type)
    branch1, keep1 = ffn(inner1, f_in0, f_out0)
    stream2 = stream1 + branch1
    memory = norm(stream2, 2).astype(low_type)
    memory, dec_chosen = lax.optimization_barrier((memory, dec_maps[0]))
    dec_found = contract(dec_rows, dec_chosen, 0, 1)
    dec_found = later_rounds(dec_rounds, dec_found, lambda turn: fetch(round_of(dec_ask, turn)))
    target0 = dec_found * root + tgt_wave
    inner3 = norm(target0, 3).astype(low_type)
    branch3, keep3 = self_attention(inner3, w_in1, w_out1, self_spans)
    target1 = target0 + branch3
    inner4 = norm(target1, 4).astype(low_type)
    branch4, keep4 = cross_attention(inner4, memory, w_in2, w_out2, cross_spans)
    target2 = target1 + branch4
    inner5 = norm(target2, 5).astype(low_type)
    branch5, keep5 = ffn(inner5, f_in1, f_out1)
    target3 = target2 + branch5
    final = norm(target3, 6).astype(low_type)

    def pack(slots, rows):
        own_chosen, own_slots, far_slots = packing(slots, rows)
        far = swap(contract(own_chosen, final, 1, 1).astype(low_type), "seq", 1)
        packed = contract(own_slots, final, 1, 1) + contract(far_slots, far, 1, 0)
        return jnp.pad(packed.astype(low_type), ((0, seqs * span - slots), (0, 0)))

    def unpack(slots, rows):
        own_chosen, own_slots, far_slots = packing(slots, rows)
        high = lax.reduce_precision(d_pieces[:slots], 8, 7)
        rest = (d_pieces[:slots] - high).astype(low_type)
        high = high.astype(low_type)
        far = swap(contract(far_slots, high, 0, 0).astype(low_type), "seq", 1)
        return (
            contract(high, own_slots, 0, 0)
            + contract(rest, own_slots, 0, 0)
            + contract(far, own_chosen, 0, 0)
        )

    if seqs == 2:
        pieces = lax.cond(
            more, lambda: pack(2 * span, span), lambda: pack(min(2 * cut, 2 * span), cut)
        )
    else:
        own_slots = packing(seqs * span, span)[1]
        pieces = lax.psum(contract(own_slots, final, 1, 1), "seq").astype(low_type)
    turned = pieces.T
    every = gather_seq(head_stats(plan, table_part, turned), 0)
    top_logit = jnp.max(every[:, 0], 0)
    totals = jnp.sum(every[:, 1] * jnp.exp(every[:, 0] - top_logit[None]), 0)
    log_total = top_logit + jnp.log(jnp.where(valid, totals, 1.0))
    own_start = pick(starts_at, 0, side)
    mine = (slot_index >= own_start) & (slot_index < own_start + pick(counts, 0, side))
    token_local = jnp.sum(jnp.where(mine, log_total, 0.0))
    logs = jnp.where(valid, log_total + jnp.log(count), 1e30)
    weights = jnp.where(valid, 1.0 / count, 0.0)
    split = halving_fits(own_words, width, False)
    *d_table, d_pieces, picks = head_back(
        plan, table_part, pieces, turned, targets, logs[None], weights[None], split and own_words
    )
    token_local = token_local - jnp.sum(picks)
    if split:
        arrived = swap(d_table[1], "dp", 1)
    if seqs == 2:
        d_final = lax.cond(
            more, lambda: unpack(2 * span, span), lambda: unpack(min(2 * cut, 2 * span), cut)
        )
    else:
        d_pieces = lax.psum(d_pieces, "seq")
        high = lax.reduce_precision(d_pieces, 8, 7)
        rest = (d_pieces - high).astype(low_type)
        d_final = contract(high.astype(low_type), own_slots, 0, 0) + contract(rest, own_slots, 0, 0)

    first_place = own_places[None, :] == src_start[:, None]
    mine = jnp.any(first_place, -1)
    first_rows = contract(first_place.astype(low_type), memory, 1, 1).astype(low_type)
    len_logits = contract(first_rows, w_len, 1, 0)
    len_label = jnp.minimum(tgt_length, classes - 1)
    len_hot = jnp.arange(classes)[None, :] == len_label[:, None]
    len_loss = jax.nn.logsumexp(len_logits, -1) - jnp.sum(jnp.where(len_hot, len_logits, 0.0), -1)
    len_local = jnp.sum(jnp.where(mine, len_loss, 0.0))
    sentences = rows_here * src_lengths.shape[1] * owners
    len_prob = jax.nn.softmax(len_logits, -1)
    d_len_logits = (
        jnp.where(mine[:, None], len_prob - len_hot.astype(f32), 0.0) * (0.1 / sentences)
    ).astype(low_type)
    d_w_len = contract(first_rows, d_len_logits, 0, 0)
    d_first = contract(d_len_logits, w_len, 1, 1)
    d_memory = lax.dot_general(
        d_first,
        first_place.astype(f32),
        (((0,), (0,)), ((), ())),
        precision=lax.Precision.HIGHEST,
        preferred_element_type=f32,
    )

    def owned(grad):
        return grad.reshape(owners, -1, grad.shape[1])

    def owned_columns(grad):
        whole = owned(grad)
        return [whole[:, at : at + share] for at in range(0, whole.shape[1], share)]

    none = jnp.zeros_like(stream0)
    d_target3, scale6 = norm_backward(target3, gains[6], d_final, none)
    d_inner5, d_fin1, d_fout1 = ffn_back(inner5, f_in1, f_out1, keep5, d_target3)
    if split:
        d_inner5, d_target3, arrived = lax.optimization_barrier((d_inner5, d_target3, arrived))
        table_grad = table_to_owner(d_table[0], arrived)
    else:
        table_grad = lax.psum_scatter(d_table[0], "dp", scatter_dimension=0, tiled=True)
    chain_a = LayerChain([owned(d_fin1)] + owned_columns(d_fout1))
    d_target2, scale5 = norm_backward(target2, gains[5], d_inner5, d_target3)
    d_inner4, d_cross, d_win2, d_wout2 = cross_attention_back(
        inner4, memory, w_in2, w_out2, cross_spans, keep4, d_target2
    )
    chains = [chain_a]
    d_inner4, d_target2, d_cross = advance((d_inner4, d_target2, d_cross), chains)
    chain_b = LayerChain([owned(d_win2), owned(d_wout2)])
    d_target1, scale4 = norm_backward(target1, gains[4], d_inner4, d_target2)
    d_inner3, d_win1, d_wout1 = self_attention_back(
        inner3, w_in1, w_out1, self_spans, keep3, d_target1
    )
    chains += [chain_b]
    d_inner3, d_target1 = advance((d_inner3, d_target1), chains)
    chain_c = LayerChain([owned(d_win1), owned(d_wout1)])
    d_target0, scale3 = norm_backward(target0, gains[3], d_inner3, d_target1)
    dec_grad = d_target0 * root
    dec_sums = give_rows(dec_maps[0], dec_grad)
    d_stream2, scale2 = norm_backward(stream2, gains[2], d_memory + d_cross, none)
    d_inner1, d_fin0, d_fout0 = ffn_back(inner1, f_in0, f_out0, keep1, d_stream2)
    chains += [chain_c]
    d_inner1, d_stream2 = advance((d_inner1, d_stream2), chains)
    chain_d = LayerChain([owned(d_fin0)] + owned_columns(d_fout0))
    d_stream1, scale1 = norm_backward(stream1, gains[1], d_inner1, d_stream2)
    d_inner0, d_win0, d_wout0 = self_attention_back(
        inner0, w_in0, w_out0, enc_spans, keep0, d_stream1
    )
    chains += [chain_d]
    d_inner0, d_stream1, dec_sums = advance((d_inner0, d_stream1, dec_sums), chains)
    d_stream0, scale0 = norm_backward(stream0, gains[0], d_inner0, d_stream1)
    src_grad = d_stream0 * root
    src_sums = give_rows(src_maps[0], src_grad)
    chain_e = LayerChain([owned(d_win0), owned(d_wout0), owned(d_w_len)])
    norm_share = norms.shape[2]
    scales = jnp.sum(jnp.stack([scale0, scale1, scale2, scale3, scale4, scale5, scale6], 1), 3)
    scales = scales.reshape(2 * norm_count, owners, norm_share).transpose(1, 0, 2)
    scales = jnp.broadcast_to(scales[None], (seqs,) + scales.shape)
    scales = to_each(scales.reshape((devices,) + scales.shape[2:]))
    chains += [chain_e]
    advance((), chains)
    src_sums, scales = advance((src_sums, scales), chains)
    while any(chain.pending is not None for chain in chains):
        advance((), chains)
    layer_chains = [chain_a, chain_b, chain_c, chain_d, chain_e]
    for chain in layer_chains:
        chain.finish()

    g_norms = jnp.sum(scales, 0)
    norm_square = jnp.where(side == 0, jnp.sum(g_norms * g_norms), 0.0)
    given = contract(dec_maps[1], dec_sums, 0, 0) + contract(src_maps[1], src_sums, 0, 0)
    given = later_rounds(
        jnp.maximum(src_rounds, dec_rounds),
        given,
        lambda turn: give(round_of(dec_ask, turn), dec_grad)
        + give(round_of(src_ask, turn), src_grad),
    )
    table_grad = table_grad + given
    square = sum(chain.square for chain in layer_chains)
    square = square + jnp.sum(table_grad * table_grad) + norm_square
    sums = jnp.pad(jnp.stack([token_local, len_local, square]), (0, 5))
    sums = jnp.sum(to_each(jnp.broadcast_to(sums[None], (devices, 8))), 0)
    token_sum, len_sum, grad_norm = sums[0], sums[1], jnp.sqrt(sums[2])
    factor = jnp.minimum(1.0, clip_limit / (grad_norm + 1e-06))

    def cut_columns(chain, sizes):
        result, at = [], 0
        value = chain.value.reshape(share, -1)
        for size in sizes:
            result.append(value[:, at : at + size])
            at += size
        return result

    hidden_width = ffn_in.shape[2]
    ffn_sizes = [hidden_width] + [width] * out_pieces
    attn_sizes = [3 * width, width]
    g_fin1, *g_fout1 = cut_columns(chain_a, ffn_sizes)
    g_win2, g_wout2 = cut_columns(chain_b, attn_sizes)
    g_win1, g_wout1 = cut_columns(chain_c, attn_sizes)
    g_fin0, *g_fout0 = cut_columns(chain_d, ffn_sizes)
    g_win0, g_wout0, g_len = cut_columns(chain_e, attn_sizes + [classes])
    grads = (
        jnp.stack([g_win0, g_win1, g_win2]),
        jnp.stack([g_wout0, g_wout1, g_wout2]),
        jnp.stack([g_fin0, g_fin1]),
        jnp.stack([jnp.concatenate(g_fout0, 0), jnp.concatenate(g_fout1, 0)]),
        g_len,
        g_norms.reshape(norms.shape),
        table_grad,
    )
    masters = (attn_in, attn_out, ffn_in, ffn_out, len_head, norms, table)
    firsts = (attn_in_m1, attn_out_m1, ffn_in_m1, ffn_out_m1, len_head_m1, norms_m1, table_m1)
    seconds = (attn_in_m2, attn_out_m2, ffn_in_m2, ffn_out_m2, len_head_m2, norms_m2, table_m2)
    updates = []
    for weight, first, second, grad, rate in zip(masters, firsts, seconds, grads, step_rates):
        updates.extend(adam_update(weight, first, second, grad * factor, rate))
    return (token_sum, count, len_sum, grad_norm, *updates)


def solution(mesh):
    layer, head, scales, words = P(None, "dp", None), P("dp", None), P(None, None, "dp"), P(("seq", "dp"), None)
    owned = (layer,) * 12 + (head,) * 3 + (scales,) * 3 + (words,) * 3
    ids, lengths = P("dp", "seq"), P("dp", None)
    in_specs = (ids, ids, lengths, lengths, ids) + owned
    out_specs = (P(), P(), P(), P()) + owned
    return jax.shard_map(
        on_device, mesh=mesh, in_specs=in_specs, out_specs=out_specs, check_vma=False
    )
```

```python
import functools
import math

import jax
import jax.numpy as jnp
from jax import lax
from jax.experimental import pallas as pl
from jax.experimental.pallas import tpu as pltpu
from jax.sharding import PartitionSpec as P

HEADS = 8
STEP = 10


length_token = 1
mask_token = 2
clip_limit = 0.002
beta_one = 0.9
beta_two = 0.98
adam_eps = 1e-08
weight_decay = 0.01
step_rates = (0.05, 0.25, 0.05, 0.025, 0.05, 0.5, 0.1)

low_type = jnp.bfloat16
f32 = jnp.float32
query_block = 256
key_block = 128
place_block = 512
vmem_bytes = 56 * 1024 * 1024


def sinusoid(positions, width):
    half_width = width // 2
    frequency = jnp.exp(jnp.arange(half_width).astype(f32) * (-math.log(10000.0) / half_width))
    angles = frequency[:, None] * positions.astype(f32)[None, :]
    return jnp.concatenate([jnp.sin(angles), jnp.cos(angles)], 0)


def layer_norm(stream, norm_gain, norm_bias):
    average = jnp.mean(stream, 0, keepdims=True)
    centred = stream - average
    variance = jnp.mean(centred * centred, 0, keepdims=True)
    inverse = lax.rsqrt(variance + 1e-05)
    normed = centred * inverse * norm_gain[:, None] + norm_bias[:, None]
    return normed.astype(low_type), (stream, average, inverse)


def contract(left, right, left_dim, right_dim):
    return lax.dot_general(
        left, right, (((left_dim,), (right_dim,)), ((), ())), preferred_element_type=f32
    )


def attend_forward_kernel(bounds, q_ref, k_ref, v_ref, span_ref, out_ref, lse_ref, hold, *, head):
    step = pl.program_id(0)
    first, last = bounds[0, step], bounds[1, step]
    width, queries = q_ref.shape
    heads = width // head
    scale = head**-0.5
    low, high = span_ref[0:1, :], span_ref[1:2, :]
    inner = lax.broadcasted_iota(jnp.int32, (key_block, queries), 0)

    def fold(values, op):
        return op(values.reshape(key_block // 8, 8, queries), axis=0)

    def score(block, tops):
        start = pl.multiple_of(block * key_block, key_block)
        place = inner + start
        allowed = (place >= low) & (place < high)
        result = []
        for h in range(heads):
            rows = slice(h * head, (h + 1) * head)
            s = contract(k_ref[rows, pl.ds(start, key_block)], q_ref[rows, :], 0, 0) * scale
            s = jnp.where(allowed, s, -1e30)
            hold[h, pl.ds(start, key_block), :] = s
            result.append(jnp.maximum(tops[h], fold(s, jnp.max)))
        return tuple(result)

    tops = lax.fori_loop(
        first, last, score, tuple(jnp.full((8, queries), -1e30, f32) for _ in range(heads))
    )
    tops = [jnp.max(t, axis=0, keepdims=True) for t in tops]

    def power(block, sums):
        start = pl.multiple_of(block * key_block, key_block)
        result = []
        for h in range(heads):
            e = jnp.exp(hold[h, pl.ds(start, key_block), :] - tops[h])
            hold[h, pl.ds(start, key_block), :] = e
            result.append(sums[h] + fold(e, jnp.sum))
        return tuple(result)

    sums = lax.fori_loop(
        first, last, power, tuple(jnp.zeros((8, queries), f32) for _ in range(heads))
    )
    sums = [jnp.maximum(jnp.sum(t, axis=0, keepdims=True), 1e-30) for t in sums]
    inverse = [1.0 / t for t in sums]

    def mix(block, outs):
        start = pl.multiple_of(block * key_block, key_block)
        result = []
        for h in range(heads):
            rows = slice(h * head, (h + 1) * head)
            p = (hold[h, pl.ds(start, key_block), :] * inverse[h]).astype(low_type)
            result.append(outs[h] + contract(v_ref[rows, pl.ds(start, key_block)], p, 1, 0))
        return tuple(result)

    outs = lax.fori_loop(
        first, last, mix, tuple(jnp.zeros((head, queries), f32) for _ in range(heads))
    )
    for h in range(heads):
        out_ref[h * head : (h + 1) * head, :] = outs[h].astype(low_type)
        lse_ref[h : h + 1, :] = tops[h] + jnp.log(sums[h])


def attend_backward_kernel(
    bounds, q_ref, k_ref, v_ref, span_ref, lse_ref, do_ref, dq_ref, dkv_ref, p_hold, d_hold, acc,
    *, head
):
    step = pl.program_id(0)
    first, last = bounds[0, step], bounds[1, step]
    width, queries = q_ref.shape
    heads = width // head
    scale = head**-0.5
    low, high = span_ref[0:1, :], span_ref[1:2, :]
    inner = lax.broadcasted_iota(jnp.int32, (key_block, queries), 0)

    @pl.when(step == 0)
    def _():
        acc[...] = jnp.zeros_like(acc)

    def one(block, deltas):
        start = pl.multiple_of(block * key_block, key_block)
        keys = pl.ds(start, key_block)
        place = inner + start
        allowed = (place >= low) & (place < high)
        result = []
        for h in range(heads):
            rows = slice(h * head, (h + 1) * head)
            s = contract(k_ref[rows, keys], q_ref[rows, :], 0, 0) * scale
            p = jnp.exp(jnp.where(allowed, s, -1e30) - lse_ref[h : h + 1, :])
            dp = contract(v_ref[rows, keys], do_ref[rows, :], 0, 0)
            p_hold[h, keys, :] = p
            d_hold[h, keys, :] = dp
            result.append(
                deltas[h] + jnp.sum((p * dp).reshape(key_block // 8, 8, queries), axis=0)
            )
            below = slice(width + h * head, width + (h + 1) * head)
            acc[below, keys] += contract(do_ref[rows, :], p.astype(low_type), 1, 1)
        return tuple(result)

    deltas = lax.fori_loop(
        first, last, one, tuple(jnp.zeros((8, queries), f32) for _ in range(heads))
    )
    deltas = [jnp.sum(t, axis=0, keepdims=True) for t in deltas]

    def two(block, outs):
        start = pl.multiple_of(block * key_block, key_block)
        keys = pl.ds(start, key_block)
        result = []
        for h in range(heads):
            rows = slice(h * head, (h + 1) * head)
            ds = (p_hold[h, keys, :] * (d_hold[h, keys, :] - deltas[h])).astype(low_type)
            result.append(outs[h] + contract(k_ref[rows, keys], ds, 1, 0))
            acc[rows, keys] += contract(q_ref[rows, :], ds, 1, 1) * scale
        return tuple(result)

    outs = lax.fori_loop(
        first, last, two, tuple(jnp.zeros((head, queries), f32) for _ in range(heads))
    )
    for h in range(heads):
        dq_ref[h * head : (h + 1) * head, :] = (outs[h] * scale).astype(low_type)

    @pl.when(step == pl.num_programs(0) - 1)
    def _():
        dkv_ref[...] = acc[...].astype(low_type)


def attend_specs(width, length, block, shared):
    key_row = 1 if shared else 0
    return [
        pl.BlockSpec((width, block), lambda i, *_: (0, i)),
        pl.BlockSpec((width, length), lambda i, *_: (key_row, 0)),
        pl.BlockSpec((width, length), lambda i, *_: (key_row + 1, 0)),
        pl.BlockSpec((2, block), lambda i, *_: (0, i)),
    ]


def attend_forward(queries, keys, shared, spans, bounds):
    width = keys.shape[0] // (3 if shared else 2)
    places, length = queries.shape[1], keys.shape[1]
    block = min(query_block, places)
    return pl.pallas_call(
        functools.partial(attend_forward_kernel, head=width // HEADS),
        grid_spec=pltpu.PrefetchScalarGridSpec(
            num_scalar_prefetch=1,
            grid=(places // block,),
            in_specs=attend_specs(width, length, block, shared),
            out_specs=[
                pl.BlockSpec((width, block), lambda i, *_: (0, i)),
                pl.BlockSpec((HEADS, block), lambda i, *_: (0, i)),
            ],
            scratch_shapes=[pltpu.VMEM((HEADS, length, block), f32)],
        ),
        out_shape=[
            jax.ShapeDtypeStruct((width, places), low_type),
            jax.ShapeDtypeStruct((HEADS, places), f32),
        ],
        compiler_params=pltpu.CompilerParams(vmem_limit_bytes=vmem_bytes),
        name="attend_forward",
    )(bounds, queries, keys, keys, spans)


def attend_backward(queries, keys, shared, spans, bounds, lse, d_mixed):
    width = keys.shape[0] // (3 if shared else 2)
    places, length = queries.shape[1], keys.shape[1]
    block = min(query_block, places)
    return pl.pallas_call(
        functools.partial(attend_backward_kernel, head=width // HEADS),
        grid_spec=pltpu.PrefetchScalarGridSpec(
            num_scalar_prefetch=1,
            grid=(places // block,),
            in_specs=attend_specs(width, length, block, shared)
            + [
                pl.BlockSpec((HEADS, block), lambda i, *_: (0, i)),
                pl.BlockSpec((width, block), lambda i, *_: (0, i)),
            ],
            out_specs=[
                pl.BlockSpec((width, block), lambda i, *_: (0, i)),
                pl.BlockSpec((2 * width, length), lambda i, *_: (0, 0)),
            ],
            scratch_shapes=[
                pltpu.VMEM((HEADS, length, block), f32),
                pltpu.VMEM((HEADS, length, block), f32),
                pltpu.VMEM((2 * width, length), f32),
            ],
        ),
        out_shape=[
            jax.ShapeDtypeStruct((width, places), low_type),
            jax.ShapeDtypeStruct((2 * width, length), low_type),
        ],
        compiler_params=pltpu.CompilerParams(vmem_limit_bytes=vmem_bytes),
        name="attend_backward",
    )(bounds, queries, keys, keys, spans, lse, d_mixed)


def norm_back_kernel(stream_ref, average_ref, inverse_ref, gain_ref, grad_ref, *refs):
    (*rest_refs, out_ref, sums_ref) = refs

    @pl.when(pl.program_id(0) == 0)
    def _():
        sums_ref[...] = jnp.zeros_like(sums_ref)

    inverse, grad = inverse_ref[...], grad_ref[...]
    unit = (stream_ref[...] - average_ref[...]) * inverse
    width, places = grad.shape
    scaled = grad * gain_ref[...]
    along = jnp.mean(scaled * unit, 0, keepdims=True)
    level = jnp.mean(scaled, 0, keepdims=True)
    out = (scaled - level - unit * along) * inverse
    for rest_ref in rest_refs:
        out = out + rest_ref[...]
    out_ref[...] = out
    weighted = grad * unit
    for at in range(0, places, 128):
        sums_ref[0] += weighted[:, at : at + 128]
        sums_ref[1] += grad[:, at : at + 128]


def norm_backward(kept, gain, grad, *rests):
    stream, average, inverse = kept
    width, places = stream.shape
    columns = min(256, places)
    block = pl.BlockSpec((width, columns), lambda i: (0, i))
    row = pl.BlockSpec((1, columns), lambda i: (0, i))
    out, sums = pl.pallas_call(
        norm_back_kernel,
        grid=(places // columns,),
        in_specs=[block, row, row, pl.BlockSpec((width, 1), lambda i: (0, 0)), block]
        + [block] * len(rests),
        out_specs=[block, pl.BlockSpec((2, width, 128), lambda i: (0, 0, 0))],
        out_shape=[
            jax.ShapeDtypeStruct((width, places), f32),
            jax.ShapeDtypeStruct((2, width, 128), f32),
        ],
        compiler_params=pltpu.CompilerParams(vmem_limit_bytes=vmem_bytes),
        name="norm_backward",
    )(stream, average, inverse, gain[:, None], grad, *rests)
    return out, jnp.sum(sums, 2)


def chunk_plan(total):
    quarter = place_block // 4
    units = (jnp.maximum(total - place_block, 0) + quarter - 1) // quarter
    left = units % 4
    wides = units // 4 + (left == 3).astype(jnp.int32)
    return jnp.stack([wides, left == 2, left == 1]).astype(jnp.int32)


def each_chunk(plan, visit):
    visit(0, place_block, True)

    def wide(index, carry):
        visit(pl.multiple_of((index + 1) * place_block, place_block), place_block, False)
        return carry

    lax.fori_loop(0, plan[0], wide, 0)
    after = pl.multiple_of((plan[0] + 1) * place_block, place_block)
    for index, share in ((1, 2), (2, 4)):

        @pl.when(plan[index] > 0)
        def _(share=share):
            visit(after, place_block // share, False)


def parts_of(words):
    for count in (5, 4, 2):
        if words % (16 * count) == 0:
            return [slice(i * (words // count), (i + 1) * (words // count)) for i in range(count)]
    return [slice(0, words)]


def head_stats_kernel(plan, table_ref, turned_ref, stats_ref, tops, sums):
    step = pl.program_id(0)

    @pl.when(step == 0)
    def _():
        tops[...] = jnp.full_like(tops, -1e30)
        sums[...] = jnp.zeros_like(sums)

    def visit(start, size, first):
        here = pl.ds(start, size)
        turned = turned_ref[:, here]
        old, total = tops[:, here], sums[:, here]
        for part in parts_of(table_ref.shape[0]):
            logits = contract(table_ref[part, :], turned, 1, 0)
            logits = logits.reshape(logits.shape[0] // 8, 8, size)
            top = jnp.maximum(old, jnp.max(logits, axis=0))
            powers = jnp.sum(jnp.exp(logits - top[None]), axis=0)
            total = total * jnp.exp(old - top) + powers
            old = top
        sums[:, here] = total
        tops[:, here] = old

    each_chunk(plan, visit)

    @pl.when(step == pl.num_programs(0) - 1)
    def _():
        top = jnp.max(tops[...], axis=0, keepdims=True)
        stats_ref[0:1, :] = top
        stats_ref[1:2, :] = jnp.sum(sums[...] * jnp.exp(tops[...] - top), axis=0, keepdims=True)


def head_back_kernel(
    plan, table_ref, rows_ref, turned_ref, target_ref, log_ref, weight_ref, *refs, owned
):
    (*out_refs, dr_ref, pick_ref, acc) = refs
    step = pl.program_id(0)
    words, width = table_ref.shape

    @pl.when(step == 0)
    def _():
        dr_ref[...] = jnp.zeros_like(dr_ref)
        pick_ref[...] = jnp.zeros_like(pick_ref)

    def visit(start, size, first):
        here = pl.ds(start, size)
        rows, turned = rows_ref[here, :], turned_ref[:, here]
        target = target_ref[:, here] - step * words
        log, weight = log_ref[:, here], weight_ref[:, here]
        found = jnp.zeros((8, size), f32)
        for part in parts_of(words):
            block = table_ref[part, :]
            count = block.shape[0]
            inner = lax.broadcasted_iota(jnp.int32, (count, size), 0) + part.start
            logits = contract(block, turned, 1, 0)
            scaled = jnp.exp(logits - log)
            hit = inner == target
            found += jnp.sum(jnp.where(hit, logits, 0.0).reshape(count // 8, 8, size), axis=0)
            d_logits = jnp.where(hit, scaled - weight, scaled).astype(low_type)
            if first:
                acc[part, :] = contract(d_logits, rows, 1, 0)
            else:
                acc[part, :] += contract(d_logits, rows, 1, 0)
            dr_ref[here, :] += contract(d_logits, block, 0, 0)
        pick_ref[:, here] += found

    each_chunk(plan, visit)
    if not owned:
        out_refs[0][...] = acc[...]
        return
    mine = plan[3]
    keep = pl.ds(pl.multiple_of(mine * owned, 8), owned)
    away = pl.ds(pl.multiple_of((1 - mine) * owned, 8), owned)
    half = width // 2
    out_refs[0][0] = acc[keep, :half]
    out_refs[1][0] = acc[keep, half:]
    out_refs[2][0] = acc[away, :half].astype(low_type)
    out_refs[3][0] = acc[away, half:].astype(low_type)


def word_block(words):
    return max(n for n in range(16, 1601, 16) if words % n == 0)


def head_stats(plan, table_part, turned):
    words = word_block(table_part.shape[0])
    width, places = turned.shape
    return pl.pallas_call(
        head_stats_kernel,
        grid_spec=pltpu.PrefetchScalarGridSpec(
            num_scalar_prefetch=1,
            grid=(table_part.shape[0] // words,),
            in_specs=[
                pl.BlockSpec((words, width), lambda i, *_: (i, 0)),
                pl.BlockSpec((width, places), lambda i, *_: (0, 0)),
            ],
            out_specs=pl.BlockSpec((2, places), lambda i, *_: (0, 0)),
            scratch_shapes=[pltpu.VMEM((8, places), f32) for _ in range(2)],
        ),
        out_shape=jax.ShapeDtypeStruct((2, places), f32),
        compiler_params=pltpu.CompilerParams(vmem_limit_bytes=vmem_bytes),
        name="head_stats",
    )(plan, table_part, turned)


def head_back(plan, table_part, rows, turned, targets, logs, weights, owned):
    total = table_part.shape[0]
    words = 2 * owned if owned else word_block(total)
    places, width = rows.shape
    row = pl.BlockSpec((1, places), lambda i, *_: (0, 0))
    if owned:
        out_specs = [pl.BlockSpec((1, owned, width // 2), lambda i, *_: (i, 0, 0))] * 4
        shape = (total // words, owned, width // 2)
        out_shape = [jax.ShapeDtypeStruct(shape, t) for t in (f32, f32, low_type, low_type)]
    else:
        out_specs = [pl.BlockSpec((words, width), lambda i, *_: (i, 0))]
        out_shape = [jax.ShapeDtypeStruct((total, width), f32)]
    return pl.pallas_call(
        functools.partial(head_back_kernel, owned=owned),
        grid_spec=pltpu.PrefetchScalarGridSpec(
            num_scalar_prefetch=1,
            grid=(total // words,),
            in_specs=[
                pl.BlockSpec((words, width), lambda i, *_: (i, 0)),
                pl.BlockSpec((places, width), lambda i, *_: (0, 0)),
                pl.BlockSpec((width, places), lambda i, *_: (0, 0)),
                row,
                row,
                row,
            ],
            out_specs=out_specs
            + [
                pl.BlockSpec((places, width), lambda i, *_: (0, 0)),
                pl.BlockSpec((8, places), lambda i, *_: (0, 0)),
            ],
            scratch_shapes=[pltpu.VMEM((words, width), f32)],
        ),
        out_shape=out_shape
        + [
            jax.ShapeDtypeStruct((places, width), f32),
            jax.ShapeDtypeStruct((8, places), f32),
        ],
        compiler_params=pltpu.CompilerParams(vmem_limit_bytes=vmem_bytes),
        name="head_back",
    )(plan, table_part, rows, turned, targets, logs, weights)


def swap(values, axis, bit):
    size = lax.axis_size(axis)
    return lax.ppermute(values, axis, [(i, i ^ bit) for i in range(size)])


def power_of_two(size):
    return size & (size - 1) == 0


def pick(values, dim, index):
    return lax.dynamic_index_in_dim(values, index, dim, False)


def gather_seq(values, dim):
    if lax.axis_size("seq") == 2:
        other = swap(values, "seq", 1)
        first = lax.axis_index("seq") == 0
        return jnp.stack([jnp.where(first, values, other), jnp.where(first, other, values)], dim)
    return lax.all_gather(values, "seq", axis=dim)


def to_each(values):
    return lax.all_to_all(values, ("seq", "dp"), 0, 0)


def halving_fits(rows, columns, joint):
    owners, seqs = lax.axis_size("dp"), lax.axis_size("seq")
    fits = power_of_two(owners) and owners > 2 and columns % 128 == 0
    return fits and (rows % 16 == 0 and seqs == 2 if joint else rows % 8 == 0)


class Chain:
    pending = value = square = None

class LayerChain(Chain):
    def __init__(self, parts):
        self.parts, self.step = parts, 0
        self.rows = parts[0].shape[1]
        self.fast = halving_fits(self.rows, parts[0].shape[2], True)
        if self.fast:
            self.launch()

    def launch(self):
        owners = lax.axis_size("dp")
        if self.step == 4:
            return
        if self.step == 3:
            self.pending = swap(self.part, "seq", 1)
        elif self.step == 2:
            groups = [list(range(core, owners, 2)) for core in range(2)]
            whole = (self.part + self.got.astype(f32)).astype(low_type)
            self.pending = lax.all_to_all(whole, "dp", 0, 0, axis_index_groups=groups)
        else:
            axis = ("dp", "seq")[self.step]
            mine = lax.axis_index(axis) & 1
            if self.step == 1:
                self.rows //= 2

            def half(side):
                if self.step == 0:
                    shape = (owners // 2, 2, self.rows)
                    parts = [part.reshape(shape + part.shape[2:]) for part in self.parts]
                    return jnp.concatenate([pick(part, 1, side) for part in parts], 2)
                shape = (owners // 2, 2, self.rows, -1)
                first, second = self.part.reshape(shape), self.got.reshape(shape)
                return pick(first, 1, side) + pick(second, 1, side).astype(f32)

            away = half(1 - mine).astype(low_type)
            self.part = half(mine)
            self.pending = swap(away, axis, 1)

    def absorb(self, got):
        self.pending = None
        self.step += 1
        if self.step < 3:
            self.got = got
        elif self.step == 3:
            self.part = jnp.sum(got.astype(f32), 0)
            self.square = jnp.sum(self.part * self.part)
        else:
            first = lax.axis_index("seq") == 0
            part = self.part
            self.value = jnp.concatenate(
                [jnp.where(first, part, got), jnp.where(first, got, part)], 0
            )

    def finish(self):
        if not self.fast:
            whole = jnp.concatenate(self.parts, 2)
            part = lax.psum(lax.psum_scatter(whole, "dp", scatter_dimension=0), "seq")
            self.value = part
            self.square = jnp.where(lax.axis_index("seq") == 0, jnp.sum(part * part), 0.0)


class TableChain(Chain):
    def __init__(self, keep, away):
        self.part, self.got = keep, None
        self.rows, self.bit = keep.shape[1], 2
        self.pending = swap(away, "dp", 1)

    def launch(self):
        if self.bit == lax.axis_size("dp"):
            return
        mine = (lax.axis_index("dp") // self.bit) & 1
        shape = (-1, 2, self.rows, self.part.shape[2])
        first, second = self.part.reshape(shape), self.got.reshape(shape)

        def half(side):
            return pick(first, 1, side) + pick(second, 1, side).astype(f32)

        away = half(1 - mine).astype(low_type)
        self.part = half(mine)
        self.pending = swap(away, "dp", self.bit)
        self.bit *= 2

    def absorb(self, got):
        self.pending, self.got = None, got
        if self.bit == lax.axis_size("dp"):
            self.value = (self.part + got.astype(f32)).reshape(self.rows, -1)


def advance(main, chains):
    live = [chain for chain in chains if chain.pending is not None]
    main, got = lax.optimization_barrier((main, [chain.pending for chain in live]))
    for chain, arrived in zip(live, got):
        chain.absorb(arrived)
    for chain in live:
        chain.launch()
    return main


def adam_update(weight, first, second, grad, rate):
    first = beta_one * first + (1 - beta_one) * grad
    second = beta_two * second + (1 - beta_two) * grad * grad
    first_hat = first / (1 - beta_one**STEP)
    second_hat = second / (1 - beta_two**STEP)
    weight = weight - rate * (first_hat / (jnp.sqrt(second_hat) + adam_eps) + weight_decay * weight)
    return (weight, first, second)


def place_spans(starts, places):
    covered = places[:, None] >= starts[None, :]
    number = jnp.sum(covered.astype(jnp.int32), -1) - 1
    return number, jnp.max(jnp.where(covered, starts[None, :], 0), -1)


def key_spans(number, starts, lengths, block):
    hot = number[:, None] == jnp.arange(starts.shape[0])[None, :]
    first = jnp.sum(jnp.where(hot, starts[None, :], 0), -1)
    last = jnp.sum(jnp.where(hot, (starts + lengths)[None, :], 0), -1)
    first_block = jnp.min(first.reshape(-1, block), -1) // key_block
    last_block = (jnp.max(last.reshape(-1, block), -1) + key_block - 1) // key_block
    return (
        jnp.stack([first, last]).astype(jnp.int32),
        jnp.stack([first_block, last_block]).astype(jnp.int32),
    )


def on_device(
    src_ids,
    tgt_ids,
    src_lengths,
    tgt_lengths,
    tgt_mask,
    attn_in,
    attn_in_m1,
    attn_in_m2,
    attn_out,
    attn_out_m1,
    attn_out_m2,
    ffn_in,
    ffn_in_m1,
    ffn_in_m2,
    ffn_out,
    ffn_out_m1,
    ffn_out_m2,
    len_head,
    len_head_m1,
    len_head_m2,
    norms,
    norms_m1,
    norms_m2,
    table,
    table_m1,
    table_m2,
):
    rows_here, seq_rows = src_ids.shape
    seqs, owners = lax.axis_size("seq"), lax.axis_size("dp")
    devices = seqs * owners
    row_len = seq_rows * seqs
    side = lax.axis_index("seq")
    group = seqs // rows_here
    span = row_len // group
    row, offset = side // group, (side % group) * span
    sharers = [[r * group + i for i in range(group)] for r in range(rows_here)]
    own_words, width = table.shape
    classes = len_head.shape[1]
    vocab_width = own_words * owners
    vocab_base = side * vocab_width
    norm_count = norms.shape[1]
    norm_columns = 128

    def columns_of(weight, rows):
        return [weight[at : at + rows] for at in range(0, weight.shape[0], rows)]

    def cut_parts(whole, parts):
        result, at = [], 0
        for part in parts:
            result.append(whole[:, at : at + part.shape[1]])
            at += part.shape[1]
        return result

    def gather_columns(parts):
        joined = jnp.concatenate([part.astype(low_type) for part in parts], 1)
        if joined.shape[0] % (16 * seqs) == 0:
            rows = joined.shape[0] // seqs
            joined = lax.dynamic_slice_in_dim(joined, side * rows, rows, 0)
            whole = lax.all_gather(joined, ("dp", "seq"), axis=0, tiled=True)
        else:
            whole = lax.all_gather(joined, "dp", axis=0, tiled=True)
        return cut_parts(whole, parts)

    def join_rows(pieces):
        blocks = [piece.reshape(owners, -1, piece.shape[1]) for piece in pieces]
        return jnp.concatenate(blocks, 1).reshape(-1, pieces[0].shape[1])

    share = attn_in.shape[1]
    norm_part = jnp.pad(
        norms.reshape(-1, norms.shape[2]).T, ((0, 0), (0, norm_columns - 2 * norm_count))
    )
    out_pieces = ffn_out.shape[1] // share
    parts = [attn_in[0], attn_out[0], len_head, norm_part, ffn_in[0]]
    parts += columns_of(ffn_out[0], share)
    parts += [attn_in[1], attn_out[1], attn_in[2], attn_out[2], ffn_in[1]]
    parts += columns_of(ffn_out[1], share)
    w_in0, w_out0, w_len, norm_low, f_in0, *others = gather_columns(parts)
    f_out0 = join_rows(others[:out_pieces])
    w_in1, w_out1, w_in2, w_out2, f_in1, *f_out1 = others[out_pieces:]
    f_out1 = join_rows(f_out1)
    table_low = table.astype(low_type)
    table_part = lax.all_gather(table_low, "dp", axis=0, tiled=True)
    norm_low = norm_low[:, : 2 * norm_count].T.astype(f32)
    gains, biases = norm_low[:norm_count], norm_low[norm_count:]

    ids = gather_seq(jnp.stack([src_ids, tgt_ids, tgt_mask]), 2).reshape(3, rows_here, row_len)
    src_starts = jnp.cumsum(src_lengths, -1) - src_lengths
    tgt_starts = jnp.cumsum(tgt_lengths, -1) - tgt_lengths
    places = jnp.arange(row_len)
    opens = jnp.any(places[None, :, None] == src_starts[:, None, :], -1)
    src_in = pick(jnp.where(opens, length_token, ids[0]).reshape(seqs, span), 0, side)
    masked = (ids[2] == 1).reshape(seqs, span)
    labels = ids[1].reshape(seqs, span)
    dec_in = pick(jnp.where(masked, mask_token, labels), 0, side)
    counts = jnp.sum(masked.astype(jnp.int32), -1)

    def slots_for(expected):
        return max(-(-expected // 16) * 16, 16)

    src_slots, dec_slots = slots_for(2 * span // devices), slots_for(3 * span // (2 * devices))

    def ask(token_ids, slots):
        same = token_ids[:, None] == token_ids[None, :]
        index = jnp.arange(span)
        earlier = index[None, :] < index[:, None]
        leader = jnp.logical_not(jnp.any(same & earlier, 1))
        holder = token_ids // own_words
        rank = jnp.sum(
            (earlier & leader[None, :] & (holder[:, None] == holder[None, :])).astype(jnp.int32), 1
        )
        rank = jnp.sum(jnp.where(same & leader[None, :], rank[None, :], 0), 1)
        return token_ids % own_words, holder, rank, slots

    def chosen_of(asked, turn):
        local, holder, rank, slots = asked
        code = jnp.where(rank // slots == turn, holder * slots + rank % slots, -1)
        return code[:, None] == jnp.arange(devices * slots)[None, :]

    def wanted_of(asked, chosen):
        return jnp.max(jnp.where(chosen, asked[0][:, None], -1), 0).reshape(devices, -1)

    def maps_of(chosen, wanted):
        held = wanted.reshape(-1)[:, None] == jnp.arange(own_words)[None, :]
        return chosen.astype(low_type), held.astype(low_type)

    def round_of(asked, turn):
        chosen = chosen_of(asked, turn)
        return maps_of(chosen, to_each(wanted_of(asked, chosen)))

    def send_rows(held):
        found = contract(held, table_low, 1, 0).astype(low_type)
        return to_each(found.reshape(devices, -1, width)).reshape(-1, width)

    def fetch(maps):
        chosen, held = maps
        return contract(send_rows(held), chosen, 0, 1)

    def give_rows(chosen, grads):
        sums = contract(chosen, grads.astype(low_type), 0, 1).astype(low_type)
        return to_each(sums.reshape(devices, -1, width)).reshape(-1, width)

    def give(maps, grads):
        return contract(maps[1], give_rows(maps[0], grads), 0, 0)

    def later_rounds(rounds, value, visit):
        return lax.fori_loop(1, rounds, lambda turn, carry: carry + visit(turn), value)

    src_ask, dec_ask = ask(src_in, src_slots), ask(dec_in, dec_slots)
    src_chosen, dec_chosen = chosen_of(src_ask, 0), chosen_of(dec_ask, 0)
    facts = jnp.stack(
        [
            jnp.sum(tgt_mask),
            jnp.max(counts),
            jnp.max(src_ask[2]) // src_slots + 1,
            jnp.max(dec_ask[2]) // dec_slots + 1,
        ]
    )
    facts = jnp.broadcast_to(jnp.pad(facts, (0, 12))[None, :], (devices, 16))
    asked = [wanted_of(src_ask, src_chosen), wanted_of(dec_ask, dec_chosen), facts]
    asked = to_each(jnp.concatenate(asked, 1).astype(jnp.int32))
    facts = asked[:, src_slots + dec_slots :]
    count = jnp.sum(facts[:, 0]).astype(f32)
    cut = -(-(span * 3 // 8) // 128) * 128
    more = jnp.max(facts[:, 1]) > cut
    src_rounds, dec_rounds = jnp.max(facts[:, 2]), jnp.max(facts[:, 3])
    src_maps = maps_of(src_chosen, asked[:, :src_slots])
    src_found = fetch(src_maps)
    dec_maps = maps_of(dec_chosen, asked[:, src_slots : src_slots + dec_slots])
    dec_rows = send_rows(dec_maps[1])

    starts_at = jnp.cumsum(counts) - counts
    total = jnp.sum(counts)
    rank = jnp.where(masked, jnp.cumsum(masked.astype(jnp.int32), -1) - 1, -1)
    slot_of = jnp.where(masked, rank + starts_at[:, None], -1)
    slot_index = jnp.arange(seqs * span)
    slot_label = jnp.sum(
        jnp.where(slot_of.reshape(1, -1) == slot_index[:, None], labels.reshape(1, -1), 0), -1
    )
    valid = slot_index < total
    targets = jnp.where(valid, slot_label - vocab_base, -1).reshape(1, -1)
    plan = jnp.concatenate([chunk_plan(total), lax.axis_index("dp")[None] & 1]).astype(jnp.int32)
    own_rank, own_slot = pick(rank, 0, side), pick(slot_of, 0, side)

    def packing(slots, rows):
        slot, index = jnp.arange(slots), jnp.arange(rows)
        far_start, far_count = pick(starts_at, 0, 1 - side), pick(counts, 0, 1 - side)
        far = jnp.where(index < far_count, index + far_start, -1)
        return (
            (own_rank[None, :] == index[:, None]).astype(low_type),
            (own_slot[None, :] == slot[:, None]).astype(low_type),
            (far[None, :] == slot[:, None]).astype(low_type),
        )

    own_places = offset + jnp.arange(span)
    src_start, src_length = pick(src_starts, 0, row), pick(src_lengths, 0, row)
    tgt_start, tgt_length = pick(tgt_starts, 0, row), pick(tgt_lengths, 0, row)
    src_number, src_open = place_spans(src_start, own_places)
    tgt_number, tgt_open = place_spans(tgt_start, own_places)
    block = min(query_block, span)
    enc_spans = key_spans(src_number, src_start, src_length, block)
    self_spans = key_spans(tgt_number, tgt_start, tgt_length, block)
    cross_spans = key_spans(tgt_number, src_start, src_length, block)
    src_wave, tgt_wave = lax.optimization_barrier(
        (sinusoid(own_places - src_open, width), sinusoid(own_places - tgt_open, width))
    )

    root = math.sqrt(width)
    src_found = later_rounds(src_rounds, src_found, lambda turn: fetch(round_of(src_ask, turn)))
    stream0 = src_found * root + src_wave

    def norm(stream, index):
        return layer_norm(stream, gains[index], biases[index])

    def keys_of_row(part):
        if group == 1:
            return part
        return lax.all_gather(part, "seq", axis=1, tiled=True, axis_index_groups=sharers)

    def keys_to_place(part):
        if group == 1:
            return part
        return lax.psum_scatter(
            part, "seq", scatter_dimension=1, tiled=True, axis_index_groups=sharers
        )

    def self_attention(inner, weight_in, weight_out, spans):
        triple = contract(weight_in, inner, 0, 0).astype(low_type)
        keys = triple if group == 1 else keys_of_row(triple[width:])
        mixed, lse = attend_forward(triple, keys, group == 1, *spans)
        return contract(weight_out, mixed, 0, 0), (triple, keys, mixed, lse)

    def self_attention_back(inner, weight_in, weight_out, spans, kept, grad, before, after):
        triple, keys, mixed, lse = kept
        grad_low = grad.astype(low_type)
        d_out = contract(mixed, grad_low, 1, 1)
        d_mixed = contract(weight_out, grad_low, 1, 0).astype(low_type)
        d_mixed = advance(d_mixed, before)
        d_query, d_keys = attend_backward(triple, keys, group == 1, *spans, lse, d_mixed)
        d_query, d_keys = advance((d_query, d_keys), after)
        d_triple = jnp.concatenate([d_query, keys_to_place(d_keys)], 0)
        return contract(weight_in, d_triple, 1, 0), contract(inner, d_triple, 1, 1), d_out

    def cross_attention(inner, memory, weight_in, weight_out, spans):
        queries = contract(weight_in[:, :width], inner, 0, 0).astype(low_type)
        keys = keys_of_row(contract(weight_in[:, width:], memory, 0, 0).astype(low_type))
        mixed, lse = attend_forward(queries, keys, False, *spans)
        return contract(weight_out, mixed, 0, 0), (queries, keys, mixed, lse)

    def cross_attention_back(inner, memory, weight_in, weight_out, spans, kept, grad, before, after):
        queries, keys, mixed, lse = kept
        grad_low = grad.astype(low_type)
        d_out = contract(mixed, grad_low, 1, 1)
        d_mixed = contract(weight_out, grad_low, 1, 0).astype(low_type)
        d_mixed = advance(d_mixed, before)
        d_query, d_keys = attend_backward(queries, keys, False, *spans, lse, d_mixed)
        d_query, d_keys = advance((d_query, d_keys), after)
        d_keys = keys_to_place(d_keys)
        d_in = jnp.concatenate([contract(inner, d_query, 1, 1), contract(memory, d_keys, 1, 1)], 1)
        return (
            contract(weight_in[:, :width], d_query, 1, 0),
            contract(weight_in[:, width:], d_keys, 1, 0),
            d_in,
            d_out,
        )

    def ffn(inner, weight_one, weight_two):
        hidden = contract(weight_one, inner, 0, 0)
        active = jax.nn.gelu(hidden).astype(low_type)
        return contract(weight_two, active, 0, 0), (hidden, active)

    def ffn_back(inner, weight_one, weight_two, kept, grad):
        hidden, active = kept
        grad_low = grad.astype(low_type)
        d_two = contract(active, grad_low, 1, 1)
        d_active = contract(weight_two, grad_low, 1, 0)
        d_hidden = jax.vjp(jax.nn.gelu, hidden)[1](d_active)[0].astype(low_type)
        return contract(weight_one, d_hidden, 1, 0), contract(inner, d_hidden, 1, 1), d_two

    inner0, norm0 = norm(stream0, 0)
    branch0, keep0 = self_attention(inner0, w_in0, w_out0, enc_spans)
    stream1 = stream0 + branch0
    stream1, dec_rows = lax.optimization_barrier((stream1, dec_rows))
    inner1, norm1 = norm(stream1, 1)
    branch1, keep1 = ffn(inner1, f_in0, f_out0)
    stream2 = stream1 + branch1
    memory, norm2 = norm(stream2, 2)
    memory, dec_chosen = lax.optimization_barrier((memory, dec_maps[0]))
    dec_found = contract(dec_rows, dec_chosen, 0, 1)
    dec_found = later_rounds(dec_rounds, dec_found, lambda turn: fetch(round_of(dec_ask, turn)))
    target0 = dec_found * root + tgt_wave
    inner3, norm3 = norm(target0, 3)
    branch3, keep3 = self_attention(inner3, w_in1, w_out1, self_spans)
    target1 = target0 + branch3
    inner4, norm4 = norm(target1, 4)
    branch4, keep4 = cross_attention(inner4, memory, w_in2, w_out2, cross_spans)
    target2 = target1 + branch4
    inner5, norm5 = norm(target2, 5)
    branch5, keep5 = ffn(inner5, f_in1, f_out1)
    target3 = target2 + branch5
    final, norm6 = norm(target3, 6)

    def pack(slots, rows):
        own_chosen, own_slots, far_slots = packing(slots, rows)
        far = swap(contract(own_chosen, final, 1, 1).astype(low_type), "seq", 1)
        packed = contract(own_slots, final, 1, 1) + contract(far_slots, far, 1, 0)
        return jnp.pad(packed.astype(low_type), ((0, seqs * span - slots), (0, 0)))

    def unpack(slots, rows):
        own_chosen, own_slots, far_slots = packing(slots, rows)
        high = lax.reduce_precision(d_pieces[:slots], 8, 7)
        rest = (d_pieces[:slots] - high).astype(low_type)
        high = high.astype(low_type)
        far = swap(contract(far_slots, high, 0, 0).astype(low_type), "seq", 1)
        return (
            contract(high, own_slots, 0, 0)
            + contract(rest, own_slots, 0, 0)
            + contract(far, own_chosen, 0, 0)
        )

    if seqs == 2:
        pieces = lax.cond(
            more, lambda: pack(2 * span, span), lambda: pack(min(2 * cut, 2 * span), cut)
        )
    else:
        own_slots = packing(seqs * span, span)[1]
        pieces = lax.psum(contract(own_slots, final, 1, 1), "seq").astype(low_type)
    turned = pieces.T
    every = gather_seq(head_stats(plan, table_part, turned), 0)
    top_logit = jnp.max(every[:, 0], 0)
    totals = jnp.sum(every[:, 1] * jnp.exp(every[:, 0] - top_logit[None]), 0)
    log_total = top_logit + jnp.log(jnp.where(valid, totals, 1.0))
    own_start = pick(starts_at, 0, side)
    mine = (slot_index >= own_start) & (slot_index < own_start + pick(counts, 0, side))
    token_local = jnp.sum(jnp.where(mine, log_total, 0.0))
    logs = jnp.where(valid, log_total + jnp.log(count), 1e30)
    weights = jnp.where(valid, 1.0 / count, 0.0)
    split = halving_fits(own_words, width // 2, False)
    *d_table, d_pieces, picks = head_back(
        plan, table_part, pieces, turned, targets, logs[None], weights[None], split and own_words
    )
    token_local = token_local - jnp.sum(picks)
    table_one = [TableChain(d_table[0], d_table[2])] if split else []
    if seqs == 2:
        d_final = lax.cond(
            more, lambda: unpack(2 * span, span), lambda: unpack(min(2 * cut, 2 * span), cut)
        )
    else:
        d_pieces = lax.psum(d_pieces, "seq")
        high = lax.reduce_precision(d_pieces, 8, 7)
        rest = (d_pieces - high).astype(low_type)
        d_final = contract(high.astype(low_type), own_slots, 0, 0) + contract(rest, own_slots, 0, 0)

    first_place = own_places[None, :] == src_start[:, None]
    mine = jnp.any(first_place, -1)
    first_rows = contract(first_place.astype(low_type), memory, 1, 1).astype(low_type)
    len_logits = contract(first_rows, w_len, 1, 0)
    len_label = jnp.minimum(tgt_length, classes - 1)
    len_hot = jnp.arange(classes)[None, :] == len_label[:, None]
    len_loss = jax.nn.logsumexp(len_logits, -1) - jnp.sum(jnp.where(len_hot, len_logits, 0.0), -1)
    len_local = jnp.sum(jnp.where(mine, len_loss, 0.0))
    sentences = rows_here * src_lengths.shape[1] * owners
    len_prob = jax.nn.softmax(len_logits, -1)
    d_len_logits = (
        jnp.where(mine[:, None], len_prob - len_hot.astype(f32), 0.0) * (0.1 / sentences)
    ).astype(low_type)
    d_w_len = contract(first_rows, d_len_logits, 0, 0)
    d_first = contract(d_len_logits, w_len, 1, 1)
    d_memory = lax.dot_general(
        d_first,
        first_place.astype(f32),
        (((0,), (0,)), ((), ())),
        precision=lax.Precision.HIGHEST,
        preferred_element_type=f32,
    )

    def owned(grad):
        return grad.reshape(owners, -1, grad.shape[1])

    def owned_columns(grad):
        whole = owned(grad)
        return [whole[:, at : at + share] for at in range(0, whole.shape[1], share)]

    d_target3, scale6 = norm_backward(norm6, gains[6], d_final)
    d_inner5, d_fin1, d_fout1 = ffn_back(inner5, f_in1, f_out1, keep5, d_target3)
    d_inner5, d_target3, d_table = advance((d_inner5, d_target3, d_table), table_one)
    table_two = [TableChain(d_table[1], d_table[3])] if split else []
    chain_a = LayerChain([owned(d_fin1)] + owned_columns(d_fout1))
    d_target2, scale5 = norm_backward(norm5, gains[5], d_inner5, d_target3)
    d_inner4, d_cross, d_win2, d_wout2 = cross_attention_back(
        inner4, memory, w_in2, w_out2, cross_spans, keep4, d_target2, [], table_one + [chain_a]
    )
    chain_b = LayerChain([owned(d_win2), owned(d_wout2)])
    d_target1, scale4 = norm_backward(norm4, gains[4], d_inner4, d_target2)
    d_inner3, d_win1, d_wout1 = self_attention_back(
        inner3,
        w_in1,
        w_out1,
        self_spans,
        keep3,
        d_target1,
        table_two,
        table_one + [chain_a, chain_b],
    )
    chain_c = LayerChain([owned(d_win1), owned(d_wout1)])
    d_target0, scale3 = norm_backward(norm3, gains[3], d_inner3, d_target1)
    d_stream2, scale2 = norm_backward(norm2, gains[2], d_memory + d_cross)
    d_stream2, d_target0 = advance((d_stream2, d_target0), [chain_b])
    dec_grad = d_target0 * root
    dec_sums = give_rows(dec_maps[0], dec_grad)
    d_inner1, d_fin0, d_fout0 = ffn_back(inner1, f_in0, f_out0, keep1, d_stream2)
    chains = table_one + table_two + [chain_a, chain_c]
    d_inner1, d_stream2 = advance((d_inner1, d_stream2), chains)
    chain_d = LayerChain([owned(d_fin0)] + owned_columns(d_fout0))
    d_stream1, scale1 = norm_backward(norm1, gains[1], d_inner1, d_stream2)
    d_inner0, d_win0, d_wout0 = self_attention_back(
        inner0,
        w_in0,
        w_out0,
        enc_spans,
        keep0,
        d_stream1,
        [chain_b, chain_c, chain_d],
        table_two + [chain_a, chain_c, chain_d],
    )
    chain_e = LayerChain([owned(d_win0), owned(d_wout0), owned(d_w_len)])
    d_stream0, scale0 = norm_backward(norm0, gains[0], d_inner0, d_stream1)
    late = table_two + [chain_b, chain_c, chain_d, chain_e]
    d_stream0, dec_sums = advance((d_stream0, dec_sums), late)
    src_grad = d_stream0 * root
    src_sums = give_rows(src_maps[0], src_grad)
    norm_share = norms.shape[2]
    scales = jnp.stack([scale0, scale1, scale2, scale3, scale4, scale5, scale6], 1)
    scales = scales.reshape(2 * norm_count, owners, norm_share).transpose(1, 0, 2)
    scales = jnp.broadcast_to(scales[None], (seqs,) + scales.shape)
    scales = to_each(scales.reshape((devices,) + scales.shape[2:]))
    chains = table_one + table_two + [chain_a, chain_b, chain_c, chain_d, chain_e]
    advance((), chains)
    src_sums, scales = advance((src_sums, scales), chains)
    while any(chain.pending is not None for chain in chains):
        advance((), chains)
    layer_chains = [chain_a, chain_b, chain_c, chain_d, chain_e]
    for chain in layer_chains:
        chain.finish()

    g_norms = jnp.sum(scales, 0)
    norm_square = jnp.where(side == 0, jnp.sum(g_norms * g_norms), 0.0)
    given = contract(dec_maps[1], dec_sums, 0, 0) + contract(src_maps[1], src_sums, 0, 0)
    given = later_rounds(
        jnp.maximum(src_rounds, dec_rounds),
        given,
        lambda turn: give(round_of(dec_ask, turn), dec_grad)
        + give(round_of(src_ask, turn), src_grad),
    )
    if split:
        table_grad = jnp.concatenate([chain.value for chain in table_one + table_two], 1)
    else:
        table_grad = lax.psum_scatter(d_table[0], "dp", scatter_dimension=0, tiled=True)
    table_grad = table_grad + given
    square = sum(chain.square for chain in layer_chains)
    square = square + jnp.sum(table_grad * table_grad) + norm_square
    sums = jnp.pad(jnp.stack([token_local, len_local, square]), (0, 5))
    sums = jnp.sum(to_each(jnp.broadcast_to(sums[None], (devices, 8))), 0)
    token_sum, len_sum, grad_norm = sums[0], sums[1], jnp.sqrt(sums[2])
    factor = jnp.minimum(1.0, clip_limit / (grad_norm + 1e-06))

    def cut_columns(chain, sizes):
        result, at = [], 0
        value = chain.value.reshape(share, -1)
        for size in sizes:
            result.append(value[:, at : at + size])
            at += size
        return result

    hidden_width = ffn_in.shape[2]
    ffn_sizes = [hidden_width] + [width] * out_pieces
    attn_sizes = [3 * width, width]
    g_fin1, *g_fout1 = cut_columns(chain_a, ffn_sizes)
    g_win2, g_wout2 = cut_columns(chain_b, attn_sizes)
    g_win1, g_wout1 = cut_columns(chain_c, attn_sizes)
    g_fin0, *g_fout0 = cut_columns(chain_d, ffn_sizes)
    g_win0, g_wout0, g_len = cut_columns(chain_e, attn_sizes + [classes])
    grads = (
        jnp.stack([g_win0, g_win1, g_win2]),
        jnp.stack([g_wout0, g_wout1, g_wout2]),
        jnp.stack([g_fin0, g_fin1]),
        jnp.stack([jnp.concatenate(g_fout0, 0), jnp.concatenate(g_fout1, 0)]),
        g_len,
        g_norms.reshape(norms.shape),
        table_grad,
    )
    masters = (attn_in, attn_out, ffn_in, ffn_out, len_head, norms, table)
    firsts = (attn_in_m1, attn_out_m1, ffn_in_m1, ffn_out_m1, len_head_m1, norms_m1, table_m1)
    seconds = (attn_in_m2, attn_out_m2, ffn_in_m2, ffn_out_m2, len_head_m2, norms_m2, table_m2)
    updates = []
    for weight, first, second, grad, rate in zip(masters, firsts, seconds, grads, step_rates):
        updates.extend(adam_update(weight, first, second, grad * factor, rate))
    return (token_sum, count, len_sum, grad_norm, *updates)


def solution(mesh):
    layer, head, scales, words = P(None, "dp", None), P("dp", None), P(None, None, "dp"), P(("seq", "dp"), None)
    owned = (layer,) * 12 + (head,) * 3 + (scales,) * 3 + (words,) * 3
    ids, lengths = P("dp", "seq"), P("dp", None)
    in_specs = (ids, ids, lengths, lengths, ids) + owned
    out_specs = (P(), P(), P(), P()) + owned
    return jax.shard_map(
        on_device, mesh=mesh, in_specs=in_specs, out_specs=out_specs, check_vma=False
    )
```

```python
import functools
import math

import jax
import jax.numpy as jnp
from jax import lax
from jax.experimental import pallas as pl
from jax.experimental.pallas import tpu as pltpu
from jax.sharding import PartitionSpec as P

HEADS = 8
STEP = 10


length_token = 1
mask_token = 2
clip_limit = 0.002
beta_one = 0.9
beta_two = 0.98
adam_eps = 1e-08
weight_decay = 0.01
step_rates = (0.05, 0.25, 0.05, 0.025, 0.05, 0.5, 0.1)

low_type = jnp.bfloat16
f32 = jnp.float32
query_block = 256
key_block = 128
place_block = 512
vmem_bytes = 56 * 1024 * 1024


def sinusoid(positions, width):
    half_width = width // 2
    frequency = jnp.exp(jnp.arange(half_width).astype(f32) * (-math.log(10000.0) / half_width))
    angles = frequency[:, None] * positions.astype(f32)[None, :]
    return jnp.concatenate([jnp.sin(angles), jnp.cos(angles)], 0)


def layer_norm(stream, norm_gain, norm_bias):
    average = jnp.mean(stream, 0, keepdims=True)
    centred = stream - average
    variance = jnp.mean(centred * centred, 0, keepdims=True)
    inverse = lax.rsqrt(variance + 1e-05)
    normed = centred * inverse * norm_gain[:, None] + norm_bias[:, None]
    return normed.astype(low_type), (stream, average, inverse)


def contract(left, right, left_dim, right_dim):
    return lax.dot_general(
        left, right, (((left_dim,), (right_dim,)), ((), ())), preferred_element_type=f32
    )


def attend_forward_kernel(bounds, q_ref, k_ref, v_ref, span_ref, out_ref, lse_ref, hold, *, head):
    step = pl.program_id(0)
    first, last = bounds[0, step], bounds[1, step]
    width, queries = q_ref.shape
    heads = width // head
    scale = head**-0.5
    low, high = span_ref[0:1, :], span_ref[1:2, :]
    inner = lax.broadcasted_iota(jnp.int32, (key_block, queries), 0)

    def fold(values, op):
        return op(values.reshape(key_block // 8, 8, queries), axis=0)

    def score(block, tops):
        start = pl.multiple_of(block * key_block, key_block)
        place = inner + start
        allowed = (place >= low) & (place < high)
        result = []
        for h in range(heads):
            rows = slice(h * head, (h + 1) * head)
            s = contract(k_ref[rows, pl.ds(start, key_block)], q_ref[rows, :], 0, 0) * scale
            s = jnp.where(allowed, s, -1e30)
            hold[h, pl.ds(start, key_block), :] = s
            result.append(jnp.maximum(tops[h], fold(s, jnp.max)))
        return tuple(result)

    tops = lax.fori_loop(
        first, last, score, tuple(jnp.full((8, queries), -1e30, f32) for _ in range(heads))
    )
    tops = [jnp.max(t, axis=0, keepdims=True) for t in tops]

    def power(block, sums):
        start = pl.multiple_of(block * key_block, key_block)
        result = []
        for h in range(heads):
            e = jnp.exp(hold[h, pl.ds(start, key_block), :] - tops[h])
            hold[h, pl.ds(start, key_block), :] = e
            result.append(sums[h] + fold(e, jnp.sum))
        return tuple(result)

    sums = lax.fori_loop(
        first, last, power, tuple(jnp.zeros((8, queries), f32) for _ in range(heads))
    )
    sums = [jnp.maximum(jnp.sum(t, axis=0, keepdims=True), 1e-30) for t in sums]
    inverse = [1.0 / t for t in sums]

    def mix(block, outs):
        start = pl.multiple_of(block * key_block, key_block)
        result = []
        for h in range(heads):
            rows = slice(h * head, (h + 1) * head)
            p = (hold[h, pl.ds(start, key_block), :] * inverse[h]).astype(low_type)
            result.append(outs[h] + contract(v_ref[rows, pl.ds(start, key_block)], p, 1, 0))
        return tuple(result)

    outs = lax.fori_loop(
        first, last, mix, tuple(jnp.zeros((head, queries), f32) for _ in range(heads))
    )
    for h in range(heads):
        out_ref[h * head : (h + 1) * head, :] = outs[h].astype(low_type)
        lse_ref[h : h + 1, :] = tops[h] + jnp.log(sums[h])


def attend_backward_kernel(
    bounds, q_ref, k_ref, v_ref, span_ref, lse_ref, do_ref, dq_ref, dkv_ref, p_hold, d_hold, acc,
    *, head
):
    step = pl.program_id(0)
    first, last = bounds[0, step], bounds[1, step]
    width, queries = q_ref.shape
    heads = width // head
    scale = head**-0.5
    low, high = span_ref[0:1, :], span_ref[1:2, :]
    inner = lax.broadcasted_iota(jnp.int32, (key_block, queries), 0)

    @pl.when(step == 0)
    def _():
        acc[...] = jnp.zeros_like(acc)

    def one(block, deltas):
        start = pl.multiple_of(block * key_block, key_block)
        keys = pl.ds(start, key_block)
        place = inner + start
        allowed = (place >= low) & (place < high)
        result = []
        for h in range(heads):
            rows = slice(h * head, (h + 1) * head)
            s = contract(k_ref[rows, keys], q_ref[rows, :], 0, 0) * scale
            p = jnp.exp(jnp.where(allowed, s, -1e30) - lse_ref[h : h + 1, :])
            dp = contract(v_ref[rows, keys], do_ref[rows, :], 0, 0)
            p_hold[h, keys, :] = p
            d_hold[h, keys, :] = dp
            result.append(
                deltas[h] + jnp.sum((p * dp).reshape(key_block // 8, 8, queries), axis=0)
            )
            below = slice(width + h * head, width + (h + 1) * head)
            acc[below, keys] += contract(do_ref[rows, :], p.astype(low_type), 1, 1)
        return tuple(result)

    deltas = lax.fori_loop(
        first, last, one, tuple(jnp.zeros((8, queries), f32) for _ in range(heads))
    )
    deltas = [jnp.sum(t, axis=0, keepdims=True) for t in deltas]

    def two(block, outs):
        start = pl.multiple_of(block * key_block, key_block)
        keys = pl.ds(start, key_block)
        result = []
        for h in range(heads):
            rows = slice(h * head, (h + 1) * head)
            ds = (p_hold[h, keys, :] * (d_hold[h, keys, :] - deltas[h])).astype(low_type)
            result.append(outs[h] + contract(k_ref[rows, keys], ds, 1, 0))
            acc[rows, keys] += contract(q_ref[rows, :], ds, 1, 1) * scale
        return tuple(result)

    outs = lax.fori_loop(
        first, last, two, tuple(jnp.zeros((head, queries), f32) for _ in range(heads))
    )
    for h in range(heads):
        dq_ref[h * head : (h + 1) * head, :] = (outs[h] * scale).astype(low_type)

    @pl.when(step == pl.num_programs(0) - 1)
    def _():
        dkv_ref[...] = acc[...].astype(low_type)


def attend_specs(width, length, block, shared):
    key_row = 1 if shared else 0
    return [
        pl.BlockSpec((width, block), lambda i, *_: (0, i)),
        pl.BlockSpec((width, length), lambda i, *_: (key_row, 0)),
        pl.BlockSpec((width, length), lambda i, *_: (key_row + 1, 0)),
        pl.BlockSpec((2, block), lambda i, *_: (0, i)),
    ]


def attend_forward(queries, keys, shared, spans, bounds):
    width = keys.shape[0] // (3 if shared else 2)
    places, length = queries.shape[1], keys.shape[1]
    block = min(query_block, places)
    return pl.pallas_call(
        functools.partial(attend_forward_kernel, head=width // HEADS),
        grid_spec=pltpu.PrefetchScalarGridSpec(
            num_scalar_prefetch=1,
            grid=(places // block,),
            in_specs=attend_specs(width, length, block, shared),
            out_specs=[
                pl.BlockSpec((width, block), lambda i, *_: (0, i)),
                pl.BlockSpec((HEADS, block), lambda i, *_: (0, i)),
            ],
            scratch_shapes=[pltpu.VMEM((HEADS, length, block), f32)],
        ),
        out_shape=[
            jax.ShapeDtypeStruct((width, places), low_type),
            jax.ShapeDtypeStruct((HEADS, places), f32),
        ],
        compiler_params=pltpu.CompilerParams(vmem_limit_bytes=vmem_bytes),
        name="attend_forward",
    )(bounds, queries, keys, keys, spans)


def attend_backward(queries, keys, shared, spans, bounds, lse, d_mixed):
    width = keys.shape[0] // (3 if shared else 2)
    places, length = queries.shape[1], keys.shape[1]
    block = min(query_block, places)
    return pl.pallas_call(
        functools.partial(attend_backward_kernel, head=width // HEADS),
        grid_spec=pltpu.PrefetchScalarGridSpec(
            num_scalar_prefetch=1,
            grid=(places // block,),
            in_specs=attend_specs(width, length, block, shared)
            + [
                pl.BlockSpec((HEADS, block), lambda i, *_: (0, i)),
                pl.BlockSpec((width, block), lambda i, *_: (0, i)),
            ],
            out_specs=[
                pl.BlockSpec((width, block), lambda i, *_: (0, i)),
                pl.BlockSpec((2 * width, length), lambda i, *_: (0, 0)),
            ],
            scratch_shapes=[
                pltpu.VMEM((HEADS, length, block), f32),
                pltpu.VMEM((HEADS, length, block), f32),
                pltpu.VMEM((2 * width, length), f32),
            ],
        ),
        out_shape=[
            jax.ShapeDtypeStruct((width, places), low_type),
            jax.ShapeDtypeStruct((2 * width, length), low_type),
        ],
        compiler_params=pltpu.CompilerParams(vmem_limit_bytes=vmem_bytes),
        name="attend_backward",
    )(bounds, queries, keys, keys, spans, lse, d_mixed)


def norm_back_kernel(stream_ref, average_ref, inverse_ref, gain_ref, grad_ref, *refs):
    (*rest_refs, out_ref, sums_ref, parts) = refs

    @pl.when(pl.program_id(0) == 0)
    def _():
        parts[...] = jnp.zeros_like(parts)

    inverse, grad = inverse_ref[...], grad_ref[...]
    unit = (stream_ref[...] - average_ref[...]) * inverse
    width, places = grad.shape
    scaled = grad * gain_ref[...]
    along = jnp.mean(scaled * unit, 0, keepdims=True)
    level = jnp.mean(scaled, 0, keepdims=True)
    out = (scaled - level - unit * along) * inverse
    for rest_ref in rest_refs:
        out = out + rest_ref[...]
    out_ref[...] = out
    weighted = grad * unit
    for at in range(0, places, 128):
        parts[0] += weighted[:, at : at + 128]
        parts[1] += grad[:, at : at + 128]

    @pl.when(pl.program_id(0) == pl.num_programs(0) - 1)
    def _():
        sums_ref[...] = jnp.sum(parts[...], 2, keepdims=True)


def norm_backward(kept, gain, grad, *rests):
    stream, average, inverse = kept
    width, places = stream.shape
    columns = min(256, places)
    block = pl.BlockSpec((width, columns), lambda i: (0, i))
    row = pl.BlockSpec((1, columns), lambda i: (0, i))
    out, sums = pl.pallas_call(
        norm_back_kernel,
        grid=(places // columns,),
        in_specs=[block, row, row, pl.BlockSpec((width, 1), lambda i: (0, 0)), block]
        + [block] * len(rests),
        out_specs=[block, pl.BlockSpec((2, width, 1), lambda i: (0, 0, 0))],
        out_shape=[
            jax.ShapeDtypeStruct((width, places), f32),
            jax.ShapeDtypeStruct((2, width, 1), f32),
        ],
        scratch_shapes=[pltpu.VMEM((2, width, 128), f32)],
        compiler_params=pltpu.CompilerParams(vmem_limit_bytes=vmem_bytes),
        name="norm_backward",
    )(stream, average, inverse, gain[:, None], grad, *rests)
    return out, sums[:, :, 0]


def chunk_plan(total):
    quarter = place_block // 4
    units = (jnp.maximum(total - place_block, 0) + quarter - 1) // quarter
    left = units % 4
    wides = units // 4 + (left == 3).astype(jnp.int32)
    return jnp.stack([wides, left == 2, left == 1]).astype(jnp.int32)


def each_chunk(plan, visit):
    visit(0, place_block, True)

    def wide(index, carry):
        visit(pl.multiple_of((index + 1) * place_block, place_block), place_block, False)
        return carry

    lax.fori_loop(0, plan[0], wide, 0)
    after = pl.multiple_of((plan[0] + 1) * place_block, place_block)
    for index, share in ((1, 2), (2, 4)):

        @pl.when(plan[index] > 0)
        def _(share=share):
            visit(after, place_block // share, False)


def parts_of(words):
    for count in (5, 4, 2):
        if words % (16 * count) == 0:
            return [slice(i * (words // count), (i + 1) * (words // count)) for i in range(count)]
    return [slice(0, words)]


def head_stats_kernel(plan, table_ref, turned_ref, stats_ref, tops, sums):
    step = pl.program_id(0)

    @pl.when(step == 0)
    def _():
        tops[...] = jnp.full_like(tops, -1e30)
        sums[...] = jnp.zeros_like(sums)

    def visit(start, size, first):
        here = pl.ds(start, size)
        turned = turned_ref[:, here]
        old, total = tops[:, here], sums[:, here]
        for part in parts_of(table_ref.shape[0]):
            logits = contract(table_ref[part, :], turned, 1, 0)
            logits = logits.reshape(logits.shape[0] // 8, 8, size)
            top = jnp.maximum(old, jnp.max(logits, axis=0))
            powers = jnp.sum(jnp.exp(logits - top[None]), axis=0)
            total = total * jnp.exp(old - top) + powers
            old = top
        sums[:, here] = total
        tops[:, here] = old

    each_chunk(plan, visit)

    @pl.when(step == pl.num_programs(0) - 1)
    def _():
        top = jnp.max(tops[...], axis=0, keepdims=True)
        stats_ref[0:1, :] = top
        stats_ref[1:2, :] = jnp.sum(sums[...] * jnp.exp(tops[...] - top), axis=0, keepdims=True)


def head_back_kernel(
    plan, table_ref, rows_ref, turned_ref, target_ref, log_ref, weight_ref, *refs, owned
):
    (*out_refs, dr_ref, pick_ref, acc) = refs
    step = pl.program_id(0)
    words, width = table_ref.shape

    @pl.when(step == 0)
    def _():
        dr_ref[...] = jnp.zeros_like(dr_ref)
        pick_ref[...] = jnp.zeros_like(pick_ref)

    def visit(start, size, first):
        here = pl.ds(start, size)
        rows, turned = rows_ref[here, :], turned_ref[:, here]
        target = target_ref[:, here] - step * words
        log, weight = log_ref[:, here], weight_ref[:, here]
        found = jnp.zeros((8, size), f32)
        for part in parts_of(words):
            block = table_ref[part, :]
            count = block.shape[0]
            inner = lax.broadcasted_iota(jnp.int32, (count, size), 0) + part.start
            logits = contract(block, turned, 1, 0)
            scaled = jnp.exp(logits - log)
            hit = inner == target
            found += jnp.sum(jnp.where(hit, logits, 0.0).reshape(count // 8, 8, size), axis=0)
            d_logits = jnp.where(hit, scaled - weight, scaled).astype(low_type)
            if first:
                acc[part, :] = contract(d_logits, rows, 1, 0)
            else:
                acc[part, :] += contract(d_logits, rows, 1, 0)
            dr_ref[here, :] += contract(d_logits, block, 0, 0)
        pick_ref[:, here] += found

    each_chunk(plan, visit)
    if not owned:
        out_refs[0][...] = acc[...]
        return
    mine = plan[3]
    keep = pl.ds(pl.multiple_of(mine * owned, 8), owned)
    away = pl.ds(pl.multiple_of((1 - mine) * owned, 8), owned)
    half = width // 2
    out_refs[0][0] = acc[keep, :half]
    out_refs[1][0] = acc[keep, half:]
    out_refs[2][0] = acc[away, :half].astype(low_type)
    out_refs[3][0] = acc[away, half:].astype(low_type)


def word_block(words):
    return max(n for n in range(16, 1601, 16) if words % n == 0)


def head_stats(plan, table_part, turned):
    words = word_block(table_part.shape[0])
    width, places = turned.shape
    return pl.pallas_call(
        head_stats_kernel,
        grid_spec=pltpu.PrefetchScalarGridSpec(
            num_scalar_prefetch=1,
            grid=(table_part.shape[0] // words,),
            in_specs=[
                pl.BlockSpec((words, width), lambda i, *_: (i, 0)),
                pl.BlockSpec((width, places), lambda i, *_: (0, 0)),
            ],
            out_specs=pl.BlockSpec((2, places), lambda i, *_: (0, 0)),
            scratch_shapes=[pltpu.VMEM((8, places), f32) for _ in range(2)],
        ),
        out_shape=jax.ShapeDtypeStruct((2, places), f32),
        compiler_params=pltpu.CompilerParams(vmem_limit_bytes=vmem_bytes),
        name="head_stats",
    )(plan, table_part, turned)


def head_back(plan, table_part, rows, turned, targets, logs, weights, owned):
    total = table_part.shape[0]
    words = 2 * owned if owned else word_block(total)
    places, width = rows.shape
    row = pl.BlockSpec((1, places), lambda i, *_: (0, 0))
    if owned:
        out_specs = [pl.BlockSpec((1, owned, width // 2), lambda i, *_: (i, 0, 0))] * 4
        shape = (total // words, owned, width // 2)
        out_shape = [jax.ShapeDtypeStruct(shape, t) for t in (f32, f32, low_type, low_type)]
    else:
        out_specs = [pl.BlockSpec((words, width), lambda i, *_: (i, 0))]
        out_shape = [jax.ShapeDtypeStruct((total, width), f32)]
    return pl.pallas_call(
        functools.partial(head_back_kernel, owned=owned),
        grid_spec=pltpu.PrefetchScalarGridSpec(
            num_scalar_prefetch=1,
            grid=(total // words,),
            in_specs=[
                pl.BlockSpec((words, width), lambda i, *_: (i, 0)),
                pl.BlockSpec((places, width), lambda i, *_: (0, 0)),
                pl.BlockSpec((width, places), lambda i, *_: (0, 0)),
                row,
                row,
                row,
            ],
            out_specs=out_specs
            + [
                pl.BlockSpec((places, width), lambda i, *_: (0, 0)),
                pl.BlockSpec((8, places), lambda i, *_: (0, 0)),
            ],
            scratch_shapes=[pltpu.VMEM((words, width), f32)],
        ),
        out_shape=out_shape
        + [
            jax.ShapeDtypeStruct((places, width), f32),
            jax.ShapeDtypeStruct((8, places), f32),
        ],
        compiler_params=pltpu.CompilerParams(vmem_limit_bytes=vmem_bytes),
        name="head_back",
    )(plan, table_part, rows, turned, targets, logs, weights)


def swap(values, axis, bit):
    size = lax.axis_size(axis)
    return lax.ppermute(values, axis, [(i, i ^ bit) for i in range(size)])


def power_of_two(size):
    return size & (size - 1) == 0


def pick(values, dim, index):
    return lax.dynamic_index_in_dim(values, index, dim, False)


def gather_seq(values, dim):
    if lax.axis_size("seq") == 2:
        other = swap(values, "seq", 1)
        first = lax.axis_index("seq") == 0
        return jnp.stack([jnp.where(first, values, other), jnp.where(first, other, values)], dim)
    return lax.all_gather(values, "seq", axis=dim)


def to_each(values):
    return lax.all_to_all(values, ("seq", "dp"), 0, 0)


def halving_fits(rows, columns, joint):
    owners, seqs = lax.axis_size("dp"), lax.axis_size("seq")
    fits = power_of_two(owners) and owners > 2 and columns % 128 == 0
    return fits and (rows % 16 == 0 and seqs == 2 if joint else rows % 8 == 0)


class Chain:
    pending = value = square = None

class LayerChain(Chain):
    def __init__(self, parts):
        self.parts, self.step = parts, 0
        self.rows = parts[0].shape[1]
        self.fast = halving_fits(self.rows, parts[0].shape[2], True)
        if self.fast:
            self.launch()

    def launch(self):
        owners = lax.axis_size("dp")
        if self.step == 4:
            return
        if self.step == 3:
            self.pending = swap(self.part, "seq", 1)
        elif self.step == 2:
            groups = [list(range(core, owners, 2)) for core in range(2)]
            whole = (self.part + self.got.astype(f32)).astype(low_type)
            self.pending = lax.all_to_all(whole, "dp", 0, 0, axis_index_groups=groups)
        else:
            axis = ("dp", "seq")[self.step]
            mine = lax.axis_index(axis) & 1
            if self.step == 1:
                self.rows //= 2

            def half(side):
                if self.step == 0:
                    shape = (owners // 2, 2, self.rows)
                    parts = [part.reshape(shape + part.shape[2:]) for part in self.parts]
                    return jnp.concatenate([pick(part, 1, side) for part in parts], 2)
                shape = (owners // 2, 2, self.rows, -1)
                first, second = self.part.reshape(shape), self.got.reshape(shape)
                return pick(first, 1, side) + pick(second, 1, side).astype(f32)

            away = half(1 - mine).astype(low_type)
            self.part = half(mine)
            self.pending = swap(away, axis, 1)

    def absorb(self, got):
        self.pending = None
        self.step += 1
        if self.step < 3:
            self.got = got
        elif self.step == 3:
            self.part = jnp.sum(got.astype(f32), 0)
            self.square = jnp.sum(self.part * self.part)
        else:
            first = lax.axis_index("seq") == 0
            part = self.part
            self.value = jnp.concatenate(
                [jnp.where(first, part, got), jnp.where(first, got, part)], 0
            )

    def finish(self):
        if not self.fast:
            whole = jnp.concatenate(self.parts, 2)
            part = lax.psum(lax.psum_scatter(whole, "dp", scatter_dimension=0), "seq")
            self.value = part
            self.square = jnp.where(lax.axis_index("seq") == 0, jnp.sum(part * part), 0.0)


class TableChain(Chain):
    def __init__(self, keep, away):
        self.part, self.got = keep, None
        self.rows, self.bit = keep.shape[1], 2
        self.pending = swap(away, "dp", 1)

    def launch(self):
        if self.bit == lax.axis_size("dp"):
            return
        mine = (lax.axis_index("dp") // self.bit) & 1
        shape = (-1, 2, self.rows, self.part.shape[2])
        first, second = self.part.reshape(shape), self.got.reshape(shape)

        def half(side):
            return pick(first, 1, side) + pick(second, 1, side).astype(f32)

        away = half(1 - mine).astype(low_type)
        self.part = half(mine)
        self.pending = swap(away, "dp", self.bit)
        self.bit *= 2

    def absorb(self, got):
        self.pending, self.got = None, got
        if self.bit == lax.axis_size("dp"):
            self.value = (self.part + got.astype(f32)).reshape(self.rows, -1)


def advance(main, chains):
    live = [chain for chain in chains if chain.pending is not None]
    main, got = lax.optimization_barrier((main, [chain.pending for chain in live]))
    for chain, arrived in zip(live, got):
        chain.absorb(arrived)
    for chain in live:
        chain.launch()
    return main


def adam_update(weight, first, second, grad, rate):
    first = beta_one * first + (1 - beta_one) * grad
    second = beta_two * second + (1 - beta_two) * grad * grad
    first_hat = first / (1 - beta_one**STEP)
    second_hat = second / (1 - beta_two**STEP)
    weight = weight - rate * (first_hat / (jnp.sqrt(second_hat) + adam_eps) + weight_decay * weight)
    return (weight, first, second)


def place_spans(starts, places):
    covered = places[:, None] >= starts[None, :]
    number = jnp.sum(covered.astype(jnp.int32), -1) - 1
    return number, jnp.max(jnp.where(covered, starts[None, :], 0), -1)


def key_spans(number, starts, lengths, block):
    hot = number[:, None] == jnp.arange(starts.shape[0])[None, :]
    first = jnp.sum(jnp.where(hot, starts[None, :], 0), -1)
    last = jnp.sum(jnp.where(hot, (starts + lengths)[None, :], 0), -1)
    first_block = jnp.min(first.reshape(-1, block), -1) // key_block
    last_block = (jnp.max(last.reshape(-1, block), -1) + key_block - 1) // key_block
    return (
        jnp.stack([first, last]).astype(jnp.int32),
        jnp.stack([first_block, last_block]).astype(jnp.int32),
    )


def on_device(
    src_ids,
    tgt_ids,
    src_lengths,
    tgt_lengths,
    tgt_mask,
    attn_in,
    attn_in_m1,
    attn_in_m2,
    attn_out,
    attn_out_m1,
    attn_out_m2,
    ffn_in,
    ffn_in_m1,
    ffn_in_m2,
    ffn_out,
    ffn_out_m1,
    ffn_out_m2,
    len_head,
    len_head_m1,
    len_head_m2,
    norms,
    norms_m1,
    norms_m2,
    table,
    table_m1,
    table_m2,
):
    rows_here, seq_rows = src_ids.shape
    seqs, owners = lax.axis_size("seq"), lax.axis_size("dp")
    devices = seqs * owners
    row_len = seq_rows * seqs
    side = lax.axis_index("seq")
    group = seqs // rows_here
    span = row_len // group
    row, offset = side // group, (side % group) * span
    sharers = [[r * group + i for i in range(group)] for r in range(rows_here)]
    own_words, width = table.shape
    classes = len_head.shape[1]
    vocab_width = own_words * owners
    vocab_base = side * vocab_width
    norm_count = norms.shape[1]
    norm_columns = 128

    def columns_of(weight, rows):
        return [weight[at : at + rows] for at in range(0, weight.shape[0], rows)]

    def cut_parts(whole, parts):
        result, at = [], 0
        for part in parts:
            result.append(whole[:, at : at + part.shape[1]])
            at += part.shape[1]
        return result

    def gather_columns(parts):
        joined = jnp.concatenate([part.astype(low_type) for part in parts], 1)
        if joined.shape[0] % (16 * seqs) == 0:
            rows = joined.shape[0] // seqs
            joined = lax.dynamic_slice_in_dim(joined, side * rows, rows, 0)
            whole = lax.all_gather(joined, ("dp", "seq"), axis=0, tiled=True)
        else:
            whole = lax.all_gather(joined, "dp", axis=0, tiled=True)
        return cut_parts(whole, parts)

    def join_rows(pieces):
        blocks = [piece.reshape(owners, -1, piece.shape[1]) for piece in pieces]
        return jnp.concatenate(blocks, 1).reshape(-1, pieces[0].shape[1])

    share = attn_in.shape[1]
    norm_part = jnp.pad(
        norms.reshape(-1, norms.shape[2]).T, ((0, 0), (0, norm_columns - 2 * norm_count))
    )
    out_pieces = ffn_out.shape[1] // share
    parts = [attn_in[0], attn_out[0], len_head, norm_part, ffn_in[0]]
    parts += columns_of(ffn_out[0], share)
    parts += [attn_in[1], attn_out[1], attn_in[2], attn_out[2], ffn_in[1]]
    parts += columns_of(ffn_out[1], share)
    w_in0, w_out0, w_len, norm_low, f_in0, *others = gather_columns(parts)
    f_out0 = join_rows(others[:out_pieces])
    w_in1, w_out1, w_in2, w_out2, f_in1, *f_out1 = others[out_pieces:]
    f_out1 = join_rows(f_out1)
    table_low = table.astype(low_type)
    table_part = lax.all_gather(table_low, "dp", axis=0, tiled=True)
    norm_low = norm_low[:, : 2 * norm_count].T.astype(f32)
    gains, biases = norm_low[:norm_count], norm_low[norm_count:]

    ids = gather_seq(jnp.stack([src_ids, tgt_ids, tgt_mask]), 2).reshape(3, rows_here, row_len)
    src_starts = jnp.cumsum(src_lengths, -1) - src_lengths
    tgt_starts = jnp.cumsum(tgt_lengths, -1) - tgt_lengths
    places = jnp.arange(row_len)
    opens = jnp.any(places[None, :, None] == src_starts[:, None, :], -1)
    src_in = pick(jnp.where(opens, length_token, ids[0]).reshape(seqs, span), 0, side)
    masked = (ids[2] == 1).reshape(seqs, span)
    labels = ids[1].reshape(seqs, span)
    dec_in = pick(jnp.where(masked, mask_token, labels), 0, side)
    counts = jnp.sum(masked.astype(jnp.int32), -1)

    def slots_for(expected):
        return max(-(-expected // 16) * 16, 16)

    src_slots, dec_slots = slots_for(2 * span // devices), slots_for(3 * span // (2 * devices))

    def ask(token_ids, slots):
        same = token_ids[:, None] == token_ids[None, :]
        index = jnp.arange(span)
        earlier = index[None, :] < index[:, None]
        leader = jnp.logical_not(jnp.any(same & earlier, 1))
        holder = token_ids // own_words
        rank = jnp.sum(
            (earlier & leader[None, :] & (holder[:, None] == holder[None, :])).astype(jnp.int32), 1
        )
        rank = jnp.sum(jnp.where(same & leader[None, :], rank[None, :], 0), 1)
        return token_ids % own_words, holder, rank, slots

    def chosen_of(asked, turn):
        local, holder, rank, slots = asked
        code = jnp.where(rank // slots == turn, holder * slots + rank % slots, -1)
        return code[:, None] == jnp.arange(devices * slots)[None, :]

    def wanted_of(asked, chosen):
        return jnp.max(jnp.where(chosen, asked[0][:, None], -1), 0).reshape(devices, -1)

    def maps_of(chosen, wanted):
        held = wanted.reshape(-1)[:, None] == jnp.arange(own_words)[None, :]
        return chosen.astype(low_type), held.astype(low_type)

    def round_of(asked, turn):
        chosen = chosen_of(asked, turn)
        return maps_of(chosen, to_each(wanted_of(asked, chosen)))

    def send_rows(held):
        found = contract(held, table_low, 1, 0).astype(low_type)
        return to_each(found.reshape(devices, -1, width)).reshape(-1, width)

    def fetch(maps):
        chosen, held = maps
        return contract(send_rows(held), chosen, 0, 1)

    def give_rows(chosen, grads):
        sums = contract(chosen, grads.astype(low_type), 0, 1).astype(low_type)
        return to_each(sums.reshape(devices, -1, width)).reshape(-1, width)

    def give(maps, grads):
        return contract(maps[1], give_rows(maps[0], grads), 0, 0)

    def later_rounds(rounds, value, visit):
        return lax.fori_loop(1, rounds, lambda turn, carry: carry + visit(turn), value)

    src_ask, dec_ask = ask(src_in, src_slots), ask(dec_in, dec_slots)
    src_chosen, dec_chosen = chosen_of(src_ask, 0), chosen_of(dec_ask, 0)
    facts = jnp.stack(
        [
            jnp.sum(tgt_mask),
            jnp.max(counts),
            jnp.max(src_ask[2]) // src_slots + 1,
            jnp.max(dec_ask[2]) // dec_slots + 1,
        ]
    )
    facts = jnp.broadcast_to(jnp.pad(facts, (0, 12))[None, :], (devices, 16))
    asked = [wanted_of(src_ask, src_chosen), wanted_of(dec_ask, dec_chosen), facts]
    asked = to_each(jnp.concatenate(asked, 1).astype(jnp.int32))
    facts = asked[:, src_slots + dec_slots :]
    count = jnp.sum(facts[:, 0]).astype(f32)
    cut = -(-(span * 3 // 8) // 128) * 128
    more = jnp.max(facts[:, 1]) > cut
    src_rounds, dec_rounds = jnp.max(facts[:, 2]), jnp.max(facts[:, 3])
    src_maps = maps_of(src_chosen, asked[:, :src_slots])
    src_found = fetch(src_maps)
    dec_maps = maps_of(dec_chosen, asked[:, src_slots : src_slots + dec_slots])
    dec_rows = send_rows(dec_maps[1])

    starts_at = jnp.cumsum(counts) - counts
    total = jnp.sum(counts)
    rank = jnp.where(masked, jnp.cumsum(masked.astype(jnp.int32), -1) - 1, -1)
    slot_of = jnp.where(masked, rank + starts_at[:, None], -1)
    slot_index = jnp.arange(seqs * span)
    slot_label = jnp.sum(
        jnp.where(slot_of.reshape(1, -1) == slot_index[:, None], labels.reshape(1, -1), 0), -1
    )
    valid = slot_index < total
    targets = jnp.where(valid, slot_label - vocab_base, -1).reshape(1, -1)
    plan = jnp.concatenate([chunk_plan(total), lax.axis_index("dp")[None] & 1]).astype(jnp.int32)
    own_rank, own_slot = pick(rank, 0, side), pick(slot_of, 0, side)

    def packing(slots, rows):
        slot, index = jnp.arange(slots), jnp.arange(rows)
        far_start, far_count = pick(starts_at, 0, 1 - side), pick(counts, 0, 1 - side)
        far = jnp.where(index < far_count, index + far_start, -1)
        return (
            (own_rank[None, :] == index[:, None]).astype(low_type),
            (own_slot[None, :] == slot[:, None]).astype(low_type),
            (far[None, :] == slot[:, None]).astype(low_type),
        )

    own_places = offset + jnp.arange(span)
    src_start, src_length = pick(src_starts, 0, row), pick(src_lengths, 0, row)
    tgt_start, tgt_length = pick(tgt_starts, 0, row), pick(tgt_lengths, 0, row)
    src_number, src_open = place_spans(src_start, own_places)
    tgt_number, tgt_open = place_spans(tgt_start, own_places)
    block = min(query_block, span)
    enc_spans = key_spans(src_number, src_start, src_length, block)
    self_spans = key_spans(tgt_number, tgt_start, tgt_length, block)
    cross_spans = key_spans(tgt_number, src_start, src_length, block)
    src_wave, tgt_wave = lax.optimization_barrier(
        (sinusoid(own_places - src_open, width), sinusoid(own_places - tgt_open, width))
    )

    root = math.sqrt(width)
    src_found = later_rounds(src_rounds, src_found, lambda turn: fetch(round_of(src_ask, turn)))
    stream0 = src_found * root + src_wave

    def norm(stream, index):
        return layer_norm(stream, gains[index], biases[index])

    def keys_of_row(part):
        if group == 1:
            return part
        return lax.all_gather(part, "seq", axis=1, tiled=True, axis_index_groups=sharers)

    def keys_to_place(part):
        if group == 1:
            return part
        return lax.psum_scatter(
            part, "seq", scatter_dimension=1, tiled=True, axis_index_groups=sharers
        )

    def self_attention(inner, weight_in, weight_out, spans):
        triple = contract(weight_in, inner, 0, 0).astype(low_type)
        keys = triple if group == 1 else keys_of_row(triple[width:])
        mixed, lse = attend_forward(triple, keys, group == 1, *spans)
        return contract(weight_out, mixed, 0, 0), (triple, keys, mixed, lse)

    def self_attention_back(inner, weight_in, weight_out, spans, kept, grad, before, after):
        triple, keys, mixed, lse = kept
        grad_low = grad.astype(low_type)
        d_out = contract(mixed, grad_low, 1, 1)
        d_mixed = contract(weight_out, grad_low, 1, 0).astype(low_type)
        d_mixed = advance(d_mixed, before)
        d_query, d_keys = attend_backward(triple, keys, group == 1, *spans, lse, d_mixed)
        d_query, d_keys = advance((d_query, d_keys), after)
        d_triple = jnp.concatenate([d_query, keys_to_place(d_keys)], 0)
        return contract(weight_in, d_triple, 1, 0), contract(inner, d_triple, 1, 1), d_out

    def cross_attention(inner, memory, weight_in, weight_out, spans):
        queries = contract(weight_in[:, :width], inner, 0, 0).astype(low_type)
        keys = keys_of_row(contract(weight_in[:, width:], memory, 0, 0).astype(low_type))
        mixed, lse = attend_forward(queries, keys, False, *spans)
        return contract(weight_out, mixed, 0, 0), (queries, keys, mixed, lse)

    def cross_attention_back(inner, memory, weight_in, weight_out, spans, kept, grad, before, after):
        queries, keys, mixed, lse = kept
        grad_low = grad.astype(low_type)
        d_out = contract(mixed, grad_low, 1, 1)
        d_mixed = contract(weight_out, grad_low, 1, 0).astype(low_type)
        d_mixed = advance(d_mixed, before)
        d_query, d_keys = attend_backward(queries, keys, False, *spans, lse, d_mixed)
        d_query, d_keys = advance((d_query, d_keys), after)
        d_keys = keys_to_place(d_keys)
        d_in = jnp.concatenate([contract(inner, d_query, 1, 1), contract(memory, d_keys, 1, 1)], 1)
        return (
            contract(weight_in[:, :width], d_query, 1, 0),
            contract(weight_in[:, width:], d_keys, 1, 0),
            d_in,
            d_out,
        )

    def ffn(inner, weight_one, weight_two):
        hidden = contract(weight_one, inner, 0, 0)
        active = jax.nn.gelu(hidden).astype(low_type)
        return contract(weight_two, active, 0, 0), (hidden, active)

    def ffn_back(inner, weight_one, weight_two, kept, grad):
        hidden, active = kept
        grad_low = grad.astype(low_type)
        d_two = contract(active, grad_low, 1, 1)
        d_active = contract(weight_two, grad_low, 1, 0)
        d_hidden = jax.vjp(jax.nn.gelu, hidden)[1](d_active)[0].astype(low_type)
        return contract(weight_one, d_hidden, 1, 0), contract(inner, d_hidden, 1, 1), d_two

    inner0, norm0 = norm(stream0, 0)
    branch0, keep0 = self_attention(inner0, w_in0, w_out0, enc_spans)
    stream1 = stream0 + branch0
    stream1, dec_rows = lax.optimization_barrier((stream1, dec_rows))
    inner1, norm1 = norm(stream1, 1)
    branch1, keep1 = ffn(inner1, f_in0, f_out0)
    stream2 = stream1 + branch1
    memory, norm2 = norm(stream2, 2)
    memory, dec_chosen = lax.optimization_barrier((memory, dec_maps[0]))
    dec_found = contract(dec_rows, dec_chosen, 0, 1)
    dec_found = later_rounds(dec_rounds, dec_found, lambda turn: fetch(round_of(dec_ask, turn)))
    target0 = dec_found * root + tgt_wave
    inner3, norm3 = norm(target0, 3)
    branch3, keep3 = self_attention(inner3, w_in1, w_out1, self_spans)
    target1 = target0 + branch3
    inner4, norm4 = norm(target1, 4)
    branch4, keep4 = cross_attention(inner4, memory, w_in2, w_out2, cross_spans)
    target2 = target1 + branch4
    inner5, norm5 = norm(target2, 5)
    branch5, keep5 = ffn(inner5, f_in1, f_out1)
    target3 = target2 + branch5
    final, norm6 = norm(target3, 6)

    def pack(slots, rows):
        own_chosen, own_slots, far_slots = packing(slots, rows)
        far = swap(contract(own_chosen, final, 1, 1).astype(low_type), "seq", 1)
        packed = contract(own_slots, final, 1, 1) + contract(far_slots, far, 1, 0)
        return jnp.pad(packed.astype(low_type), ((0, seqs * span - slots), (0, 0)))

    def unpack(slots, rows):
        own_chosen, own_slots, far_slots = packing(slots, rows)
        high = lax.reduce_precision(d_pieces[:slots], 8, 7)
        rest = (d_pieces[:slots] - high).astype(low_type)
        high = high.astype(low_type)
        far = swap(contract(far_slots, high, 0, 0).astype(low_type), "seq", 1)
        return (
            contract(high, own_slots, 0, 0)
            + contract(rest, own_slots, 0, 0)
            + contract(far, own_chosen, 0, 0)
        )

    if seqs == 2:
        pieces = lax.cond(
            more, lambda: pack(2 * span, span), lambda: pack(min(2 * cut, 2 * span), cut)
        )
    else:
        own_slots = packing(seqs * span, span)[1]
        pieces = lax.psum(contract(own_slots, final, 1, 1), "seq").astype(low_type)
    turned = pieces.T
    every = gather_seq(head_stats(plan, table_part, turned), 0)
    top_logit = jnp.max(every[:, 0], 0)
    totals = jnp.sum(every[:, 1] * jnp.exp(every[:, 0] - top_logit[None]), 0)
    log_total = top_logit + jnp.log(jnp.where(valid, totals, 1.0))
    own_start = pick(starts_at, 0, side)
    mine = (slot_index >= own_start) & (slot_index < own_start + pick(counts, 0, side))
    token_local = jnp.sum(jnp.where(mine, log_total, 0.0))
    logs = jnp.where(valid, log_total + jnp.log(count), 1e30)
    weights = jnp.where(valid, 1.0 / count, 0.0)
    split = halving_fits(own_words, width // 2, False)
    *d_table, d_pieces, picks = head_back(
        plan, table_part, pieces, turned, targets, logs[None], weights[None], split and own_words
    )
    token_local = token_local - jnp.sum(picks)
    table_one = [TableChain(d_table[0], d_table[2])] if split else []
    if seqs == 2:
        d_final = lax.cond(
            more, lambda: unpack(2 * span, span), lambda: unpack(min(2 * cut, 2 * span), cut)
        )
    else:
        d_pieces = lax.psum(d_pieces, "seq")
        high = lax.reduce_precision(d_pieces, 8, 7)
        rest = (d_pieces - high).astype(low_type)
        d_final = contract(high.astype(low_type), own_slots, 0, 0) + contract(rest, own_slots, 0, 0)

    first_place = own_places[None, :] == src_start[:, None]
    mine = jnp.any(first_place, -1)
    first_rows = contract(first_place.astype(low_type), memory, 1, 1).astype(low_type)
    len_logits = contract(first_rows, w_len, 1, 0)
    len_label = jnp.minimum(tgt_length, classes - 1)
    len_hot = jnp.arange(classes)[None, :] == len_label[:, None]
    len_loss = jax.nn.logsumexp(len_logits, -1) - jnp.sum(jnp.where(len_hot, len_logits, 0.0), -1)
    len_local = jnp.sum(jnp.where(mine, len_loss, 0.0))
    sentences = rows_here * src_lengths.shape[1] * owners
    len_prob = jax.nn.softmax(len_logits, -1)
    d_len_logits = (
        jnp.where(mine[:, None], len_prob - len_hot.astype(f32), 0.0) * (0.1 / sentences)
    ).astype(low_type)
    d_w_len = contract(first_rows, d_len_logits, 0, 0)
    d_first = contract(d_len_logits, w_len, 1, 1)
    d_memory = lax.dot_general(
        d_first,
        first_place.astype(f32),
        (((0,), (0,)), ((), ())),
        precision=lax.Precision.HIGHEST,
        preferred_element_type=f32,
    )

    def owned(grad):
        return grad.reshape(owners, -1, grad.shape[1])

    def owned_columns(grad):
        whole = owned(grad)
        return [whole[:, at : at + share] for at in range(0, whole.shape[1], share)]

    d_target3, scale6 = norm_backward(norm6, gains[6], d_final)
    d_inner5, d_fin1, d_fout1 = ffn_back(inner5, f_in1, f_out1, keep5, d_target3)
    d_inner5, d_target3, d_table = advance((d_inner5, d_target3, d_table), table_one)
    table_two = [TableChain(d_table[1], d_table[3])] if split else []
    chain_a = LayerChain([owned(d_fin1)] + owned_columns(d_fout1))
    d_target2, scale5 = norm_backward(norm5, gains[5], d_inner5, d_target3)
    d_inner4, d_cross, d_win2, d_wout2 = cross_attention_back(
        inner4, memory, w_in2, w_out2, cross_spans, keep4, d_target2, [], table_one + [chain_a]
    )
    chain_b = LayerChain([owned(d_win2), owned(d_wout2)])
    d_target1, scale4 = norm_backward(norm4, gains[4], d_inner4, d_target2)
    d_inner3, d_win1, d_wout1 = self_attention_back(
        inner3,
        w_in1,
        w_out1,
        self_spans,
        keep3,
        d_target1,
        table_two,
        table_one + [chain_a, chain_b],
    )
    chain_c = LayerChain([owned(d_win1), owned(d_wout1)])
    d_target0, scale3 = norm_backward(norm3, gains[3], d_inner3, d_target1)
    d_stream2, scale2 = norm_backward(norm2, gains[2], d_memory + d_cross)
    d_stream2, d_target0 = advance((d_stream2, d_target0), [chain_b])
    dec_grad = d_target0 * root
    dec_sums = give_rows(dec_maps[0], dec_grad)
    d_inner1, d_fin0, d_fout0 = ffn_back(inner1, f_in0, f_out0, keep1, d_stream2)
    chains = table_one + table_two + [chain_a, chain_c]
    d_inner1, d_stream2 = advance((d_inner1, d_stream2), chains)
    chain_d = LayerChain([owned(d_fin0)] + owned_columns(d_fout0))
    d_stream1, scale1 = norm_backward(norm1, gains[1], d_inner1, d_stream2)
    d_inner0, d_win0, d_wout0 = self_attention_back(
        inner0,
        w_in0,
        w_out0,
        enc_spans,
        keep0,
        d_stream1,
        [chain_b, chain_c, chain_d],
        table_two + [chain_a, chain_c, chain_d],
    )
    chain_e = LayerChain([owned(d_win0), owned(d_wout0), owned(d_w_len)])
    d_stream0, scale0 = norm_backward(norm0, gains[0], d_inner0, d_stream1)
    d_stream0 = advance(d_stream0, [chain_b, chain_c, chain_d, chain_e])
    src_grad = d_stream0 * root
    src_sums = give_rows(src_maps[0], src_grad)
    norm_share = norms.shape[2]
    scales = jnp.stack([scale0, scale1, scale2, scale3, scale4, scale5, scale6], 1)
    scales = scales.reshape(2 * norm_count, owners, norm_share).transpose(1, 0, 2)
    scales = jnp.broadcast_to(scales[None], (seqs,) + scales.shape)
    scales = to_each(scales.reshape((devices,) + scales.shape[2:]))
    chains = table_one + table_two + [chain_a, chain_b, chain_c, chain_d, chain_e]
    src_sums, dec_sums, scales = advance((src_sums, dec_sums, scales), chains)
    while any(chain.pending is not None for chain in chains):
        advance((), chains)
    layer_chains = [chain_a, chain_b, chain_c, chain_d, chain_e]
    for chain in layer_chains:
        chain.finish()

    g_norms = jnp.sum(scales, 0)
    norm_square = jnp.where(side == 0, jnp.sum(g_norms * g_norms), 0.0)
    given = contract(dec_maps[1], dec_sums, 0, 0) + contract(src_maps[1], src_sums, 0, 0)
    given = later_rounds(
        jnp.maximum(src_rounds, dec_rounds),
        given,
        lambda turn: give(round_of(dec_ask, turn), dec_grad)
        + give(round_of(src_ask, turn), src_grad),
    )
    if split:
        table_grad = jnp.concatenate([chain.value for chain in table_one + table_two], 1)
    else:
        table_grad = lax.psum_scatter(d_table[0], "dp", scatter_dimension=0, tiled=True)
    table_grad = table_grad + given
    square = sum(chain.square for chain in layer_chains)
    square = square + jnp.sum(table_grad * table_grad) + norm_square
    sums = jnp.pad(jnp.stack([token_local, len_local, square]), (0, 5))
    sums = jnp.sum(to_each(jnp.broadcast_to(sums[None], (devices, 8))), 0)
    token_sum, len_sum, grad_norm = sums[0], sums[1], jnp.sqrt(sums[2])
    factor = jnp.minimum(1.0, clip_limit / (grad_norm + 1e-06))

    def cut_columns(chain, sizes):
        result, at = [], 0
        value = chain.value.reshape(share, -1)
        for size in sizes:
            result.append(value[:, at : at + size])
            at += size
        return result

    hidden_width = ffn_in.shape[2]
    ffn_sizes = [hidden_width] + [width] * out_pieces
    attn_sizes = [3 * width, width]
    g_fin1, *g_fout1 = cut_columns(chain_a, ffn_sizes)
    g_win2, g_wout2 = cut_columns(chain_b, attn_sizes)
    g_win1, g_wout1 = cut_columns(chain_c, attn_sizes)
    g_fin0, *g_fout0 = cut_columns(chain_d, ffn_sizes)
    g_win0, g_wout0, g_len = cut_columns(chain_e, attn_sizes + [classes])
    grads = (
        jnp.stack([g_win0, g_win1, g_win2]),
        jnp.stack([g_wout0, g_wout1, g_wout2]),
        jnp.stack([g_fin0, g_fin1]),
        jnp.stack([jnp.concatenate(g_fout0, 0), jnp.concatenate(g_fout1, 0)]),
        g_len,
        g_norms.reshape(norms.shape),
        table_grad,
    )
    masters = (attn_in, attn_out, ffn_in, ffn_out, len_head, norms, table)
    firsts = (attn_in_m1, attn_out_m1, ffn_in_m1, ffn_out_m1, len_head_m1, norms_m1, table_m1)
    seconds = (attn_in_m2, attn_out_m2, ffn_in_m2, ffn_out_m2, len_head_m2, norms_m2, table_m2)
    updates = []
    for weight, first, second, grad, rate in zip(masters, firsts, seconds, grads, step_rates):
        updates.extend(adam_update(weight, first, second, grad * factor, rate))
    return (token_sum, count, len_sum, grad_norm, *updates)


def solution(mesh):
    layer, head, scales, words = P(None, "dp", None), P("dp", None), P(None, None, "dp"), P(("seq", "dp"), None)
    owned = (layer,) * 12 + (head,) * 3 + (scales,) * 3 + (words,) * 3
    ids, lengths = P("dp", "seq"), P("dp", None)
    in_specs = (ids, ids, lengths, lengths, ids) + owned
    out_specs = (P(), P(), P(), P()) + owned
    return jax.shard_map(
        on_device, mesh=mesh, in_specs=in_specs, out_specs=out_specs, check_vma=False
    )
```

```python
import functools
import math

import jax
import jax.numpy as jnp
from jax import lax
from jax.experimental import pallas as pl
from jax.experimental.pallas import tpu as pltpu
from jax.sharding import PartitionSpec as P

HEADS = 8
STEP = 10


length_token = 1
mask_token = 2
clip_limit = 0.002
beta_one = 0.9
beta_two = 0.98
adam_eps = 1e-08
weight_decay = 0.01
step_rates = (0.05, 0.25, 0.05, 0.025, 0.05, 0.5, 0.1)

low_type = jnp.bfloat16
f32 = jnp.float32
query_block = 256
key_block = 128
place_block = 512
vmem_bytes = 56 * 1024 * 1024


def sinusoid(positions, width):
    half_width = width // 2
    frequency = jnp.exp(jnp.arange(half_width).astype(f32) * (-math.log(10000.0) / half_width))
    angles = frequency[:, None] * positions.astype(f32)[None, :]
    return jnp.concatenate([jnp.sin(angles), jnp.cos(angles)], 0)


def layer_norm(stream, norm_gain, norm_bias):
    average = jnp.mean(stream, 0, keepdims=True)
    centred = stream - average
    variance = jnp.mean(centred * centred, 0, keepdims=True)
    inverse = lax.rsqrt(variance + 1e-05)
    normed = centred * inverse * norm_gain[:, None] + norm_bias[:, None]
    return normed.astype(low_type), (stream, average, inverse)


def contract(left, right, left_dim, right_dim):
    return lax.dot_general(
        left, right, (((left_dim,), (right_dim,)), ((), ())), preferred_element_type=f32
    )


def attend_forward_kernel(bounds, q_ref, k_ref, v_ref, span_ref, out_ref, lse_ref, hold, *, head):
    step = pl.program_id(0)
    first, last = bounds[0, step], bounds[1, step]
    width, queries = q_ref.shape
    heads = width // head
    scale = head**-0.5
    low, high = span_ref[0:1, :], span_ref[1:2, :]
    inner = lax.broadcasted_iota(jnp.int32, (key_block, queries), 0)

    def fold(values, op):
        return op(values.reshape(key_block // 8, 8, queries), axis=0)

    def score(block, tops):
        start = pl.multiple_of(block * key_block, key_block)
        place = inner + start
        allowed = (place >= low) & (place < high)
        result = []
        for h in range(heads):
            rows = slice(h * head, (h + 1) * head)
            s = contract(k_ref[rows, pl.ds(start, key_block)], q_ref[rows, :], 0, 0) * scale
            s = jnp.where(allowed, s, -1e30)
            hold[h, pl.ds(start, key_block), :] = s
            result.append(jnp.maximum(tops[h], fold(s, jnp.max)))
        return tuple(result)

    tops = lax.fori_loop(
        first, last, score, tuple(jnp.full((8, queries), -1e30, f32) for _ in range(heads))
    )
    tops = [jnp.max(t, axis=0, keepdims=True) for t in tops]

    def power(block, sums):
        start = pl.multiple_of(block * key_block, key_block)
        result = []
        for h in range(heads):
            e = jnp.exp(hold[h, pl.ds(start, key_block), :] - tops[h])
            hold[h, pl.ds(start, key_block), :] = e
            result.append(sums[h] + fold(e, jnp.sum))
        return tuple(result)

    sums = lax.fori_loop(
        first, last, power, tuple(jnp.zeros((8, queries), f32) for _ in range(heads))
    )
    sums = [jnp.maximum(jnp.sum(t, axis=0, keepdims=True), 1e-30) for t in sums]
    inverse = [1.0 / t for t in sums]

    def mix(block, outs):
        start = pl.multiple_of(block * key_block, key_block)
        result = []
        for h in range(heads):
            rows = slice(h * head, (h + 1) * head)
            p = (hold[h, pl.ds(start, key_block), :] * inverse[h]).astype(low_type)
            result.append(outs[h] + contract(v_ref[rows, pl.ds(start, key_block)], p, 1, 0))
        return tuple(result)

    outs = lax.fori_loop(
        first, last, mix, tuple(jnp.zeros((head, queries), f32) for _ in range(heads))
    )
    for h in range(heads):
        out_ref[h * head : (h + 1) * head, :] = outs[h].astype(low_type)
        lse_ref[h : h + 1, :] = tops[h] + jnp.log(sums[h])


def attend_backward_kernel(
    bounds, q_ref, k_ref, v_ref, span_ref, lse_ref, do_ref, dq_ref, dkv_ref, p_hold, d_hold, acc,
    *, head
):
    step = pl.program_id(0)
    first, last = bounds[0, step], bounds[1, step]
    width, queries = q_ref.shape
    heads = width // head
    scale = head**-0.5
    low, high = span_ref[0:1, :], span_ref[1:2, :]
    inner = lax.broadcasted_iota(jnp.int32, (key_block, queries), 0)

    @pl.when(step == 0)
    def _():
        acc[...] = jnp.zeros_like(acc)

    def one(block, deltas):
        start = pl.multiple_of(block * key_block, key_block)
        keys = pl.ds(start, key_block)
        place = inner + start
        allowed = (place >= low) & (place < high)
        result = []
        for h in range(heads):
            rows = slice(h * head, (h + 1) * head)
            s = contract(k_ref[rows, keys], q_ref[rows, :], 0, 0) * scale
            p = jnp.exp(jnp.where(allowed, s, -1e30) - lse_ref[h : h + 1, :])
            dp = contract(v_ref[rows, keys], do_ref[rows, :], 0, 0)
            p_hold[h, keys, :] = p
            d_hold[h, keys, :] = dp
            result.append(
                deltas[h] + jnp.sum((p * dp).reshape(key_block // 8, 8, queries), axis=0)
            )
            below = slice(width + h * head, width + (h + 1) * head)
            acc[below, keys] += contract(do_ref[rows, :], p.astype(low_type), 1, 1)
        return tuple(result)

    deltas = lax.fori_loop(
        first, last, one, tuple(jnp.zeros((8, queries), f32) for _ in range(heads))
    )
    deltas = [jnp.sum(t, axis=0, keepdims=True) for t in deltas]

    def two(block, outs):
        start = pl.multiple_of(block * key_block, key_block)
        keys = pl.ds(start, key_block)
        result = []
        for h in range(heads):
            rows = slice(h * head, (h + 1) * head)
            ds = (p_hold[h, keys, :] * (d_hold[h, keys, :] - deltas[h])).astype(low_type)
            result.append(outs[h] + contract(k_ref[rows, keys], ds, 1, 0))
            acc[rows, keys] += contract(q_ref[rows, :], ds, 1, 1) * scale
        return tuple(result)

    outs = lax.fori_loop(
        first, last, two, tuple(jnp.zeros((head, queries), f32) for _ in range(heads))
    )
    for h in range(heads):
        dq_ref[h * head : (h + 1) * head, :] = (outs[h] * scale).astype(low_type)

    @pl.when(step == pl.num_programs(0) - 1)
    def _():
        dkv_ref[...] = acc[...].astype(low_type)


def attend_specs(width, length, block, shared):
    key_row = 1 if shared else 0
    return [
        pl.BlockSpec((width, block), lambda i, *_: (0, i)),
        pl.BlockSpec((width, length), lambda i, *_: (key_row, 0)),
        pl.BlockSpec((width, length), lambda i, *_: (key_row + 1, 0)),
        pl.BlockSpec((2, block), lambda i, *_: (0, i)),
    ]


def attend_forward(queries, keys, shared, spans, bounds):
    width = keys.shape[0] // (3 if shared else 2)
    places, length = queries.shape[1], keys.shape[1]
    block = min(query_block, places)
    return pl.pallas_call(
        functools.partial(attend_forward_kernel, head=width // HEADS),
        grid_spec=pltpu.PrefetchScalarGridSpec(
            num_scalar_prefetch=1,
            grid=(places // block,),
            in_specs=attend_specs(width, length, block, shared),
            out_specs=[
                pl.BlockSpec((width, block), lambda i, *_: (0, i)),
                pl.BlockSpec((HEADS, block), lambda i, *_: (0, i)),
            ],
            scratch_shapes=[pltpu.VMEM((HEADS, length, block), f32)],
        ),
        out_shape=[
            jax.ShapeDtypeStruct((width, places), low_type),
            jax.ShapeDtypeStruct((HEADS, places), f32),
        ],
        compiler_params=pltpu.CompilerParams(vmem_limit_bytes=vmem_bytes),
        name="attend_forward",
    )(bounds, queries, keys, keys, spans)


def attend_backward(queries, keys, shared, spans, bounds, lse, d_mixed):
    width = keys.shape[0] // (3 if shared else 2)
    places, length = queries.shape[1], keys.shape[1]
    block = min(query_block, places)
    return pl.pallas_call(
        functools.partial(attend_backward_kernel, head=width // HEADS),
        grid_spec=pltpu.PrefetchScalarGridSpec(
            num_scalar_prefetch=1,
            grid=(places // block,),
            in_specs=attend_specs(width, length, block, shared)
            + [
                pl.BlockSpec((HEADS, block), lambda i, *_: (0, i)),
                pl.BlockSpec((width, block), lambda i, *_: (0, i)),
            ],
            out_specs=[
                pl.BlockSpec((width, block), lambda i, *_: (0, i)),
                pl.BlockSpec((2 * width, length), lambda i, *_: (0, 0)),
            ],
            scratch_shapes=[
                pltpu.VMEM((HEADS, length, block), f32),
                pltpu.VMEM((HEADS, length, block), f32),
                pltpu.VMEM((2 * width, length), f32),
            ],
        ),
        out_shape=[
            jax.ShapeDtypeStruct((width, places), low_type),
            jax.ShapeDtypeStruct((2 * width, length), low_type),
        ],
        compiler_params=pltpu.CompilerParams(vmem_limit_bytes=vmem_bytes),
        name="attend_backward",
    )(bounds, queries, keys, keys, spans, lse, d_mixed)


def norm_back_kernel(stream_ref, average_ref, inverse_ref, gain_ref, grad_ref, *refs):
    (*rest_refs, out_ref, sums_ref, parts) = refs

    @pl.when(pl.program_id(0) == 0)
    def _():
        parts[...] = jnp.zeros_like(parts)

    inverse, grad = inverse_ref[...], grad_ref[...]
    unit = (stream_ref[...] - average_ref[...]) * inverse
    width, places = grad.shape
    scaled = grad * gain_ref[...]
    along = jnp.mean(scaled * unit, 0, keepdims=True)
    level = jnp.mean(scaled, 0, keepdims=True)
    out = (scaled - level - unit * along) * inverse
    for rest_ref in rest_refs:
        out = out + rest_ref[...]
    out_ref[...] = out
    weighted = grad * unit
    for at in range(0, places, 128):
        parts[0] += weighted[:, at : at + 128]
        parts[1] += grad[:, at : at + 128]

    @pl.when(pl.program_id(0) == pl.num_programs(0) - 1)
    def _():
        sums_ref[...] = jnp.sum(parts[...], 2, keepdims=True)


def norm_backward(kept, gain, grad, *rests):
    stream, average, inverse = kept
    width, places = stream.shape
    columns = min(256, places)
    block = pl.BlockSpec((width, columns), lambda i: (0, i))
    row = pl.BlockSpec((1, columns), lambda i: (0, i))
    out, sums = pl.pallas_call(
        norm_back_kernel,
        grid=(places // columns,),
        in_specs=[block, row, row, pl.BlockSpec((width, 1), lambda i: (0, 0)), block]
        + [block] * len(rests),
        out_specs=[block, pl.BlockSpec((2, width, 1), lambda i: (0, 0, 0))],
        out_shape=[
            jax.ShapeDtypeStruct((width, places), f32),
            jax.ShapeDtypeStruct((2, width, 1), f32),
        ],
        scratch_shapes=[pltpu.VMEM((2, width, 128), f32)],
        compiler_params=pltpu.CompilerParams(vmem_limit_bytes=vmem_bytes),
        name="norm_backward",
    )(stream, average, inverse, gain[:, None], grad, *rests)
    return out, sums[:, :, 0]


def chunk_plan(total):
    quarter = place_block // 4
    units = (jnp.maximum(total - place_block, 0) + quarter - 1) // quarter
    left = units % 4
    wides = units // 4 + (left == 3).astype(jnp.int32)
    return jnp.stack([wides, left == 2, left == 1]).astype(jnp.int32)


def each_chunk(plan, visit):
    visit(0, place_block, True)

    def wide(index, carry):
        visit(pl.multiple_of((index + 1) * place_block, place_block), place_block, False)
        return carry

    lax.fori_loop(0, plan[0], wide, 0)
    after = pl.multiple_of((plan[0] + 1) * place_block, place_block)
    for index, share in ((1, 2), (2, 4)):

        @pl.when(plan[index] > 0)
        def _(share=share):
            visit(after, place_block // share, False)


def parts_of(words):
    for count in (5, 4, 2):
        if words % (16 * count) == 0:
            return [slice(i * (words // count), (i + 1) * (words // count)) for i in range(count)]
    return [slice(0, words)]


def head_stats_kernel(plan, table_ref, turned_ref, stats_ref, tops, sums):
    step = pl.program_id(0)

    @pl.when(step == 0)
    def _():
        tops[...] = jnp.full_like(tops, -1e30)
        sums[...] = jnp.zeros_like(sums)

    def visit(start, size, first):
        here = pl.ds(start, size)
        turned = turned_ref[:, here]
        old, total = tops[:, here], sums[:, here]
        for part in parts_of(table_ref.shape[0]):
            logits = contract(table_ref[part, :], turned, 1, 0)
            logits = logits.reshape(logits.shape[0] // 8, 8, size)
            top = jnp.maximum(old, jnp.max(logits, axis=0))
            powers = jnp.sum(jnp.exp(logits - top[None]), axis=0)
            total = total * jnp.exp(old - top) + powers
            old = top
        sums[:, here] = total
        tops[:, here] = old

    each_chunk(plan, visit)

    @pl.when(step == pl.num_programs(0) - 1)
    def _():
        top = jnp.max(tops[...], axis=0, keepdims=True)
        stats_ref[0:1, :] = top
        stats_ref[1:2, :] = jnp.sum(sums[...] * jnp.exp(tops[...] - top), axis=0, keepdims=True)


def head_back_kernel(
    plan, table_ref, rows_ref, turned_ref, target_ref, log_ref, weight_ref, *refs, owned
):
    (*out_refs, dr_ref, pick_ref, acc) = refs
    step = pl.program_id(0)
    words, width = table_ref.shape

    @pl.when(step == 0)
    def _():
        dr_ref[...] = jnp.zeros_like(dr_ref)
        pick_ref[...] = jnp.zeros_like(pick_ref)

    def visit(start, size, first):
        here = pl.ds(start, size)
        rows, turned = rows_ref[here, :], turned_ref[:, here]
        target = target_ref[:, here] - step * words
        log, weight = log_ref[:, here], weight_ref[:, here]
        found = jnp.zeros((8, size), f32)
        for part in parts_of(words):
            block = table_ref[part, :]
            count = block.shape[0]
            inner = lax.broadcasted_iota(jnp.int32, (count, size), 0) + part.start
            logits = contract(block, turned, 1, 0)
            scaled = jnp.exp(logits - log)
            hit = inner == target
            found += jnp.sum(jnp.where(hit, logits, 0.0).reshape(count // 8, 8, size), axis=0)
            d_logits = jnp.where(hit, scaled - weight, scaled).astype(low_type)
            if first:
                acc[part, :] = contract(d_logits, rows, 1, 0)
            else:
                acc[part, :] += contract(d_logits, rows, 1, 0)
            dr_ref[here, :] += contract(d_logits, block, 0, 0)
        pick_ref[:, here] += found

    each_chunk(plan, visit)
    if not owned:
        out_refs[0][...] = acc[...]
        return
    mine = plan[3]
    keep = pl.ds(pl.multiple_of(mine * owned, 8), owned)
    away = pl.ds(pl.multiple_of((1 - mine) * owned, 8), owned)
    half = width // 2
    out_refs[0][0] = acc[keep, :half]
    out_refs[1][0] = acc[keep, half:]
    out_refs[2][0] = acc[away, :half].astype(low_type)
    out_refs[3][0] = acc[away, half:].astype(low_type)


def word_block(words):
    return max(n for n in range(16, 1601, 16) if words % n == 0)


def head_stats(plan, table_part, turned):
    words = word_block(table_part.shape[0])
    width, places = turned.shape
    return pl.pallas_call(
        head_stats_kernel,
        grid_spec=pltpu.PrefetchScalarGridSpec(
            num_scalar_prefetch=1,
            grid=(table_part.shape[0] // words,),
            in_specs=[
                pl.BlockSpec((words, width), lambda i, *_: (i, 0)),
                pl.BlockSpec((width, places), lambda i, *_: (0, 0)),
            ],
            out_specs=pl.BlockSpec((2, places), lambda i, *_: (0, 0)),
            scratch_shapes=[pltpu.VMEM((8, places), f32) for _ in range(2)],
        ),
        out_shape=jax.ShapeDtypeStruct((2, places), f32),
        compiler_params=pltpu.CompilerParams(vmem_limit_bytes=vmem_bytes),
        name="head_stats",
    )(plan, table_part, turned)


def head_back(plan, table_part, rows, turned, targets, logs, weights, owned):
    total = table_part.shape[0]
    words = 2 * owned if owned else word_block(total)
    places, width = rows.shape
    row = pl.BlockSpec((1, places), lambda i, *_: (0, 0))
    if owned:
        out_specs = [pl.BlockSpec((1, owned, width // 2), lambda i, *_: (i, 0, 0))] * 4
        shape = (total // words, owned, width // 2)
        out_shape = [jax.ShapeDtypeStruct(shape, t) for t in (f32, f32, low_type, low_type)]
    else:
        out_specs = [pl.BlockSpec((words, width), lambda i, *_: (i, 0))]
        out_shape = [jax.ShapeDtypeStruct((total, width), f32)]
    return pl.pallas_call(
        functools.partial(head_back_kernel, owned=owned),
        grid_spec=pltpu.PrefetchScalarGridSpec(
            num_scalar_prefetch=1,
            grid=(total // words,),
            in_specs=[
                pl.BlockSpec((words, width), lambda i, *_: (i, 0)),
                pl.BlockSpec((places, width), lambda i, *_: (0, 0)),
                pl.BlockSpec((width, places), lambda i, *_: (0, 0)),
                row,
                row,
                row,
            ],
            out_specs=out_specs
            + [
                pl.BlockSpec((places, width), lambda i, *_: (0, 0)),
                pl.BlockSpec((8, places), lambda i, *_: (0, 0)),
            ],
            scratch_shapes=[pltpu.VMEM((words, width), f32)],
        ),
        out_shape=out_shape
        + [
            jax.ShapeDtypeStruct((places, width), f32),
            jax.ShapeDtypeStruct((8, places), f32),
        ],
        compiler_params=pltpu.CompilerParams(vmem_limit_bytes=vmem_bytes),
        name="head_back",
    )(plan, table_part, rows, turned, targets, logs, weights)


def swap(values, axis, bit):
    size = lax.axis_size(axis)
    return lax.ppermute(values, axis, [(i, i ^ bit) for i in range(size)])


def power_of_two(size):
    return size & (size - 1) == 0


def pick(values, dim, index):
    return lax.dynamic_index_in_dim(values, index, dim, False)


def gather_seq(values, dim):
    if lax.axis_size("seq") == 2:
        other = swap(values, "seq", 1)
        first = lax.axis_index("seq") == 0
        return jnp.stack([jnp.where(first, values, other), jnp.where(first, other, values)], dim)
    return lax.all_gather(values, "seq", axis=dim)


def to_each(values):
    return lax.all_to_all(values, ("seq", "dp"), 0, 0)


def halving_fits(rows, columns, joint):
    owners, seqs = lax.axis_size("dp"), lax.axis_size("seq")
    fits = power_of_two(owners) and owners > 2 and columns % 128 == 0
    return fits and (rows % 16 == 0 and seqs == 2 if joint else rows % 8 == 0)


class Chain:
    pending = value = square = None

class LayerChain(Chain):
    def __init__(self, parts):
        self.parts, self.step = parts, 0
        self.rows = parts[0].shape[1]
        self.fast = halving_fits(self.rows, parts[0].shape[2], True)
        if self.fast:
            self.launch()

    def launch(self):
        owners = lax.axis_size("dp")
        if self.step == 4:
            return
        if self.step == 3:
            self.pending = swap(self.part, "seq", 1)
        elif self.step == 2:
            groups = [list(range(core, owners, 2)) for core in range(2)]
            whole = (self.part + self.got.astype(f32)).astype(low_type)
            self.pending = lax.all_to_all(whole, "dp", 0, 0, axis_index_groups=groups)
        else:
            axis = ("dp", "seq")[self.step]
            mine = lax.axis_index(axis) & 1
            if self.step == 1:
                self.rows //= 2

            def half(side):
                if self.step == 0:
                    shape = (owners // 2, 2, self.rows)
                    parts = [part.reshape(shape + part.shape[2:]) for part in self.parts]
                    return jnp.concatenate([pick(part, 1, side) for part in parts], 2)
                shape = (owners // 2, 2, self.rows, -1)
                first, second = self.part.reshape(shape), self.got.reshape(shape)
                return pick(first, 1, side) + pick(second, 1, side).astype(f32)

            away = half(1 - mine).astype(low_type)
            self.part = half(mine)
            self.pending = swap(away, axis, 1)

    def absorb(self, got):
        self.pending = None
        self.step += 1
        if self.step < 3:
            self.got = got
        elif self.step == 3:
            self.part = jnp.sum(got.astype(f32), 0)
            self.square = jnp.sum(self.part * self.part)
        else:
            first = lax.axis_index("seq") == 0
            part = self.part
            self.value = jnp.concatenate(
                [jnp.where(first, part, got), jnp.where(first, got, part)], 0
            )

    def finish(self):
        if not self.fast:
            whole = jnp.concatenate(self.parts, 2)
            part = lax.psum(lax.psum_scatter(whole, "dp", scatter_dimension=0), "seq")
            self.value = part
            self.square = jnp.where(lax.axis_index("seq") == 0, jnp.sum(part * part), 0.0)


class TableChain(Chain):
    def __init__(self, keep, away):
        self.part, self.got = keep, None
        self.rows, self.bit = keep.shape[1], 2
        self.pending = swap(away, "dp", 1)

    def launch(self):
        if self.bit == lax.axis_size("dp"):
            return
        mine = (lax.axis_index("dp") // self.bit) & 1
        shape = (-1, 2, self.rows, self.part.shape[2])
        first, second = self.part.reshape(shape), self.got.reshape(shape)

        def half(side):
            return pick(first, 1, side) + pick(second, 1, side).astype(f32)

        away = half(1 - mine).astype(low_type)
        self.part = half(mine)
        self.pending = swap(away, "dp", self.bit)
        self.bit *= 2

    def absorb(self, got):
        self.pending, self.got = None, got
        if self.bit == lax.axis_size("dp"):
            self.value = (self.part + got.astype(f32)).reshape(self.rows, -1)


def advance(main, chains):
    live = [chain for chain in chains if chain.pending is not None]
    main, got = lax.optimization_barrier((main, [chain.pending for chain in live]))
    for chain, arrived in zip(live, got):
        chain.absorb(arrived)
    for chain in live:
        chain.launch()
    return main


def adam_update(weight, first, second, grad, rate):
    first = beta_one * first + (1 - beta_one) * grad
    second = beta_two * second + (1 - beta_two) * grad * grad
    first_hat = first / (1 - beta_one**STEP)
    second_hat = second / (1 - beta_two**STEP)
    weight = weight - rate * (first_hat / (jnp.sqrt(second_hat) + adam_eps) + weight_decay * weight)
    return (weight, first, second)


def place_spans(starts, places):
    covered = places[:, None] >= starts[None, :]
    number = jnp.sum(covered.astype(jnp.int32), -1) - 1
    return number, jnp.max(jnp.where(covered, starts[None, :], 0), -1)


def key_spans(number, starts, lengths, block):
    hot = number[:, None] == jnp.arange(starts.shape[0])[None, :]
    first = jnp.sum(jnp.where(hot, starts[None, :], 0), -1)
    last = jnp.sum(jnp.where(hot, (starts + lengths)[None, :], 0), -1)
    first_block = jnp.min(first.reshape(-1, block), -1) // key_block
    last_block = (jnp.max(last.reshape(-1, block), -1) + key_block - 1) // key_block
    return (
        jnp.stack([first, last]).astype(jnp.int32),
        jnp.stack([first_block, last_block]).astype(jnp.int32),
    )


def on_device(
    src_ids,
    tgt_ids,
    src_lengths,
    tgt_lengths,
    tgt_mask,
    attn_in,
    attn_in_m1,
    attn_in_m2,
    attn_out,
    attn_out_m1,
    attn_out_m2,
    ffn_in,
    ffn_in_m1,
    ffn_in_m2,
    ffn_out,
    ffn_out_m1,
    ffn_out_m2,
    len_head,
    len_head_m1,
    len_head_m2,
    norms,
    norms_m1,
    norms_m2,
    table,
    table_m1,
    table_m2,
):
    rows_here, seq_rows = src_ids.shape
    seqs, owners = lax.axis_size("seq"), lax.axis_size("dp")
    devices = seqs * owners
    row_len = seq_rows * seqs
    side = lax.axis_index("seq")
    group = seqs // rows_here
    span = row_len // group
    row, offset = side // group, (side % group) * span
    sharers = [[r * group + i for i in range(group)] for r in range(rows_here)]
    own_words, width = table.shape
    classes = len_head.shape[1]
    vocab_width = own_words * owners
    vocab_base = side * vocab_width
    norm_count = norms.shape[1]
    norm_columns = 128

    def columns_of(weight, rows):
        return [weight[at : at + rows] for at in range(0, weight.shape[0], rows)]

    def cut_parts(whole, parts):
        result, at = [], 0
        for part in parts:
            result.append(whole[:, at : at + part.shape[1]])
            at += part.shape[1]
        return result

    def gather_columns(parts):
        joined = jnp.concatenate([part.astype(low_type) for part in parts], 1)
        if joined.shape[0] % (16 * seqs) == 0:
            rows = joined.shape[0] // seqs
            joined = lax.dynamic_slice_in_dim(joined, side * rows, rows, 0)
            whole = lax.all_gather(joined, ("dp", "seq"), axis=0, tiled=True)
        else:
            whole = lax.all_gather(joined, "dp", axis=0, tiled=True)
        return cut_parts(whole, parts)

    def join_rows(pieces):
        blocks = [piece.reshape(owners, -1, piece.shape[1]) for piece in pieces]
        return jnp.concatenate(blocks, 1).reshape(-1, pieces[0].shape[1])

    share = attn_in.shape[1]
    norm_part = jnp.pad(
        norms.reshape(-1, norms.shape[2]).T, ((0, 0), (0, norm_columns - 2 * norm_count))
    )
    out_pieces = ffn_out.shape[1] // share
    parts = [attn_in[0], attn_out[0], len_head, norm_part, ffn_in[0]]
    parts += columns_of(ffn_out[0], share)
    parts += [attn_in[1], attn_out[1], attn_in[2], attn_out[2], ffn_in[1]]
    parts += columns_of(ffn_out[1], share)
    w_in0, w_out0, w_len, norm_low, f_in0, *others = gather_columns(parts)
    f_out0 = join_rows(others[:out_pieces])
    w_in1, w_out1, w_in2, w_out2, f_in1, *f_out1 = others[out_pieces:]
    f_out1 = join_rows(f_out1)
    table_low = table.astype(low_type)
    table_part = lax.all_gather(table_low, "dp", axis=0, tiled=True)
    norm_low = norm_low[:, : 2 * norm_count].T.astype(f32)
    gains, biases = norm_low[:norm_count], norm_low[norm_count:]

    ids = gather_seq(jnp.stack([src_ids, tgt_ids, tgt_mask]), 2).reshape(3, rows_here, row_len)
    src_starts = jnp.cumsum(src_lengths, -1) - src_lengths
    tgt_starts = jnp.cumsum(tgt_lengths, -1) - tgt_lengths
    places = jnp.arange(row_len)
    opens = jnp.any(places[None, :, None] == src_starts[:, None, :], -1)
    src_in = pick(jnp.where(opens, length_token, ids[0]).reshape(seqs, span), 0, side)
    masked = (ids[2] == 1).reshape(seqs, span)
    labels = ids[1].reshape(seqs, span)
    dec_in = pick(jnp.where(masked, mask_token, labels), 0, side)
    counts = jnp.sum(masked.astype(jnp.int32), -1)

    def slots_for(expected):
        return max(-(-expected // 16) * 16, 16)

    src_slots, dec_slots = slots_for(2 * span // devices), slots_for(3 * span // (2 * devices))

    def ask(token_ids, slots):
        same = token_ids[:, None] == token_ids[None, :]
        index = jnp.arange(span)
        earlier = index[None, :] < index[:, None]
        leader = jnp.logical_not(jnp.any(same & earlier, 1))
        holder = token_ids // own_words
        rank = jnp.sum(
            (earlier & leader[None, :] & (holder[:, None] == holder[None, :])).astype(jnp.int32), 1
        )
        rank = jnp.sum(jnp.where(same & leader[None, :], rank[None, :], 0), 1)
        return token_ids % own_words, holder, rank, slots

    def chosen_of(asked, turn):
        local, holder, rank, slots = asked
        code = jnp.where(rank // slots == turn, holder * slots + rank % slots, -1)
        return code[:, None] == jnp.arange(devices * slots)[None, :]

    def wanted_of(asked, chosen):
        return jnp.max(jnp.where(chosen, asked[0][:, None], -1), 0).reshape(devices, -1)

    def maps_of(chosen, wanted):
        held = wanted.reshape(-1)[:, None] == jnp.arange(own_words)[None, :]
        return chosen.astype(low_type), held.astype(low_type)

    def round_of(asked, turn):
        chosen = chosen_of(asked, turn)
        return maps_of(chosen, to_each(wanted_of(asked, chosen)))

    def send_rows(held):
        found = contract(held, table_low, 1, 0).astype(low_type)
        return to_each(found.reshape(devices, -1, width)).reshape(-1, width)

    def fetch(maps):
        chosen, held = maps
        return contract(send_rows(held), chosen, 0, 1)

    def give_rows(chosen, grads):
        sums = contract(chosen, grads.astype(low_type), 0, 1).astype(low_type)
        return to_each(sums.reshape(devices, -1, width)).reshape(-1, width)

    def give(maps, grads):
        return contract(maps[1], give_rows(maps[0], grads), 0, 0)

    def later_rounds(rounds, value, visit):
        return lax.fori_loop(1, rounds, lambda turn, carry: carry + visit(turn), value)

    src_ask, dec_ask = ask(src_in, src_slots), ask(dec_in, dec_slots)
    src_chosen, dec_chosen = chosen_of(src_ask, 0), chosen_of(dec_ask, 0)
    facts = jnp.stack(
        [
            jnp.sum(tgt_mask),
            jnp.max(counts),
            jnp.max(src_ask[2]) // src_slots + 1,
            jnp.max(dec_ask[2]) // dec_slots + 1,
        ]
    )
    facts = jnp.broadcast_to(jnp.pad(facts, (0, 12))[None, :], (devices, 16))
    asked = [wanted_of(src_ask, src_chosen), wanted_of(dec_ask, dec_chosen), facts]
    asked = to_each(jnp.concatenate(asked, 1).astype(jnp.int32))
    facts = asked[:, src_slots + dec_slots :]
    count = jnp.sum(facts[:, 0]).astype(f32)
    cut = -(-(span * 3 // 8) // 128) * 128
    more = jnp.max(facts[:, 1]) > cut
    src_rounds, dec_rounds = jnp.max(facts[:, 2]), jnp.max(facts[:, 3])
    src_maps = maps_of(src_chosen, asked[:, :src_slots])
    src_found = fetch(src_maps)
    dec_maps = maps_of(dec_chosen, asked[:, src_slots : src_slots + dec_slots])
    dec_rows = send_rows(dec_maps[1])

    starts_at = jnp.cumsum(counts) - counts
    total = jnp.sum(counts)
    rank = jnp.where(masked, jnp.cumsum(masked.astype(jnp.int32), -1) - 1, -1)
    slot_of = jnp.where(masked, rank + starts_at[:, None], -1)
    slot_index = jnp.arange(seqs * span)
    slot_label = jnp.sum(
        jnp.where(slot_of.reshape(1, -1) == slot_index[:, None], labels.reshape(1, -1), 0), -1
    )
    valid = slot_index < total
    targets = jnp.where(valid, slot_label - vocab_base, -1).reshape(1, -1)
    plan = jnp.concatenate([chunk_plan(total), lax.axis_index("dp")[None] & 1]).astype(jnp.int32)
    own_rank, own_slot = pick(rank, 0, side), pick(slot_of, 0, side)

    def packing(slots, rows):
        slot, index = jnp.arange(slots), jnp.arange(rows)
        far_start, far_count = pick(starts_at, 0, 1 - side), pick(counts, 0, 1 - side)
        far = jnp.where(index < far_count, index + far_start, -1)
        return (
            (own_rank[None, :] == index[:, None]).astype(low_type),
            (own_slot[None, :] == slot[:, None]).astype(low_type),
            (far[None, :] == slot[:, None]).astype(low_type),
        )

    own_places = offset + jnp.arange(span)
    src_start, src_length = pick(src_starts, 0, row), pick(src_lengths, 0, row)
    tgt_start, tgt_length = pick(tgt_starts, 0, row), pick(tgt_lengths, 0, row)
    src_number, src_open = place_spans(src_start, own_places)
    tgt_number, tgt_open = place_spans(tgt_start, own_places)
    block = min(query_block, span)
    enc_spans = key_spans(src_number, src_start, src_length, block)
    self_spans = key_spans(tgt_number, tgt_start, tgt_length, block)
    cross_spans = key_spans(tgt_number, src_start, src_length, block)
    src_wave, tgt_wave = lax.optimization_barrier(
        (sinusoid(own_places - src_open, width), sinusoid(own_places - tgt_open, width))
    )

    root = math.sqrt(width)
    src_found = later_rounds(src_rounds, src_found, lambda turn: fetch(round_of(src_ask, turn)))
    stream0 = src_found * root + src_wave

    def norm(stream, index):
        return layer_norm(stream, gains[index], biases[index])

    def keys_of_row(part):
        if group == 1:
            return part
        return lax.all_gather(part, "seq", axis=1, tiled=True, axis_index_groups=sharers)

    def keys_to_place(part):
        if group == 1:
            return part
        return lax.psum_scatter(
            part, "seq", scatter_dimension=1, tiled=True, axis_index_groups=sharers
        )

    def self_attention(inner, weight_in, weight_out, spans):
        triple = contract(weight_in, inner, 0, 0).astype(low_type)
        keys = triple if group == 1 else keys_of_row(triple[width:])
        mixed, lse = attend_forward(triple, keys, group == 1, *spans)
        return contract(weight_out, mixed, 0, 0), (triple, keys, mixed, lse)

    def self_attention_back(inner, weight_in, weight_out, spans, kept, grad, before, after):
        triple, keys, mixed, lse = kept
        grad_low = grad.astype(low_type)
        d_out = contract(mixed, grad_low, 1, 1)
        d_mixed = contract(weight_out, grad_low, 1, 0).astype(low_type)
        d_mixed = advance(d_mixed, before)
        d_query, d_keys = attend_backward(triple, keys, group == 1, *spans, lse, d_mixed)
        d_query, d_keys = advance((d_query, d_keys), after)
        d_triple = jnp.concatenate([d_query, keys_to_place(d_keys)], 0)
        return contract(weight_in, d_triple, 1, 0), contract(inner, d_triple, 1, 1), d_out

    def cross_attention(inner, memory, weight_in, weight_out, spans):
        queries = contract(weight_in[:, :width], inner, 0, 0).astype(low_type)
        keys = keys_of_row(contract(weight_in[:, width:], memory, 0, 0).astype(low_type))
        mixed, lse = attend_forward(queries, keys, False, *spans)
        return contract(weight_out, mixed, 0, 0), (queries, keys, mixed, lse)

    def cross_attention_back(inner, memory, weight_in, weight_out, spans, kept, grad, before, after):
        queries, keys, mixed, lse = kept
        grad_low = grad.astype(low_type)
        d_out = contract(mixed, grad_low, 1, 1)
        d_mixed = contract(weight_out, grad_low, 1, 0).astype(low_type)
        d_mixed = advance(d_mixed, before)
        d_query, d_keys = attend_backward(queries, keys, False, *spans, lse, d_mixed)
        d_query, d_keys = advance((d_query, d_keys), after)
        d_keys = keys_to_place(d_keys)
        d_in = jnp.concatenate([contract(inner, d_query, 1, 1), contract(memory, d_keys, 1, 1)], 1)
        return (
            contract(weight_in[:, :width], d_query, 1, 0),
            contract(weight_in[:, width:], d_keys, 1, 0),
            d_in,
            d_out,
        )

    def ffn(inner, weight_one, weight_two):
        hidden = contract(weight_one, inner, 0, 0)
        active = jax.nn.gelu(hidden).astype(low_type)
        return contract(weight_two, active, 0, 0), (hidden, active)

    def ffn_back(inner, weight_one, weight_two, kept, grad):
        hidden, active = kept
        grad_low = grad.astype(low_type)
        d_two = contract(active, grad_low, 1, 1)
        d_active = contract(weight_two, grad_low, 1, 0)
        d_hidden = jax.vjp(jax.nn.gelu, hidden)[1](d_active)[0].astype(low_type)
        return contract(weight_one, d_hidden, 1, 0), contract(inner, d_hidden, 1, 1), d_two

    inner0, norm0 = norm(stream0, 0)
    branch0, keep0 = self_attention(inner0, w_in0, w_out0, enc_spans)
    stream1 = stream0 + branch0
    stream1, dec_rows = lax.optimization_barrier((stream1, dec_rows))
    inner1, norm1 = norm(stream1, 1)
    branch1, keep1 = ffn(inner1, f_in0, f_out0)
    stream2 = stream1 + branch1
    memory, norm2 = norm(stream2, 2)
    memory, dec_chosen = lax.optimization_barrier((memory, dec_maps[0]))
    dec_found = contract(dec_rows, dec_chosen, 0, 1)
    dec_found = later_rounds(dec_rounds, dec_found, lambda turn: fetch(round_of(dec_ask, turn)))
    target0 = dec_found * root + tgt_wave
    inner3, norm3 = norm(target0, 3)
    branch3, keep3 = self_attention(inner3, w_in1, w_out1, self_spans)
    target1 = target0 + branch3
    inner4, norm4 = norm(target1, 4)
    branch4, keep4 = cross_attention(inner4, memory, w_in2, w_out2, cross_spans)
    target2 = target1 + branch4
    inner5, norm5 = norm(target2, 5)
    branch5, keep5 = ffn(inner5, f_in1, f_out1)
    target3 = target2 + branch5
    final, norm6 = norm(target3, 6)

    def pack(slots, rows):
        own_chosen, own_slots, far_slots = packing(slots, rows)
        far = swap(contract(own_chosen, final, 1, 1).astype(low_type), "seq", 1)
        packed = contract(own_slots, final, 1, 1) + contract(far_slots, far, 1, 0)
        return jnp.pad(packed.astype(low_type), ((0, seqs * span - slots), (0, 0)))

    def unpack(slots, rows):
        own_chosen, own_slots, far_slots = packing(slots, rows)
        high = lax.reduce_precision(d_pieces[:slots], 8, 7)
        rest = (d_pieces[:slots] - high).astype(low_type)
        high = high.astype(low_type)
        far = swap(contract(far_slots, high, 0, 0).astype(low_type), "seq", 1)
        return (
            contract(high, own_slots, 0, 0)
            + contract(rest, own_slots, 0, 0)
            + contract(far, own_chosen, 0, 0)
        )

    if seqs == 2:
        pieces = lax.cond(
            more, lambda: pack(2 * span, span), lambda: pack(min(2 * cut, 2 * span), cut)
        )
    else:
        own_slots = packing(seqs * span, span)[1]
        pieces = lax.psum(contract(own_slots, final, 1, 1), "seq").astype(low_type)
    turned = pieces.T
    every = gather_seq(head_stats(plan, table_part, turned), 0)
    top_logit = jnp.max(every[:, 0], 0)
    totals = jnp.sum(every[:, 1] * jnp.exp(every[:, 0] - top_logit[None]), 0)
    log_total = top_logit + jnp.log(jnp.where(valid, totals, 1.0))
    own_start = pick(starts_at, 0, side)
    mine = (slot_index >= own_start) & (slot_index < own_start + pick(counts, 0, side))
    token_local = jnp.sum(jnp.where(mine, log_total, 0.0))
    logs = jnp.where(valid, log_total + jnp.log(count), 1e30)
    weights = jnp.where(valid, 1.0 / count, 0.0)
    split = halving_fits(own_words, width // 2, False)
    *d_table, d_pieces, picks = head_back(
        plan, table_part, pieces, turned, targets, logs[None], weights[None], split and own_words
    )
    token_local = token_local - jnp.sum(picks)
    table_one = [TableChain(d_table[0], d_table[2])] if split else []
    if seqs == 2:
        d_final = lax.cond(
            more, lambda: unpack(2 * span, span), lambda: unpack(min(2 * cut, 2 * span), cut)
        )
    else:
        d_pieces = lax.psum(d_pieces, "seq")
        high = lax.reduce_precision(d_pieces, 8, 7)
        rest = (d_pieces - high).astype(low_type)
        d_final = contract(high.astype(low_type), own_slots, 0, 0) + contract(rest, own_slots, 0, 0)

    first_place = own_places[None, :] == src_start[:, None]
    mine = jnp.any(first_place, -1)
    first_rows = contract(first_place.astype(low_type), memory, 1, 1).astype(low_type)
    len_logits = contract(first_rows, w_len, 1, 0)
    len_label = jnp.minimum(tgt_length, classes - 1)
    len_hot = jnp.arange(classes)[None, :] == len_label[:, None]
    len_loss = jax.nn.logsumexp(len_logits, -1) - jnp.sum(jnp.where(len_hot, len_logits, 0.0), -1)
    len_local = jnp.sum(jnp.where(mine, len_loss, 0.0))
    sentences = rows_here * src_lengths.shape[1] * owners
    len_prob = jax.nn.softmax(len_logits, -1)
    d_len_logits = (
        jnp.where(mine[:, None], len_prob - len_hot.astype(f32), 0.0) * (0.1 / sentences)
    ).astype(low_type)
    d_w_len = contract(first_rows, d_len_logits, 0, 0)
    d_first = contract(d_len_logits, w_len, 1, 1)
    d_memory = lax.dot_general(
        d_first,
        first_place.astype(f32),
        (((0,), (0,)), ((), ())),
        precision=lax.Precision.HIGHEST,
        preferred_element_type=f32,
    )

    def owned(grad):
        return grad.reshape(owners, -1, grad.shape[1])

    def owned_columns(grad):
        whole = owned(grad)
        return [whole[:, at : at + share] for at in range(0, whole.shape[1], share)]

    d_target3, scale6 = norm_backward(norm6, gains[6], d_final)
    d_inner5, d_fin1, d_fout1 = ffn_back(inner5, f_in1, f_out1, keep5, d_target3)
    d_inner5, d_target3, d_table = advance((d_inner5, d_target3, d_table), table_one)
    table_two = [TableChain(d_table[1], d_table[3])] if split else []
    chain_a = LayerChain([owned(d_fin1)] + owned_columns(d_fout1))
    d_target2, scale5 = norm_backward(norm5, gains[5], d_inner5, d_target3)
    d_inner4, d_cross, d_win2, d_wout2 = cross_attention_back(
        inner4, memory, w_in2, w_out2, cross_spans, keep4, d_target2, [], table_one + [chain_a]
    )
    chain_b = LayerChain([owned(d_win2), owned(d_wout2)])
    d_target1, scale4 = norm_backward(norm4, gains[4], d_inner4, d_target2)
    d_inner3, d_win1, d_wout1 = self_attention_back(
        inner3,
        w_in1,
        w_out1,
        self_spans,
        keep3,
        d_target1,
        table_two,
        table_one + [chain_a, chain_b],
    )
    chain_c = LayerChain([owned(d_win1), owned(d_wout1)])
    d_target0, scale3 = norm_backward(norm3, gains[3], d_inner3, d_target1)
    d_stream2, scale2 = norm_backward(norm2, gains[2], d_memory + d_cross)
    d_stream2, d_target0 = advance((d_stream2, d_target0), [chain_b])
    dec_grad = d_target0 * root
    dec_sums = give_rows(dec_maps[0], dec_grad)
    d_inner1, d_fin0, d_fout0 = ffn_back(inner1, f_in0, f_out0, keep1, d_stream2)
    chains = table_one + table_two + [chain_a, chain_c]
    d_inner1, d_stream2 = advance((d_inner1, d_stream2), chains)
    chain_d = LayerChain([owned(d_fin0)] + owned_columns(d_fout0))
    d_stream1, scale1 = norm_backward(norm1, gains[1], d_inner1, d_stream2)
    d_inner0, d_win0, d_wout0 = self_attention_back(
        inner0,
        w_in0,
        w_out0,
        enc_spans,
        keep0,
        d_stream1,
        table_two + [chain_b, chain_c, chain_d],
        table_two + [chain_a, chain_c, chain_d],
    )
    chain_e = LayerChain([owned(d_win0), owned(d_wout0), owned(d_w_len)])
    d_stream0, scale0 = norm_backward(norm0, gains[0], d_inner0, d_stream1)
    d_stream0 = advance(d_stream0, [chain_b, chain_c, chain_e])
    src_grad = d_stream0 * root
    src_sums = give_rows(src_maps[0], src_grad)
    norm_share = norms.shape[2]
    scales = jnp.stack([scale0, scale1, scale2, scale3, scale4, scale5, scale6], 1)
    scales = scales.reshape(2 * norm_count, owners, norm_share).transpose(1, 0, 2)
    scales = jnp.broadcast_to(scales[None], (seqs,) + scales.shape)
    scales = to_each(scales.reshape((devices,) + scales.shape[2:]))
    chains = table_one + table_two + [chain_a, chain_b, chain_c, chain_d, chain_e]
    src_sums, dec_sums = advance((src_sums, dec_sums), chains)
    scales = advance(scales, chains)
    while any(chain.pending is not None for chain in chains):
        advance((), chains)
    layer_chains = [chain_a, chain_b, chain_c, chain_d, chain_e]
    for chain in layer_chains:
        chain.finish()

    g_norms = jnp.sum(scales, 0)
    norm_square = jnp.where(side == 0, jnp.sum(g_norms * g_norms), 0.0)
    given = contract(dec_maps[1], dec_sums, 0, 0) + contract(src_maps[1], src_sums, 0, 0)
    given = later_rounds(
        jnp.maximum(src_rounds, dec_rounds),
        given,
        lambda turn: give(round_of(dec_ask, turn), dec_grad)
        + give(round_of(src_ask, turn), src_grad),
    )
    if split:
        table_grad = jnp.concatenate([chain.value for chain in table_one + table_two], 1)
    else:
        table_grad = lax.psum_scatter(d_table[0], "dp", scatter_dimension=0, tiled=True)
    table_grad = table_grad + given
    square = sum(chain.square for chain in layer_chains)
    square = square + jnp.sum(table_grad * table_grad) + norm_square
    sums = jnp.pad(jnp.stack([token_local, len_local, square]), (0, 5))
    sums = jnp.sum(to_each(jnp.broadcast_to(sums[None], (devices, 8))), 0)
    token_sum, len_sum, grad_norm = sums[0], sums[1], jnp.sqrt(sums[2])
    factor = jnp.minimum(1.0, clip_limit / (grad_norm + 1e-06))

    def cut_columns(chain, sizes):
        result, at = [], 0
        value = chain.value.reshape(share, -1)
        for size in sizes:
            result.append(value[:, at : at + size])
            at += size
        return result

    hidden_width = ffn_in.shape[2]
    ffn_sizes = [hidden_width] + [width] * out_pieces
    attn_sizes = [3 * width, width]
    g_fin1, *g_fout1 = cut_columns(chain_a, ffn_sizes)
    g_win2, g_wout2 = cut_columns(chain_b, attn_sizes)
    g_win1, g_wout1 = cut_columns(chain_c, attn_sizes)
    g_fin0, *g_fout0 = cut_columns(chain_d, ffn_sizes)
    g_win0, g_wout0, g_len = cut_columns(chain_e, attn_sizes + [classes])
    grads = (
        jnp.stack([g_win0, g_win1, g_win2]),
        jnp.stack([g_wout0, g_wout1, g_wout2]),
        jnp.stack([g_fin0, g_fin1]),
        jnp.stack([jnp.concatenate(g_fout0, 0), jnp.concatenate(g_fout1, 0)]),
        g_len,
        g_norms.reshape(norms.shape),
        table_grad,
    )
    masters = (attn_in, attn_out, ffn_in, ffn_out, len_head, norms, table)
    firsts = (attn_in_m1, attn_out_m1, ffn_in_m1, ffn_out_m1, len_head_m1, norms_m1, table_m1)
    seconds = (attn_in_m2, attn_out_m2, ffn_in_m2, ffn_out_m2, len_head_m2, norms_m2, table_m2)
    updates = []
    for weight, first, second, grad, rate in zip(masters, firsts, seconds, grads, step_rates):
        updates.extend(adam_update(weight, first, second, grad * factor, rate))
    return (token_sum, count, len_sum, grad_norm, *updates)


def solution(mesh):
    layer, head, scales, words = P(None, "dp", None), P("dp", None), P(None, None, "dp"), P(("seq", "dp"), None)
    owned = (layer,) * 12 + (head,) * 3 + (scales,) * 3 + (words,) * 3
    ids, lengths = P("dp", "seq"), P("dp", None)
    in_specs = (ids, ids, lengths, lengths, ids) + owned
    out_specs = (P(), P(), P(), P()) + owned
    return jax.shard_map(
        on_device, mesh=mesh, in_specs=in_specs, out_specs=out_specs, check_vma=False
    )
```
